32 devices in a mesh: tm: 8 (over z, x), chan: 4 (over y, core).
Axes of the slice: x: 2, y: 2, z: 4, core: 2. Of those that a mesh axis runs over, the one named last changes fastest.
Arguments:
- features: bfloat16 [512, 4, 512], P('tm', None, 'chan'), may hold values from -6 to 6
- conv1_weight: bfloat16 [3, 3, 512, 1024], P(None, None, None, 'chan'), may hold values from -0.09375 to 0.09375
- norm1_gain: float32 [1024], P('chan'), may hold values from 0.1 to 1.9
- norm1_bias: float32 [1024], P('chan'), may hold values from -0.5 to 0.5
- conv2_weight: bfloat16 [3, 3, 1024, 1024], P(None, None, None, 'chan'), may hold values from -0.0625 to 0.0625
- norm2_gain: float32 [1024], P('chan'), may hold values from 0.1 to 1.9
- norm2_bias: float32 [1024], P('chan'), may hold values from -0.5 to 0.5
- clip_starts: int32 [3], replicated, may hold values from 0 to 506, as said below
- valid: int32 [512], P('tm'), may hold values from 0 to 1, as said below
- readout_grad: float32 [256, 1024], P('tm', 'chan'), may hold values from -6 to 6
Outputs:
- readout: float32 [256, 1024], P('tm', 'chan')
- features_grad: float32 [512, 4, 512], P('tm', None, 'chan')
- conv1_weight_grad: float32 [3, 3, 512, 1024], P(None, None, None, 'chan')
- norm1_gain_grad: float32 [1024], P('chan')
- norm1_bias_grad: float32 [1024], P('chan')
- conv2_weight_grad: float32 [3, 3, 1024, 1024], P(None, None, None, 'chan')
- norm2_gain_grad: float32 [1024], P('chan')
- norm2_bias_grad: float32 [1024], P('chan')
The draws below stay inside these ranges and needn't reach their ends.
Inputs may be any that keep to these rules, and one draw needn't show every extreme that they name: `clip_starts`: increasing even frame numbers, the first 0. Every clip has 6 to 32 frames, except one that begins within the first 64 frames and ends within the last 64. `valid`: within each clip, 1 on the leading frames and 0 on a tail of even length; the first two frames of every clip are 1; the clip that crosses the stream ends in a tail of 0s.
All inputs are finite; a program needn't handle non-finite values.
Results may differ from the reference program's by a relative error of at most 0.0054.
Values may be sent and summed in bfloat16 or wider, within the bound.
No kernel may reach another device: no remote copies, remote signals or barrier semaphores. Data moves between devices by JAX's collectives and lax.ppermute only.
A program may use at most 128 MiB of HBM per device.

```python
import jax
import jax.numpy as jnp
from jax import lax

C0 = 512
C1 = 1024
M = 4
CLIP_MIN = 6
CLIP_MAX = 32
SIDE = 1
NSEG = 3
NFRAMES = 512
NPOOL = 256


def clip_plan(key):
    length_key = jax.random.fold_in(key, 11)
    trim_key = jax.random.fold_in(key, 12)
    long_key = jax.random.fold_in(key, 13)
    step_count = (CLIP_MAX - CLIP_MIN) // 2 + 1
    lengths = CLIP_MIN + 2 * jax.random.randint(length_key, (2 * SIDE,), 0, step_count)
    leading = lengths[:SIDE]
    trailing = lengths[SIDE:]
    long_start = jnp.sum(leading)
    tail_begin = NFRAMES - jnp.sum(trailing)
    starts = jnp.concatenate([jnp.cumsum(leading) - leading, long_start[None], tail_begin + jnp.cumsum(trailing) - trailing]).astype(jnp.int32)
    clip_spans = jnp.concatenate([leading, (tail_begin - long_start)[None], trailing]).astype(jnp.int32)
    random_bits = jax.random.randint(trim_key, (NSEG,), 0, 1 << 20)
    short_trim = 2 * (random_bits % ((clip_spans - 2) // 2 + 1))
    long_trim = 2 + 2 * jax.random.randint(long_key, (), 0, NFRAMES // 8)
    clip_trims = jnp.where(jnp.arange(NSEG) == SIDE, long_trim, short_trim).astype(jnp.int32)
    return (starts, clip_spans, clip_trims)


def draw_clip_starts(key, part):
    starts, clip_spans, clip_trims = clip_plan(key)
    return starts


def draw_valid(key, part):
    starts, clip_spans, clip_trims = clip_plan(key)
    position = jnp.arange(NFRAMES, dtype=jnp.int32)
    segment = jnp.sum((starts[None, :] <= position[:, None]).astype(jnp.int32), axis=1) - 1
    offset = position - starts[segment]
    live_frames = clip_spans[segment] - clip_trims[segment]
    return (offset < live_frames).astype(jnp.int32)


def block_levels(key, shape, shards, smallest, high):
    level = 1.0
    for dim, blocks in shards:
        draws = jax.random.uniform(jax.random.fold_in(jax.random.fold_in(key, 6), dim), (blocks,), jnp.float32, smallest / len(shards), high / len(shards))
        level = level * jnp.repeat(jnp.exp(draws), shape[dim] // blocks).reshape((-1,) + (1,) * (len(shape) - 1 - dim))
    return level


def scatter_about(stream_key, shape, deviation, bound, pieces=(), kind=jnp.bfloat16):
    values = deviation * jax.random.normal(stream_key, shape, jnp.float32)
    if pieces:
        values = values * block_levels(stream_key, shape, pieces, -0.22, 0.18)
    return jnp.clip(values, -bound, bound).astype(kind)


def setup_inputs(seed: int = 0) -> dict:
    key_of = jax.random.split(jax.random.key(seed), 11)
    return {
        "features": scatter_about(key_of[0], (NFRAMES, M, C0), 1.0, 6.0, ((0, 8), (2, 4))),
        "conv1_weight": scatter_about(key_of[1], (3, 3, C0, C1), (9 * C0) ** -0.5, 0.09375, ((3, 4),)),
        "norm1_gain": jnp.clip(1.0 + 0.18 * jax.random.normal(key_of[2], (C1,), jnp.float32), 0.1, 1.9),
        "norm1_bias": jnp.clip(jax.random.uniform(key_of[3], (C1,), jnp.float32, -0.5, 0.5) * block_levels(key_of[3], (C1,), ((0, 4),), -0.4, 0.0), -0.5, 0.5),
        "conv2_weight": scatter_about(key_of[4], (3, 3, C1, C1), (9 * C1) ** -0.5, 0.0625, ((3, 4),)),
        "norm2_gain": jnp.clip(1.0 + 0.18 * jax.random.normal(key_of[5], (C1,), jnp.float32), 0.1, 1.9),
        "norm2_bias": jnp.clip(jax.random.uniform(key_of[6], (C1,), jnp.float32, -0.5, 0.5) * block_levels(key_of[6], (C1,), ((0, 4),), -0.4, 0.0), -0.5, 0.5),
        "clip_starts": draw_clip_starts(jax.random.fold_in(key_of[10], 71), 0),
        "valid": draw_valid(jax.random.fold_in(key_of[10], 71), 0),
        "readout_grad": scatter_about(key_of[9], (NPOOL, C1), 1.0, 6.0, ((0, 8), (1, 4)), jnp.float32),
    }


EPS = 1e-05
highest = lax.Precision.HIGHEST

@jax.custom_vjp
def low(v):
    return lax.optimization_barrier(v.astype(jnp.bfloat16)).astype(jnp.float32)

@jax.custom_vjp
def low_back(v):
    return v

def low_keep(v):
    return (low(v), None)

def low_pass(kept, grad):
    return (grad,)

def back_keep(v):
    return (v, None)

def back_low(kept, grad):
    return (low(grad),)
low.defvjp(low_keep, low_pass)
low_back.defvjp(back_keep, back_low)

def frame_segments(clip_starts):
    position = jnp.arange(NFRAMES, dtype=jnp.int32)
    segment = lax.optimization_barrier(jnp.sum((clip_starts[None, :] <= position[:, None]).astype(jnp.int32), axis=1)) - 1
    closed = jnp.zeros((1,), dtype=bool)
    before_same = jnp.concatenate([closed, segment[1:] == segment[:-1]])
    after_same = jnp.concatenate([segment[:-1] == segment[1:], closed])
    return (segment, before_same, after_same)

@jax.checkpoint
def convolve(field_in, weight, before_same, after_same):
    frame_count = field_in.shape[0]
    mel_count = field_in.shape[1]
    padded = jnp.pad(field_in, ((1, 1), (1, 1), (0, 0)))
    factors = (before_same.astype(jnp.float32), jnp.ones((frame_count,), jnp.float32), after_same.astype(jnp.float32))
    result = jnp.zeros((frame_count, mel_count, weight.shape[3]), jnp.float32)
    for tap_row in range(3):
        partial_value = jnp.zeros((frame_count * mel_count, weight.shape[3]), jnp.float32)
        for tap_col in range(3):
            window = padded[tap_row:tap_row + frame_count, tap_col:tap_col + mel_count, :].reshape(frame_count * mel_count, -1)
            partial_value = partial_value + jnp.dot(window, weight[tap_row, tap_col], precision=highest, preferred_element_type=jnp.float32)
        result = result + partial_value.reshape(frame_count, mel_count, -1) * factors[tap_row][:, None, None]
    return result

def normalize(field_in, gain_vec, shift_vec, keep_cube, pixel_count):
    value_sums = lax.optimization_barrier(jnp.sum(field_in * keep_cube, axis=(0, 1)))
    squares = lax.optimization_barrier(jnp.sum(field_in * field_in * keep_cube, axis=(0, 1)))
    center = value_sums / pixel_count
    variance = squares / pixel_count - center * center
    return gain_vec * (field_in - center) * lax.rsqrt(variance + EPS) + shift_vec

def join_runs(earlier_item, later_item):
    first_flag, first_count, first_total, first_expsum = earlier_item
    second_flag, second_count, second_total, second_expsum = later_item
    wide_flag = second_flag[..., None]
    return (first_flag | second_flag, jnp.where(second_flag, second_count, first_count + second_count), jnp.where(wide_flag, second_total, first_total + second_total), jnp.where(wide_flag, second_expsum, first_expsum + second_expsum))

def passing(pooled, pooled_keep, run_start):
    exponent = jnp.exp(pooled)
    items = (run_start, pooled_keep, pooled_keep[:, None] * pooled, pooled_keep[:, None] * exponent)
    flags_out, counts, totals, expsums = lax.associative_scan(join_runs, items)
    return totals / counts[:, None] + jnp.log(expsums)

def reference(features, conv1_weight, norm1_gain, norm1_bias, conv2_weight, norm2_gain, norm2_bias, clip_starts, valid, readout_grad):
    segment, before_same, after_same = frame_segments(clip_starts)
    keep_mask = valid.astype(jnp.float32)
    keep_cube = keep_mask[:, None, None]
    pixel_count = jnp.sum(keep_mask) * M
    pooled_keep = keep_mask[0::2]
    pooled_segment = segment[0::2]
    run_start = jnp.concatenate([jnp.ones((1,), dtype=bool), pooled_segment[1:] != pooled_segment[:-1]])

    def forward(inputs, weight_one, gain_one, shift_one, weight_two, gain_two, shift_two):
        first_pre = low_back(convolve(inputs * keep_cube, weight_one, before_same, after_same))
        first_norm = normalize(first_pre, gain_one, shift_one, keep_cube, pixel_count)
        hidden = low(jax.nn.gelu(first_norm, approximate=False) * keep_cube)
        second_pre = low_back(convolve(hidden, weight_two, before_same, after_same))
        second_norm = normalize(second_pre, gain_two, shift_two, keep_cube, pixel_count)
        output = jax.nn.gelu(second_norm, approximate=False) * keep_cube
        pooled = output.reshape(NFRAMES // 2, 2, M, C1).mean(axis=(1, 2))
        return passing(pooled, pooled_keep, run_start)
    primals = (features.astype(jnp.float32), conv1_weight.astype(jnp.float32), norm1_gain, norm1_bias, conv2_weight.astype(jnp.float32), norm2_gain, norm2_bias)
    readout, pullback = jax.vjp(forward, *primals)
    gradients = pullback(readout_grad)
    return (readout, gradients[0], gradients[1], gradients[2], gradients[3], gradients[4], gradients[5], gradients[6])
```

```python
import functools

import jax
import jax.numpy as jnp
from jax import lax
from jax.experimental import pallas as pl
from jax.experimental.pallas import tpu as pltpu
from jax.sharding import PartitionSpec as P

EPS = 1e-05
highest = lax.Precision.HIGHEST
f32 = jnp.float32
bf16 = jnp.bfloat16


def padded_2(shard, sides, width):
    for axis, dim in sides:
        count, length = (lax.axis_size(axis), shard.shape[dim])
        up = [(i, (i + 1) % count) for i in range(count - 1)]
        down = [(j, i) for i, j in up]
        last = lax.slice_in_dim(shard, length - width, length, axis=dim)
        leading = lax.slice_in_dim(shard, 0, width, axis=dim)
        before = lax.ppermute(last, axis, up)
        after = lax.ppermute(leading, axis, down)
        shard = jnp.concatenate([before, shard, after], axis=dim)
    return shard


def entering(part, axis, combine, identity, reverse):
    count = lax.axis_size(axis)
    place = lax.axis_index(axis)
    ahead = count - 1 - place if reverse else place
    gathered = jax.tree.map(lambda a: lax.all_gather(a, axis), part)
    state = jax.tree.map(lambda a, e: jnp.zeros_like(a) + jnp.asarray(e, a.dtype), part, identity)

    def one(step, state):
        source = count - 1 - step if reverse else step
        return combine(
            state, jax.tree.map(lambda a: lax.dynamic_index_in_dim(a, source, 0, False), gathered)
        )

    return lax.fori_loop(0, ahead, one, state)


def frame_flags(clip_starts, first_frame, frame_count, frame_total):
    position = first_frame - 2 + jnp.arange(frame_count + 4, dtype=jnp.int32)
    segment = jnp.sum((clip_starts[None, :] <= position[:, None]).astype(jnp.int32), axis=1) - 1
    inside = (position >= 0) & (position < frame_total)
    middle = segment[1:-1]
    before_same = inside[1:-1] & inside[:-2] & (middle == segment[:-2])
    after_same = inside[1:-1] & inside[2:] & (middle == segment[2:])
    return (segment[2:-2], before_same, after_same)


def conv_forward(padded, weight, factors):
    frame_count = padded.shape[0] - 2
    mel_count = padded.shape[1]
    wide_field = jnp.pad(padded, ((0, 0), (1, 1), (0, 0)))
    result = jnp.zeros((frame_count, mel_count, weight.shape[3]), jnp.float32)
    for tap_row in range(3):
        partial_value = jnp.zeros((frame_count * mel_count, weight.shape[3]), jnp.float32)
        for tap_col in range(3):
            window = wide_field[
                tap_row : tap_row + frame_count, tap_col : tap_col + mel_count, :
            ].reshape(frame_count * mel_count, -1)
            partial_value = partial_value + jnp.dot(
                window, weight[tap_row, tap_col], preferred_element_type=jnp.float32
            )
        result = (
            result
            + partial_value.reshape(frame_count, mel_count, -1) * factors[tap_row][:, None, None]
        )
    return result


def conv_weight_grad(padded, grad_out, factors):
    frame_count = grad_out.shape[0]
    mel_count = grad_out.shape[1]
    wide_field = jnp.pad(padded, ((0, 0), (1, 1), (0, 0)))
    rows_out = []
    for tap_row in range(3):
        scaled = (grad_out * factors[tap_row][:, None, None].astype(jnp.bfloat16)).reshape(
            frame_count * mel_count, -1
        )
        taps_out = []
        for tap_col in range(3):
            window = wide_field[
                tap_row : tap_row + frame_count, tap_col : tap_col + mel_count, :
            ].reshape(frame_count * mel_count, -1)
            taps_out.append(
                lax.dot_general(
                    window, scaled, (((0,), (0,)), ((), ())), preferred_element_type=jnp.float32
                )
            )
        rows_out.append(jnp.stack(taps_out))
    return jnp.stack(rows_out)


def conv_input_grad(grad_padded, weight, edge_factors):
    frame_count = grad_padded.shape[0] - 2
    mel_count = grad_padded.shape[1]
    wide_field = jnp.pad(grad_padded, ((0, 0), (1, 1), (0, 0)))
    result = jnp.zeros((frame_count * mel_count, weight.shape[2]), jnp.float32)
    for tap_row in range(3):
        scaled = wide_field * edge_factors[tap_row][:, None, None]
        for tap_col in range(3):
            window = scaled[
                2 - tap_row : 2 - tap_row + frame_count, 2 - tap_col : 2 - tap_col + mel_count, :
            ].reshape(frame_count * mel_count, -1)
            result = result + lax.dot_general(
                window,
                weight[tap_row, tap_col],
                (((1,), (1,)), ((), ())),
                preferred_element_type=jnp.float32,
            )
    return result.reshape(frame_count, mel_count, -1)


def join_keyed(earlier_item, later_item):
    keep_first = later_item[0] < 0.0
    same_key = later_item[0] == earlier_item[0]
    merged = [jnp.where(keep_first, earlier_item[0], later_item[0])]
    for first_part, second_part in zip(earlier_item[1:], later_item[1:]):
        extra = (1,) * (first_part.ndim - keep_first.ndim)
        keep_wide = jnp.reshape(keep_first, keep_first.shape + extra)
        same_wide = jnp.reshape(same_key, same_key.shape + extra)
        merged.append(
            jnp.where(
                keep_wide, first_part, jnp.where(same_wide, first_part + second_part, second_part)
            )
        )
    return tuple(merged)


def smooth(argument):
    return jax.nn.gelu(argument, approximate=False)


def split_frames(
    features,
    conv1_weight,
    norm1_gain,
    norm1_bias,
    conv2_weight,
    norm2_gain,
    norm2_bias,
    clip_starts,
    valid,
    readout_grad,
):
    frame_count = features.shape[0]
    mel_count = features.shape[1]
    cycle_size = lax.axis_size("tm")
    cycle_index = lax.axis_index("tm")
    segment, before_same, after_same = frame_flags(
        clip_starts, cycle_index * frame_count, frame_count, frame_count * cycle_size
    )
    keep_mask = valid.astype(jnp.float32)
    keep_cube = keep_mask[:, None, None]
    own_factors = (
        before_same[1:-1].astype(jnp.float32),
        jnp.ones((frame_count,), jnp.float32),
        after_same[1:-1].astype(jnp.float32),
    )
    edge_factors = (
        before_same.astype(jnp.bfloat16),
        jnp.ones((frame_count + 2,), jnp.bfloat16),
        after_same.astype(jnp.bfloat16),
    )
    local_count = jnp.sum(keep_mask) * mel_count

    def spread(shard):
        padded = padded_2(shard, (("tm", 0),), 1)
        return lax.all_gather(padded, "chan", axis=2, tiled=True)

    def normalize(field_in, gain_vec, shift_vec):
        value_sums, squares, pixel_count = lax.psum(
            (
                jnp.sum(field_in * keep_cube, axis=(0, 1)),
                jnp.sum(field_in * field_in * keep_cube, axis=(0, 1)),
                local_count,
            ),
            "tm",
        )
        center = value_sums / pixel_count
        variance = squares / pixel_count - center * center
        inverse_std = lax.rsqrt(variance + EPS)
        normed = (field_in - center) * inverse_std
        return (gain_vec * normed + shift_vec, normed, inverse_std, pixel_count)

    def norm_back(grad_norm, normed, inverse_std, gain_vec, pixel_count):
        bias_grad, gain_grad = lax.psum(
            (jnp.sum(grad_norm, axis=(0, 1)), jnp.sum(grad_norm * normed, axis=(0, 1))), "tm"
        )
        grad_pre = (
            keep_cube
            * (gain_vec * inverse_std)
            * (grad_norm - bias_grad / pixel_count - normed * (gain_grad / pixel_count))
        )
        return (grad_pre.astype(jnp.bfloat16), gain_grad, bias_grad)

    def send_back(grad_pre, weight):
        padded = padded_2(grad_pre, (("tm", 0),), 1)
        partial_sum = conv_input_grad(padded, weight, edge_factors)
        return lax.psum_scatter(partial_sum, "chan", scatter_dimension=2, tiled=True)

    wide_in = spread(features * keep_cube.astype(jnp.bfloat16))
    first_pre = conv_forward(wide_in, conv1_weight, own_factors)
    first_norm, first_hat, first_scale, pixel_count = normalize(first_pre, norm1_gain, norm1_bias)
    first_act, first_pull = jax.vjp(smooth, first_norm)
    hidden = (first_act * keep_cube).astype(jnp.bfloat16)
    wide_mid = spread(hidden)
    second_pre = conv_forward(wide_mid, conv2_weight, own_factors)
    second_norm, second_hat, second_scale, pixel_count = normalize(
        second_pre, norm2_gain, norm2_bias
    )
    second_act, second_pull = jax.vjp(smooth, second_norm)
    pooled = (second_act * keep_cube).reshape(frame_count // 2, 2, mel_count, -1).mean(axis=(1, 2))
    pooled_keep = keep_mask[0::2]
    pooled_segment = segment[0::2]
    segment_key = pooled_segment.astype(jnp.float32)
    row_order = jnp.arange(frame_count // 2)
    lower_runs = (
        (pooled_segment[:, None] == pooled_segment[None, :])
        & (row_order[:, None] >= row_order[None, :])
    ).astype(jnp.float32)
    exponent = jnp.exp(pooled)
    counts = jnp.dot(lower_runs, pooled_keep, precision=highest)
    totals = jnp.dot(lower_runs, pooled_keep[:, None] * pooled, precision=highest)
    expsums = jnp.dot(lower_runs, pooled_keep[:, None] * exponent, precision=highest)
    zero_row = jnp.zeros_like(totals[0])
    prior_runs = entering(
        (segment_key[-1], counts[-1], totals[-1], expsums[-1]),
        "tm",
        join_keyed,
        (jnp.float32(-1.0), jnp.float32(0.0), zero_row, zero_row),
        False,
    )
    joined = (segment_key == prior_runs[0]).astype(jnp.float32)
    counts = counts + joined * prior_runs[1]
    totals = totals + joined[:, None] * prior_runs[2]
    expsums = expsums + joined[:, None] * prior_runs[3]
    readout = totals / counts[:, None] + jnp.log(expsums)
    by_count = readout_grad / counts[:, None]
    by_expsum = readout_grad / expsums
    later_mean = lax.dot_general(lower_runs, by_count, (((0,), (0,)), ((), ())), precision=highest)
    later_soft = lax.dot_general(lower_runs, by_expsum, (((0,), (0,)), ((), ())), precision=highest)
    beyond = entering(
        (segment_key[0], later_mean[0], later_soft[0]),
        "tm",
        join_keyed,
        (jnp.float32(-1.0), zero_row, zero_row),
        True,
    )
    joined_back = (segment_key == beyond[0]).astype(jnp.float32)[:, None]
    later_mean = later_mean + joined_back * beyond[1]
    later_soft = later_soft + joined_back * beyond[2]
    pooled_grad = pooled_keep[:, None] * (later_mean + exponent * later_soft)
    spread_grad = jnp.broadcast_to(
        (pooled_grad / (2 * mel_count))[:, None, None, :],
        (frame_count // 2, 2, mel_count, pooled_grad.shape[1]),
    )
    act_grad = spread_grad.reshape(frame_count, mel_count, -1) * keep_cube
    second_grad_norm = second_pull(act_grad)[0]
    second_grad_pre, gain2_grad, bias2_grad = norm_back(
        second_grad_norm, second_hat, second_scale, norm2_gain, pixel_count
    )
    weight2_grad = conv_weight_grad(wide_mid, second_grad_pre, own_factors)
    weight2_grad = lax.psum(weight2_grad, "tm")
    hidden_grad = send_back(second_grad_pre, conv2_weight)
    first_grad_norm = first_pull(hidden_grad * keep_cube)[0]
    first_grad_pre, gain1_grad, bias1_grad = norm_back(
        first_grad_norm, first_hat, first_scale, norm1_gain, pixel_count
    )
    weight1_grad = conv_weight_grad(wide_in, first_grad_pre, own_factors)
    weight1_grad = lax.psum(weight1_grad, "tm")
    input_grad = send_back(first_grad_pre, conv1_weight) * keep_cube
    return (
        readout,
        input_grad,
        weight1_grad,
        gain1_grad,
        bias1_grad,
        weight2_grad,
        gain2_grad,
        bias2_grad,
    )


ABSENT = 1024.0
ROWS = 32
TILE = 8
LANES = 128


def whole_spec():
    return pl.BlockSpec(memory_space=pltpu.VMEM)


def place_spec():
    return pl.BlockSpec(memory_space=pl.ANY)


def scalar_spec():
    return pl.BlockSpec(memory_space=pltpu.SMEM)


def call(body, operands, in_specs, outs, out_specs, scratch, flops, megabytes):
    return pl.pallas_call(
        body,
        out_shape=tuple(jax.ShapeDtypeStruct(s, d) for s, d in outs),
        in_specs=in_specs,
        out_specs=tuple(out_specs),
        scratch_shapes=scratch,
        compiler_params=pltpu.CompilerParams(vmem_limit_bytes=megabytes * 2**20),
        cost_estimate=pl.CostEstimate(flops=flops, bytes_accessed=2**22, transcendentals=0),
    )(*operands)


def swap(shard, axis, bit):
    count = lax.axis_size(axis)
    return lax.ppermute(shard, axis, [(i, i ^ bit) for i in range(count)])


def swap_both(shard, first, first_bit, second, second_bit):
    rows, columns = lax.axis_size(first), lax.axis_size(second)
    pairs = [
        (i * columns + j, (i ^ first_bit) * columns + (j ^ second_bit))
        for i in range(rows)
        for j in range(columns)
    ]
    return lax.ppermute(shard, (first, second), pairs)


def same_clip(starts, at, shape, total):
    frame = lax.broadcasted_iota(jnp.int32, shape, 0) + at
    before = frame != starts[0]
    after = frame != total - 1
    for k in range(1, starts.shape[0]):
        before = before & (frame != starts[k])
        after = after & (frame != starts[k] - 1)
    return before, after


def widen(mask, width):
    return jnp.concatenate([mask] * (width // mask.shape[1]), axis=1)


def fold(value):
    total = value[:TILE]
    for k in range(TILE, value.shape[0], TILE):
        total = total + value[k : k + TILE]
    return total


def column_sum(value):
    return jnp.sum(value, axis=0, keepdims=True)


def taps(mel, mel_count):
    return [b for b in range(3) if 0 <= mel + b - 1 < mel_count]


def convolve(fields, weights, lower, middle, upper, total, add):
    mel_count = middle.shape[0]
    for m in range(mel_count):
        for a in range(3):
            acc = None
            for field, weight in zip(fields, weights):
                for b in taps(m, mel_count):
                    part = jnp.dot(field(m + b - 1), weight(a, b), preferred_element_type=f32)
                    acc = part if acc is None else acc + part
            if a == 0:
                lower[m, TILE : TILE + total] = acc
            elif a == 1:
                middle[m] = middle[m] + acc if add else acc
            else:
                upper[m, TILE : TILE + total] = acc


def convolve_back(fields, weights, lower, middle, upper, total):
    mel_count = middle.shape[0]
    for n in range(mel_count):
        for a in range(3):
            acc = None
            for field, weight in zip(fields, weights):
                for b in range(3):
                    if 0 <= n - b + 1 < mel_count:
                        part = lax.dot_general(
                            field(n - b + 1),
                            weight(a, b),
                            (((1,), (1,)), ((), ())),
                            preferred_element_type=f32,
                        )
                        acc = part if acc is None else acc + part
            if a == 2:
                lower[n, TILE : TILE + total] = acc
            elif a == 1:
                middle[n] = acc
            else:
                upper[n, TILE : TILE + total] = acc


def joined(lower, middle, upper, m, at, before, after):
    low = lower[m, pl.ds(at, ROWS + 2 * TILE)]
    high = upper[m, pl.ds(at, ROWS + 2 * TILE)]
    return (
        middle[m, pl.ds(at, ROWS)]
        + jnp.where(before, low[TILE - 1 : TILE - 1 + ROWS], 0.0)
        + jnp.where(after, high[TILE + 1 : TILE + 1 + ROWS], 0.0)
    )


def by_rows(total, body, init):
    return lax.fori_loop(
        0, total // ROWS, lambda i, c: body(pl.multiple_of(i * ROWS, ROWS), c), init
    )


def clear_edges(lower, upper, total):
    for m in range(lower.shape[0]):
        for ref in (lower, upper):
            ref[m, :TILE] = jnp.zeros((TILE, ref.shape[2]), f32)
            ref[m, TILE + total :] = jnp.zeros((TILE, ref.shape[2]), f32)


def moments(field, keep, count):
    first, second = column_sum(field[0]), column_sum(field[1])
    center = first / count
    return center, lax.rsqrt(second / count - center * center + EPS)


def phi_parts(value):
    return 0.5 * (1.0 + lax.erf(value * 0.7071067811865476))


def bell(value):
    return 0.3989422804014327 * jnp.exp(-0.5 * value * value)


def first_kernel(starts, *refs):
    blocks, (weight_in, gain, shift) = refs[:8], refs[8:11]
    hidden, field_out, pre_out, keep, stats = refs[11:16]
    field, weight, lower, middle, upper, sems = refs[16:]
    mel_count, total, width = field.shape
    out_width = middle.shape[2]
    place, column = lax.axis_index("tm"), lax.axis_index("chan")
    copies = [pltpu.make_async_copy(weight_in, weight, sems.at[0])]
    frames, lanes = blocks[0].shape[2], blocks[0].shape[3]
    count = blocks[0].shape[0]
    for i, block in enumerate(blocks):
        core, row, side = i // 4, (i // 2) % 2, i % 2
        from_column = column ^ (2 * row + core)
        for k in range(count):
            from_place = place ^ (2 * k + side)
            copies.append(
                pltpu.make_async_copy(
                    block.at[k],
                    field.at[
                        :,
                        pl.ds(pl.multiple_of(from_place * frames, frames), frames),
                        pl.ds(pl.multiple_of(from_column * lanes, lanes), lanes),
                    ],
                    sems.at[1 + i * count + k],
                )
            )
    for copy in copies:
        copy.start()
    clear_edges(lower, upper, total)
    for copy in copies:
        copy.wait()

    def decode(at, carry):
        for m in range(mel_count):
            rows = field[m, pl.ds(at, ROWS)]
            if m == 0:
                keep[pl.ds(at, ROWS)] = (rows[:, :LANES].astype(f32) < ABSENT / 2).astype(f32)
            field[m, pl.ds(at, ROWS)] = jnp.where(rows < ABSENT / 2, rows, jnp.zeros_like(rows))
        return carry

    by_rows(total, decode, 0)
    save = pltpu.make_async_copy(field, field_out, sems.at[1])
    save.start()
    convolve(
        [lambda m: field[m]], [lambda a, b: weight[a, b]], lower, middle, upper, total, False
    )

    def combine(at, sums):
        before, after = same_clip(starts, at, (ROWS, out_width), total)
        mask = widen(keep[pl.ds(at, ROWS)], out_width)
        one, two, num = sums
        num = num + fold(mask)
        for m in range(mel_count):
            rows = joined(lower, middle, upper, m, at, before, after)
            middle[m, pl.ds(at, ROWS)] = rows
            kept = rows * mask
            one = one + fold(kept)
            two = two + fold(kept * rows)
        return one, two, num

    blank = jnp.zeros((TILE, out_width), f32)
    one, two, num = by_rows(total, combine, (blank, blank, blank))
    save_pre = pltpu.make_async_copy(middle, pre_out, sems.at[0])
    save_pre.start()
    pixels = column_sum(num) * mel_count
    center, inverse = moments((one, two), keep, pixels)
    stats[0:1] = center
    stats[1:2] = inverse
    stats[2:3] = pixels
    scale = gain[...] * inverse
    offset = shift[...] - center * scale

    def activate(at, carry):
        mask = widen(keep[pl.ds(at, ROWS)], out_width)
        for m in range(mel_count):
            value = middle[m, pl.ds(at, ROWS)] * scale + offset
            hidden[m, pl.ds(at, ROWS)] = (value * phi_parts(value) * mask).astype(bf16)
        return carry

    by_rows(total, activate, 0)
    save.wait()
    save_pre.wait()


def first_block(blocks, weight, gain, shift, starts, total):
    count, mel_count, frames, lanes = blocks[0].shape
    width, out_width = weight.shape[2], weight.shape[3]
    padded = (mel_count, total + 2 * TILE, out_width)
    return call(
        first_kernel,
        (starts, *blocks, weight, gain, shift),
        [scalar_spec()] + [place_spec()] * 9 + [whole_spec()] * 2,
        [
            ((mel_count, total, out_width), bf16),
            ((mel_count, total, width), bf16),
            ((mel_count, total, out_width), f32),
            ((total, LANES), f32),
            ((TILE, out_width), f32),
        ],
        [whole_spec(), place_spec(), place_spec(), whole_spec(), whole_spec()],
        [
            pltpu.VMEM((mel_count, total, width), bf16),
            pltpu.VMEM(weight.shape, bf16),
            pltpu.VMEM(padded, f32),
            pltpu.VMEM((mel_count, total, out_width), f32),
            pltpu.VMEM(padded, f32),
            pltpu.SemaphoreType.DMA((1 + 8 * count,)),
        ],
        2 * 9 * mel_count * total * width * out_width,
        32,
    )


def slope_kernel(pre, stats, gain, shift, keep, slope):
    mel_count, total, width = pre.shape
    center, inverse = stats[0:1], stats[1:2]
    scale = gain[...] * inverse
    offset = shift[...] - center * scale

    def rows(at, carry):
        mask = widen(keep[pl.ds(at, ROWS)], width)
        for m in range(mel_count):
            value = pre[m, pl.ds(at, ROWS)] * scale + offset
            slope[m, pl.ds(at, ROWS)] = mask * (phi_parts(value) + value * bell(value))
        return carry

    by_rows(total, rows, 0)


def first_slope(pre, stats, gain, shift, keep):
    return call(
        slope_kernel,
        (pre, stats, gain, shift, keep),
        [whole_spec()] * 5,
        [(pre.shape, f32)],
        [whole_spec()],
        [],
        2**28,
        10,
    )[0]


def partial_kernel(places, starts, one, two, weight, out, lower, upper):
    mel_count, total, width = out.shape
    column = lax.axis_index("chan")

    def group(place):
        start = pl.multiple_of((column ^ place) * width, width)
        return lambda a, b: weight[a, b, pl.ds(start, width)]

    clear_edges(lower, upper, total)
    convolve(
        [lambda m: one[m], lambda m: two[m]],
        [group(p) for p in places],
        lower,
        out,
        upper,
        total,
        False,
    )

    def combine(at, carry):
        before, after = same_clip(starts, at, (ROWS, width), total)
        for m in range(mel_count):
            out[m, pl.ds(at, ROWS)] = joined(lower, out, upper, m, at, before, after)
        return carry

    by_rows(total, combine, 0)


def second_partial(one, two, weight, starts):
    mel_count, total, width = one.shape
    padded = (mel_count, total + 2 * TILE, width)
    return call(
        functools.partial(partial_kernel, (0, 1)),
        (starts, one, two, weight),
        [scalar_spec()] + [whole_spec()] * 3,
        [((mel_count, total, width), f32)],
        [whole_spec()],
        [pltpu.VMEM(padded, f32)] * 2,
        2 * 18 * mel_count * total * width * width,
        20,
    )[0]


def second_kernel(starts, one, two, weight, middle_in, keep, gain, shift, cotangents, *refs):
    readout, grad, gain_grad, shift_grad = refs[:4]
    middle, slope, lower, upper, hold, wide, full, sems = refs[4:]
    mel_count, total, width = one.shape
    place, column = lax.axis_index("tm"), lax.axis_index("chan")
    pooled_total = total // 2
    own = readout.shape[0]
    copies = []
    for k in range(cotangents.shape[0]):
        copies.append(
            pltpu.make_async_copy(
                cotangents.at[k],
                full.at[pl.ds(pl.multiple_of((place ^ k) * own, own), own)],
                sems.at[k],
            )
        )
    for copy in copies:
        copy.start()

    def group(bit):
        start = pl.multiple_of((column ^ bit) * width, width)
        return lambda a, b: weight[a, b, pl.ds(start, width)]

    clear_edges(lower, upper, total)
    convolve(
        [lambda m: one[m], lambda m: two[m]], [group(2), group(3)], lower, middle, upper, total, False
    )
    blank = jnp.zeros((TILE, width), f32)

    def combine(at, sums):
        before, after = same_clip(starts, at, (ROWS, width), total)
        mask = widen(keep[pl.ds(at, ROWS)], width)
        first, second, num = sums
        num = num + fold(mask)
        for m in range(mel_count):
            rows = joined(lower, middle, upper, m, at, before, after)
            rows = rows + middle_in[m, pl.ds(at, ROWS)]
            middle[m, pl.ds(at, ROWS)] = rows
            kept = rows * mask
            first = first + fold(kept)
            second = second + fold(kept * rows)
        return first, second, num

    first, second, num = by_rows(total, combine, (blank, blank, blank))
    pixels = column_sum(num) * mel_count
    center, inverse = moments((first, second), keep, pixels)
    scale = gain[...] * inverse
    offset = shift[...] - center * scale

    def activate(at, carry):
        mask = widen(keep[pl.ds(at, ROWS)], width)
        pooled = jnp.zeros((ROWS, width), f32)
        for m in range(mel_count):
            value = middle[m, pl.ds(at, ROWS)] * scale + offset
            share = phi_parts(value)
            pooled = pooled + value * share
            slope[m, pl.ds(at, ROWS)] = mask * (share + value * bell(value))
        pooled = pooled * mask
        for c in range(width // LANES):
            hold[c, pl.ds(at, ROWS)] = pooled[:, c * LANES : (c + 1) * LANES]
        return carry

    by_rows(total, activate, 0)

    even = pl.ds(0, pooled_total, stride=2)
    odd = pl.ds(1, pooled_total, stride=2)
    pooled = jnp.concatenate(
        [hold[c, even] + hold[c, odd] for c in range(width // LANES)], axis=1
    ) * (0.5 / mel_count)
    present = widen(keep[even], width)
    square = (pooled_total, pooled_total)
    row = lax.broadcasted_iota(jnp.int32, square, 0)
    col = lax.broadcasted_iota(jnp.int32, square, 1)
    same = row >= col
    back = row <= col
    for k in range(1, starts.shape[0]):
        crossed = (2 * row < starts[k]) != (2 * col < starts[k])
        same = same & ~crossed
        back = back & ~crossed
    ahead, behind = same.astype(f32), back.astype(f32)
    exact = functools.partial(jnp.dot, precision=highest, preferred_element_type=f32)
    exponent = jnp.exp(pooled)
    counts = jnp.dot(ahead, present, preferred_element_type=f32)
    totals = exact(ahead, present * pooled)
    sums = exact(ahead, present * exponent)
    wide[...] = totals / counts + jnp.log(sums)
    readout[...] = wide[pl.ds(pl.multiple_of(place * own, own), own)]
    for copy in copies:
        copy.wait()
    cotangent = full[...]
    by_count = exact(behind, cotangent / counts)
    by_sum = exact(behind, cotangent / sums)
    down = present * (by_count + exponent * by_sum) * (0.5 / mel_count)
    for c in range(width // LANES):
        hold[c, even] = down[:, c * LANES : (c + 1) * LANES]
        hold[c, odd] = down[:, c * LANES : (c + 1) * LANES]

    def slopes(at, sums):
        down_rows = jnp.concatenate(
            [hold[c, pl.ds(at, ROWS)] for c in range(width // LANES)], axis=1
        )
        plain, along = sums
        for m in range(mel_count):
            step = down_rows * slope[m, pl.ds(at, ROWS)]
            slope[m, pl.ds(at, ROWS)] = step
            plain = plain + fold(step)
            along = along + fold(step * ((middle[m, pl.ds(at, ROWS)] - center) * inverse))
        return plain, along

    plain, along = by_rows(total, slopes, (blank, blank))
    plain, along = column_sum(plain), column_sum(along)
    shift_grad[...] = plain
    gain_grad[...] = along
    plain, along = plain / pixels, along / pixels

    def finish(at, carry):
        mask = widen(keep[pl.ds(at, ROWS)], width)
        for m in range(mel_count):
            normed = (middle[m, pl.ds(at, ROWS)] - center) * inverse
            rows = slope[m, pl.ds(at, ROWS)] - plain - normed * along
            grad[m, pl.ds(at, ROWS)] = (mask * (scale * rows)).astype(bf16)
        return carry

    by_rows(total, finish, 0)


def second_block(one, two, weight, partial, keep, gain, shift, starts, cotangents, own):
    mel_count, total, width = one.shape
    padded = (mel_count, total + 2 * TILE, width)
    full = (mel_count, total, width)
    return call(
        second_kernel,
        (starts, one, two, weight, partial, keep, gain, shift, cotangents),
        [scalar_spec()] + [whole_spec()] * 7 + [place_spec()],
        [((own, width), f32), (full, bf16), ((1, width), f32), ((1, width), f32)],
        [whole_spec()] * 4,
        [
            pltpu.VMEM(full, f32),
            pltpu.VMEM(full, f32),
            pltpu.VMEM(padded, f32),
            pltpu.VMEM(padded, f32),
            pltpu.VMEM((width // LANES, total, LANES), f32),
            pltpu.VMEM((total // 2, width), f32),
            pltpu.VMEM((total // 2, width), f32),
            pltpu.SemaphoreType.DMA((cotangents.shape[0],)),
        ],
        2 * 18 * mel_count * total * width * width,
        40,
    )


def back_kernel(bit, starts, one, two, weight, weight_two, out, lower, middle, upper):
    mel_count, total, width = one.shape
    column = lax.axis_index("chan")
    start = pl.multiple_of((column ^ bit) * width, width)
    clear_edges(lower, upper, total)
    convolve_back(
        [lambda m: one[m], lambda m: two[m]],
        [
            lambda a, b: weight[a, b, pl.ds(start, width)],
            lambda a, b: weight_two[a, b, pl.ds(start, width)],
        ],
        lower,
        middle,
        upper,
        total,
    )

    def combine(at, carry):
        before, after = same_clip(starts, at, (ROWS, width), total)
        for m in range(mel_count):
            rows = joined(lower, middle, upper, m, at, before, after)
            out[m, pl.ds(at, ROWS)] = rows.astype(out.dtype)
        return carry

    by_rows(total, combine, 0)


def hidden_back(bit, one, two, weight, weight_two, starts, kind):
    mel_count, total, width = one.shape
    padded = (mel_count, total + 2 * TILE, width)
    return call(
        functools.partial(back_kernel, bit),
        (starts, one, two, weight, weight_two),
        [scalar_spec()] + [whole_spec()] * 4,
        [((mel_count, total, width), kind)],
        [whole_spec()],
        [
            pltpu.VMEM(padded, f32),
            pltpu.VMEM((mel_count, total, width), f32),
            pltpu.VMEM(padded, f32),
        ],
        2 * 18 * mel_count * total * width * width,
        28,
    )[0]


def norm_kernel(mine, other, slope, pre, stats, gain, keep, *refs):
    grad, window, gain_grad, shift_grad, padded = refs
    mel_count, total, width = mine.shape
    center, inverse, pixels = stats[0:1], stats[1:2], stats[2:3]
    blank = jnp.zeros((TILE, width), f32)
    edge = (padded.shape[1] - total) // 2
    reach = window.shape[1]
    frames = reach - 2 * edge
    place = lax.axis_index("tm")

    def slopes(at, sums):
        plain, along = sums
        for m in range(mel_count):
            rows = mine[m, pl.ds(at, ROWS)] + other[m, pl.ds(at, ROWS)].astype(f32)
            step = rows * slope[m, pl.ds(at, ROWS)]
            mine[m, pl.ds(at, ROWS)] = step
            plain = plain + fold(step)
            along = along + fold(step * ((pre[m, pl.ds(at, ROWS)] - center) * inverse))
        return plain, along

    plain, along = by_rows(total, slopes, (blank, blank))
    plain, along = column_sum(plain), column_sum(along)
    shift_grad[...] = plain
    gain_grad[...] = along
    plain, along = plain / pixels, along / pixels
    scale = gain[...] * inverse
    for m in range(mel_count):
        padded[m, :edge] = jnp.zeros((edge, width), bf16)
        padded[m, edge + total :] = jnp.zeros((edge, width), bf16)

    def finish(at, carry):
        mask = widen(keep[pl.ds(at, ROWS)], width)
        for m in range(mel_count):
            normed = (pre[m, pl.ds(at, ROWS)] - center) * inverse
            rows = mine[m, pl.ds(at, ROWS)] - plain - normed * along
            rows = (mask * (scale * rows)).astype(bf16)
            grad[m, pl.ds(at, ROWS)] = rows
            padded[m, pl.ds(pl.multiple_of(at + edge, 16), ROWS)] = rows
        return carry

    by_rows(total, finish, 0)
    for m in range(mel_count):
        window[m] = padded[m, pl.ds(pl.multiple_of(place * frames, frames), reach)]


def norm_back_first(mine, other, slope, pre, stats, gain, keep, frames):
    mel_count, total, width = mine.shape
    edge = 16
    return call(
        norm_kernel,
        (mine, other, slope, pre, stats, gain, keep),
        [whole_spec()] * 7,
        [
            ((mel_count, total, width), bf16),
            ((mel_count, frames + 2 * edge, width), bf16),
            ((1, width), f32),
            ((1, width), f32),
        ],
        [whole_spec()] * 4,
        [pltpu.VMEM((mel_count, total + 2 * edge, width), bf16)],
        2**28,
        20,
    )


def weight_kernel(group_count, starts, *refs):
    fields = refs[:group_count]
    grad, out = refs[group_count : group_count + 2]
    spaced, steps, results, sems = refs[group_count + 2 :]
    mel_count, total, out_width = grad.shape
    column = lax.axis_index("chan")
    for m in range(mel_count):
        spaced[m, :TILE] = jnp.zeros((TILE, out_width), f32)
        spaced[m, TILE + total :] = jnp.zeros((TILE, out_width), f32)

    def expand(at, carry):
        for m in range(mel_count):
            spaced[m, pl.ds(pl.multiple_of(at + TILE, TILE), ROWS)] = grad[
                m, pl.ds(at, ROWS)
            ].astype(f32)
        return carry

    by_rows(total, expand, 0)

    def shift(at, carry):
        before, after = same_clip(starts, at, (ROWS, out_width), total)
        for m in range(mel_count):
            rows = spaced[m, pl.ds(at, ROWS + 2 * TILE)]
            ahead = jnp.where(after, rows[TILE + 1 : TILE + 1 + ROWS], 0.0)
            behind = jnp.where(before, rows[TILE - 1 : TILE - 1 + ROWS], 0.0)
            steps[0, m, pl.ds(at, ROWS)] = ahead.astype(bf16)
            steps[1, m, pl.ds(at, ROWS)] = behind.astype(bf16)
        return carry

    by_rows(total, shift, 0)
    width = results.shape[3]
    copies = [None, None]
    count = 0
    for i, field in enumerate(fields):
        for part in range(field.shape[2] // width):
            slot = count % 2
            if copies[slot] is not None:
                copies[slot].wait()
            for a in range(3):
                for b in range(3):
                    acc = None
                    for m in range(mel_count):
                        if 0 <= m + b - 1 < mel_count:
                            right = grad[m] if a == 1 else steps[a // 2, m]
                            left = field[m + b - 1, :, part * width : (part + 1) * width]
                            piece = lax.dot_general(
                                left,
                                right,
                                (((0,), (0,)), ((), ())),
                                preferred_element_type=f32,
                            )
                            acc = piece if acc is None else acc + piece
                    results[slot, 3 * a + b] = acc
            if group_count > 1:
                start = pl.multiple_of((column ^ i) * width, width)
            else:
                start = part * width
            copies[slot] = pltpu.make_async_copy(
                results.at[slot], out.at[:, pl.ds(start, width)], sems.at[slot]
            )
            copies[slot].start()
            count += 1
    for copy in copies:
        if copy is not None:
            copy.wait()


def weight_back(fields, grad, starts):
    mel_count, total, out_width = grad.shape
    in_width = sum(f.shape[2] for f in fields)
    width = 256
    out = call(
        functools.partial(weight_kernel, len(fields)),
        (starts, *fields, grad),
        [scalar_spec()] + [whole_spec()] * (len(fields) + 1),
        [((9, in_width, out_width), f32)],
        [place_spec()],
        [
            pltpu.VMEM((mel_count, total + 2 * TILE, out_width), f32),
            pltpu.VMEM((2, mel_count, total, out_width), bf16),
            pltpu.VMEM((2, 9, width, out_width), f32),
            pltpu.SemaphoreType.DMA((2,)),
        ],
        2 * 9 * mel_count * total * in_width * out_width,
        24,
    )[0]
    return out.reshape(3, 3, in_width, out_width)


def input_kernel(starts, one, two, weight, weight_two, mine, other, lower, middle, upper):
    mel_count, reach, width = one.shape
    frames, lanes = mine.shape[1], mine.shape[2]
    edge = (reach - frames) // 2
    total = frames * lax.axis_size("tm")
    place, column = lax.axis_index("tm"), lax.axis_index("chan")
    for bit, out in ((2, other), (0, mine)):
        start = pl.multiple_of((column ^ bit) * lanes, lanes)
        convolve_back(
            [lambda m: one[m], lambda m: two[m]],
            [
                lambda a, b: weight[a, b, pl.ds(start, lanes)],
                lambda a, b: weight_two[a, b, pl.ds(start, lanes)],
            ],
            lower,
            middle,
            upper,
            reach,
        )
        before, after = same_clip(starts, place * frames, (frames, lanes), total)
        for m in range(mel_count):
            low = lower[m, TILE + edge - 1 : TILE + edge - 1 + frames]
            high = upper[m, TILE + edge + 1 : TILE + edge + 1 + frames]
            out[m] = (
                middle[m, edge : edge + frames]
                + jnp.where(before, low, 0.0)
                + jnp.where(after, high, 0.0)
            )


def input_back(one, two, weight, weight_two, starts, frames, lanes):
    mel_count, reach, width = one.shape
    shape = (mel_count, frames, lanes)
    return call(
        input_kernel,
        (starts, one, two, weight, weight_two),
        [scalar_spec()] + [whole_spec()] * 4,
        [(shape, f32), (shape, f32)],
        [whole_spec()] * 2,
        [
            pltpu.VMEM((mel_count, reach + 2 * TILE, lanes), f32),
            pltpu.VMEM((mel_count, reach, lanes), f32),
            pltpu.VMEM((mel_count, reach + 2 * TILE, lanes), f32),
        ],
        2**28,
        20,
    )


def whole_frames(
    features,
    conv1_weight,
    norm1_gain,
    norm1_bias,
    conv2_weight,
    norm2_gain,
    norm2_bias,
    clip_starts,
    valid,
    readout_grad,
):
    frames, mel_count, lanes = features.shape
    places = lax.axis_size("tm")
    total = frames * places
    gain1, shift1 = norm1_gain[None], norm1_bias[None]
    gain2, shift2 = norm2_gain[None], norm2_bias[None]

    marked = jnp.where(valid[:, None, None] > 0, features, jnp.asarray(ABSENT, bf16))
    own = jnp.transpose(marked, (1, 0, 2))
    along = jnp.stack([own] + [swap(own, "tm", 2 * k) for k in range(1, places // 2)])
    near = [
        along,
        swap(along, "tm", 1),
        swap(along, "chan", 2),
        swap_both(along, "tm", 1, "chan", 2),
    ]
    blocks = near + [swap(block, "chan", 1) for block in near]
    other_conv2 = swap(conv2_weight, "chan", 1)
    other_conv1 = swap(conv1_weight, "chan", 1)
    cotangent = readout_grad[None]
    bit = 1
    while bit < places:
        cotangent = jnp.concatenate([cotangent, swap(cotangent, "tm", bit)])
        bit *= 2

    hidden, field, pre, keep, stats = first_block(
        blocks, conv1_weight, gain1, shift1, clip_starts, total
    )
    hidden_far = swap(hidden, "chan", 2)
    hidden_near = swap(hidden, "chan", 1)
    slope = first_slope(pre, stats, gain1, shift1, keep)
    partial = second_partial(hidden, hidden_near, conv2_weight, clip_starts)
    hidden_last = swap(hidden_far, "chan", 1)
    readout, grad2, gain2_grad, shift2_grad = second_block(
        hidden_far,
        hidden_last,
        conv2_weight,
        partial,
        keep,
        gain2,
        shift2,
        clip_starts,
        cotangent,
        readout_grad.shape[0],
    )
    grad2_near = swap(grad2, "chan", 1)
    away = hidden_back(2, grad2, grad2_near, conv2_weight, other_conv2, clip_starts, bf16)
    came = swap(away, "chan", 2)
    mine = hidden_back(0, grad2, grad2_near, conv2_weight, other_conv2, clip_starts, f32)
    weight2_grad = weight_back(
        [hidden, hidden_near, hidden_far, hidden_last], grad2, clip_starts
    )
    grad1, window, gain1_grad, shift1_grad = norm_back_first(
        mine, came, slope, pre, stats, gain1, keep, frames
    )
    window_near = swap(window, "chan", 1)
    input_mine, input_away = input_back(
        window, window_near, conv1_weight, other_conv1, clip_starts, frames, lanes
    )
    input_came = swap(input_away, "chan", 2)
    weight1_grad = weight_back([field], grad1, clip_starts)
    live = (valid > 0).astype(f32)[None, :, None]
    input_grad = jnp.transpose((input_mine + input_came) * live, (1, 0, 2))
    return (
        readout,
        input_grad,
        weight1_grad,
        gain1_grad[0],
        shift1_grad[0],
        weight2_grad,
        gain2_grad[0],
        shift2_grad[0],
    )


def fits_whole(frames, places, columns, widths):
    return (
        places > 1
        and places & (places - 1) == 0
        and columns == 4
        and frames % 32 == 0
        and frames * places <= 512
        and all(w % (columns * LANES) == 0 for w in widths)
        and widths[1] == columns * 256
    )


def shards(*arrays):
    features, conv1_weight, conv2_weight = arrays[0], arrays[1], arrays[4]
    if fits_whole(
        features.shape[0],
        lax.axis_size("tm"),
        lax.axis_size("chan"),
        (conv1_weight.shape[2], conv2_weight.shape[2]),
    ):
        return whole_frames(*arrays)
    return split_frames(*arrays)


def solution(mesh):
    return jax.shard_map(
        shards,
        mesh=mesh,
        in_specs=(
            P("tm", None, "chan"),
            P(None, None, None, "chan"),
            P("chan"),
            P("chan"),
            P(None, None, None, "chan"),
            P("chan"),
            P("chan"),
            P(),
            P("tm"),
            P("tm", "chan"),
        ),
        out_specs=(
            P("tm", "chan"),
            P("tm", None, "chan"),
            P(None, None, None, "chan"),
            P("chan"),
            P("chan"),
            P(None, None, None, "chan"),
            P("chan"),
            P("chan"),
        ),
        check_vma=False,
    )
```

```python
import functools

import jax
import jax.numpy as jnp
from jax import lax
from jax.experimental import pallas as pl
from jax.experimental.pallas import tpu as pltpu
from jax.sharding import PartitionSpec as P

EPS = 1e-05
highest = lax.Precision.HIGHEST
f32 = jnp.float32
bf16 = jnp.bfloat16


def padded_2(shard, sides, width):
    for axis, dim in sides:
        count, length = (lax.axis_size(axis), shard.shape[dim])
        up = [(i, (i + 1) % count) for i in range(count - 1)]
        down = [(j, i) for i, j in up]
        last = lax.slice_in_dim(shard, length - width, length, axis=dim)
        leading = lax.slice_in_dim(shard, 0, width, axis=dim)
        before = lax.ppermute(last, axis, up)
        after = lax.ppermute(leading, axis, down)
        shard = jnp.concatenate([before, shard, after], axis=dim)
    return shard


def entering(part, axis, combine, identity, reverse):
    count = lax.axis_size(axis)
    place = lax.axis_index(axis)
    ahead = count - 1 - place if reverse else place
    gathered = jax.tree.map(lambda a: lax.all_gather(a, axis), part)
    state = jax.tree.map(lambda a, e: jnp.zeros_like(a) + jnp.asarray(e, a.dtype), part, identity)

    def one(step, state):
        source = count - 1 - step if reverse else step
        return combine(
            state, jax.tree.map(lambda a: lax.dynamic_index_in_dim(a, source, 0, False), gathered)
        )

    return lax.fori_loop(0, ahead, one, state)


def frame_flags(clip_starts, first_frame, frame_count, frame_total):
    position = first_frame - 2 + jnp.arange(frame_count + 4, dtype=jnp.int32)
    segment = jnp.sum((clip_starts[None, :] <= position[:, None]).astype(jnp.int32), axis=1) - 1
    inside = (position >= 0) & (position < frame_total)
    middle = segment[1:-1]
    before_same = inside[1:-1] & inside[:-2] & (middle == segment[:-2])
    after_same = inside[1:-1] & inside[2:] & (middle == segment[2:])
    return (segment[2:-2], before_same, after_same)


def conv_forward(padded, weight, factors):
    frame_count = padded.shape[0] - 2
    mel_count = padded.shape[1]
    wide_field = jnp.pad(padded, ((0, 0), (1, 1), (0, 0)))
    result = jnp.zeros((frame_count, mel_count, weight.shape[3]), jnp.float32)
    for tap_row in range(3):
        partial_value = jnp.zeros((frame_count * mel_count, weight.shape[3]), jnp.float32)
        for tap_col in range(3):
            window = wide_field[
                tap_row : tap_row + frame_count, tap_col : tap_col + mel_count, :
            ].reshape(frame_count * mel_count, -1)
            partial_value = partial_value + jnp.dot(
                window, weight[tap_row, tap_col], preferred_element_type=jnp.float32
            )
        result = (
            result
            + partial_value.reshape(frame_count, mel_count, -1) * factors[tap_row][:, None, None]
        )
    return result


def conv_weight_grad(padded, grad_out, factors):
    frame_count = grad_out.shape[0]
    mel_count = grad_out.shape[1]
    wide_field = jnp.pad(padded, ((0, 0), (1, 1), (0, 0)))
    rows_out = []
    for tap_row in range(3):
        scaled = (grad_out * factors[tap_row][:, None, None].astype(jnp.bfloat16)).reshape(
            frame_count * mel_count, -1
        )
        taps_out = []
        for tap_col in range(3):
            window = wide_field[
                tap_row : tap_row + frame_count, tap_col : tap_col + mel_count, :
            ].reshape(frame_count * mel_count, -1)
            taps_out.append(
                lax.dot_general(
                    window, scaled, (((0,), (0,)), ((), ())), preferred_element_type=jnp.float32
                )
            )
        rows_out.append(jnp.stack(taps_out))
    return jnp.stack(rows_out)


def conv_input_grad(grad_padded, weight, edge_factors):
    frame_count = grad_padded.shape[0] - 2
    mel_count = grad_padded.shape[1]
    wide_field = jnp.pad(grad_padded, ((0, 0), (1, 1), (0, 0)))
    result = jnp.zeros((frame_count * mel_count, weight.shape[2]), jnp.float32)
    for tap_row in range(3):
        scaled = wide_field * edge_factors[tap_row][:, None, None]
        for tap_col in range(3):
            window = scaled[
                2 - tap_row : 2 - tap_row + frame_count, 2 - tap_col : 2 - tap_col + mel_count, :
            ].reshape(frame_count * mel_count, -1)
            result = result + lax.dot_general(
                window,
                weight[tap_row, tap_col],
                (((1,), (1,)), ((), ())),
                preferred_element_type=jnp.float32,
            )
    return result.reshape(frame_count, mel_count, -1)


def join_keyed(earlier_item, later_item):
    keep_first = later_item[0] < 0.0
    same_key = later_item[0] == earlier_item[0]
    merged = [jnp.where(keep_first, earlier_item[0], later_item[0])]
    for first_part, second_part in zip(earlier_item[1:], later_item[1:]):
        extra = (1,) * (first_part.ndim - keep_first.ndim)
        keep_wide = jnp.reshape(keep_first, keep_first.shape + extra)
        same_wide = jnp.reshape(same_key, same_key.shape + extra)
        merged.append(
            jnp.where(
                keep_wide, first_part, jnp.where(same_wide, first_part + second_part, second_part)
            )
        )
    return tuple(merged)


def smooth(argument):
    return jax.nn.gelu(argument, approximate=False)


def split_frames(
    features,
    conv1_weight,
    norm1_gain,
    norm1_bias,
    conv2_weight,
    norm2_gain,
    norm2_bias,
    clip_starts,
    valid,
    readout_grad,
):
    frame_count = features.shape[0]
    mel_count = features.shape[1]
    cycle_size = lax.axis_size("tm")
    cycle_index = lax.axis_index("tm")
    segment, before_same, after_same = frame_flags(
        clip_starts, cycle_index * frame_count, frame_count, frame_count * cycle_size
    )
    keep_mask = valid.astype(jnp.float32)
    keep_cube = keep_mask[:, None, None]
    own_factors = (
        before_same[1:-1].astype(jnp.float32),
        jnp.ones((frame_count,), jnp.float32),
        after_same[1:-1].astype(jnp.float32),
    )
    edge_factors = (
        before_same.astype(jnp.bfloat16),
        jnp.ones((frame_count + 2,), jnp.bfloat16),
        after_same.astype(jnp.bfloat16),
    )
    local_count = jnp.sum(keep_mask) * mel_count

    def spread(shard):
        padded = padded_2(shard, (("tm", 0),), 1)
        return lax.all_gather(padded, "chan", axis=2, tiled=True)

    def normalize(field_in, gain_vec, shift_vec):
        value_sums, squares, pixel_count = lax.psum(
            (
                jnp.sum(field_in * keep_cube, axis=(0, 1)),
                jnp.sum(field_in * field_in * keep_cube, axis=(0, 1)),
                local_count,
            ),
            "tm",
        )
        center = value_sums / pixel_count
        variance = squares / pixel_count - center * center
        inverse_std = lax.rsqrt(variance + EPS)
        normed = (field_in - center) * inverse_std
        return (gain_vec * normed + shift_vec, normed, inverse_std, pixel_count)

    def norm_back(grad_norm, normed, inverse_std, gain_vec, pixel_count):
        bias_grad, gain_grad = lax.psum(
            (jnp.sum(grad_norm, axis=(0, 1)), jnp.sum(grad_norm * normed, axis=(0, 1))), "tm"
        )
        grad_pre = (
            keep_cube
            * (gain_vec * inverse_std)
            * (grad_norm - bias_grad / pixel_count - normed * (gain_grad / pixel_count))
        )
        return (grad_pre.astype(jnp.bfloat16), gain_grad, bias_grad)

    def send_back(grad_pre, weight):
        padded = padded_2(grad_pre, (("tm", 0),), 1)
        partial_sum = conv_input_grad(padded, weight, edge_factors)
        return lax.psum_scatter(partial_sum, "chan", scatter_dimension=2, tiled=True)

    wide_in = spread(features * keep_cube.astype(jnp.bfloat16))
    first_pre = conv_forward(wide_in, conv1_weight, own_factors)
    first_norm, first_hat, first_scale, pixel_count = normalize(first_pre, norm1_gain, norm1_bias)
    first_act, first_pull = jax.vjp(smooth, first_norm)
    hidden = (first_act * keep_cube).astype(jnp.bfloat16)
    wide_mid = spread(hidden)
    second_pre = conv_forward(wide_mid, conv2_weight, own_factors)
    second_norm, second_hat, second_scale, pixel_count = normalize(
        second_pre, norm2_gain, norm2_bias
    )
    second_act, second_pull = jax.vjp(smooth, second_norm)
    pooled = (second_act * keep_cube).reshape(frame_count // 2, 2, mel_count, -1).mean(axis=(1, 2))
    pooled_keep = keep_mask[0::2]
    pooled_segment = segment[0::2]
    segment_key = pooled_segment.astype(jnp.float32)
    row_order = jnp.arange(frame_count // 2)
    lower_runs = (
        (pooled_segment[:, None] == pooled_segment[None, :])
        & (row_order[:, None] >= row_order[None, :])
    ).astype(jnp.float32)
    exponent = jnp.exp(pooled)
    counts = jnp.dot(lower_runs, pooled_keep, precision=highest)
    totals = jnp.dot(lower_runs, pooled_keep[:, None] * pooled, precision=highest)
    expsums = jnp.dot(lower_runs, pooled_keep[:, None] * exponent, precision=highest)
    zero_row = jnp.zeros_like(totals[0])
    prior_runs = entering(
        (segment_key[-1], counts[-1], totals[-1], expsums[-1]),
        "tm",
        join_keyed,
        (jnp.float32(-1.0), jnp.float32(0.0), zero_row, zero_row),
        False,
    )
    joined = (segment_key == prior_runs[0]).astype(jnp.float32)
    counts = counts + joined * prior_runs[1]
    totals = totals + joined[:, None] * prior_runs[2]
    expsums = expsums + joined[:, None] * prior_runs[3]
    readout = totals / counts[:, None] + jnp.log(expsums)
    by_count = readout_grad / counts[:, None]
    by_expsum = readout_grad / expsums
    later_mean = lax.dot_general(lower_runs, by_count, (((0,), (0,)), ((), ())), precision=highest)
    later_soft = lax.dot_general(lower_runs, by_expsum, (((0,), (0,)), ((), ())), precision=highest)
    beyond = entering(
        (segment_key[0], later_mean[0], later_soft[0]),
        "tm",
        join_keyed,
        (jnp.float32(-1.0), zero_row, zero_row),
        True,
    )
    joined_back = (segment_key == beyond[0]).astype(jnp.float32)[:, None]
    later_mean = later_mean + joined_back * beyond[1]
    later_soft = later_soft + joined_back * beyond[2]
    pooled_grad = pooled_keep[:, None] * (later_mean + exponent * later_soft)
    spread_grad = jnp.broadcast_to(
        (pooled_grad / (2 * mel_count))[:, None, None, :],
        (frame_count // 2, 2, mel_count, pooled_grad.shape[1]),
    )
    act_grad = spread_grad.reshape(frame_count, mel_count, -1) * keep_cube
    second_grad_norm = second_pull(act_grad)[0]
    second_grad_pre, gain2_grad, bias2_grad = norm_back(
        second_grad_norm, second_hat, second_scale, norm2_gain, pixel_count
    )
    weight2_grad = conv_weight_grad(wide_mid, second_grad_pre, own_factors)
    weight2_grad = lax.psum(weight2_grad, "tm")
    hidden_grad = send_back(second_grad_pre, conv2_weight)
    first_grad_norm = first_pull(hidden_grad * keep_cube)[0]
    first_grad_pre, gain1_grad, bias1_grad = norm_back(
        first_grad_norm, first_hat, first_scale, norm1_gain, pixel_count
    )
    weight1_grad = conv_weight_grad(wide_in, first_grad_pre, own_factors)
    weight1_grad = lax.psum(weight1_grad, "tm")
    input_grad = send_back(first_grad_pre, conv1_weight) * keep_cube
    return (
        readout,
        input_grad,
        weight1_grad,
        gain1_grad,
        bias1_grad,
        weight2_grad,
        gain2_grad,
        bias2_grad,
    )


ABSENT = 1024.0
ROWS = 32
TILE = 8
LANES = 128


def whole_spec():
    return pl.BlockSpec(memory_space=pltpu.VMEM)


def place_spec():
    return pl.BlockSpec(memory_space=pl.ANY)


def scalar_spec():
    return pl.BlockSpec(memory_space=pltpu.SMEM)


def call(body, operands, in_specs, outs, out_specs, scratch, flops, megabytes):
    return pl.pallas_call(
        body,
        out_shape=tuple(jax.ShapeDtypeStruct(s, d) for s, d in outs),
        in_specs=in_specs,
        out_specs=tuple(out_specs),
        scratch_shapes=scratch,
        compiler_params=pltpu.CompilerParams(vmem_limit_bytes=megabytes * 2**20),
        cost_estimate=pl.CostEstimate(flops=flops, bytes_accessed=2**22, transcendentals=0),
    )(*operands)


def swap(shard, axis, bit):
    count = lax.axis_size(axis)
    return lax.ppermute(shard, axis, [(i, i ^ bit) for i in range(count)])


def swap_both(shard, first, first_bit, second, second_bit):
    rows, columns = lax.axis_size(first), lax.axis_size(second)
    pairs = [
        (i * columns + j, (i ^ first_bit) * columns + (j ^ second_bit))
        for i in range(rows)
        for j in range(columns)
    ]
    return lax.ppermute(shard, (first, second), pairs)


def same_clip(starts, at, shape, total):
    frame = lax.broadcasted_iota(jnp.int32, shape, 0) + at
    before = frame != starts[0]
    after = frame != total - 1
    for k in range(1, starts.shape[0]):
        before = before & (frame != starts[k])
        after = after & (frame != starts[k] - 1)
    return before, after


def widen(mask, width):
    return jnp.concatenate([mask] * (width // mask.shape[1]), axis=1)


def fold(value):
    total = value[:TILE]
    for k in range(TILE, value.shape[0], TILE):
        total = total + value[k : k + TILE]
    return total


def column_sum(value):
    return jnp.sum(value, axis=0, keepdims=True)


def taps(mel, mel_count):
    return [b for b in range(3) if 0 <= mel + b - 1 < mel_count]


def convolve(fields, weights, lower, middle, upper, total, add):
    mel_count = middle.shape[0]
    for m in range(mel_count):
        for a in range(3):
            acc = None
            for field, weight in zip(fields, weights):
                for b in taps(m, mel_count):
                    part = jnp.dot(field(m + b - 1), weight(a, b), preferred_element_type=f32)
                    acc = part if acc is None else acc + part
            if a == 0:
                lower[m, TILE : TILE + total] = acc
            elif a == 1:
                middle[m] = middle[m] + acc if add else acc
            else:
                upper[m, TILE : TILE + total] = acc


def convolve_back(fields, weights, lower, middle, upper, total):
    mel_count = middle.shape[0]
    for n in range(mel_count):
        for a in range(3):
            acc = None
            for field, weight in zip(fields, weights):
                for b in range(3):
                    if 0 <= n - b + 1 < mel_count:
                        part = lax.dot_general(
                            field(n - b + 1),
                            weight(a, b),
                            (((1,), (1,)), ((), ())),
                            preferred_element_type=f32,
                        )
                        acc = part if acc is None else acc + part
            if a == 2:
                lower[n, TILE : TILE + total] = acc
            elif a == 1:
                middle[n] = acc
            else:
                upper[n, TILE : TILE + total] = acc


def joined(lower, middle, upper, m, at, before, after):
    low = lower[m, pl.ds(at, ROWS + 2 * TILE)]
    high = upper[m, pl.ds(at, ROWS + 2 * TILE)]
    return (
        middle[m, pl.ds(at, ROWS)]
        + jnp.where(before, low[TILE - 1 : TILE - 1 + ROWS], 0.0)
        + jnp.where(after, high[TILE + 1 : TILE + 1 + ROWS], 0.0)
    )


def by_rows(total, body, init):
    return lax.fori_loop(
        0, total // ROWS, lambda i, c: body(pl.multiple_of(i * ROWS, ROWS), c), init
    )


def clear_edges(lower, upper, total):
    for m in range(lower.shape[0]):
        for ref in (lower, upper):
            ref[m, :TILE] = jnp.zeros((TILE, ref.shape[2]), f32)
            ref[m, TILE + total :] = jnp.zeros((TILE, ref.shape[2]), f32)


def moments(field, keep, count):
    first, second = column_sum(field[0]), column_sum(field[1])
    center = first / count
    return center, lax.rsqrt(second / count - center * center + EPS)


def phi_parts(value):
    return 0.5 * (1.0 + lax.erf(value * 0.7071067811865476))


def bell(value):
    return 0.3989422804014327 * jnp.exp(-0.5 * value * value)


def first_kernel(starts, *refs):
    blocks, (weight_in, scales) = refs[:8], refs[8:10]
    hidden, field_out, pre_out, keep, stats = refs[10:15]
    field, weight, lower, middle, upper, sems = refs[15:]
    mel_count, total, width = field.shape
    out_width = middle.shape[2]
    place, column = lax.axis_index("tm"), lax.axis_index("chan")
    copies = [pltpu.make_async_copy(weight_in, weight, sems.at[0])]
    frames, lanes = blocks[0].shape[2], blocks[0].shape[3]
    count = blocks[0].shape[0]
    for i, block in enumerate(blocks):
        core, row, side = i // 4, (i // 2) % 2, i % 2
        from_column = column ^ (2 * row + core)
        for k in range(count):
            from_place = place ^ (2 * k + side)
            copies.append(
                pltpu.make_async_copy(
                    block.at[k],
                    field.at[
                        :,
                        pl.ds(pl.multiple_of(from_place * frames, frames), frames),
                        pl.ds(pl.multiple_of(from_column * lanes, lanes), lanes),
                    ],
                    sems.at[1 + i * count + k],
                )
            )
    for copy in copies:
        copy.start()
    clear_edges(lower, upper, total)
    for copy in copies:
        copy.wait()

    def decode(at, carry):
        for m in range(mel_count):
            rows = field[m, pl.ds(at, ROWS)]
            if m == 0:
                keep[pl.ds(at, ROWS)] = (rows[:, :LANES].astype(f32) < ABSENT / 2).astype(f32)
            field[m, pl.ds(at, ROWS)] = jnp.where(rows < ABSENT / 2, rows, jnp.zeros_like(rows))
        return carry

    by_rows(total, decode, 0)
    save = pltpu.make_async_copy(field, field_out, sems.at[1])
    save.start()
    convolve(
        [lambda m: field[m]], [lambda a, b: weight[a, b]], lower, middle, upper, total, False
    )

    def combine(at, sums):
        before, after = same_clip(starts, at, (ROWS, out_width), total)
        mask = widen(keep[pl.ds(at, ROWS)], out_width)
        one, two, num = sums
        num = num + fold(mask)
        for m in range(mel_count):
            rows = joined(lower, middle, upper, m, at, before, after)
            middle[m, pl.ds(at, ROWS)] = rows
            kept = rows * mask
            one = one + fold(kept)
            two = two + fold(kept * rows)
        return one, two, num

    blank = jnp.zeros((TILE, out_width), f32)
    one, two, num = by_rows(total, combine, (blank, blank, blank))
    save_pre = pltpu.make_async_copy(middle, pre_out, sems.at[0])
    save_pre.start()
    pixels = column_sum(num) * mel_count
    center, inverse = moments((one, two), keep, pixels)
    stats[0:1] = center
    stats[1:2] = inverse
    stats[2:3] = pixels
    scale = scales[0:1] * inverse
    offset = scales[1:2] - center * scale

    def activate(at, carry):
        mask = widen(keep[pl.ds(at, ROWS)], out_width)
        for m in range(mel_count):
            value = middle[m, pl.ds(at, ROWS)] * scale + offset
            hidden[m, pl.ds(at, ROWS)] = (value * phi_parts(value) * mask).astype(bf16)
        return carry

    by_rows(total, activate, 0)
    save.wait()
    save_pre.wait()


def first_block(blocks, weight, scales, starts, total):
    count, mel_count, frames, lanes = blocks[0].shape
    width, out_width = weight.shape[2], weight.shape[3]
    padded = (mel_count, total + 2 * TILE, out_width)
    return call(
        first_kernel,
        (starts, *blocks, weight, scales),
        [scalar_spec()] + [place_spec()] * 9 + [whole_spec()],
        [
            ((mel_count, total, out_width), bf16),
            ((mel_count, total, width), bf16),
            ((mel_count, total, out_width), f32),
            ((total, LANES), f32),
            ((TILE, out_width), f32),
        ],
        [whole_spec(), place_spec(), place_spec(), whole_spec(), whole_spec()],
        [
            pltpu.VMEM((mel_count, total, width), bf16),
            pltpu.VMEM(weight.shape, bf16),
            pltpu.VMEM(padded, f32),
            pltpu.VMEM((mel_count, total, out_width), f32),
            pltpu.VMEM(padded, f32),
            pltpu.SemaphoreType.DMA((1 + 8 * count,)),
        ],
        2 * 9 * mel_count * total * width * out_width,
        16,
    )


def slope_kernel(pre, stats, scales, keep, slope):
    mel_count, total, width = pre.shape
    center, inverse = stats[0:1], stats[1:2]
    scale = scales[0:1] * inverse
    offset = scales[1:2] - center * scale

    def rows(at, carry):
        mask = widen(keep[pl.ds(at, ROWS)], width)
        for m in range(mel_count):
            value = pre[m, pl.ds(at, ROWS)] * scale + offset
            slope[m, pl.ds(at, ROWS)] = mask * (phi_parts(value) + value * bell(value))
        return carry

    by_rows(total, rows, 0)


def first_slope(pre, stats, scales, keep):
    return call(
        slope_kernel,
        (pre, stats, scales, keep),
        [whole_spec()] * 4,
        [(pre.shape, f32)],
        [whole_spec()],
        [],
        2**28,
        6,
    )[0]


def partial_kernel(places, starts, one, two, weight, out, lower, upper):
    mel_count, total, width = out.shape
    column = lax.axis_index("chan")

    def group(place):
        start = pl.multiple_of((column ^ place) * width, width)
        return lambda a, b: weight[a, b, pl.ds(start, width)]

    clear_edges(lower, upper, total)
    convolve(
        [lambda m: one[m], lambda m: two[m]],
        [group(p) for p in places],
        lower,
        out,
        upper,
        total,
        False,
    )

    def combine(at, carry):
        before, after = same_clip(starts, at, (ROWS, width), total)
        for m in range(mel_count):
            out[m, pl.ds(at, ROWS)] = joined(lower, out, upper, m, at, before, after)
        return carry

    by_rows(total, combine, 0)


def second_partial(one, two, weight, starts):
    mel_count, total, width = one.shape
    padded = (mel_count, total + 2 * TILE, width)
    return call(
        functools.partial(partial_kernel, (0, 1)),
        (starts, one, two, weight),
        [scalar_spec()] + [whole_spec()] * 3,
        [((mel_count, total, width), f32)],
        [whole_spec()],
        [pltpu.VMEM(padded, f32)] * 2,
        2 * 18 * mel_count * total * width * width,
        14,
    )[0]


def second_kernel(starts, one, two, weight, middle_in, keep, scales, cotangents, *refs):
    readout, grad, gain_grad, shift_grad = refs[:4]
    middle, slope, lower, upper, hold, wide, full, sems = refs[4:]
    mel_count, total, width = one.shape
    place, column = lax.axis_index("tm"), lax.axis_index("chan")
    pooled_total = total // 2
    own = readout.shape[0]
    copies = []
    for k in range(cotangents.shape[0]):
        copies.append(
            pltpu.make_async_copy(
                cotangents.at[k],
                full.at[pl.ds(pl.multiple_of((place ^ k) * own, own), own)],
                sems.at[k],
            )
        )
    for copy in copies:
        copy.start()

    def group(bit):
        start = pl.multiple_of((column ^ bit) * width, width)
        return lambda a, b: weight[a, b, pl.ds(start, width)]

    clear_edges(lower, upper, total)
    convolve(
        [lambda m: one[m], lambda m: two[m]], [group(2), group(3)], lower, middle, upper, total, False
    )
    blank = jnp.zeros((TILE, width), f32)

    def combine(at, sums):
        before, after = same_clip(starts, at, (ROWS, width), total)
        mask = widen(keep[pl.ds(at, ROWS)], width)
        first, second, num = sums
        num = num + fold(mask)
        for m in range(mel_count):
            rows = joined(lower, middle, upper, m, at, before, after)
            rows = rows + middle_in[m, pl.ds(at, ROWS)]
            middle[m, pl.ds(at, ROWS)] = rows
            kept = rows * mask
            first = first + fold(kept)
            second = second + fold(kept * rows)
        return first, second, num

    first, second, num = by_rows(total, combine, (blank, blank, blank))
    pixels = column_sum(num) * mel_count
    center, inverse = moments((first, second), keep, pixels)
    scale = scales[2:3] * inverse
    offset = scales[3:4] - center * scale

    def activate(at, carry):
        mask = widen(keep[pl.ds(at, ROWS)], width)
        pooled = jnp.zeros((ROWS, width), f32)
        for m in range(mel_count):
            value = middle[m, pl.ds(at, ROWS)] * scale + offset
            share = phi_parts(value)
            pooled = pooled + value * share
            slope[m, pl.ds(at, ROWS)] = mask * (share + value * bell(value))
        pooled = pooled * mask
        for c in range(width // LANES):
            hold[c, pl.ds(at, ROWS)] = pooled[:, c * LANES : (c + 1) * LANES]
        return carry

    by_rows(total, activate, 0)

    even = pl.ds(0, pooled_total, stride=2)
    odd = pl.ds(1, pooled_total, stride=2)
    pooled = jnp.concatenate(
        [hold[c, even] + hold[c, odd] for c in range(width // LANES)], axis=1
    ) * (0.5 / mel_count)
    present = widen(keep[even], width)
    square = (pooled_total, pooled_total)
    row = lax.broadcasted_iota(jnp.int32, square, 0)
    col = lax.broadcasted_iota(jnp.int32, square, 1)
    same = row >= col
    back = row <= col
    for k in range(1, starts.shape[0]):
        crossed = (2 * row < starts[k]) != (2 * col < starts[k])
        same = same & ~crossed
        back = back & ~crossed
    ahead, behind = same.astype(f32), back.astype(f32)
    exact = functools.partial(jnp.dot, precision=highest, preferred_element_type=f32)
    exponent = jnp.exp(pooled)
    counts = jnp.dot(ahead, present, preferred_element_type=f32)
    totals = exact(ahead, present * pooled)
    sums = exact(ahead, present * exponent)
    wide[...] = totals / counts + jnp.log(sums)
    readout[...] = wide[pl.ds(pl.multiple_of(place * own, own), own)]
    for copy in copies:
        copy.wait()
    cotangent = full[...]
    by_count = exact(behind, cotangent / counts)
    by_sum = exact(behind, cotangent / sums)
    down = present * (by_count + exponent * by_sum) * (0.5 / mel_count)
    for c in range(width // LANES):
        hold[c, even] = down[:, c * LANES : (c + 1) * LANES]
        hold[c, odd] = down[:, c * LANES : (c + 1) * LANES]

    def slopes(at, sums):
        down_rows = jnp.concatenate(
            [hold[c, pl.ds(at, ROWS)] for c in range(width // LANES)], axis=1
        )
        plain, along = sums
        for m in range(mel_count):
            step = down_rows * slope[m, pl.ds(at, ROWS)]
            slope[m, pl.ds(at, ROWS)] = step
            plain = plain + fold(step)
            along = along + fold(step * ((middle[m, pl.ds(at, ROWS)] - center) * inverse))
        return plain, along

    plain, along = by_rows(total, slopes, (blank, blank))
    plain, along = column_sum(plain), column_sum(along)
    shift_grad[...] = plain
    gain_grad[...] = along
    plain, along = plain / pixels, along / pixels

    def finish(at, carry):
        mask = widen(keep[pl.ds(at, ROWS)], width)
        for m in range(mel_count):
            normed = (middle[m, pl.ds(at, ROWS)] - center) * inverse
            rows = slope[m, pl.ds(at, ROWS)] - plain - normed * along
            grad[m, pl.ds(at, ROWS)] = (mask * (scale * rows)).astype(bf16)
        return carry

    by_rows(total, finish, 0)


def second_block(one, two, weight, partial, keep, scales, starts, cotangents, own):
    mel_count, total, width = one.shape
    padded = (mel_count, total + 2 * TILE, width)
    full = (mel_count, total, width)
    return call(
        second_kernel,
        (starts, one, two, weight, partial, keep, scales, cotangents),
        [scalar_spec()] + [whole_spec()] * 6 + [place_spec()],
        [((own, width), f32), (full, bf16), ((1, width), f32), ((1, width), f32)],
        [whole_spec()] * 4,
        [
            pltpu.VMEM(full, f32),
            pltpu.VMEM(full, f32),
            pltpu.VMEM(padded, f32),
            pltpu.VMEM(padded, f32),
            pltpu.VMEM((width // LANES, total, LANES), f32),
            pltpu.VMEM((total // 2, width), f32),
            pltpu.VMEM((total // 2, width), f32),
            pltpu.SemaphoreType.DMA((cotangents.shape[0],)),
        ],
        2 * 18 * mel_count * total * width * width,
        22,
    )


def back_kernel(bit, starts, one, two, weight, weight_two, out, lower, middle, upper):
    mel_count, total, width = one.shape
    column = lax.axis_index("chan")
    start = pl.multiple_of((column ^ bit) * width, width)
    clear_edges(lower, upper, total)
    convolve_back(
        [lambda m: one[m], lambda m: two[m]],
        [
            lambda a, b: weight[a, b, pl.ds(start, width)],
            lambda a, b: weight_two[a, b, pl.ds(start, width)],
        ],
        lower,
        middle,
        upper,
        total,
    )

    def combine(at, carry):
        before, after = same_clip(starts, at, (ROWS, width), total)
        for m in range(mel_count):
            rows = joined(lower, middle, upper, m, at, before, after)
            out[m, pl.ds(at, ROWS)] = rows.astype(out.dtype)
        return carry

    by_rows(total, combine, 0)


def hidden_back(bit, one, two, weight, weight_two, starts, kind):
    mel_count, total, width = one.shape
    padded = (mel_count, total + 2 * TILE, width)
    return call(
        functools.partial(back_kernel, bit),
        (starts, one, two, weight, weight_two),
        [scalar_spec()] + [whole_spec()] * 4,
        [((mel_count, total, width), kind)],
        [whole_spec()],
        [
            pltpu.VMEM(padded, f32),
            pltpu.VMEM((mel_count, total, width), f32),
            pltpu.VMEM(padded, f32),
        ],
        2 * 18 * mel_count * total * width * width,
        14,
    )[0]


def norm_kernel(mine, other, slope, pre, stats, scales, keep, *refs):
    grad, window, gain_grad, shift_grad, padded = refs
    mel_count, total, width = mine.shape
    center, inverse, pixels = stats[0:1], stats[1:2], stats[2:3]
    blank = jnp.zeros((TILE, width), f32)
    edge = (padded.shape[1] - total) // 2
    reach = window.shape[1]
    frames = reach - 2 * edge
    place = lax.axis_index("tm")

    def slopes(at, sums):
        plain, along = sums
        for m in range(mel_count):
            rows = mine[m, pl.ds(at, ROWS)] + other[m, pl.ds(at, ROWS)].astype(f32)
            step = rows * slope[m, pl.ds(at, ROWS)]
            mine[m, pl.ds(at, ROWS)] = step
            plain = plain + fold(step)
            along = along + fold(step * ((pre[m, pl.ds(at, ROWS)] - center) * inverse))
        return plain, along

    plain, along = by_rows(total, slopes, (blank, blank))
    plain, along = column_sum(plain), column_sum(along)
    shift_grad[...] = plain
    gain_grad[...] = along
    plain, along = plain / pixels, along / pixels
    scale = scales[0:1] * inverse
    for m in range(mel_count):
        padded[m, :edge] = jnp.zeros((edge, width), bf16)
        padded[m, edge + total :] = jnp.zeros((edge, width), bf16)

    def finish(at, carry):
        mask = widen(keep[pl.ds(at, ROWS)], width)
        for m in range(mel_count):
            normed = (pre[m, pl.ds(at, ROWS)] - center) * inverse
            rows = mine[m, pl.ds(at, ROWS)] - plain - normed * along
            rows = (mask * (scale * rows)).astype(bf16)
            grad[m, pl.ds(at, ROWS)] = rows
            padded[m, pl.ds(pl.multiple_of(at + edge, 16), ROWS)] = rows
        return carry

    by_rows(total, finish, 0)
    for m in range(mel_count):
        window[m] = padded[m, pl.ds(pl.multiple_of(place * frames, frames), reach)]


def norm_back_first(mine, other, slope, pre, stats, scales, keep, frames):
    mel_count, total, width = mine.shape
    edge = 16
    return call(
        norm_kernel,
        (mine, other, slope, pre, stats, scales, keep),
        [whole_spec()] * 7,
        [
            ((mel_count, total, width), bf16),
            ((mel_count, frames + 2 * edge, width), bf16),
            ((1, width), f32),
            ((1, width), f32),
        ],
        [whole_spec()] * 4,
        [pltpu.VMEM((mel_count, total + 2 * edge, width), bf16)],
        2**28,
        12,
    )


def weight_kernel(group_count, starts, *refs):
    fields = refs[:group_count]
    grad, out = refs[group_count : group_count + 2]
    spaced, steps, results, sems = refs[group_count + 2 :]
    mel_count, total, out_width = grad.shape
    column = lax.axis_index("chan")
    for m in range(mel_count):
        spaced[m, :TILE] = jnp.zeros((TILE, out_width), f32)
        spaced[m, TILE + total :] = jnp.zeros((TILE, out_width), f32)

    def expand(at, carry):
        for m in range(mel_count):
            spaced[m, pl.ds(pl.multiple_of(at + TILE, TILE), ROWS)] = grad[
                m, pl.ds(at, ROWS)
            ].astype(f32)
        return carry

    by_rows(total, expand, 0)

    def shift(at, carry):
        before, after = same_clip(starts, at, (ROWS, out_width), total)
        for m in range(mel_count):
            rows = spaced[m, pl.ds(at, ROWS + 2 * TILE)]
            ahead = jnp.where(after, rows[TILE + 1 : TILE + 1 + ROWS], 0.0)
            behind = jnp.where(before, rows[TILE - 1 : TILE - 1 + ROWS], 0.0)
            steps[0, m, pl.ds(at, ROWS)] = ahead.astype(bf16)
            steps[1, m, pl.ds(at, ROWS)] = behind.astype(bf16)
        return carry

    by_rows(total, shift, 0)
    width = results.shape[3]
    copies = [None, None]
    count = 0
    for i, field in enumerate(fields):
        for part in range(field.shape[2] // width):
            slot = count % 2
            if copies[slot] is not None:
                copies[slot].wait()
            for a in range(3):
                for b in range(3):
                    acc = None
                    for m in range(mel_count):
                        if 0 <= m + b - 1 < mel_count:
                            right = grad[m] if a == 1 else steps[a // 2, m]
                            left = field[m + b - 1, :, part * width : (part + 1) * width]
                            piece = lax.dot_general(
                                left,
                                right,
                                (((0,), (0,)), ((), ())),
                                preferred_element_type=f32,
                            )
                            acc = piece if acc is None else acc + piece
                    results[slot, 3 * a + b] = acc
            if group_count > 1:
                start = pl.multiple_of((column ^ i) * width, width)
            else:
                start = part * width
            copies[slot] = pltpu.make_async_copy(
                results.at[slot], out.at[:, pl.ds(start, width)], sems.at[slot]
            )
            copies[slot].start()
            count += 1
    for copy in copies:
        if copy is not None:
            copy.wait()


def weight_back(fields, grad, starts):
    mel_count, total, out_width = grad.shape
    in_width = sum(f.shape[2] for f in fields)
    width = 256
    out = call(
        functools.partial(weight_kernel, len(fields)),
        (starts, *fields, grad),
        [scalar_spec()] + [whole_spec()] * (len(fields) + 1),
        [((9, in_width, out_width), f32)],
        [place_spec()],
        [
            pltpu.VMEM((mel_count, total + 2 * TILE, out_width), f32),
            pltpu.VMEM((2, mel_count, total, out_width), bf16),
            pltpu.VMEM((2, 9, width, out_width), f32),
            pltpu.SemaphoreType.DMA((2,)),
        ],
        2 * 9 * mel_count * total * in_width * out_width,
        14,
    )[0]
    return out.reshape(3, 3, in_width, out_width)


def input_kernel(starts, one, two, weight, weight_two, mine, other, lower, middle, upper):
    mel_count, reach, width = one.shape
    frames, lanes = mine.shape[1], mine.shape[2]
    edge = (reach - frames) // 2
    total = frames * lax.axis_size("tm")
    place, column = lax.axis_index("tm"), lax.axis_index("chan")
    for bit, out in ((2, other), (0, mine)):
        start = pl.multiple_of((column ^ bit) * lanes, lanes)
        convolve_back(
            [lambda m: one[m], lambda m: two[m]],
            [
                lambda a, b: weight[a, b, pl.ds(start, lanes)],
                lambda a, b: weight_two[a, b, pl.ds(start, lanes)],
            ],
            lower,
            middle,
            upper,
            reach,
        )
        before, after = same_clip(starts, place * frames, (frames, lanes), total)
        for m in range(mel_count):
            low = lower[m, TILE + edge - 1 : TILE + edge - 1 + frames]
            high = upper[m, TILE + edge + 1 : TILE + edge + 1 + frames]
            out[m] = (
                middle[m, edge : edge + frames]
                + jnp.where(before, low, 0.0)
                + jnp.where(after, high, 0.0)
            )


def input_back(one, two, weight, weight_two, starts, frames, lanes):
    mel_count, reach, width = one.shape
    shape = (mel_count, frames, lanes)
    return call(
        input_kernel,
        (starts, one, two, weight, weight_two),
        [scalar_spec()] + [whole_spec()] * 4,
        [(shape, f32), (shape, f32)],
        [whole_spec()] * 2,
        [
            pltpu.VMEM((mel_count, reach + 2 * TILE, lanes), f32),
            pltpu.VMEM((mel_count, reach, lanes), f32),
            pltpu.VMEM((mel_count, reach + 2 * TILE, lanes), f32),
        ],
        2**28,
        8,
    )


def whole_frames(
    features,
    conv1_weight,
    norm1_gain,
    norm1_bias,
    conv2_weight,
    norm2_gain,
    norm2_bias,
    clip_starts,
    valid,
    readout_grad,
):
    frames, mel_count, lanes = features.shape
    places = lax.axis_size("tm")
    total = frames * places
    scales = jnp.stack([norm1_gain, norm1_bias, norm2_gain, norm2_bias])

    marked = jnp.where(valid[:, None, None] > 0, features, jnp.asarray(ABSENT, bf16))
    own = jnp.transpose(marked, (1, 0, 2))
    along = jnp.stack([own] + [swap(own, "tm", 2 * k) for k in range(1, places // 2)])
    near = [
        along,
        swap(along, "tm", 1),
        swap(along, "chan", 2),
        swap_both(along, "tm", 1, "chan", 2),
    ]
    blocks = near + [swap(block, "chan", 1) for block in near]

    hidden, field, pre, keep, stats = first_block(
        blocks, conv1_weight, scales, clip_starts, total
    )
    hidden_near = swap(hidden, "chan", 1)
    hidden_far = swap(hidden, "chan", 2)

    conv2_weight, conv1_weight, readout_grad, hidden_near = lax.optimization_barrier(
        (conv2_weight, conv1_weight, readout_grad, hidden_near)
    )
    partial = second_partial(hidden, hidden_near, conv2_weight, clip_starts)
    slope = first_slope(pre, stats, scales, keep)
    cotangent = readout_grad[None]
    bit = 1
    while bit < places:
        cotangent = jnp.concatenate([cotangent, swap(cotangent, "tm", bit)])
        bit *= 2
    other_conv2 = swap(conv2_weight, "chan", 1)
    other_conv1 = swap(conv1_weight, "chan", 1)
    hidden_far, partial, slope, cotangent, other_conv2, other_conv1 = lax.optimization_barrier(
        (hidden_far, partial, slope, cotangent, other_conv2, other_conv1)
    )

    hidden_last = swap(hidden_far, "chan", 1)
    readout, grad2, gain2_grad, shift2_grad = second_block(
        hidden_far,
        hidden_last,
        conv2_weight,
        partial,
        keep,
        scales,
        clip_starts,
        cotangent,
        readout_grad.shape[0],
    )
    grad2_near = swap(grad2, "chan", 1)
    away = hidden_back(2, grad2, grad2_near, conv2_weight, other_conv2, clip_starts, bf16)
    came = swap(away, "chan", 2)

    mine = hidden_back(0, grad2, grad2_near, conv2_weight, other_conv2, clip_starts, f32)
    weight2_grad = weight_back(
        [hidden, hidden_near, hidden_far, hidden_last], grad2, clip_starts
    )
    came, mine, weight2_grad = lax.optimization_barrier((came, mine, weight2_grad))

    grad1, window, gain1_grad, shift1_grad = norm_back_first(
        mine, came, slope, pre, stats, scales, keep, frames
    )
    window_near = swap(window, "chan", 1)
    input_mine, input_away = input_back(
        window, window_near, conv1_weight, other_conv1, clip_starts, frames, lanes
    )
    input_came = swap(input_away, "chan", 2)
    weight1_grad = weight_back([field], grad1, clip_starts)
    input_came, weight1_grad = lax.optimization_barrier((input_came, weight1_grad))
    live = (valid > 0).astype(f32)[None, :, None]
    input_grad = jnp.transpose((input_mine + input_came) * live, (1, 0, 2))
    return (
        readout,
        input_grad,
        weight1_grad,
        gain1_grad[0],
        shift1_grad[0],
        weight2_grad,
        gain2_grad[0],
        shift2_grad[0],
    )


def fits_whole(frames, places, columns, widths):
    return (
        places > 1
        and places & (places - 1) == 0
        and columns == 4
        and frames % 32 == 0
        and frames * places <= 512
        and all(w % (columns * LANES) == 0 for w in widths)
        and widths[1] == columns * 256
    )


def shards(*arrays):
    features, conv1_weight, conv2_weight = arrays[0], arrays[1], arrays[4]
    if fits_whole(
        features.shape[0],
        lax.axis_size("tm"),
        lax.axis_size("chan"),
        (conv1_weight.shape[2], conv2_weight.shape[2]),
    ):
        return whole_frames(*arrays)
    return split_frames(*arrays)


def solution(mesh):
    return jax.shard_map(
        shards,
        mesh=mesh,
        in_specs=(
            P("tm", None, "chan"),
            P(None, None, None, "chan"),
            P("chan"),
            P("chan"),
            P(None, None, None, "chan"),
            P("chan"),
            P("chan"),
            P(),
            P("tm"),
            P("tm", "chan"),
        ),
        out_specs=(
            P("tm", "chan"),
            P("tm", None, "chan"),
            P(None, None, None, "chan"),
            P("chan"),
            P("chan"),
            P(None, None, None, "chan"),
            P("chan"),
            P("chan"),
        ),
        check_vma=False,
    )
```

```python
import functools

import jax
import jax.numpy as jnp
from jax import lax
from jax.experimental import pallas as pl
from jax.experimental.pallas import tpu as pltpu
from jax.sharding import PartitionSpec as P

EPS = 1e-05
highest = lax.Precision.HIGHEST
f32 = jnp.float32
bf16 = jnp.bfloat16


def padded_2(shard, sides, width):
    for axis, dim in sides:
        count, length = (lax.axis_size(axis), shard.shape[dim])
        up = [(i, (i + 1) % count) for i in range(count - 1)]
        down = [(j, i) for i, j in up]
        last = lax.slice_in_dim(shard, length - width, length, axis=dim)
        leading = lax.slice_in_dim(shard, 0, width, axis=dim)
        before = lax.ppermute(last, axis, up)
        after = lax.ppermute(leading, axis, down)
        shard = jnp.concatenate([before, shard, after], axis=dim)
    return shard


def entering(part, axis, combine, identity, reverse):
    count = lax.axis_size(axis)
    place = lax.axis_index(axis)
    ahead = count - 1 - place if reverse else place
    gathered = jax.tree.map(lambda a: lax.all_gather(a, axis), part)
    state = jax.tree.map(lambda a, e: jnp.zeros_like(a) + jnp.asarray(e, a.dtype), part, identity)

    def one(step, state):
        source = count - 1 - step if reverse else step
        return combine(
            state, jax.tree.map(lambda a: lax.dynamic_index_in_dim(a, source, 0, False), gathered)
        )

    return lax.fori_loop(0, ahead, one, state)


def frame_flags(clip_starts, first_frame, frame_count, frame_total):
    position = first_frame - 2 + jnp.arange(frame_count + 4, dtype=jnp.int32)
    segment = jnp.sum((clip_starts[None, :] <= position[:, None]).astype(jnp.int32), axis=1) - 1
    inside = (position >= 0) & (position < frame_total)
    middle = segment[1:-1]
    before_same = inside[1:-1] & inside[:-2] & (middle == segment[:-2])
    after_same = inside[1:-1] & inside[2:] & (middle == segment[2:])
    return (segment[2:-2], before_same, after_same)


def conv_forward(padded, weight, factors):
    frame_count = padded.shape[0] - 2
    mel_count = padded.shape[1]
    wide_field = jnp.pad(padded, ((0, 0), (1, 1), (0, 0)))
    result = jnp.zeros((frame_count, mel_count, weight.shape[3]), jnp.float32)
    for tap_row in range(3):
        partial_value = jnp.zeros((frame_count * mel_count, weight.shape[3]), jnp.float32)
        for tap_col in range(3):
            window = wide_field[
                tap_row : tap_row + frame_count, tap_col : tap_col + mel_count, :
            ].reshape(frame_count * mel_count, -1)
            partial_value = partial_value + jnp.dot(
                window, weight[tap_row, tap_col], preferred_element_type=jnp.float32
            )
        result = (
            result
            + partial_value.reshape(frame_count, mel_count, -1) * factors[tap_row][:, None, None]
        )
    return result


def conv_weight_grad(padded, grad_out, factors):
    frame_count = grad_out.shape[0]
    mel_count = grad_out.shape[1]
    wide_field = jnp.pad(padded, ((0, 0), (1, 1), (0, 0)))
    rows_out = []
    for tap_row in range(3):
        scaled = (grad_out * factors[tap_row][:, None, None].astype(jnp.bfloat16)).reshape(
            frame_count * mel_count, -1
        )
        taps_out = []
        for tap_col in range(3):
            window = wide_field[
                tap_row : tap_row + frame_count, tap_col : tap_col + mel_count, :
            ].reshape(frame_count * mel_count, -1)
            taps_out.append(
                lax.dot_general(
                    window, scaled, (((0,), (0,)), ((), ())), preferred_element_type=jnp.float32
                )
            )
        rows_out.append(jnp.stack(taps_out))
    return jnp.stack(rows_out)


def conv_input_grad(grad_padded, weight, edge_factors):
    frame_count = grad_padded.shape[0] - 2
    mel_count = grad_padded.shape[1]
    wide_field = jnp.pad(grad_padded, ((0, 0), (1, 1), (0, 0)))
    result = jnp.zeros((frame_count * mel_count, weight.shape[2]), jnp.float32)
    for tap_row in range(3):
        scaled = wide_field * edge_factors[tap_row][:, None, None]
        for tap_col in range(3):
            window = scaled[
                2 - tap_row : 2 - tap_row + frame_count, 2 - tap_col : 2 - tap_col + mel_count, :
            ].reshape(frame_count * mel_count, -1)
            result = result + lax.dot_general(
                window,
                weight[tap_row, tap_col],
                (((1,), (1,)), ((), ())),
                preferred_element_type=jnp.float32,
            )
    return result.reshape(frame_count, mel_count, -1)


def join_keyed(earlier_item, later_item):
    keep_first = later_item[0] < 0.0
    same_key = later_item[0] == earlier_item[0]
    merged = [jnp.where(keep_first, earlier_item[0], later_item[0])]
    for first_part, second_part in zip(earlier_item[1:], later_item[1:]):
        extra = (1,) * (first_part.ndim - keep_first.ndim)
        keep_wide = jnp.reshape(keep_first, keep_first.shape + extra)
        same_wide = jnp.reshape(same_key, same_key.shape + extra)
        merged.append(
            jnp.where(
                keep_wide, first_part, jnp.where(same_wide, first_part + second_part, second_part)
            )
        )
    return tuple(merged)


def smooth(argument):
    return jax.nn.gelu(argument, approximate=False)


def split_frames(
    features,
    conv1_weight,
    norm1_gain,
    norm1_bias,
    conv2_weight,
    norm2_gain,
    norm2_bias,
    clip_starts,
    valid,
    readout_grad,
):
    frame_count = features.shape[0]
    mel_count = features.shape[1]
    cycle_size = lax.axis_size("tm")
    cycle_index = lax.axis_index("tm")
    segment, before_same, after_same = frame_flags(
        clip_starts, cycle_index * frame_count, frame_count, frame_count * cycle_size
    )
    keep_mask = valid.astype(jnp.float32)
    keep_cube = keep_mask[:, None, None]
    own_factors = (
        before_same[1:-1].astype(jnp.float32),
        jnp.ones((frame_count,), jnp.float32),
        after_same[1:-1].astype(jnp.float32),
    )
    edge_factors = (
        before_same.astype(jnp.bfloat16),
        jnp.ones((frame_count + 2,), jnp.bfloat16),
        after_same.astype(jnp.bfloat16),
    )
    local_count = jnp.sum(keep_mask) * mel_count

    def spread(shard):
        padded = padded_2(shard, (("tm", 0),), 1)
        return lax.all_gather(padded, "chan", axis=2, tiled=True)

    def normalize(field_in, gain_vec, shift_vec):
        value_sums, squares, pixel_count = lax.psum(
            (
                jnp.sum(field_in * keep_cube, axis=(0, 1)),
                jnp.sum(field_in * field_in * keep_cube, axis=(0, 1)),
                local_count,
            ),
            "tm",
        )
        center = value_sums / pixel_count
        variance = squares / pixel_count - center * center
        inverse_std = lax.rsqrt(variance + EPS)
        normed = (field_in - center) * inverse_std
        return (gain_vec * normed + shift_vec, normed, inverse_std, pixel_count)

    def norm_back(grad_norm, normed, inverse_std, gain_vec, pixel_count):
        bias_grad, gain_grad = lax.psum(
            (jnp.sum(grad_norm, axis=(0, 1)), jnp.sum(grad_norm * normed, axis=(0, 1))), "tm"
        )
        grad_pre = (
            keep_cube
            * (gain_vec * inverse_std)
            * (grad_norm - bias_grad / pixel_count - normed * (gain_grad / pixel_count))
        )
        return (grad_pre.astype(jnp.bfloat16), gain_grad, bias_grad)

    def send_back(grad_pre, weight):
        padded = padded_2(grad_pre, (("tm", 0),), 1)
        partial_sum = conv_input_grad(padded, weight, edge_factors)
        return lax.psum_scatter(partial_sum, "chan", scatter_dimension=2, tiled=True)

    wide_in = spread(features * keep_cube.astype(jnp.bfloat16))
    first_pre = conv_forward(wide_in, conv1_weight, own_factors)
    first_norm, first_hat, first_scale, pixel_count = normalize(first_pre, norm1_gain, norm1_bias)
    first_act, first_pull = jax.vjp(smooth, first_norm)
    hidden = (first_act * keep_cube).astype(jnp.bfloat16)
    wide_mid = spread(hidden)
    second_pre = conv_forward(wide_mid, conv2_weight, own_factors)
    second_norm, second_hat, second_scale, pixel_count = normalize(
        second_pre, norm2_gain, norm2_bias
    )
    second_act, second_pull = jax.vjp(smooth, second_norm)
    pooled = (second_act * keep_cube).reshape(frame_count // 2, 2, mel_count, -1).mean(axis=(1, 2))
    pooled_keep = keep_mask[0::2]
    pooled_segment = segment[0::2]
    segment_key = pooled_segment.astype(jnp.float32)
    row_order = jnp.arange(frame_count // 2)
    lower_runs = (
        (pooled_segment[:, None] == pooled_segment[None, :])
        & (row_order[:, None] >= row_order[None, :])
    ).astype(jnp.float32)
    exponent = jnp.exp(pooled)
    counts = jnp.dot(lower_runs, pooled_keep, precision=highest)
    totals = jnp.dot(lower_runs, pooled_keep[:, None] * pooled, precision=highest)
    expsums = jnp.dot(lower_runs, pooled_keep[:, None] * exponent, precision=highest)
    zero_row = jnp.zeros_like(totals[0])
    prior_runs = entering(
        (segment_key[-1], counts[-1], totals[-1], expsums[-1]),
        "tm",
        join_keyed,
        (jnp.float32(-1.0), jnp.float32(0.0), zero_row, zero_row),
        False,
    )
    joined = (segment_key == prior_runs[0]).astype(jnp.float32)
    counts = counts + joined * prior_runs[1]
    totals = totals + joined[:, None] * prior_runs[2]
    expsums = expsums + joined[:, None] * prior_runs[3]
    readout = totals / counts[:, None] + jnp.log(expsums)
    by_count = readout_grad / counts[:, None]
    by_expsum = readout_grad / expsums
    later_mean = lax.dot_general(lower_runs, by_count, (((0,), (0,)), ((), ())), precision=highest)
    later_soft = lax.dot_general(lower_runs, by_expsum, (((0,), (0,)), ((), ())), precision=highest)
    beyond = entering(
        (segment_key[0], later_mean[0], later_soft[0]),
        "tm",
        join_keyed,
        (jnp.float32(-1.0), zero_row, zero_row),
        True,
    )
    joined_back = (segment_key == beyond[0]).astype(jnp.float32)[:, None]
    later_mean = later_mean + joined_back * beyond[1]
    later_soft = later_soft + joined_back * beyond[2]
    pooled_grad = pooled_keep[:, None] * (later_mean + exponent * later_soft)
    spread_grad = jnp.broadcast_to(
        (pooled_grad / (2 * mel_count))[:, None, None, :],
        (frame_count // 2, 2, mel_count, pooled_grad.shape[1]),
    )
    act_grad = spread_grad.reshape(frame_count, mel_count, -1) * keep_cube
    second_grad_norm = second_pull(act_grad)[0]
    second_grad_pre, gain2_grad, bias2_grad = norm_back(
        second_grad_norm, second_hat, second_scale, norm2_gain, pixel_count
    )
    weight2_grad = conv_weight_grad(wide_mid, second_grad_pre, own_factors)
    weight2_grad = lax.psum(weight2_grad, "tm")
    hidden_grad = send_back(second_grad_pre, conv2_weight)
    first_grad_norm = first_pull(hidden_grad * keep_cube)[0]
    first_grad_pre, gain1_grad, bias1_grad = norm_back(
        first_grad_norm, first_hat, first_scale, norm1_gain, pixel_count
    )
    weight1_grad = conv_weight_grad(wide_in, first_grad_pre, own_factors)
    weight1_grad = lax.psum(weight1_grad, "tm")
    input_grad = send_back(first_grad_pre, conv1_weight) * keep_cube
    return (
        readout,
        input_grad,
        weight1_grad,
        gain1_grad,
        bias1_grad,
        weight2_grad,
        gain2_grad,
        bias2_grad,
    )


ABSENT = 1024.0
ROWS = 32
TILE = 8
LANES = 128


def whole_spec():
    return pl.BlockSpec(memory_space=pltpu.VMEM)


def place_spec():
    return pl.BlockSpec(memory_space=pl.ANY)


def far_spec():
    return pl.BlockSpec(memory_space=pltpu.HBM)


def scalar_spec():
    return pl.BlockSpec(memory_space=pltpu.SMEM)


def call(body, operands, in_specs, outs, out_specs, scratch, flops, megabytes):
    return pl.pallas_call(
        body,
        out_shape=tuple(jax.ShapeDtypeStruct(s, d) for s, d in outs),
        in_specs=in_specs,
        out_specs=tuple(out_specs),
        scratch_shapes=scratch,
        compiler_params=pltpu.CompilerParams(vmem_limit_bytes=megabytes * 2**20),
        cost_estimate=pl.CostEstimate(flops=1000, bytes_accessed=1000, transcendentals=0),
    )(*operands)


def swap(shard, axis, bit):
    count = lax.axis_size(axis)
    return lax.ppermute(shard, axis, [(i, i ^ bit) for i in range(count)])


def gather_bits(places):
    bits = [1 << k for k in range(places.bit_length() - 1)]
    return bits[2:][::-1] + bits[:2] if len(bits) > 2 else bits


def swap_both(shard, first, first_bit, second, second_bit):
    rows, columns = lax.axis_size(first), lax.axis_size(second)
    pairs = [
        (i * columns + j, (i ^ first_bit) * columns + (j ^ second_bit))
        for i in range(rows)
        for j in range(columns)
    ]
    return lax.ppermute(shard, (first, second), pairs)


def same_clip(starts, at, shape, total):
    frame = lax.broadcasted_iota(jnp.int32, shape, 0) + at
    before = frame != starts[0]
    after = frame != total - 1
    for k in range(1, starts.shape[0]):
        before = before & (frame != starts[k])
        after = after & (frame != starts[k] - 1)
    return before, after


def widen(mask, width):
    return jnp.concatenate([mask] * (width // mask.shape[1]), axis=1)


def fold(value):
    total = value[:TILE]
    for k in range(TILE, value.shape[0], TILE):
        total = total + value[k : k + TILE]
    return total


def column_sum(value):
    return jnp.sum(value, axis=0, keepdims=True)


def taps(mel, mel_count):
    return [b for b in range(3) if 0 <= mel + b - 1 < mel_count]


def convolve(fields, weights, lower, middle, upper, total, add):
    mel_count = middle.shape[0]
    for m in range(mel_count):
        for a in range(3):
            acc = None
            for field, weight in zip(fields, weights):
                for b in taps(m, mel_count):
                    part = jnp.dot(field(m + b - 1), weight(a, b), preferred_element_type=f32)
                    acc = part if acc is None else acc + part
            if a == 0:
                lower[m, TILE : TILE + total] = acc
            elif a == 1:
                middle[m] = middle[m] + acc if add else acc
            else:
                upper[m, TILE : TILE + total] = acc


def convolve_back(fields, weights, lower, middle, upper, total):
    mel_count = middle.shape[0]
    for n in range(mel_count):
        for a in range(3):
            acc = None
            for field, weight in zip(fields, weights):
                for b in range(3):
                    if 0 <= n - b + 1 < mel_count:
                        part = lax.dot_general(
                            field(n - b + 1),
                            weight(a, b),
                            (((1,), (1,)), ((), ())),
                            preferred_element_type=f32,
                        )
                        acc = part if acc is None else acc + part
            if a == 2:
                lower[n, TILE : TILE + total] = acc
            elif a == 1:
                middle[n] = acc
            else:
                upper[n, TILE : TILE + total] = acc


def joined(lower, middle, upper, m, at, before, after):
    low = lower[m, pl.ds(at, ROWS + 2 * TILE)]
    high = upper[m, pl.ds(at, ROWS + 2 * TILE)]
    return (
        middle[m, pl.ds(at, ROWS)]
        + jnp.where(before, low[TILE - 1 : TILE - 1 + ROWS], 0.0)
        + jnp.where(after, high[TILE + 1 : TILE + 1 + ROWS], 0.0)
    )


def by_rows(total, body, init):
    return lax.fori_loop(
        0, total // ROWS, lambda i, c: body(pl.multiple_of(i * ROWS, ROWS), c), init
    )


def clear_edges(lower, upper, total):
    for m in range(lower.shape[0]):
        for ref in (lower, upper):
            ref[m, :TILE] = jnp.zeros((TILE, ref.shape[2]), f32)
            ref[m, TILE + total :] = jnp.zeros((TILE, ref.shape[2]), f32)


def moments(field, keep, count):
    first, second = column_sum(field[0]), column_sum(field[1])
    center = first / count
    return center, lax.rsqrt(second / count - center * center + EPS)


def phi_parts(value):
    return 0.5 * (1.0 + lax.erf(value * 0.7071067811865476))


def bell(value):
    return 0.3989422804014327 * jnp.exp(-0.5 * value * value)


def bring_kernel(starts_in, weight_in, *refs):
    vectors, (starts, weight, scales, sems) = refs[:4], refs[4:]
    copies = [pltpu.make_async_copy(weight_in, weight, sems.at[0])]
    for k, vector in enumerate(vectors):
        copies.append(pltpu.make_async_copy(vector, scales.at[k : k + 1], sems.at[1 + k]))
    for copy in copies:
        copy.start()
    for k in range(starts.shape[0]):
        starts[k] = starts_in[k]
    for copy in copies:
        copy.wait()


def bring(starts, weight, vectors):
    return call(
        bring_kernel,
        (starts, weight, *[v[None] for v in vectors]),
        [scalar_spec()] + [far_spec()] * 5,
        [(starts.shape, jnp.int32), (weight.shape, bf16), ((TILE, vectors[0].shape[0]), f32)],
        [scalar_spec(), whole_spec(), whole_spec()],
        [pltpu.SemaphoreType.DMA((5,))],
        0,
        4,
    )


def first_kernel(*refs):
    starts, blocks, (weight, scales) = refs[0], refs[1:9], refs[9:11]
    low, high, picked, field_out, pre_out, keep, stats = refs[11:18]
    field, lower, middle, upper, sems = refs[18:]
    mel_count, total, width = field.shape
    out_width = middle.shape[2]
    place, column = lax.axis_index("tm"), lax.axis_index("chan")
    copies = []
    frames, lanes = blocks[0].shape[2], blocks[0].shape[3]
    count = blocks[0].shape[0]
    for i, block in enumerate(blocks):
        core, row, side = i // 4, (i // 2) % 2, i % 2
        from_column = column ^ (2 * row + core)
        for k in range(count):
            from_place = place ^ (2 * k + side)
            copies.append(
                pltpu.make_async_copy(
                    block.at[k],
                    field.at[
                        :,
                        pl.ds(pl.multiple_of(from_place * frames, frames), frames),
                        pl.ds(pl.multiple_of(from_column * lanes, lanes), lanes),
                    ],
                    sems.at[len(copies)],
                )
            )
    for copy in copies:
        copy.start()
    clear_edges(lower, upper, total)
    for copy in copies:
        copy.wait()

    def decode(at, carry):
        for m in range(mel_count):
            rows = field[m, pl.ds(at, ROWS)]
            if m == 0:
                keep[pl.ds(at, ROWS)] = (rows[:, :LANES].astype(f32) < ABSENT / 2).astype(f32)
            field[m, pl.ds(at, ROWS)] = jnp.where(rows < ABSENT / 2, rows, jnp.zeros_like(rows))
        return carry

    by_rows(total, decode, 0)
    save = pltpu.make_async_copy(field, field_out, sems.at[1])
    save.start()
    convolve(
        [lambda m: field[m]], [lambda a, b: weight[a, b]], lower, middle, upper, total, False
    )

    def combine(at, sums):
        before, after = same_clip(starts, at, (ROWS, out_width), total)
        mask = widen(keep[pl.ds(at, ROWS)], out_width)
        one, two, num = sums
        num = num + fold(mask)
        for m in range(mel_count):
            rows = joined(lower, middle, upper, m, at, before, after)
            middle[m, pl.ds(at, ROWS)] = rows
            kept = rows * mask
            one = one + fold(kept)
            two = two + fold(kept * rows)
        return one, two, num

    blank = jnp.zeros((TILE, out_width), f32)
    one, two, num = by_rows(total, combine, (blank, blank, blank))
    save_pre = pltpu.make_async_copy(middle, pre_out, sems.at[0])
    save_pre.start()
    pixels = column_sum(num) * mel_count
    center, inverse = moments((one, two), keep, pixels)
    stats[0:1] = center
    stats[1:2] = inverse
    stats[2:3] = pixels
    scale = scales[0:1] * inverse
    offset = scales[1:2] - center * scale

    def activate(at, carry):
        mask = widen(keep[pl.ds(at, ROWS)], out_width)
        for m in range(mel_count):
            value = middle[m, pl.ds(at, ROWS)] * scale + offset
            rows = (value * phi_parts(value) * mask).astype(bf16)
            if m < mel_count // 2:
                low[m, pl.ds(at, ROWS)] = rows
            else:
                high[m - mel_count // 2, pl.ds(at, ROWS)] = rows
        return carry

    by_rows(total, activate, 0)
    reach = picked.shape[1]
    for m in range(picked.shape[0]):
        picked[m] = high[m, pl.ds(pl.multiple_of((place % 2) * reach, reach), reach)]
    save.wait()
    save_pre.wait()


def first_block(blocks, weight, scales, starts, total):
    count, mel_count, frames, lanes = blocks[0].shape
    width, out_width = weight.shape[2], weight.shape[3]
    padded = (mel_count, total + 2 * TILE, out_width)
    return call(
        first_kernel,
        (starts, *blocks, weight, scales),
        [scalar_spec()] + [place_spec()] * 8 + [whole_spec()] * 2,
        [
            ((mel_count // 2, total, out_width), bf16),
            ((mel_count // 2, total, out_width), bf16),
            ((mel_count // 2, total // 2, out_width), bf16),
            ((mel_count, total, width), bf16),
            ((mel_count, total, out_width), f32),
            ((total, LANES), f32),
            ((TILE, out_width), f32),
        ],
        [whole_spec()] * 3 + [place_spec()] * 2 + [whole_spec()] * 2,
        [
            pltpu.VMEM((mel_count, total, width), bf16),
            pltpu.VMEM(padded, f32),
            pltpu.VMEM((mel_count, total, out_width), f32),
            pltpu.VMEM(padded, f32),
            pltpu.SemaphoreType.DMA((8 * count,)),
        ],
        2 * 9 * mel_count * total * width * out_width,
        16,
    )


def slope_kernel(pre, stats, scales, keep, slope):
    mel_count, total, width = pre.shape
    center, inverse = stats[0:1], stats[1:2]
    scale = scales[0:1] * inverse
    offset = scales[1:2] - center * scale

    def rows(at, carry):
        mask = widen(keep[pl.ds(at, ROWS)], width)
        for m in range(mel_count):
            value = pre[m, pl.ds(at, ROWS)] * scale + offset
            slope[m, pl.ds(at, ROWS)] = mask * (phi_parts(value) + value * bell(value))
        return carry

    by_rows(total, rows, 0)


def first_slope(pre, stats, scales, keep):
    return call(
        slope_kernel,
        (pre, stats, scales, keep),
        [whole_spec()] * 4,
        [(pre.shape, f32)],
        [whole_spec()],
        [],
        2**28,
        6,
    )[0]


def gather_taps(parts, groups, weight, lower, middle, upper, outputs, first=None):
    total, width = middle.shape[1], middle.shape[2]
    for k, m in enumerate(outputs):
        for a in range(3):
            acc = None
            for mels, arrays in parts:
                for j, n in enumerate(mels):
                    b = n - m + 1
                    if 0 <= b < 3:
                        for array, start in zip(arrays, groups):
                            piece = jnp.dot(
                                array[j],
                                weight[a, b, pl.ds(start, width)],
                                preferred_element_type=f32,
                            )
                            acc = piece if acc is None else acc + piece
            target, shift = ((lower, TILE), (middle, 0), (upper, TILE))[a]
            rows = total
            if first is not None:
                rows = total // 2
                empty = pl.ds(pl.multiple_of(total // 2 - first + shift, TILE), rows)
                target[k, empty] = jnp.zeros((rows, width), f32)
                target[k, pl.ds(pl.multiple_of(first + shift, TILE), rows)] = acc
            elif acc is None:
                target[k, shift : shift + rows] = jnp.zeros((rows, width), f32)
            else:
                target[k, shift : shift + rows] = acc


def group_starts(bits, width):
    column = lax.axis_index("chan")
    return [pl.multiple_of((column ^ bit) * width, width) for bit in bits]


def near_kernel(starts, low, high, low_two, high_two, weight, out, lower, upper):
    mel_count, total, width = out.shape
    half = mel_count // 2
    clear_edges(lower, upper, total)
    parts = [(range(half), (low, low_two)), (range(half, mel_count), (high, high_two))]
    groups = group_starts((0, 1), width)
    gather_taps(parts, groups, weight, lower, out, upper, range(mel_count))

    def combine(at, carry):
        before, after = same_clip(starts, at, (ROWS, width), total)
        for m in range(mel_count):
            out[m, pl.ds(at, ROWS)] = joined(lower, out, upper, m, at, before, after)
        return carry

    by_rows(total, combine, 0)


def near_part(low, high, low_two, high_two, weight, starts):
    half, total, width = low.shape
    padded = (2 * half, total + 2 * TILE, width)
    return call(
        near_kernel,
        (starts, low, high, low_two, high_two, weight),
        [scalar_spec()] + [whole_spec()] * 5,
        [((2 * half, total, width), f32)],
        [whole_spec()],
        [pltpu.VMEM(padded, f32)] * 2,
        0,
        14,
    )[0]


def early_kernel(starts, picked, picked_two, weight, early, lower, upper):
    outputs, total, width = early.shape
    mel_count = picked.shape[0] + outputs - 1
    half = mel_count - picked.shape[0]
    begin = (lax.axis_index("tm") % 2) * (total // 2)
    clear_edges(lower, upper, total)
    parts = [(range(half, mel_count), (picked, picked_two))]
    groups = group_starts((2, 3), width)
    mels = range(half - 1, mel_count)
    gather_taps(parts, groups, weight, lower, early, upper, mels, begin)

    def combine(at, carry):
        before, after = same_clip(starts, at, (ROWS, width), total)
        for k in range(outputs):
            early[k, pl.ds(at, ROWS)] = joined(lower, early, upper, k, at, before, after)
        return carry

    by_rows(total, combine, 0)


def early_part(picked, picked_two, weight, starts):
    half, rows, width = picked.shape
    total = 2 * rows
    shape = (half + 1, total, width)
    return call(
        early_kernel,
        (starts, picked, picked_two, weight),
        [scalar_spec()] + [whole_spec()] * 3,
        [(shape, f32)],
        [whole_spec()],
        [pltpu.VMEM((half + 1, total + 2 * TILE, width), f32)] * 2,
        0,
        12,
    )[0]


def run_sums(mask, plain, values):
    width = (plain + values)[0].shape[1]
    terms = list(plain)
    for value in values:
        for _ in range(3):
            term = value.astype(bf16)
            terms.append(term)
            value = value - term.astype(f32)
    out = jnp.dot(mask, jnp.concatenate(terms, axis=1), preferred_element_type=f32)
    parts = [out[:, k * width : (k + 1) * width] for k in range(len(terms))]
    results = parts[: len(plain)]
    for k in range(len(plain), len(parts), 3):
        results.append(parts[k] + (parts[k + 1] + parts[k + 2]))
    return results


def second_kernel(
    starts, near, early, far, rest, far_two, rest_two, weight, keep, scales, *refs
):
    cotangents, (readout, grad, gain_grad, shift_grad) = refs[:-15], refs[-15:-11]
    middle, slope, lower, upper, late, late_lower, late_upper, hold, wide, full, sems = refs[-11:]
    mel_count, total, width = middle.shape
    half = mel_count // 2
    place = lax.axis_index("tm")
    pooled_total = total // 2
    own = readout.shape[0]
    copies = []
    pieces = [(part, i) for part in cotangents for i in range(part.shape[0])]
    bits = gather_bits(len(pieces))
    for k, (part, i) in enumerate(pieces):
        source = place ^ sum(bit for j, bit in enumerate(bits) if k >> j & 1)
        copies.append(
            pltpu.make_async_copy(
                part.at[i],
                full.at[pl.ds(pl.multiple_of(source * own, own), own)],
                sems.at[k],
            )
        )
    for copy in copies:
        copy.start()

    groups = group_starts((2, 3), width)
    clear_edges(lower, upper, total)
    clear_edges(late_lower, late_upper, total)
    parts = [(range(half), (far, far_two))]
    gather_taps(parts, groups, weight, lower, middle, upper, range(half + 1))
    parts = [(range(half, mel_count), (rest, rest_two))]
    begin = (1 - place % 2) * (total // 2)
    outputs = range(half - 1, mel_count)
    gather_taps(parts, groups, weight, late_lower, late, late_upper, outputs, begin)
    blank = jnp.zeros((TILE, width), f32)

    def combine(at, sums):
        before, after = same_clip(starts, at, (ROWS, width), total)
        mask = widen(keep[pl.ds(at, ROWS)], width)
        first, second, num = sums
        num = num + fold(mask)
        for m in range(mel_count):
            rows = near[m, pl.ds(at, ROWS)]
            if m <= half:
                rows = rows + joined(lower, middle, upper, m, at, before, after)
            if m in outputs:
                k = m - outputs[0]
                new = joined(late_lower, late, late_upper, k, at, before, after)
                rows = rows + (early[k, pl.ds(at, ROWS)] + new)
            middle[m, pl.ds(at, ROWS)] = rows
            kept = rows * mask
            first = first + fold(kept)
            second = second + fold(kept * rows)
        return first, second, num

    first, second, num = by_rows(total, combine, (blank, blank, blank))
    pixels = column_sum(num) * mel_count
    center, inverse = moments((first, second), keep, pixels)
    scale = scales[2:3] * inverse
    offset = scales[3:4] - center * scale

    def activate(at, carry):
        mask = widen(keep[pl.ds(at, ROWS)], width)
        pooled = jnp.zeros((ROWS, width), f32)
        for m in range(mel_count):
            value = middle[m, pl.ds(at, ROWS)] * scale + offset
            share = phi_parts(value)
            pooled = pooled + value * share
            slope[m, pl.ds(at, ROWS)] = mask * (share + value * bell(value))
        pooled = pooled * mask
        for c in range(width // LANES):
            hold[c, pl.ds(at, ROWS)] = pooled[:, c * LANES : (c + 1) * LANES]
        return carry

    by_rows(total, activate, 0)

    even = pl.ds(0, pooled_total, stride=2)
    odd = pl.ds(1, pooled_total, stride=2)
    pooled = jnp.concatenate(
        [hold[c, even] + hold[c, odd] for c in range(width // LANES)], axis=1
    ) * (0.5 / mel_count)
    present = widen(keep[even], width)
    square = (pooled_total, pooled_total)
    row = lax.broadcasted_iota(jnp.int32, square, 0)
    col = lax.broadcasted_iota(jnp.int32, square, 1)
    same = row >= col
    back = row <= col
    for k in range(1, starts.shape[0]):
        crossed = (2 * row < starts[k]) != (2 * col < starts[k])
        same = same & ~crossed
        back = back & ~crossed
    ahead, behind = same.astype(f32).astype(bf16), back.astype(f32).astype(bf16)
    exponent = jnp.exp(pooled)
    counts, totals, sums = run_sums(
        ahead, (present.astype(bf16),), (present * pooled, present * exponent)
    )
    wide[...] = totals / counts + jnp.log(sums)
    readout[...] = wide[pl.ds(pl.multiple_of(place * own, own), own)]
    for copy in copies:
        copy.wait()
    cotangent = full[...]
    by_count, by_sum = run_sums(behind, (), (cotangent / counts, cotangent / sums))
    down = present * (by_count + exponent * by_sum) * (0.5 / mel_count)
    for c in range(width // LANES):
        hold[c, even] = down[:, c * LANES : (c + 1) * LANES]
        hold[c, odd] = down[:, c * LANES : (c + 1) * LANES]

    def slopes(at, sums):
        down_rows = jnp.concatenate(
            [hold[c, pl.ds(at, ROWS)] for c in range(width // LANES)], axis=1
        )
        plain, along = sums
        for m in range(mel_count):
            step = down_rows * slope[m, pl.ds(at, ROWS)]
            slope[m, pl.ds(at, ROWS)] = step
            plain = plain + fold(step)
            along = along + fold(step * ((middle[m, pl.ds(at, ROWS)] - center) * inverse))
        return plain, along

    plain, along = by_rows(total, slopes, (blank, blank))
    plain, along = column_sum(plain), column_sum(along)
    shift_grad[...] = plain
    gain_grad[...] = along
    plain, along = plain / pixels, along / pixels

    def finish(at, carry):
        mask = widen(keep[pl.ds(at, ROWS)], width)
        for m in range(mel_count):
            normed = (middle[m, pl.ds(at, ROWS)] - center) * inverse
            rows = slope[m, pl.ds(at, ROWS)] - plain - normed * along
            grad[m, pl.ds(at, ROWS)] = (mask * (scale * rows)).astype(bf16)
        return carry

    by_rows(total, finish, 0)


def second_block(near, early, arrays, weight, keep, scales, starts, cotangents, own):
    mel_count, total, width = near.shape
    outputs = early.shape[0]
    padded = (mel_count, total + 2 * TILE, width)
    full = (mel_count, total, width)
    return call(
        second_kernel,
        (starts, near, early, *arrays, weight, keep, scales, *cotangents),
        [scalar_spec()] + [whole_spec()] * (len(arrays) + 5) + [place_spec()] * len(cotangents),
        [((own, width), f32), (full, bf16), ((1, width), f32), ((1, width), f32)],
        [whole_spec()] * 4,
        [
            pltpu.VMEM(full, f32),
            pltpu.VMEM(full, f32),
            pltpu.VMEM(padded, f32),
            pltpu.VMEM(padded, f32),
            pltpu.VMEM((outputs, total, width), f32),
            pltpu.VMEM((outputs, total + 2 * TILE, width), f32),
            pltpu.VMEM((outputs, total + 2 * TILE, width), f32),
            pltpu.VMEM((width // LANES, total, LANES), f32),
            pltpu.VMEM((total // 2, width), f32),
            pltpu.VMEM((total // 2, width), f32),
            pltpu.SemaphoreType.DMA((sum(part.shape[0] for part in cotangents),)),
        ],
        0,
        26,
    )


def back_kernel(bit, mels, halved, starts, one, two, weight, weight_two, out, lower, middle, upper):
    mel_count, total, width = one.shape
    reach, rows_out = middle.shape[1], out.shape[1]
    side = lax.axis_index("tm") % 2 if halved else 0
    edge = reach - rows_out
    first = side * (total - reach)
    skip = side * edge
    if halved:
        first, skip = pl.multiple_of(first, 16), pl.multiple_of(skip, 16)
    (start,) = group_starts((bit,), width)
    for k in range(len(mels)):
        for ref in (lower, upper):
            ref[k, :TILE] = jnp.zeros((TILE, width), f32)
            ref[k, TILE + reach :] = jnp.zeros((TILE, width), f32)
    for k, n in enumerate(mels):
        for a in range(3):
            acc = None
            for field, matrix in ((one, weight), (two, weight_two)):
                for b in range(3):
                    if 0 <= n - b + 1 < mel_count:
                        part = lax.dot_general(
                            field[n - b + 1, pl.ds(first, reach)],
                            matrix[a, b, pl.ds(start, width)],
                            (((1,), (1,)), ((), ())),
                            preferred_element_type=f32,
                        )
                        acc = part if acc is None else acc + part
            if a == 2:
                lower[k, TILE : TILE + reach] = acc
            elif a == 1:
                middle[k] = acc
            else:
                upper[k, TILE : TILE + reach] = acc

    def combine(at, carry):
        near = pl.multiple_of(at + skip, TILE)
        before, after = same_clip(starts, first + near, (ROWS, width), total)
        for k in range(len(mels)):
            rows = joined(lower, middle, upper, k, near, before, after)
            out[k, pl.ds(at, ROWS)] = rows.astype(out.dtype)
        return carry

    by_rows(rows_out, combine, 0)


def hidden_back(bit, mels, halved, one, two, weight, weight_two, starts, kind):
    _, total, width = one.shape
    rows = total // 2 if halved else total
    reach = rows + 16 if halved else total
    count = len(mels)
    padded = (count, reach + 2 * TILE, width)
    return call(
        functools.partial(back_kernel, bit, mels, halved),
        (starts, one, two, weight, weight_two),
        [scalar_spec()] + [whole_spec()] * 4,
        [((count, rows, width), kind)],
        [whole_spec()],
        [
            pltpu.VMEM(padded, f32),
            pltpu.VMEM((count, reach, width), f32),
            pltpu.VMEM(padded, f32),
        ],
        0,
        14,
    )[0]


def norm_kernel(mine, other, picked, rest, slope, pre, stats, scales, keep, *refs):
    grad, window, gain_grad, shift_grad, padded = refs
    mel_count, total, width = mine.shape
    center, inverse, pixels = stats[0:1], stats[1:2], stats[2:3]
    blank = jnp.zeros((TILE, width), f32)
    edge = (padded.shape[1] - total) // 2
    reach = window.shape[1]
    frames = reach - 2 * edge
    place = lax.axis_index("tm")

    half = mel_count // 2

    def add(field, base, mels):
        def slopes(at, sums):
            plain, along = sums
            place_rows = pl.ds(pl.multiple_of(base + at, ROWS), ROWS)
            for k, m in enumerate(mels):
                rows = mine[m, place_rows] + field[k, pl.ds(at, ROWS)].astype(f32)
                step = rows * slope[m, place_rows]
                mine[m, place_rows] = step
                plain = plain + fold(step)
                along = along + fold(step * ((pre[m, place_rows] - center) * inverse))
            return plain, along

        return slopes

    side = place % 2
    sums = by_rows(total, add(other, 0, range(half)), (blank, blank))
    upper = range(half, mel_count)
    parts = []
    for field, base in ((picked, side), (rest, 1 - side)):
        parts.append(by_rows(total // 2, add(field, base * (total // 2), upper), (blank, blank)))
    plain, along = [
        a + jnp.where(side == 0, b + c, c + b) for a, b, c in zip(sums, parts[0], parts[1])
    ]
    plain, along = column_sum(plain), column_sum(along)
    shift_grad[...] = plain
    gain_grad[...] = along
    plain, along = plain / pixels, along / pixels
    scale = scales[0:1] * inverse
    for m in range(mel_count):
        padded[m, :edge] = jnp.zeros((edge, width), bf16)
        padded[m, edge + total :] = jnp.zeros((edge, width), bf16)

    def finish(at, carry):
        mask = widen(keep[pl.ds(at, ROWS)], width)
        for m in range(mel_count):
            normed = (pre[m, pl.ds(at, ROWS)] - center) * inverse
            rows = mine[m, pl.ds(at, ROWS)] - plain - normed * along
            rows = (mask * (scale * rows)).astype(bf16)
            grad[m, pl.ds(at, ROWS)] = rows
            padded[m, pl.ds(pl.multiple_of(at + edge, 16), ROWS)] = rows
        return carry

    by_rows(total, finish, 0)
    for m in range(mel_count):
        window[m] = padded[m, pl.ds(pl.multiple_of(place * frames, frames), reach)]


def norm_back_first(mine, other, picked, rest, slope, pre, stats, scales, keep, frames):
    mel_count, total, width = mine.shape
    edge = 16
    return call(
        norm_kernel,
        (mine, other, picked, rest, slope, pre, stats, scales, keep),
        [whole_spec()] * 9,
        [
            ((mel_count, total, width), bf16),
            ((mel_count, frames + 2 * edge, width), bf16),
            ((1, width), f32),
            ((1, width), f32),
        ],
        [whole_spec()] * 4,
        [pltpu.VMEM((mel_count, total + 2 * edge, width), bf16)],
        2**28,
        12,
    )


def spread_kernel(starts, grad, steps, spaced):
    mel_count, total, width = grad.shape
    for m in range(mel_count):
        spaced[m, :TILE] = jnp.zeros((TILE, width), f32)
        spaced[m, TILE + total :] = jnp.zeros((TILE, width), f32)

    def expand(at, carry):
        for m in range(mel_count):
            rows = grad[m, pl.ds(at, ROWS)].astype(f32)
            spaced[m, pl.ds(pl.multiple_of(at + TILE, TILE), ROWS)] = rows
        return carry

    by_rows(total, expand, 0)

    def shift(at, carry):
        before, after = same_clip(starts, at, (ROWS, width), total)
        for m in range(mel_count):
            rows = spaced[m, pl.ds(at, ROWS + 2 * TILE)]
            ahead = jnp.where(after, rows[TILE + 1 : TILE + 1 + ROWS], 0.0)
            behind = jnp.where(before, rows[TILE - 1 : TILE - 1 + ROWS], 0.0)
            steps[0, m, pl.ds(at, ROWS)] = ahead.astype(bf16)
            steps[1, m, pl.ds(at, ROWS)] = behind.astype(bf16)
        return carry

    by_rows(total, shift, 0)


def spread(grad, starts):
    mel_count, total, width = grad.shape
    return call(
        spread_kernel,
        (starts, grad),
        [scalar_spec(), whole_spec()],
        [((2, mel_count, total, width), bf16)],
        [whole_spec()],
        [pltpu.VMEM((mel_count, total + 2 * TILE, width), f32)],
        0,
        6,
    )[0]


def weight_kernel(layout, halves, *refs):
    count = len(refs) - 6
    fields, grad, steps = list(refs[:count]), refs[count], refs[count + 1]
    out, results, joint, sems = refs[count + 2 :]
    mel_count, total, out_width = grad.shape
    width = results.shape[2]
    side = lax.axis_index("tm") % 2
    column = lax.axis_index("chan")
    moves = []
    for i, pair in enumerate(halves):
        for index, begin in zip(pair, (side, 1 - side)):
            rows = pl.ds(pl.multiple_of(begin * (total // 2), total // 2), total // 2)
            moves.append(
                pltpu.make_async_copy(fields[index], joint.at[i, :, rows], sems.at[2 + len(moves)])
            )
            moves[-1].start()
        fields.append(joint.at[i])
    copies = [None, None]
    for i, (place, pieces) in enumerate(layout):
        slot = i % 2
        if copies[slot] is not None:
            copies[slot].wait()
        if any(piece[0] >= count for piece in pieces):
            while moves:
                moves.pop().wait()
        for a in range(3):
            for b in range(3):
                right = grad if a == 1 else steps.at[a // 2]
                acc = None
                for m in range(mel_count):
                    if 0 <= m + b - 1 < mel_count:
                        index, k, lane = pieces[m + b - 1]
                        part = lax.dot_general(
                            fields[index][k, :, lane : lane + width],
                            right[m],
                            (((0,), (0,)), ((), ())),
                            preferred_element_type=f32,
                        )
                        acc = part if acc is None else acc + part
                results[slot, 3 * a + b] = acc
        if place is None:
            start = i * width
        else:
            start = pl.multiple_of((column ^ place) * width, width)
        copies[slot] = pltpu.make_async_copy(
            results.at[slot], out.at[:, pl.ds(start, width)], sems.at[slot]
        )
        copies[slot].start()
    for copy in copies:
        if copy is not None:
            copy.wait()


def weight_back(layout, halves, fields, grad, steps, in_width):
    mel_count, total, out_width = grad.shape
    width = in_width // len(layout)
    joint = (max(len(halves), 1), mel_count // 2, total, width)
    out = call(
        functools.partial(weight_kernel, layout, halves),
        (*fields, grad, steps),
        [whole_spec()] * (len(fields) + 2),
        [((9, in_width, out_width), f32)],
        [place_spec()],
        [
            pltpu.VMEM((2, 9, width, out_width), f32),
            pltpu.VMEM(joint, bf16),
            pltpu.SemaphoreType.DMA((2 + 2 * len(halves),)),
        ],
        0,
        12,
    )[0]
    return out.reshape(3, 3, in_width, out_width)


def input_kernel(starts, one, two, weight, weight_two, mine, other, lower, middle, upper):
    mel_count, reach, width = one.shape
    frames, lanes = mine.shape[1], mine.shape[2]
    edge = (reach - frames) // 2
    total = frames * lax.axis_size("tm")
    place = lax.axis_index("tm")
    groups = group_starts((2, 0), lanes)
    for a in range(3):
        target, shift = ((upper, TILE), (middle, 0), (lower, TILE))[a]
        for b in (1, 0, 2):
            low, count = ((1, mel_count - 1), (0, mel_count), (0, mel_count - 1))[b]
            acc = None
            for field, matrix in ((one, weight), (two, weight_two)):
                rows = field[low : low + count].reshape(count * reach, width)
                wing = jnp.concatenate([matrix[a, b, pl.ds(g, lanes)] for g in groups])
                part = lax.dot_general(
                    rows, wing, (((1,), (1,)), ((), ())), preferred_element_type=f32
                )
                acc = part if acc is None else acc + part
            acc = acc.reshape(count, reach, 2 * lanes)
            for k in range(count):
                n = low + k + b - 1
                if b == 1:
                    target[n, shift : shift + reach] = acc[k]
                else:
                    target[n, shift : shift + reach] += acc[k]
    before, after = same_clip(starts, place * frames, (frames, 2 * lanes), total)
    for m in range(mel_count):
        low = lower[m, TILE + edge - 1 : TILE + edge - 1 + frames]
        high = upper[m, TILE + edge + 1 : TILE + edge + 1 + frames]
        rows = (
            middle[m, edge : edge + frames]
            + jnp.where(before, low, 0.0)
            + jnp.where(after, high, 0.0)
        )
        other[m] = rows[:, :lanes]
        mine[m] = rows[:, lanes:]


def input_back(one, two, weight, weight_two, starts, frames, lanes):
    mel_count, reach, width = one.shape
    shape = (mel_count, frames, lanes)
    return call(
        input_kernel,
        (starts, one, two, weight, weight_two),
        [scalar_spec()] + [whole_spec()] * 4,
        [(shape, f32), (shape, f32)],
        [whole_spec()] * 2,
        [
            pltpu.VMEM((mel_count, reach + 2 * TILE, 2 * lanes), f32),
            pltpu.VMEM((mel_count, reach, 2 * lanes), f32),
            pltpu.VMEM((mel_count, reach + 2 * TILE, 2 * lanes), f32),
        ],
        0,
        10,
    )


def close_kernel(mine, other, keep, out):
    mel_count, frames, lanes = mine.shape
    begin = pl.multiple_of(lax.axis_index("tm") * frames, frames)
    mask = keep[pl.ds(begin, frames)]
    for m in range(mel_count):
        out[:, m, :] = (mine[m] + other[m]) * mask


def close(mine, other, keep):
    mel_count, frames, lanes = mine.shape
    return call(
        close_kernel,
        (mine, other, keep),
        [whole_spec()] * 3,
        [((frames, mel_count, lanes), f32)],
        [whole_spec()],
        [],
        0,
        4,
    )[0]


def whole_frames(
    features,
    conv1_weight,
    norm1_gain,
    norm1_bias,
    conv2_weight,
    norm2_gain,
    norm2_bias,
    clip_starts,
    valid,
    readout_grad,
):
    frames, mel_count, lanes = features.shape
    places = lax.axis_size("tm")
    total = frames * places
    clip_starts, conv1_weight, scales = bring(
        clip_starts, conv1_weight, (norm1_gain, norm1_bias, norm2_gain, norm2_bias)
    )

    marked = jnp.where(valid[:, None, None] > 0, features, jnp.asarray(ABSENT, bf16))
    own = jnp.transpose(marked, (1, 0, 2))
    along = jnp.stack([own] + [swap(own, "tm", 2 * k) for k in range(1, places // 2)])
    near = [
        along,
        swap(along, "tm", 1),
        swap(along, "chan", 2),
        swap_both(along, "tm", 1, "chan", 2),
    ]
    near[3], clip_starts, conv1_weight, scales = lax.optimization_barrier(
        (near[3], clip_starts, conv1_weight, scales)
    )
    blocks = near + [swap(block, "chan", 1) for block in near]
    other_conv2 = swap(conv2_weight, "chan", 1)
    readout_grad, own = lax.optimization_barrier((readout_grad, own))
    cotangents = [readout_grad[None]]
    for bit in gather_bits(places):
        cotangents.append(swap(jnp.concatenate(cotangents), "tm", bit))
    blocks, other_conv2, cotangents = lax.optimization_barrier((blocks, other_conv2, cotangents))

    low, high, picked, field, pre, keep, stats = first_block(
        blocks, conv1_weight, scales, clip_starts, total
    )

    far_picked = swap(picked, "chan", 2)
    far = swap(low, "chan", 2)
    far_rest = swap(far_picked, "tm", 1)

    low_two, high_two = swap(low, "chan", 1), swap(high, "chan", 1)
    near = near_part(low, high, low_two, high_two, conv2_weight, clip_starts)
    far_picked, near = lax.optimization_barrier((far_picked, near))
    picked_two = swap(far_picked, "chan", 1)
    early = early_part(far_picked, picked_two, conv2_weight, clip_starts)
    early, pre = lax.optimization_barrier((early, pre))
    slope = first_slope(pre, stats, scales, keep)
    far, far_rest, slope = lax.optimization_barrier((far, far_rest, slope))
    far_two, rest_two = swap(far, "chan", 1), swap(far_rest, "chan", 1)

    readout, grad2, gain2_grad, shift2_grad = second_block(
        near,
        early,
        (far, far_rest, far_two, rest_two),
        conv2_weight,
        keep,
        scales,
        clip_starts,
        cotangents,
        readout_grad.shape[0],
    )
    grad2_near = swap(grad2, "chan", 1)
    steps2 = spread(grad2, clip_starts)
    grad2_near, steps2 = lax.optimization_barrier((grad2_near, steps2))
    back = functools.partial(
        hidden_back,
        one=grad2,
        two=grad2_near,
        weight=conv2_weight,
        weight_two=other_conv2,
        starts=clip_starts,
    )
    came_picked = swap(back(2, (2, 3), True, kind=bf16), "chan", 2)
    away_low = back(2, (0, 1), False, kind=bf16)
    came_low = swap(away_low, "chan", 2)

    away_low, other_conv2 = lax.optimization_barrier((away_low, other_conv2))
    mine = back(0, (0, 1, 2, 3), False, weight_two=other_conv2, kind=f32)
    came_picked, mine, conv1_weight = lax.optimization_barrier((came_picked, mine, conv1_weight))
    came_rest = swap(came_picked, "tm", 1)
    other_conv1 = swap(conv1_weight, "chan", 1)
    fields = (low, high, low_two, high_two)
    fields += (far, far_picked, far_rest, far_two, picked_two, rest_two)
    layout = [
        (0, [(0, 0, 0), (0, 1, 0), (1, 0, 0), (1, 1, 0)]),
        (1, [(2, 0, 0), (2, 1, 0), (3, 0, 0), (3, 1, 0)]),
        (2, [(4, 0, 0), (4, 1, 0), (10, 0, 0), (10, 1, 0)]),
        (3, [(7, 0, 0), (7, 1, 0), (11, 0, 0), (11, 1, 0)]),
    ]
    weight2_grad = weight_back(
        layout, ((5, 6), (8, 9)), fields, grad2, steps2, conv2_weight.shape[2]
    )
    came_low, came_rest, mine, weight2_grad, other_conv1 = lax.optimization_barrier(
        (came_low, came_rest, mine, weight2_grad, other_conv1)
    )

    grad1, window, gain1_grad, shift1_grad = norm_back_first(
        mine, came_low, came_picked, came_rest, slope, pre, stats, scales, keep, frames
    )
    window_near = swap(window, "chan", 1)
    steps1 = spread(grad1, clip_starts)
    window_near, steps1 = lax.optimization_barrier((window_near, steps1))
    input_mine, input_away = input_back(
        window, window_near, conv1_weight, other_conv1, clip_starts, frames, lanes
    )
    input_came = swap(input_away, "chan", 2)
    layout = [
        (None, [(0, m, lane) for m in range(mel_count)])
        for lane in range(0, field.shape[2], LANES)
    ]
    weight1_grad = weight_back(layout, (), (field,), grad1, steps1, field.shape[2])
    input_came, weight1_grad = lax.optimization_barrier((input_came, weight1_grad))
    return (
        readout,
        close(input_mine, input_came, keep),
        weight1_grad,
        gain1_grad[0],
        shift1_grad[0],
        weight2_grad,
        gain2_grad[0],
        shift2_grad[0],
    )


def fits_whole(frames, mels, places, columns, widths):
    return (
        places > 1
        and places & (places - 1) == 0
        and columns == 4
        and frames % 32 == 0
        and frames * places <= 512
        and mels == 4
        and all(w % (columns * LANES) == 0 for w in widths)
        and widths[1] == columns * 256
    )


def shards(*arrays):
    features, conv1_weight, conv2_weight = arrays[0], arrays[1], arrays[4]
    if fits_whole(
        features.shape[0],
        features.shape[1],
        lax.axis_size("tm"),
        lax.axis_size("chan"),
        (conv1_weight.shape[2], conv2_weight.shape[2]),
    ):
        return whole_frames(*arrays)
    return split_frames(*arrays)


def solution(mesh):
    return jax.shard_map(
        shards,
        mesh=mesh,
        in_specs=(
            P("tm", None, "chan"),
            P(None, None, None, "chan"),
            P("chan"),
            P("chan"),
            P(None, None, None, "chan"),
            P("chan"),
            P("chan"),
            P(),
            P("tm"),
            P("tm", "chan"),
        ),
        out_specs=(
            P("tm", "chan"),
            P("tm", None, "chan"),
            P(None, None, None, "chan"),
            P("chan"),
            P("chan"),
            P(None, None, None, "chan"),
            P("chan"),
            P("chan"),
        ),
        check_vma=False,
    )
```

```python
import functools

import jax
import jax.numpy as jnp
from jax import lax
from jax.experimental import pallas as pl
from jax.experimental.pallas import tpu as pltpu
from jax.sharding import PartitionSpec as P

EPS = 1e-05
highest = lax.Precision.HIGHEST
f32 = jnp.float32
bf16 = jnp.bfloat16


def padded_2(shard, sides, width):
    for axis, dim in sides:
        count, length = (lax.axis_size(axis), shard.shape[dim])
        up = [(i, (i + 1) % count) for i in range(count - 1)]
        down = [(j, i) for i, j in up]
        last = lax.slice_in_dim(shard, length - width, length, axis=dim)
        leading = lax.slice_in_dim(shard, 0, width, axis=dim)
        before = lax.ppermute(last, axis, up)
        after = lax.ppermute(leading, axis, down)
        shard = jnp.concatenate([before, shard, after], axis=dim)
    return shard


def entering(part, axis, combine, identity, reverse):
    count = lax.axis_size(axis)
    place = lax.axis_index(axis)
    ahead = count - 1 - place if reverse else place
    gathered = jax.tree.map(lambda a: lax.all_gather(a, axis), part)
    state = jax.tree.map(lambda a, e: jnp.zeros_like(a) + jnp.asarray(e, a.dtype), part, identity)

    def one(step, state):
        source = count - 1 - step if reverse else step
        return combine(
            state, jax.tree.map(lambda a: lax.dynamic_index_in_dim(a, source, 0, False), gathered)
        )

    return lax.fori_loop(0, ahead, one, state)


def frame_flags(clip_starts, first_frame, frame_count, frame_total):
    position = first_frame - 2 + jnp.arange(frame_count + 4, dtype=jnp.int32)
    segment = jnp.sum((clip_starts[None, :] <= position[:, None]).astype(jnp.int32), axis=1) - 1
    inside = (position >= 0) & (position < frame_total)
    middle = segment[1:-1]
    before_same = inside[1:-1] & inside[:-2] & (middle == segment[:-2])
    after_same = inside[1:-1] & inside[2:] & (middle == segment[2:])
    return (segment[2:-2], before_same, after_same)


def conv_forward(padded, weight, factors):
    frame_count = padded.shape[0] - 2
    mel_count = padded.shape[1]
    wide_field = jnp.pad(padded, ((0, 0), (1, 1), (0, 0)))
    result = jnp.zeros((frame_count, mel_count, weight.shape[3]), jnp.float32)
    for tap_row in range(3):
        partial_value = jnp.zeros((frame_count * mel_count, weight.shape[3]), jnp.float32)
        for tap_col in range(3):
            window = wide_field[
                tap_row : tap_row + frame_count, tap_col : tap_col + mel_count, :
            ].reshape(frame_count * mel_count, -1)
            partial_value = partial_value + jnp.dot(
                window, weight[tap_row, tap_col], preferred_element_type=jnp.float32
            )
        result = (
            result
            + partial_value.reshape(frame_count, mel_count, -1) * factors[tap_row][:, None, None]
        )
    return result


def conv_weight_grad(padded, grad_out, factors):
    frame_count = grad_out.shape[0]
    mel_count = grad_out.shape[1]
    wide_field = jnp.pad(padded, ((0, 0), (1, 1), (0, 0)))
    rows_out = []
    for tap_row in range(3):
        scaled = (grad_out * factors[tap_row][:, None, None].astype(jnp.bfloat16)).reshape(
            frame_count * mel_count, -1
        )
        taps_out = []
        for tap_col in range(3):
            window = wide_field[
                tap_row : tap_row + frame_count, tap_col : tap_col + mel_count, :
            ].reshape(frame_count * mel_count, -1)
            taps_out.append(
                lax.dot_general(
                    window, scaled, (((0,), (0,)), ((), ())), preferred_element_type=jnp.float32
                )
            )
        rows_out.append(jnp.stack(taps_out))
    return jnp.stack(rows_out)


def conv_input_grad(grad_padded, weight, edge_factors):
    frame_count = grad_padded.shape[0] - 2
    mel_count = grad_padded.shape[1]
    wide_field = jnp.pad(grad_padded, ((0, 0), (1, 1), (0, 0)))
    result = jnp.zeros((frame_count * mel_count, weight.shape[2]), jnp.float32)
    for tap_row in range(3):
        scaled = wide_field * edge_factors[tap_row][:, None, None]
        for tap_col in range(3):
            window = scaled[
                2 - tap_row : 2 - tap_row + frame_count, 2 - tap_col : 2 - tap_col + mel_count, :
            ].reshape(frame_count * mel_count, -1)
            result = result + lax.dot_general(
                window,
                weight[tap_row, tap_col],
                (((1,), (1,)), ((), ())),
                preferred_element_type=jnp.float32,
            )
    return result.reshape(frame_count, mel_count, -1)


def join_keyed(earlier_item, later_item):
    keep_first = later_item[0] < 0.0
    same_key = later_item[0] == earlier_item[0]
    merged = [jnp.where(keep_first, earlier_item[0], later_item[0])]
    for first_part, second_part in zip(earlier_item[1:], later_item[1:]):
        extra = (1,) * (first_part.ndim - keep_first.ndim)
        keep_wide = jnp.reshape(keep_first, keep_first.shape + extra)
        same_wide = jnp.reshape(same_key, same_key.shape + extra)
        merged.append(
            jnp.where(
                keep_wide, first_part, jnp.where(same_wide, first_part + second_part, second_part)
            )
        )
    return tuple(merged)


def smooth(argument):
    return jax.nn.gelu(argument, approximate=False)


def split_frames(
    features,
    conv1_weight,
    norm1_gain,
    norm1_bias,
    conv2_weight,
    norm2_gain,
    norm2_bias,
    clip_starts,
    valid,
    readout_grad,
):
    frame_count = features.shape[0]
    mel_count = features.shape[1]
    cycle_size = lax.axis_size("tm")
    cycle_index = lax.axis_index("tm")
    segment, before_same, after_same = frame_flags(
        clip_starts, cycle_index * frame_count, frame_count, frame_count * cycle_size
    )
    keep_mask = valid.astype(jnp.float32)
    keep_cube = keep_mask[:, None, None]
    own_factors = (
        before_same[1:-1].astype(jnp.float32),
        jnp.ones((frame_count,), jnp.float32),
        after_same[1:-1].astype(jnp.float32),
    )
    edge_factors = (
        before_same.astype(jnp.bfloat16),
        jnp.ones((frame_count + 2,), jnp.bfloat16),
        after_same.astype(jnp.bfloat16),
    )
    local_count = jnp.sum(keep_mask) * mel_count

    def spread(shard):
        padded = padded_2(shard, (("tm", 0),), 1)
        return lax.all_gather(padded, "chan", axis=2, tiled=True)

    def normalize(field_in, gain_vec, shift_vec):
        value_sums, squares, pixel_count = lax.psum(
            (
                jnp.sum(field_in * keep_cube, axis=(0, 1)),
                jnp.sum(field_in * field_in * keep_cube, axis=(0, 1)),
                local_count,
            ),
            "tm",
        )
        center = value_sums / pixel_count
        variance = squares / pixel_count - center * center
        inverse_std = lax.rsqrt(variance + EPS)
        normed = (field_in - center) * inverse_std
        return (gain_vec * normed + shift_vec, normed, inverse_std, pixel_count)

    def norm_back(grad_norm, normed, inverse_std, gain_vec, pixel_count):
        bias_grad, gain_grad = lax.psum(
            (jnp.sum(grad_norm, axis=(0, 1)), jnp.sum(grad_norm * normed, axis=(0, 1))), "tm"
        )
        grad_pre = (
            keep_cube
            * (gain_vec * inverse_std)
            * (grad_norm - bias_grad / pixel_count - normed * (gain_grad / pixel_count))
        )
        return (grad_pre.astype(jnp.bfloat16), gain_grad, bias_grad)

    def send_back(grad_pre, weight):
        padded = padded_2(grad_pre, (("tm", 0),), 1)
        partial_sum = conv_input_grad(padded, weight, edge_factors)
        return lax.psum_scatter(partial_sum, "chan", scatter_dimension=2, tiled=True)

    wide_in = spread(features * keep_cube.astype(jnp.bfloat16))
    first_pre = conv_forward(wide_in, conv1_weight, own_factors)
    first_norm, first_hat, first_scale, pixel_count = normalize(first_pre, norm1_gain, norm1_bias)
    first_act, first_pull = jax.vjp(smooth, first_norm)
    hidden = (first_act * keep_cube).astype(jnp.bfloat16)
    wide_mid = spread(hidden)
    second_pre = conv_forward(wide_mid, conv2_weight, own_factors)
    second_norm, second_hat, second_scale, pixel_count = normalize(
        second_pre, norm2_gain, norm2_bias
    )
    second_act, second_pull = jax.vjp(smooth, second_norm)
    pooled = (second_act * keep_cube).reshape(frame_count // 2, 2, mel_count, -1).mean(axis=(1, 2))
    pooled_keep = keep_mask[0::2]
    pooled_segment = segment[0::2]
    segment_key = pooled_segment.astype(jnp.float32)
    row_order = jnp.arange(frame_count // 2)
    lower_runs = (
        (pooled_segment[:, None] == pooled_segment[None, :])
        & (row_order[:, None] >= row_order[None, :])
    ).astype(jnp.float32)
    exponent = jnp.exp(pooled)
    counts = jnp.dot(lower_runs, pooled_keep, precision=highest)
    totals = jnp.dot(lower_runs, pooled_keep[:, None] * pooled, precision=highest)
    expsums = jnp.dot(lower_runs, pooled_keep[:, None] * exponent, precision=highest)
    zero_row = jnp.zeros_like(totals[0])
    prior_runs = entering(
        (segment_key[-1], counts[-1], totals[-1], expsums[-1]),
        "tm",
        join_keyed,
        (jnp.float32(-1.0), jnp.float32(0.0), zero_row, zero_row),
        False,
    )
    joined = (segment_key == prior_runs[0]).astype(jnp.float32)
    counts = counts + joined * prior_runs[1]
    totals = totals + joined[:, None] * prior_runs[2]
    expsums = expsums + joined[:, None] * prior_runs[3]
    readout = totals / counts[:, None] + jnp.log(expsums)
    by_count = readout_grad / counts[:, None]
    by_expsum = readout_grad / expsums
    later_mean = lax.dot_general(lower_runs, by_count, (((0,), (0,)), ((), ())), precision=highest)
    later_soft = lax.dot_general(lower_runs, by_expsum, (((0,), (0,)), ((), ())), precision=highest)
    beyond = entering(
        (segment_key[0], later_mean[0], later_soft[0]),
        "tm",
        join_keyed,
        (jnp.float32(-1.0), zero_row, zero_row),
        True,
    )
    joined_back = (segment_key == beyond[0]).astype(jnp.float32)[:, None]
    later_mean = later_mean + joined_back * beyond[1]
    later_soft = later_soft + joined_back * beyond[2]
    pooled_grad = pooled_keep[:, None] * (later_mean + exponent * later_soft)
    spread_grad = jnp.broadcast_to(
        (pooled_grad / (2 * mel_count))[:, None, None, :],
        (frame_count // 2, 2, mel_count, pooled_grad.shape[1]),
    )
    act_grad = spread_grad.reshape(frame_count, mel_count, -1) * keep_cube
    second_grad_norm = second_pull(act_grad)[0]
    second_grad_pre, gain2_grad, bias2_grad = norm_back(
        second_grad_norm, second_hat, second_scale, norm2_gain, pixel_count
    )
    weight2_grad = conv_weight_grad(wide_mid, second_grad_pre, own_factors)
    weight2_grad = lax.psum(weight2_grad, "tm")
    hidden_grad = send_back(second_grad_pre, conv2_weight)
    first_grad_norm = first_pull(hidden_grad * keep_cube)[0]
    first_grad_pre, gain1_grad, bias1_grad = norm_back(
        first_grad_norm, first_hat, first_scale, norm1_gain, pixel_count
    )
    weight1_grad = conv_weight_grad(wide_in, first_grad_pre, own_factors)
    weight1_grad = lax.psum(weight1_grad, "tm")
    input_grad = send_back(first_grad_pre, conv1_weight) * keep_cube
    return (
        readout,
        input_grad,
        weight1_grad,
        gain1_grad,
        bias1_grad,
        weight2_grad,
        gain2_grad,
        bias2_grad,
    )


ABSENT = 1024.0
ROWS = 64
TILE = 8
LANES = 128


def whole_spec():
    return pl.BlockSpec(memory_space=pltpu.VMEM)


def place_spec():
    return pl.BlockSpec(memory_space=pl.ANY)


def far_spec():
    return pl.BlockSpec(memory_space=pltpu.HBM)


def scalar_spec():
    return pl.BlockSpec(memory_space=pltpu.SMEM)


def call(body, operands, in_specs, outs, out_specs, scratch, flops, megabytes):
    return pl.pallas_call(
        body,
        out_shape=tuple(jax.ShapeDtypeStruct(s, d) for s, d in outs),
        in_specs=in_specs,
        out_specs=tuple(out_specs),
        scratch_shapes=scratch,
        compiler_params=pltpu.CompilerParams(vmem_limit_bytes=megabytes * 2**20),
        cost_estimate=pl.CostEstimate(flops=1000, bytes_accessed=1000, transcendentals=0),
    )(*operands)


def swap(shard, axis, bit):
    count = lax.axis_size(axis)
    return lax.ppermute(shard, axis, [(i, i ^ bit) for i in range(count)])


def gather_bits(places):
    bits = [1 << k for k in range(places.bit_length() - 1)]
    return bits[2:][::-1] + bits[:2] if len(bits) > 2 else bits


def swap_both(shard, first, first_bit, second, second_bit):
    rows, columns = lax.axis_size(first), lax.axis_size(second)
    pairs = [
        (i * columns + j, (i ^ first_bit) * columns + (j ^ second_bit))
        for i in range(rows)
        for j in range(columns)
    ]
    return lax.ppermute(shard, (first, second), pairs)


def same_clip(starts, at, shape, total):
    frame = lax.broadcasted_iota(jnp.int32, shape, 0) + at
    before = frame != starts[0]
    after = frame != total - 1
    for k in range(1, starts.shape[0]):
        before = before & (frame != starts[k])
        after = after & (frame != starts[k] - 1)
    return before, after


def widen(mask, width):
    return jnp.concatenate([mask] * (width // mask.shape[1]), axis=1)


def fold(value):
    total = value[:TILE]
    for k in range(TILE, value.shape[0], TILE):
        total = total + value[k : k + TILE]
    return total


def column_sum(value):
    return jnp.sum(value, axis=0, keepdims=True)


def taps(mel, mel_count):
    return [b for b in range(3) if 0 <= mel + b - 1 < mel_count]


def convolve(fields, weights, lower, middle, upper, total, add):
    mel_count = middle.shape[0]
    for m in range(mel_count):
        for a in range(3):
            acc = None
            for field, weight in zip(fields, weights):
                for b in taps(m, mel_count):
                    part = jnp.dot(field(m + b - 1), weight(a, b), preferred_element_type=f32)
                    acc = part if acc is None else acc + part
            if a == 0:
                lower[m, TILE : TILE + total] = acc
            elif a == 1:
                middle[m] = middle[m] + acc if add else acc
            else:
                upper[m, TILE : TILE + total] = acc


def convolve_back(fields, weights, lower, middle, upper, total):
    mel_count = middle.shape[0]
    for n in range(mel_count):
        for a in range(3):
            acc = None
            for field, weight in zip(fields, weights):
                for b in range(3):
                    if 0 <= n - b + 1 < mel_count:
                        part = lax.dot_general(
                            field(n - b + 1),
                            weight(a, b),
                            (((1,), (1,)), ((), ())),
                            preferred_element_type=f32,
                        )
                        acc = part if acc is None else acc + part
            if a == 2:
                lower[n, TILE : TILE + total] = acc
            elif a == 1:
                middle[n] = acc
            else:
                upper[n, TILE : TILE + total] = acc


def joined(lower, middle, upper, m, at, before, after):
    low = lower[m, pl.ds(at, ROWS + 2 * TILE)]
    high = upper[m, pl.ds(at, ROWS + 2 * TILE)]
    return (
        middle[m, pl.ds(at, ROWS)]
        + jnp.where(before, low[TILE - 1 : TILE - 1 + ROWS], 0.0)
        + jnp.where(after, high[TILE + 1 : TILE + 1 + ROWS], 0.0)
    )


def by_rows(total, body, init):
    return lax.fori_loop(
        0, total // ROWS, lambda i, c: body(pl.multiple_of(i * ROWS, ROWS), c), init
    )


def clear_edges(lower, upper, total):
    for m in range(lower.shape[0]):
        for ref in (lower, upper):
            ref[m, :TILE] = jnp.zeros((TILE, ref.shape[2]), f32)
            ref[m, TILE + total :] = jnp.zeros((TILE, ref.shape[2]), f32)


def moments(field, keep, count):
    first, second = column_sum(field[0]), column_sum(field[1])
    center = first / count
    return center, lax.rsqrt(second / count - center * center + EPS)


def phi_parts(value):
    return 0.5 * (1.0 + lax.erf(value * 0.7071067811865476))


def bell(value):
    return 0.3989422804014327 * jnp.exp(-0.5 * value * value)


def bring_kernel(starts_in, weight_in, starts, weight, sem):
    copy = pltpu.make_async_copy(weight_in, weight, sem)
    copy.start()
    for k in range(starts.shape[0]):
        starts[k] = starts_in[k]
    copy.wait()


def bring(starts, weight):
    return call(
        bring_kernel,
        (starts, weight),
        [scalar_spec(), place_spec()],
        [(starts.shape, jnp.int32), (weight.shape, bf16)],
        [scalar_spec(), whole_spec()],
        [pltpu.SemaphoreType.DMA],
        0,
        4,
    )


def first_kernel(starts, *refs):
    blocks, (weight, scales) = refs[:8], refs[8:10]
    low, high, picked, field, middle, keep, stats = refs[10:17]
    lower, upper = refs[17:]
    mel_count, total, width = field.shape
    out_width = middle.shape[2]
    place, column = lax.axis_index("tm"), lax.axis_index("chan")
    frames, lanes = blocks[0].shape[2], blocks[0].shape[3]
    clear_edges(lower, upper, total)
    for i, block in enumerate(blocks):
        core, row, side = i // 4, (i // 2) % 2, i % 2
        to_columns = pl.ds(pl.multiple_of((column ^ (2 * row + core)) * lanes, lanes), lanes)
        for k in range(block.shape[0]):
            to_rows = pl.ds(pl.multiple_of((place ^ (2 * k + side)) * frames, frames), frames)
            for m in range(mel_count):
                rows = block[k, m]
                if m == 0 and i < 2:
                    keep[to_rows] = (rows.astype(f32) < ABSENT / 2).astype(f32)
                field[m, to_rows, to_columns] = jnp.where(
                    rows < ABSENT / 2, rows, jnp.zeros_like(rows)
                )
    convolve(
        [lambda m: field[m]], [lambda a, b: weight[a, b]], lower, middle, upper, total, False
    )

    def combine(at, sums):
        before, after = same_clip(starts, at, (ROWS, out_width), total)
        mask = widen(keep[pl.ds(at, ROWS)], out_width)
        one, two, num = sums
        num = num + fold(mask)
        for m in range(mel_count):
            rows = joined(lower, middle, upper, m, at, before, after)
            middle[m, pl.ds(at, ROWS)] = rows
            kept = rows * mask
            one = one + fold(kept)
            two = two + fold(kept * rows)
        return one, two, num

    blank = jnp.zeros((TILE, out_width), f32)
    one, two, num = by_rows(total, combine, (blank, blank, blank))
    pixels = column_sum(num) * mel_count
    center, inverse = moments((one, two), keep, pixels)
    stats[0:1] = center
    stats[1:2] = inverse
    stats[2:3] = pixels
    scale = scales[0:1] * inverse
    offset = scales[1:2] - center * scale

    def activate(at, carry):
        mask = widen(keep[pl.ds(at, ROWS)], out_width)
        for m in range(mel_count):
            value = middle[m, pl.ds(at, ROWS)] * scale + offset
            rows = (value * phi_parts(value) * mask).astype(bf16)
            if m < mel_count // 2:
                low[m, pl.ds(at, ROWS)] = rows
            else:
                high[m - mel_count // 2, pl.ds(at, ROWS)] = rows
        return carry

    by_rows(total, activate, 0)
    reach = picked.shape[1]
    for m in range(picked.shape[0]):
        picked[m] = high[m, pl.ds(pl.multiple_of((place % 2) * reach, reach), reach)]


def first_block(blocks, weight, scales, starts, total):
    _, mel_count, frames, lanes = blocks[0].shape
    width, out_width = weight.shape[2], weight.shape[3]
    padded = (mel_count, total + 2 * TILE, out_width)
    half = (mel_count // 2, total, out_width)
    return call(
        first_kernel,
        (starts, *blocks, weight, scales),
        [scalar_spec()] + [whole_spec()] * 10,
        [
            (half, bf16),
            (half, bf16),
            ((mel_count // 2, total // 2, out_width), bf16),
            ((mel_count, total, width), bf16),
            ((mel_count, total, out_width), f32),
            ((total, LANES), f32),
            ((TILE, out_width), f32),
        ],
        [whole_spec()] * 7,
        [pltpu.VMEM(padded, f32), pltpu.VMEM(padded, f32)],
        0,
        16,
    )


def slope_kernel(pre, stats, scales, keep, slope):
    mel_count, total, width = pre.shape
    center, inverse = stats[0:1], stats[1:2]
    scale = scales[0:1] * inverse
    offset = scales[1:2] - center * scale

    def rows(at, carry):
        mask = widen(keep[pl.ds(at, ROWS)], width)
        for m in range(mel_count):
            value = pre[m, pl.ds(at, ROWS)] * scale + offset
            slope[m, pl.ds(at, ROWS)] = mask * (phi_parts(value) + value * bell(value))
        return carry

    by_rows(total, rows, 0)


def first_slope(pre, stats, scales, keep):
    return call(
        slope_kernel,
        (pre, stats, scales, keep),
        [whole_spec()] * 4,
        [(pre.shape, f32)],
        [whole_spec()],
        [],
        2**28,
        6,
    )[0]


def gather_taps(parts, groups, weight, lower, middle, upper, outputs, first=None):
    total, width = middle.shape[1], middle.shape[2]
    for k, m in enumerate(outputs):
        for a in range(3):
            acc = None
            for mels, arrays in parts:
                for j, n in enumerate(mels):
                    b = n - m + 1
                    if 0 <= b < 3:
                        for array, start in zip(arrays, groups):
                            piece = jnp.dot(
                                array[j],
                                weight[a, b, pl.ds(start, width)],
                                preferred_element_type=f32,
                            )
                            acc = piece if acc is None else acc + piece
            target, shift = ((lower, TILE), (middle, 0), (upper, TILE))[a]
            rows = total
            if first is not None:
                rows = total // 2
                empty = pl.ds(pl.multiple_of(total // 2 - first + shift, TILE), rows)
                target[k, empty] = jnp.zeros((rows, width), f32)
                target[k, pl.ds(pl.multiple_of(first + shift, TILE), rows)] = acc
            elif acc is None:
                target[k, shift : shift + rows] = jnp.zeros((rows, width), f32)
            else:
                target[k, shift : shift + rows] = acc


def group_starts(bits, width):
    column = lax.axis_index("chan")
    return [pl.multiple_of((column ^ bit) * width, width) for bit in bits]


def near_kernel(starts, low, high, low_two, high_two, weight, out, lower, upper):
    mel_count, total, width = out.shape
    half = mel_count // 2
    clear_edges(lower, upper, total)
    parts = [(range(half), (low, low_two)), (range(half, mel_count), (high, high_two))]
    groups = group_starts((0, 1), width)
    gather_taps(parts, groups, weight, lower, out, upper, range(mel_count))

    def combine(at, carry):
        before, after = same_clip(starts, at, (ROWS, width), total)
        for m in range(mel_count):
            out[m, pl.ds(at, ROWS)] = joined(lower, out, upper, m, at, before, after)
        return carry

    by_rows(total, combine, 0)


def near_part(low, high, low_two, high_two, weight, starts):
    half, total, width = low.shape
    padded = (2 * half, total + 2 * TILE, width)
    return call(
        near_kernel,
        (starts, low, high, low_two, high_two, weight),
        [scalar_spec()] + [whole_spec()] * 5,
        [((2 * half, total, width), f32)],
        [whole_spec()],
        [pltpu.VMEM(padded, f32)] * 2,
        0,
        14,
    )[0]


def early_kernel(starts, picked, picked_two, weight, early, lower, upper):
    outputs, total, width = early.shape
    mel_count = picked.shape[0] + outputs - 1
    half = mel_count - picked.shape[0]
    begin = (lax.axis_index("tm") % 2) * (total // 2)
    clear_edges(lower, upper, total)
    parts = [(range(half, mel_count), (picked, picked_two))]
    groups = group_starts((2, 3), width)
    mels = range(half - 1, mel_count)
    gather_taps(parts, groups, weight, lower, early, upper, mels, begin)

    def combine(at, carry):
        before, after = same_clip(starts, at, (ROWS, width), total)
        for k in range(outputs):
            early[k, pl.ds(at, ROWS)] = joined(lower, early, upper, k, at, before, after)
        return carry

    by_rows(total, combine, 0)


def early_part(picked, picked_two, weight, starts):
    half, rows, width = picked.shape
    total = 2 * rows
    shape = (half + 1, total, width)
    return call(
        early_kernel,
        (starts, picked, picked_two, weight),
        [scalar_spec()] + [whole_spec()] * 3,
        [(shape, f32)],
        [whole_spec()],
        [pltpu.VMEM((half + 1, total + 2 * TILE, width), f32)] * 2,
        0,
        12,
    )[0]


def run_sums(mask, plain, values):
    width = (plain + values)[0].shape[1]
    terms = list(plain)
    for value in values:
        for _ in range(3):
            term = value.astype(bf16)
            terms.append(term)
            value = value - term.astype(f32)
    out = jnp.dot(mask, jnp.concatenate(terms, axis=1), preferred_element_type=f32)
    parts = [out[:, k * width : (k + 1) * width] for k in range(len(terms))]
    results = parts[: len(plain)]
    for k in range(len(plain), len(parts), 3):
        results.append(parts[k] + (parts[k + 1] + parts[k + 2]))
    return results


def second_kernel(
    starts, near, early, far, rest, far_two, rest_two, weight, keep, scales, *refs
):
    cotangents, (readout, grad, gain_grad, shift_grad) = refs[:-15], refs[-15:-11]
    middle, slope, lower, upper, late, late_lower, late_upper, hold, wide, full, sems = refs[-11:]
    mel_count, total, width = middle.shape
    half = mel_count // 2
    place = lax.axis_index("tm")
    pooled_total = total // 2
    own = readout.shape[0]
    copies = []
    pieces = [(part, i) for part in cotangents for i in range(part.shape[0])]
    bits = gather_bits(len(pieces))
    for k, (part, i) in enumerate(pieces):
        source = place ^ sum(bit for j, bit in enumerate(bits) if k >> j & 1)
        copies.append(
            pltpu.make_async_copy(
                part.at[i],
                full.at[pl.ds(pl.multiple_of(source * own, own), own)],
                sems.at[k],
            )
        )
    for copy in copies:
        copy.start()

    groups = group_starts((2, 3), width)
    clear_edges(lower, upper, total)
    clear_edges(late_lower, late_upper, total)
    parts = [(range(half), (far, far_two))]
    gather_taps(parts, groups, weight, lower, middle, upper, range(half + 1))
    parts = [(range(half, mel_count), (rest, rest_two))]
    begin = (1 - place % 2) * (total // 2)
    outputs = range(half - 1, mel_count)
    gather_taps(parts, groups, weight, late_lower, late, late_upper, outputs, begin)
    blank = jnp.zeros((TILE, width), f32)

    def combine(at, sums):
        before, after = same_clip(starts, at, (ROWS, width), total)
        mask = widen(keep[pl.ds(at, ROWS)], width)
        first, second, num = sums
        num = num + fold(mask)
        for m in range(mel_count):
            rows = near[m, pl.ds(at, ROWS)]
            if m <= half:
                rows = rows + joined(lower, middle, upper, m, at, before, after)
            if m in outputs:
                k = m - outputs[0]
                new = joined(late_lower, late, late_upper, k, at, before, after)
                rows = rows + (early[k, pl.ds(at, ROWS)] + new)
            middle[m, pl.ds(at, ROWS)] = rows
            kept = rows * mask
            first = first + fold(kept)
            second = second + fold(kept * rows)
        return first, second, num

    first, second, num = by_rows(total, combine, (blank, blank, blank))
    pixels = column_sum(num) * mel_count
    center, inverse = moments((first, second), keep, pixels)
    scale = scales[2:3] * inverse
    offset = scales[3:4] - center * scale

    def activate(at, carry):
        mask = widen(keep[pl.ds(at, ROWS)], width)
        pooled = jnp.zeros((ROWS, width), f32)
        for m in range(mel_count):
            value = middle[m, pl.ds(at, ROWS)] * scale + offset
            share = phi_parts(value)
            pooled = pooled + value * share
            slope[m, pl.ds(at, ROWS)] = mask * (share + value * bell(value))
        pooled = pooled * mask
        for c in range(width // LANES):
            hold[c, pl.ds(at, ROWS)] = pooled[:, c * LANES : (c + 1) * LANES]
        return carry

    by_rows(total, activate, 0)

    even = pl.ds(0, pooled_total, stride=2)
    odd = pl.ds(1, pooled_total, stride=2)
    pooled = jnp.concatenate(
        [hold[c, even] + hold[c, odd] for c in range(width // LANES)], axis=1
    ) * (0.5 / mel_count)
    present = widen(keep[even], width)
    square = (pooled_total, pooled_total)
    row = lax.broadcasted_iota(jnp.int32, square, 0)
    col = lax.broadcasted_iota(jnp.int32, square, 1)
    same = row >= col
    back = row <= col
    for k in range(1, starts.shape[0]):
        crossed = (2 * row < starts[k]) != (2 * col < starts[k])
        same = same & ~crossed
        back = back & ~crossed
    ahead, behind = same.astype(f32).astype(bf16), back.astype(f32).astype(bf16)
    exponent = jnp.exp(pooled)
    counts, totals, sums = run_sums(
        ahead, (present.astype(bf16),), (present * pooled, present * exponent)
    )
    wide[...] = totals / counts + jnp.log(sums)
    readout[...] = wide[pl.ds(pl.multiple_of(place * own, own), own)]
    for copy in copies:
        copy.wait()
    cotangent = full[...]
    by_count, by_sum = run_sums(behind, (), (cotangent / counts, cotangent / sums))
    down = present * (by_count + exponent * by_sum) * (0.5 / mel_count)
    for c in range(width // LANES):
        hold[c, even] = down[:, c * LANES : (c + 1) * LANES]
        hold[c, odd] = down[:, c * LANES : (c + 1) * LANES]

    def slopes(at, sums):
        down_rows = jnp.concatenate(
            [hold[c, pl.ds(at, ROWS)] for c in range(width // LANES)], axis=1
        )
        plain, along = sums
        for m in range(mel_count):
            step = down_rows * slope[m, pl.ds(at, ROWS)]
            slope[m, pl.ds(at, ROWS)] = step
            plain = plain + fold(step)
            along = along + fold(step * ((middle[m, pl.ds(at, ROWS)] - center) * inverse))
        return plain, along

    plain, along = by_rows(total, slopes, (blank, blank))
    plain, along = column_sum(plain), column_sum(along)
    shift_grad[...] = plain
    gain_grad[...] = along
    plain, along = plain / pixels, along / pixels

    def finish(at, carry):
        mask = widen(keep[pl.ds(at, ROWS)], width)
        for m in range(mel_count):
            normed = (middle[m, pl.ds(at, ROWS)] - center) * inverse
            rows = slope[m, pl.ds(at, ROWS)] - plain - normed * along
            grad[m, pl.ds(at, ROWS)] = (mask * (scale * rows)).astype(bf16)
        return carry

    by_rows(total, finish, 0)


def second_block(near, early, arrays, weight, keep, scales, starts, cotangents, own):
    mel_count, total, width = near.shape
    outputs = early.shape[0]
    padded = (mel_count, total + 2 * TILE, width)
    full = (mel_count, total, width)
    return call(
        second_kernel,
        (starts, near, early, *arrays, weight, keep, scales, *cotangents),
        [scalar_spec()] + [whole_spec()] * (len(arrays) + 5) + [place_spec()] * len(cotangents),
        [((own, width), f32), (full, bf16), ((1, width), f32), ((1, width), f32)],
        [whole_spec()] * 4,
        [
            pltpu.VMEM(full, f32),
            pltpu.VMEM(full, f32),
            pltpu.VMEM(padded, f32),
            pltpu.VMEM(padded, f32),
            pltpu.VMEM((outputs, total, width), f32),
            pltpu.VMEM((outputs, total + 2 * TILE, width), f32),
            pltpu.VMEM((outputs, total + 2 * TILE, width), f32),
            pltpu.VMEM((width // LANES, total, LANES), f32),
            pltpu.VMEM((total // 2, width), f32),
            pltpu.VMEM((total // 2, width), f32),
            pltpu.SemaphoreType.DMA((sum(part.shape[0] for part in cotangents),)),
        ],
        0,
        26,
    )


def back_kernel(bit, mels, halved, starts, one, two, weight, weight_two, out, lower, middle, upper):
    mel_count, total, width = one.shape
    reach, rows_out = middle.shape[1], out.shape[1]
    side = lax.axis_index("tm") % 2 if halved else 0
    edge = reach - rows_out
    first = side * (total - reach)
    skip = side * edge
    if halved:
        first, skip = pl.multiple_of(first, 16), pl.multiple_of(skip, 16)
    (start,) = group_starts((bit,), width)
    for k in range(len(mels)):
        for ref in (lower, upper):
            ref[k, :TILE] = jnp.zeros((TILE, width), f32)
            ref[k, TILE + reach :] = jnp.zeros((TILE, width), f32)
    for k, n in enumerate(mels):
        for a in range(3):
            acc = None
            for field, matrix in ((one, weight), (two, weight_two)):
                for b in range(3):
                    if 0 <= n - b + 1 < mel_count:
                        part = lax.dot_general(
                            field[n - b + 1, pl.ds(first, reach)],
                            matrix[a, b, pl.ds(start, width)],
                            (((1,), (1,)), ((), ())),
                            preferred_element_type=f32,
                        )
                        acc = part if acc is None else acc + part
            if a == 2:
                lower[k, TILE : TILE + reach] = acc
            elif a == 1:
                middle[k] = acc
            else:
                upper[k, TILE : TILE + reach] = acc

    def combine(at, carry):
        near = pl.multiple_of(at + skip, TILE)
        before, after = same_clip(starts, first + near, (ROWS, width), total)
        for k in range(len(mels)):
            rows = joined(lower, middle, upper, k, near, before, after)
            out[k, pl.ds(at, ROWS)] = rows.astype(out.dtype)
        return carry

    by_rows(rows_out, combine, 0)


def hidden_back(bit, mels, halved, one, two, weight, weight_two, starts, kind):
    _, total, width = one.shape
    rows = total // 2 if halved else total
    reach = rows + 16 if halved else total
    count = len(mels)
    padded = (count, reach + 2 * TILE, width)
    return call(
        functools.partial(back_kernel, bit, mels, halved),
        (starts, one, two, weight, weight_two),
        [scalar_spec()] + [whole_spec()] * 4,
        [((count, rows, width), kind)],
        [whole_spec()],
        [
            pltpu.VMEM(padded, f32),
            pltpu.VMEM((count, reach, width), f32),
            pltpu.VMEM(padded, f32),
        ],
        0,
        14,
    )[0]


def norm_kernel(mine, other, picked, rest, slope, pre, stats, scales, keep, *refs):
    grad, window, gain_grad, shift_grad, padded = refs
    mel_count, total, width = mine.shape
    center, inverse, pixels = stats[0:1], stats[1:2], stats[2:3]
    blank = jnp.zeros((TILE, width), f32)
    edge = (padded.shape[1] - total) // 2
    reach = window.shape[1]
    frames = reach - 2 * edge
    place = lax.axis_index("tm")

    half = mel_count // 2

    def add(field, base, mels):
        def slopes(at, sums):
            plain, along = sums
            place_rows = pl.ds(pl.multiple_of(base + at, ROWS), ROWS)
            for k, m in enumerate(mels):
                rows = mine[m, place_rows] + field[k, pl.ds(at, ROWS)].astype(f32)
                step = rows * slope[m, place_rows]
                mine[m, place_rows] = step
                plain = plain + fold(step)
                along = along + fold(step * ((pre[m, place_rows] - center) * inverse))
            return plain, along

        return slopes

    side = place % 2
    sums = by_rows(total, add(other, 0, range(half)), (blank, blank))
    upper = range(half, mel_count)
    parts = []
    for field, base in ((picked, side), (rest, 1 - side)):
        parts.append(by_rows(total // 2, add(field, base * (total // 2), upper), (blank, blank)))
    plain, along = [
        a + jnp.where(side == 0, b + c, c + b) for a, b, c in zip(sums, parts[0], parts[1])
    ]
    plain, along = column_sum(plain), column_sum(along)
    shift_grad[...] = plain
    gain_grad[...] = along
    plain, along = plain / pixels, along / pixels
    scale = scales[0:1] * inverse
    for m in range(mel_count):
        padded[m, :edge] = jnp.zeros((edge, width), bf16)
        padded[m, edge + total :] = jnp.zeros((edge, width), bf16)

    def finish(at, carry):
        mask = widen(keep[pl.ds(at, ROWS)], width)
        for m in range(mel_count):
            normed = (pre[m, pl.ds(at, ROWS)] - center) * inverse
            rows = mine[m, pl.ds(at, ROWS)] - plain - normed * along
            rows = (mask * (scale * rows)).astype(bf16)
            grad[m, pl.ds(at, ROWS)] = rows
            padded[m, pl.ds(pl.multiple_of(at + edge, 16), ROWS)] = rows
        return carry

    by_rows(total, finish, 0)
    for m in range(mel_count):
        window[m] = padded[m, pl.ds(pl.multiple_of(place * frames, frames), reach)]


def norm_back_first(mine, other, picked, rest, slope, pre, stats, scales, keep, frames):
    mel_count, total, width = mine.shape
    edge = 16
    return call(
        norm_kernel,
        (mine, other, picked, rest, slope, pre, stats, scales, keep),
        [whole_spec()] * 9,
        [
            ((mel_count, total, width), bf16),
            ((mel_count, frames + 2 * edge, width), bf16),
            ((1, width), f32),
            ((1, width), f32),
        ],
        [whole_spec()] * 4,
        [pltpu.VMEM((mel_count, total + 2 * edge, width), bf16)],
        2**28,
        12,
    )


def spread_kernel(starts, grad, steps, spaced):
    mel_count, total, width = grad.shape
    for m in range(mel_count):
        spaced[m, :TILE] = jnp.zeros((TILE, width), f32)
        spaced[m, TILE + total :] = jnp.zeros((TILE, width), f32)

    def expand(at, carry):
        for m in range(mel_count):
            rows = grad[m, pl.ds(at, ROWS)].astype(f32)
            spaced[m, pl.ds(pl.multiple_of(at + TILE, TILE), ROWS)] = rows
        return carry

    by_rows(total, expand, 0)

    def shift(at, carry):
        before, after = same_clip(starts, at, (ROWS, width), total)
        for m in range(mel_count):
            rows = spaced[m, pl.ds(at, ROWS + 2 * TILE)]
            ahead = jnp.where(after, rows[TILE + 1 : TILE + 1 + ROWS], 0.0)
            behind = jnp.where(before, rows[TILE - 1 : TILE - 1 + ROWS], 0.0)
            steps[0, m, pl.ds(at, ROWS)] = ahead.astype(bf16)
            steps[1, m, pl.ds(at, ROWS)] = behind.astype(bf16)
        return carry

    by_rows(total, shift, 0)


def spread(grad, starts):
    mel_count, total, width = grad.shape
    return call(
        spread_kernel,
        (starts, grad),
        [scalar_spec(), whole_spec()],
        [((2, mel_count, total, width), bf16)],
        [whole_spec()],
        [pltpu.VMEM((mel_count, total + 2 * TILE, width), f32)],
        0,
        6,
    )[0]


def weight_kernel(layout, halves, *refs):
    count = len(refs) - 6
    fields, grad, steps = list(refs[:count]), refs[count], refs[count + 1]
    out, results, joint, sems = refs[count + 2 :]
    mel_count, total, out_width = grad.shape
    width = results.shape[2]
    side = lax.axis_index("tm") % 2
    column = lax.axis_index("chan")
    moves = []
    for i, pair in enumerate(halves):
        for index, begin in zip(pair, (side, 1 - side)):
            rows = pl.ds(pl.multiple_of(begin * (total // 2), total // 2), total // 2)
            moves.append(
                pltpu.make_async_copy(fields[index], joint.at[i, :, rows], sems.at[2 + len(moves)])
            )
            moves[-1].start()
        fields.append(joint.at[i])
    copies = [None, None]
    for i, (place, pieces) in enumerate(layout):
        slot = i % 2
        if copies[slot] is not None:
            copies[slot].wait()
        if any(piece[0] >= count for piece in pieces):
            while moves:
                moves.pop().wait()
        for a in range(3):
            for b in range(3):
                right = grad if a == 1 else steps.at[a // 2]
                acc = None
                for m in range(mel_count):
                    if 0 <= m + b - 1 < mel_count:
                        index, k, lane = pieces[m + b - 1]
                        part = lax.dot_general(
                            fields[index][k, :, lane : lane + width],
                            right[m],
                            (((0,), (0,)), ((), ())),
                            preferred_element_type=f32,
                        )
                        acc = part if acc is None else acc + part
                results[slot, 3 * a + b] = acc
        if place is None:
            start = i * width
        else:
            start = pl.multiple_of((column ^ place) * width, width)
        copies[slot] = pltpu.make_async_copy(
            results.at[slot], out.at[:, pl.ds(start, width)], sems.at[slot]
        )
        copies[slot].start()
    for copy in copies:
        if copy is not None:
            copy.wait()


def weight_back(layout, halves, fields, grad, steps, in_width):
    mel_count, total, out_width = grad.shape
    width = in_width // len(layout)
    joint = (max(len(halves), 1), mel_count // 2, total, width)
    out = call(
        functools.partial(weight_kernel, layout, halves),
        (*fields, grad, steps),
        [whole_spec()] * (len(fields) + 2),
        [((9, in_width, out_width), f32)],
        [place_spec()],
        [
            pltpu.VMEM((2, 9, width, out_width), f32),
            pltpu.VMEM(joint, bf16),
            pltpu.SemaphoreType.DMA((2 + 2 * len(halves),)),
        ],
        0,
        12,
    )[0]
    return out.reshape(3, 3, in_width, out_width)


def input_kernel(starts, one, two, weight, weight_two, mine, other, lower, middle, upper):
    mel_count, reach, width = one.shape
    frames, lanes = mine.shape[1], mine.shape[2]
    edge = (reach - frames) // 2
    total = frames * lax.axis_size("tm")
    place = lax.axis_index("tm")
    groups = group_starts((2, 0), lanes)
    for a in range(3):
        target, shift = ((upper, TILE), (middle, 0), (lower, TILE))[a]
        for b in (1, 0, 2):
            low, count = ((1, mel_count - 1), (0, mel_count), (0, mel_count - 1))[b]
            acc = None
            for field, matrix in ((one, weight), (two, weight_two)):
                rows = field[low : low + count].reshape(count * reach, width)
                wing = jnp.concatenate([matrix[a, b, pl.ds(g, lanes)] for g in groups])
                part = lax.dot_general(
                    rows, wing, (((1,), (1,)), ((), ())), preferred_element_type=f32
                )
                acc = part if acc is None else acc + part
            acc = acc.reshape(count, reach, 2 * lanes)
            for k in range(count):
                n = low + k + b - 1
                if b == 1:
                    target[n, shift : shift + reach] = acc[k]
                else:
                    target[n, shift : shift + reach] += acc[k]
    before, after = same_clip(starts, place * frames, (frames, 2 * lanes), total)
    for m in range(mel_count):
        low = lower[m, TILE + edge - 1 : TILE + edge - 1 + frames]
        high = upper[m, TILE + edge + 1 : TILE + edge + 1 + frames]
        rows = (
            middle[m, edge : edge + frames]
            + jnp.where(before, low, 0.0)
            + jnp.where(after, high, 0.0)
        )
        other[m] = rows[:, :lanes]
        mine[m] = rows[:, lanes:]


def input_back(one, two, weight, weight_two, starts, frames, lanes):
    mel_count, reach, width = one.shape
    shape = (mel_count, frames, lanes)
    return call(
        input_kernel,
        (starts, one, two, weight, weight_two),
        [scalar_spec()] + [whole_spec()] * 4,
        [(shape, f32), (shape, f32)],
        [whole_spec()] * 2,
        [
            pltpu.VMEM((mel_count, reach + 2 * TILE, 2 * lanes), f32),
            pltpu.VMEM((mel_count, reach, 2 * lanes), f32),
            pltpu.VMEM((mel_count, reach + 2 * TILE, 2 * lanes), f32),
        ],
        0,
        10,
    )


def close_kernel(mine, other, keep, out):
    mel_count, frames, lanes = mine.shape
    begin = pl.multiple_of(lax.axis_index("tm") * frames, frames)
    mask = keep[pl.ds(begin, frames)]
    for m in range(mel_count):
        out[:, m, :] = (mine[m] + other[m]) * mask


def close(mine, other, keep):
    mel_count, frames, lanes = mine.shape
    return call(
        close_kernel,
        (mine, other, keep),
        [whole_spec()] * 3,
        [((frames, mel_count, lanes), f32)],
        [whole_spec()],
        [],
        0,
        4,
    )[0]


def whole_frames(
    features,
    conv1_weight,
    norm1_gain,
    norm1_bias,
    conv2_weight,
    norm2_gain,
    norm2_bias,
    clip_starts,
    valid,
    readout_grad,
):
    frames, mel_count, lanes = features.shape
    places = lax.axis_size("tm")
    total = frames * places
    clip_starts, conv1_weight = bring(clip_starts, conv1_weight)
    scales = jnp.stack([norm1_gain, norm1_bias, norm2_gain, norm2_bias])

    marked = jnp.where(valid[:, None, None] > 0, features, jnp.asarray(ABSENT, bf16))
    own = jnp.transpose(marked, (1, 0, 2))
    pieces = [swap(own, "tm", 2 * k) for k in range(1, places // 2)]
    along = jnp.stack([own] + pieces)
    near = [
        along,
        swap(along, "tm", 1),
        swap(along, "chan", 2),
        swap_both(along, "tm", 1, "chan", 2),
    ]
    readout_grad, _ = lax.optimization_barrier((readout_grad, pieces[0]))
    bits = gather_bits(places)
    cotangents = [readout_grad[None]]
    cotangents.append(swap(cotangents[0], "tm", bits[0]))
    near[3], clip_starts, conv1_weight, scales, cotangents = lax.optimization_barrier(
        (near[3], clip_starts, conv1_weight, scales, cotangents)
    )
    blocks = near + [swap(block, "chan", 1) for block in near]
    other_conv2 = swap(conv2_weight, "chan", 1)
    blocks, other_conv2 = lax.optimization_barrier((blocks, other_conv2))

    low, high, picked, field, pre, keep, stats = first_block(
        blocks, conv1_weight, scales, clip_starts, total
    )

    far_picked = swap(picked, "chan", 2)
    far = swap(low, "chan", 2)
    far_rest = swap(far_picked, "tm", 1)

    low_two, high_two = swap(low, "chan", 1), swap(high, "chan", 1)
    near = near_part(low, high, low_two, high_two, conv2_weight, clip_starts)
    far_picked, near, cotangents = lax.optimization_barrier((far_picked, near, cotangents))
    picked_two = swap(far_picked, "chan", 1)
    for bit in bits[1:-1]:
        cotangents.append(swap(jnp.concatenate(cotangents), "tm", bit))
    early = early_part(far_picked, picked_two, conv2_weight, clip_starts)
    early, pre, cotangents = lax.optimization_barrier((early, pre, cotangents))
    cotangents.append(swap(jnp.concatenate(cotangents), "tm", bits[-1]))
    slope = first_slope(pre, stats, scales, keep)
    far, far_rest, slope, cotangents = lax.optimization_barrier((far, far_rest, slope, cotangents))
    far_two, rest_two = swap(far, "chan", 1), swap(far_rest, "chan", 1)

    readout, grad2, gain2_grad, shift2_grad = second_block(
        near,
        early,
        (far, far_rest, far_two, rest_two),
        conv2_weight,
        keep,
        scales,
        clip_starts,
        cotangents,
        readout_grad.shape[0],
    )
    grad2_near = swap(grad2, "chan", 1)
    steps2 = spread(grad2, clip_starts)
    grad2_near, steps2 = lax.optimization_barrier((grad2_near, steps2))
    back = functools.partial(
        hidden_back,
        one=grad2,
        two=grad2_near,
        weight=conv2_weight,
        weight_two=other_conv2,
        starts=clip_starts,
    )
    came_picked = swap(back(2, (2, 3), True, kind=bf16), "chan", 2)
    away_low = back(2, (0, 1), False, kind=bf16)
    came_low = swap(away_low, "chan", 2)

    away_low, other_conv2 = lax.optimization_barrier((away_low, other_conv2))
    mine = back(0, (0, 1, 2, 3), False, weight_two=other_conv2, kind=f32)
    came_picked, mine, conv1_weight = lax.optimization_barrier((came_picked, mine, conv1_weight))
    came_rest = swap(came_picked, "tm", 1)
    other_conv1 = swap(conv1_weight, "chan", 1)
    fields = (low, high, low_two, high_two)
    fields += (far, far_picked, far_rest, far_two, picked_two, rest_two)
    layout = [
        (0, [(0, 0, 0), (0, 1, 0), (1, 0, 0), (1, 1, 0)]),
        (1, [(2, 0, 0), (2, 1, 0), (3, 0, 0), (3, 1, 0)]),
        (2, [(4, 0, 0), (4, 1, 0), (10, 0, 0), (10, 1, 0)]),
        (3, [(7, 0, 0), (7, 1, 0), (11, 0, 0), (11, 1, 0)]),
    ]
    weight2_grad = weight_back(
        layout, ((5, 6), (8, 9)), fields, grad2, steps2, conv2_weight.shape[2]
    )
    came_low, came_rest, mine, weight2_grad, other_conv1 = lax.optimization_barrier(
        (came_low, came_rest, mine, weight2_grad, other_conv1)
    )

    grad1, window, gain1_grad, shift1_grad = norm_back_first(
        mine, came_low, came_picked, came_rest, slope, pre, stats, scales, keep, frames
    )
    window_near = swap(window, "chan", 1)
    steps1 = spread(grad1, clip_starts)
    window_near, steps1 = lax.optimization_barrier((window_near, steps1))
    input_mine, input_away = input_back(
        window, window_near, conv1_weight, other_conv1, clip_starts, frames, lanes
    )
    input_came = swap(input_away, "chan", 2)
    layout = [
        (None, [(0, m, lane) for m in range(mel_count)])
        for lane in range(0, field.shape[2], 256)
    ]
    weight1_grad = weight_back(layout, (), (field,), grad1, steps1, field.shape[2])
    input_came, weight1_grad = lax.optimization_barrier((input_came, weight1_grad))
    return (
        readout,
        close(input_mine, input_came, keep),
        weight1_grad,
        gain1_grad[0],
        shift1_grad[0],
        weight2_grad,
        gain2_grad[0],
        shift2_grad[0],
    )


def fits_whole(frames, mels, places, columns, widths):
    return (
        places > 1
        and places & (places - 1) == 0
        and columns == 4
        and frames % ROWS == 0
        and frames * places <= 512
        and mels == 4
        and all(w % (columns * LANES) == 0 for w in widths)
        and widths[1] == columns * 256
    )


def shards(*arrays):
    features, conv1_weight, conv2_weight = arrays[0], arrays[1], arrays[4]
    if fits_whole(
        features.shape[0],
        features.shape[1],
        lax.axis_size("tm"),
        lax.axis_size("chan"),
        (conv1_weight.shape[2], conv2_weight.shape[2]),
    ):
        return whole_frames(*arrays)
    return split_frames(*arrays)


def solution(mesh):
    return jax.shard_map(
        shards,
        mesh=mesh,
        in_specs=(
            P("tm", None, "chan"),
            P(None, None, None, "chan"),
            P("chan"),
            P("chan"),
            P(None, None, None, "chan"),
            P("chan"),
            P("chan"),
            P(),
            P("tm"),
            P("tm", "chan"),
        ),
        out_specs=(
            P("tm", "chan"),
            P("tm", None, "chan"),
            P(None, None, None, "chan"),
            P("chan"),
            P("chan"),
            P(None, None, None, "chan"),
            P("chan"),
            P("chan"),
        ),
        check_vma=False,
    )
```

```python
import functools

import jax
import jax.numpy as jnp
from jax import lax
from jax.experimental import pallas as pl
from jax.experimental.pallas import tpu as pltpu
from jax.sharding import PartitionSpec as P

EPS = 1e-05
highest = lax.Precision.HIGHEST
f32 = jnp.float32
bf16 = jnp.bfloat16


def padded_2(shard, sides, width):
    for axis, dim in sides:
        count, length = (lax.axis_size(axis), shard.shape[dim])
        up = [(i, (i + 1) % count) for i in range(count - 1)]
        down = [(j, i) for i, j in up]
        last = lax.slice_in_dim(shard, length - width, length, axis=dim)
        leading = lax.slice_in_dim(shard, 0, width, axis=dim)
        before = lax.ppermute(last, axis, up)
        after = lax.ppermute(leading, axis, down)
        shard = jnp.concatenate([before, shard, after], axis=dim)
    return shard


def entering(part, axis, combine, identity, reverse):
    count = lax.axis_size(axis)
    place = lax.axis_index(axis)
    ahead = count - 1 - place if reverse else place
    gathered = jax.tree.map(lambda a: lax.all_gather(a, axis), part)
    state = jax.tree.map(lambda a, e: jnp.zeros_like(a) + jnp.asarray(e, a.dtype), part, identity)

    def one(step, state):
        source = count - 1 - step if reverse else step
        return combine(
            state, jax.tree.map(lambda a: lax.dynamic_index_in_dim(a, source, 0, False), gathered)
        )

    return lax.fori_loop(0, ahead, one, state)


def frame_flags(clip_starts, first_frame, frame_count, frame_total):
    position = first_frame - 2 + jnp.arange(frame_count + 4, dtype=jnp.int32)
    segment = jnp.sum((clip_starts[None, :] <= position[:, None]).astype(jnp.int32), axis=1) - 1
    inside = (position >= 0) & (position < frame_total)
    middle = segment[1:-1]
    before_same = inside[1:-1] & inside[:-2] & (middle == segment[:-2])
    after_same = inside[1:-1] & inside[2:] & (middle == segment[2:])
    return (segment[2:-2], before_same, after_same)


def conv_forward(padded, weight, factors):
    frame_count = padded.shape[0] - 2
    mel_count = padded.shape[1]
    wide_field = jnp.pad(padded, ((0, 0), (1, 1), (0, 0)))
    result = jnp.zeros((frame_count, mel_count, weight.shape[3]), jnp.float32)
    for tap_row in range(3):
        partial_value = jnp.zeros((frame_count * mel_count, weight.shape[3]), jnp.float32)
        for tap_col in range(3):
            window = wide_field[
                tap_row : tap_row + frame_count, tap_col : tap_col + mel_count, :
            ].reshape(frame_count * mel_count, -1)
            partial_value = partial_value + jnp.dot(
                window, weight[tap_row, tap_col], preferred_element_type=jnp.float32
            )
        result = (
            result
            + partial_value.reshape(frame_count, mel_count, -1) * factors[tap_row][:, None, None]
        )
    return result


def conv_weight_grad(padded, grad_out, factors):
    frame_count = grad_out.shape[0]
    mel_count = grad_out.shape[1]
    wide_field = jnp.pad(padded, ((0, 0), (1, 1), (0, 0)))
    rows_out = []
    for tap_row in range(3):
        scaled = (grad_out * factors[tap_row][:, None, None].astype(jnp.bfloat16)).reshape(
            frame_count * mel_count, -1
        )
        taps_out = []
        for tap_col in range(3):
            window = wide_field[
                tap_row : tap_row + frame_count, tap_col : tap_col + mel_count, :
            ].reshape(frame_count * mel_count, -1)
            taps_out.append(
                lax.dot_general(
                    window, scaled, (((0,), (0,)), ((), ())), preferred_element_type=jnp.float32
                )
            )
        rows_out.append(jnp.stack(taps_out))
    return jnp.stack(rows_out)


def conv_input_grad(grad_padded, weight, edge_factors):
    frame_count = grad_padded.shape[0] - 2
    mel_count = grad_padded.shape[1]
    wide_field = jnp.pad(grad_padded, ((0, 0), (1, 1), (0, 0)))
    result = jnp.zeros((frame_count * mel_count, weight.shape[2]), jnp.float32)
    for tap_row in range(3):
        scaled = wide_field * edge_factors[tap_row][:, None, None]
        for tap_col in range(3):
            window = scaled[
                2 - tap_row : 2 - tap_row + frame_count, 2 - tap_col : 2 - tap_col + mel_count, :
            ].reshape(frame_count * mel_count, -1)
            result = result + lax.dot_general(
                window,
                weight[tap_row, tap_col],
                (((1,), (1,)), ((), ())),
                preferred_element_type=jnp.float32,
            )
    return result.reshape(frame_count, mel_count, -1)


def join_keyed(earlier_item, later_item):
    keep_first = later_item[0] < 0.0
    same_key = later_item[0] == earlier_item[0]
    merged = [jnp.where(keep_first, earlier_item[0], later_item[0])]
    for first_part, second_part in zip(earlier_item[1:], later_item[1:]):
        extra = (1,) * (first_part.ndim - keep_first.ndim)
        keep_wide = jnp.reshape(keep_first, keep_first.shape + extra)
        same_wide = jnp.reshape(same_key, same_key.shape + extra)
        merged.append(
            jnp.where(
                keep_wide, first_part, jnp.where(same_wide, first_part + second_part, second_part)
            )
        )
    return tuple(merged)


def smooth(argument):
    return jax.nn.gelu(argument, approximate=False)


def split_frames(
    features,
    conv1_weight,
    norm1_gain,
    norm1_bias,
    conv2_weight,
    norm2_gain,
    norm2_bias,
    clip_starts,
    valid,
    readout_grad,
):
    frame_count = features.shape[0]
    mel_count = features.shape[1]
    cycle_size = lax.axis_size("tm")
    cycle_index = lax.axis_index("tm")
    segment, before_same, after_same = frame_flags(
        clip_starts, cycle_index * frame_count, frame_count, frame_count * cycle_size
    )
    keep_mask = valid.astype(jnp.float32)
    keep_cube = keep_mask[:, None, None]
    own_factors = (
        before_same[1:-1].astype(jnp.float32),
        jnp.ones((frame_count,), jnp.float32),
        after_same[1:-1].astype(jnp.float32),
    )
    edge_factors = (
        before_same.astype(jnp.bfloat16),
        jnp.ones((frame_count + 2,), jnp.bfloat16),
        after_same.astype(jnp.bfloat16),
    )
    local_count = jnp.sum(keep_mask) * mel_count

    def spread(shard):
        padded = padded_2(shard, (("tm", 0),), 1)
        return lax.all_gather(padded, "chan", axis=2, tiled=True)

    def normalize(field_in, gain_vec, shift_vec):
        value_sums, squares, pixel_count = lax.psum(
            (
                jnp.sum(field_in * keep_cube, axis=(0, 1)),
                jnp.sum(field_in * field_in * keep_cube, axis=(0, 1)),
                local_count,
            ),
            "tm",
        )
        center = value_sums / pixel_count
        variance = squares / pixel_count - center * center
        inverse_std = lax.rsqrt(variance + EPS)
        normed = (field_in - center) * inverse_std
        return (gain_vec * normed + shift_vec, normed, inverse_std, pixel_count)

    def norm_back(grad_norm, normed, inverse_std, gain_vec, pixel_count):
        bias_grad, gain_grad = lax.psum(
            (jnp.sum(grad_norm, axis=(0, 1)), jnp.sum(grad_norm * normed, axis=(0, 1))), "tm"
        )
        grad_pre = (
            keep_cube
            * (gain_vec * inverse_std)
            * (grad_norm - bias_grad / pixel_count - normed * (gain_grad / pixel_count))
        )
        return (grad_pre.astype(jnp.bfloat16), gain_grad, bias_grad)

    def send_back(grad_pre, weight):
        padded = padded_2(grad_pre, (("tm", 0),), 1)
        partial_sum = conv_input_grad(padded, weight, edge_factors)
        return lax.psum_scatter(partial_sum, "chan", scatter_dimension=2, tiled=True)

    wide_in = spread(features * keep_cube.astype(jnp.bfloat16))
    first_pre = conv_forward(wide_in, conv1_weight, own_factors)
    first_norm, first_hat, first_scale, pixel_count = normalize(first_pre, norm1_gain, norm1_bias)
    first_act, first_pull = jax.vjp(smooth, first_norm)
    hidden = (first_act * keep_cube).astype(jnp.bfloat16)
    wide_mid = spread(hidden)
    second_pre = conv_forward(wide_mid, conv2_weight, own_factors)
    second_norm, second_hat, second_scale, pixel_count = normalize(
        second_pre, norm2_gain, norm2_bias
    )
    second_act, second_pull = jax.vjp(smooth, second_norm)
    pooled = (second_act * keep_cube).reshape(frame_count // 2, 2, mel_count, -1).mean(axis=(1, 2))
    pooled_keep = keep_mask[0::2]
    pooled_segment = segment[0::2]
    segment_key = pooled_segment.astype(jnp.float32)
    row_order = jnp.arange(frame_count // 2)
    lower_runs = (
        (pooled_segment[:, None] == pooled_segment[None, :])
        & (row_order[:, None] >= row_order[None, :])
    ).astype(jnp.float32)
    exponent = jnp.exp(pooled)
    counts = jnp.dot(lower_runs, pooled_keep, precision=highest)
    totals = jnp.dot(lower_runs, pooled_keep[:, None] * pooled, precision=highest)
    expsums = jnp.dot(lower_runs, pooled_keep[:, None] * exponent, precision=highest)
    zero_row = jnp.zeros_like(totals[0])
    prior_runs = entering(
        (segment_key[-1], counts[-1], totals[-1], expsums[-1]),
        "tm",
        join_keyed,
        (jnp.float32(-1.0), jnp.float32(0.0), zero_row, zero_row),
        False,
    )
    joined = (segment_key == prior_runs[0]).astype(jnp.float32)
    counts = counts + joined * prior_runs[1]
    totals = totals + joined[:, None] * prior_runs[2]
    expsums = expsums + joined[:, None] * prior_runs[3]
    readout = totals / counts[:, None] + jnp.log(expsums)
    by_count = readout_grad / counts[:, None]
    by_expsum = readout_grad / expsums
    later_mean = lax.dot_general(lower_runs, by_count, (((0,), (0,)), ((), ())), precision=highest)
    later_soft = lax.dot_general(lower_runs, by_expsum, (((0,), (0,)), ((), ())), precision=highest)
    beyond = entering(
        (segment_key[0], later_mean[0], later_soft[0]),
        "tm",
        join_keyed,
        (jnp.float32(-1.0), zero_row, zero_row),
        True,
    )
    joined_back = (segment_key == beyond[0]).astype(jnp.float32)[:, None]
    later_mean = later_mean + joined_back * beyond[1]
    later_soft = later_soft + joined_back * beyond[2]
    pooled_grad = pooled_keep[:, None] * (later_mean + exponent * later_soft)
    spread_grad = jnp.broadcast_to(
        (pooled_grad / (2 * mel_count))[:, None, None, :],
        (frame_count // 2, 2, mel_count, pooled_grad.shape[1]),
    )
    act_grad = spread_grad.reshape(frame_count, mel_count, -1) * keep_cube
    second_grad_norm = second_pull(act_grad)[0]
    second_grad_pre, gain2_grad, bias2_grad = norm_back(
        second_grad_norm, second_hat, second_scale, norm2_gain, pixel_count
    )
    weight2_grad = conv_weight_grad(wide_mid, second_grad_pre, own_factors)
    weight2_grad = lax.psum(weight2_grad, "tm")
    hidden_grad = send_back(second_grad_pre, conv2_weight)
    first_grad_norm = first_pull(hidden_grad * keep_cube)[0]
    first_grad_pre, gain1_grad, bias1_grad = norm_back(
        first_grad_norm, first_hat, first_scale, norm1_gain, pixel_count
    )
    weight1_grad = conv_weight_grad(wide_in, first_grad_pre, own_factors)
    weight1_grad = lax.psum(weight1_grad, "tm")
    input_grad = send_back(first_grad_pre, conv1_weight) * keep_cube
    return (
        readout,
        input_grad,
        weight1_grad,
        gain1_grad,
        bias1_grad,
        weight2_grad,
        gain2_grad,
        bias2_grad,
    )


ABSENT = 1024.0
ROWS = 64
TILE = 8
LANES = 128


def whole_spec():
    return pl.BlockSpec(memory_space=pltpu.VMEM)


def place_spec():
    return pl.BlockSpec(memory_space=pl.ANY)


def far_spec():
    return pl.BlockSpec(memory_space=pltpu.HBM)


def scalar_spec():
    return pl.BlockSpec(memory_space=pltpu.SMEM)


def call(body, operands, in_specs, outs, out_specs, scratch, flops, megabytes):
    return pl.pallas_call(
        body,
        out_shape=tuple(jax.ShapeDtypeStruct(s, d) for s, d in outs),
        in_specs=in_specs,
        out_specs=tuple(out_specs),
        scratch_shapes=scratch,
        compiler_params=pltpu.CompilerParams(vmem_limit_bytes=megabytes * 2**20),
        cost_estimate=pl.CostEstimate(flops=1000, bytes_accessed=1000, transcendentals=0),
    )(*operands)


def swap(shard, axis, bit):
    count = lax.axis_size(axis)
    return lax.ppermute(shard, axis, [(i, i ^ bit) for i in range(count)])


def gather_bits(places):
    bits = [1 << k for k in range(places.bit_length() - 1)]
    return bits[2:][::-1] + bits[:2] if len(bits) > 2 else bits


def swap_both(shard, first, first_bit, second, second_bit):
    rows, columns = lax.axis_size(first), lax.axis_size(second)
    pairs = [
        (i * columns + j, (i ^ first_bit) * columns + (j ^ second_bit))
        for i in range(rows)
        for j in range(columns)
    ]
    return lax.ppermute(shard, (first, second), pairs)


def same_clip(starts, at, shape, total):
    frame = lax.broadcasted_iota(jnp.int32, shape, 0) + at
    before = frame != starts[0]
    after = frame != total - 1
    for k in range(1, starts.shape[0]):
        before = before & (frame != starts[k])
        after = after & (frame != starts[k] - 1)
    return before, after


def widen(mask, width):
    return jnp.concatenate([mask] * (width // mask.shape[1]), axis=1)


def fold(value):
    total = value[:TILE]
    for k in range(TILE, value.shape[0], TILE):
        total = total + value[k : k + TILE]
    return total


def column_sum(value):
    return jnp.sum(value, axis=0, keepdims=True)


def joined(lower, middle, upper, m, at, before, after):
    low = lower[m, pl.ds(at, ROWS + 2 * TILE)]
    high = upper[m, pl.ds(at, ROWS + 2 * TILE)]
    return (
        middle[m, pl.ds(at, ROWS)]
        + jnp.where(before, low[TILE - 1 : TILE - 1 + ROWS], 0.0)
        + jnp.where(after, high[TILE + 1 : TILE + 1 + ROWS], 0.0)
    )


def by_rows(total, body, init):
    return lax.fori_loop(
        0, total // ROWS, lambda i, c: body(pl.multiple_of(i * ROWS, ROWS), c), init
    )


def clear_edges(lower, upper, total):
    for m in range(lower.shape[0]):
        for ref in (lower, upper):
            ref[m, :TILE] = jnp.zeros((TILE, ref.shape[2]), f32)
            ref[m, TILE + total :] = jnp.zeros((TILE, ref.shape[2]), f32)


def moments(field, keep, count):
    first, second = column_sum(field[0]), column_sum(field[1])
    center = first / count
    return center, lax.rsqrt(second / count - center * center + EPS)


def phi_parts(value):
    return 0.5 * (1.0 + lax.erf(value * 0.7071067811865476))


def bell(value):
    return 0.3989422804014327 * jnp.exp(-0.5 * value * value)


def bring_kernel(starts_in, weight_in, starts, weight, sem):
    copy = pltpu.make_async_copy(weight_in, weight, sem)
    copy.start()
    for k in range(starts.shape[0]):
        starts[k] = starts_in[k]
    copy.wait()


def bring(starts, weight):
    return call(
        bring_kernel,
        (starts, weight),
        [scalar_spec(), place_spec()],
        [(starts.shape, jnp.int32), (weight.shape, bf16)],
        [scalar_spec(), whole_spec()],
        [pltpu.SemaphoreType.DMA],
        0,
        4,
    )


def settle(blocks, field, keep):
    mel_count = field.shape[0]
    place = lax.axis_index("tm")
    frames, lanes = blocks[0].shape[2], blocks[0].shape[3]
    for i, block in enumerate(blocks):
        row, side = i // 2, i % 2
        to_columns = slice(row * lanes, (row + 1) * lanes)
        for k in range(block.shape[0]):
            to_rows = pl.ds(pl.multiple_of((place ^ (2 * k + side)) * frames, frames), frames)
            for m in range(mel_count):
                rows = block[k, m]
                if m == 0 and row == 0 and keep is not None:
                    keep[to_rows] = (rows.astype(f32) < ABSENT / 2).astype(f32)
                field[m, to_rows, to_columns] = jnp.where(
                    rows < ABSENT / 2, rows, jnp.zeros_like(rows)
                )


def products(field, weight, bits, targets, sources=None):
    mel_count, total, width = field.shape
    lanes = width // len(bits)
    groups = group_starts(bits, lanes)
    for m in range(mel_count):
        for a in range(3):
            target, at = targets[a]
            acc = None
            for b in range(3):
                if 0 <= m + b - 1 < mel_count:
                    wing = jnp.concatenate([weight[a, b, pl.ds(g, lanes)] for g in groups])
                    part = jnp.dot(field[m + b - 1], wing, preferred_element_type=f32)
                    acc = part if acc is None else acc + part
            if sources is not None:
                acc = acc + sources[a][m, at : at + total]
            target[m, at : at + total] = acc


def column_kernel(*refs):
    blocks, weight, (field, keep, lower, middle, upper) = refs[:4], refs[4], refs[5:]
    clear_edges(lower, upper, middle.shape[1])
    settle(blocks, field, keep)
    products(field, weight, (0, 2), ((lower, TILE), (middle, 0), (upper, TILE)))


def column_part(blocks, weight, total):
    _, mel_count, frames, lanes = blocks[0].shape
    out_width = weight.shape[3]
    padded = (mel_count, total + 2 * TILE, out_width)
    return call(
        column_kernel,
        (*blocks, weight),
        [whole_spec()] * 5,
        [
            ((mel_count, total, 2 * lanes), bf16),
            ((total, LANES), f32),
            (padded, f32),
            ((mel_count, total, out_width), f32),
            (padded, f32),
        ],
        [whole_spec()] * 5,
        [],
        0,
        8,
    )


def first_kernel(starts, *refs):
    blocks, (weight, scales, keep), sources = refs[:4], refs[4:7], refs[7:10]
    low, high, picked, field, middle, stats = refs[10:16]
    lower, upper = refs[16:]
    mel_count, total, _ = field.shape
    out_width = middle.shape[2]
    place = lax.axis_index("tm")
    clear_edges(lower, upper, total)
    settle(blocks, field, None)
    targets = ((lower, TILE), (middle, 0), (upper, TILE))
    products(field, weight, (1, 3), targets, sources)

    def combine(at, sums):
        before, after = same_clip(starts, at, (ROWS, out_width), total)
        mask = widen(keep[pl.ds(at, ROWS)], out_width)
        one, two, num = sums
        num = num + fold(mask)
        for m in range(mel_count):
            rows = joined(lower, middle, upper, m, at, before, after)
            middle[m, pl.ds(at, ROWS)] = rows
            kept = rows * mask
            one = one + fold(kept)
            two = two + fold(kept * rows)
        return one, two, num

    blank = jnp.zeros((TILE, out_width), f32)
    one, two, num = by_rows(total, combine, (blank, blank, blank))
    pixels = column_sum(num) * mel_count
    center, inverse = moments((one, two), keep, pixels)
    stats[0:1] = center
    stats[1:2] = inverse
    stats[2:3] = pixels
    scale = scales[0:1] * inverse
    offset = scales[1:2] - center * scale

    def activate(at, carry):
        mask = widen(keep[pl.ds(at, ROWS)], out_width)
        for m in range(mel_count):
            value = middle[m, pl.ds(at, ROWS)] * scale + offset
            rows = (value * phi_parts(value) * mask).astype(bf16)
            if m < mel_count // 2:
                low[m, pl.ds(at, ROWS)] = rows
            else:
                high[m - mel_count // 2, pl.ds(at, ROWS)] = rows
        return carry

    by_rows(total, activate, 0)
    reach = picked.shape[1]
    for m in range(picked.shape[0]):
        picked[m] = high[m, pl.ds(pl.multiple_of((place % 2) * reach, reach), reach)]


def first_block(blocks, weight, scales, keep, sources, starts, total):
    _, mel_count, frames, lanes = blocks[0].shape
    out_width = weight.shape[3]
    padded = (mel_count, total + 2 * TILE, out_width)
    half = (mel_count // 2, total, out_width)
    return call(
        first_kernel,
        (starts, *blocks, weight, scales, keep, *sources),
        [scalar_spec()] + [whole_spec()] * 10,
        [
            (half, bf16),
            (half, bf16),
            ((mel_count // 2, total // 2, out_width), bf16),
            ((mel_count, total, 2 * lanes), bf16),
            ((mel_count, total, out_width), f32),
            ((TILE, out_width), f32),
        ],
        [whole_spec()] * 6,
        [pltpu.VMEM(padded, f32), pltpu.VMEM(padded, f32)],
        0,
        16,
    )


def slope_kernel(pre, stats, scales, keep, slope):
    mel_count, total, width = pre.shape
    center, inverse = stats[0:1], stats[1:2]
    scale = scales[0:1] * inverse
    offset = scales[1:2] - center * scale

    def rows(at, carry):
        mask = widen(keep[pl.ds(at, ROWS)], width)
        for m in range(mel_count):
            value = pre[m, pl.ds(at, ROWS)] * scale + offset
            slope[m, pl.ds(at, ROWS)] = mask * (phi_parts(value) + value * bell(value))
        return carry

    by_rows(total, rows, 0)


def first_slope(pre, stats, scales, keep):
    return call(
        slope_kernel,
        (pre, stats, scales, keep),
        [whole_spec()] * 4,
        [(pre.shape, f32)],
        [whole_spec()],
        [],
        2**28,
        6,
    )[0]


def group_sums(fields, weight, starts, targets, sources=None):
    mel_count, (_, total, width) = len(fields[0]), targets[1][0].shape
    for m in range(mel_count):
        for a in range(3):
            acc = None
            for mels, start in zip(fields, starts):
                for b in range(3):
                    if 0 <= m + b - 1 < mel_count:
                        part = jnp.dot(
                            mels[m + b - 1][...],
                            weight[a, b, pl.ds(start, width)],
                            preferred_element_type=f32,
                        )
                        acc = part if acc is None else acc + part
            if sources is not None:
                acc = acc + sources[a, m]
            target, at = targets[a]
            target[m, at : at + total] = acc


def join_halves(pair, joint, sems):
    side = lax.axis_index("tm") % 2
    half = pair[0].shape[1]
    copies = []
    for i, (part, begin) in enumerate(zip(pair, (side, 1 - side))):
        rows = pl.ds(pl.multiple_of(begin * half, half), half)
        copies.append(pltpu.make_async_copy(part, joint.at[:, rows], sems.at[i]))
        copies[-1].start()
    return copies


def group_starts(bits, width):
    column = lax.axis_index("chan")
    return [pl.multiple_of((column ^ bit) * width, width) for bit in bits]


def near_kernel(low, high, low_two, high_two, weight, sums):
    half, _, width = low.shape
    fields = [
        [a.at[k] for a in pair for k in range(half)] for pair in ((low, high), (low_two, high_two))
    ]
    targets = [(sums.at[a], 0) for a in range(3)]
    group_sums(fields, weight, group_starts((0, 1), width), targets)


def near_part(low, high, low_two, high_two, weight):
    half, total, width = low.shape
    return call(
        near_kernel,
        (low, high, low_two, high_two, weight),
        [whole_spec()] * 5,
        [((3, 2 * half, total, width), f32)],
        [whole_spec()],
        [],
        0,
        6,
    )[0]


def far_kernel(far, picked, rest, weight, near, sums, joint, sems):
    half, _, width = far.shape
    copies = join_halves((picked, rest), joint, sems)
    for copy in copies:
        copy.wait()
    fields = [[a.at[k] for a in (far, joint) for k in range(half)]]
    targets = [(sums.at[a], 0) for a in range(3)]
    group_sums(fields, weight, group_starts((2,), width), targets, near)


def far_part(far, picked, rest, weight, near):
    return call(
        far_kernel,
        (far, picked, rest, weight, near),
        [whole_spec()] * 5,
        [(near.shape, f32)],
        [whole_spec()],
        [pltpu.VMEM(far.shape, bf16), pltpu.SemaphoreType.DMA((2,))],
        0,
        8,
    )[0]


def run_sums(mask, plain, values):
    width = (plain + values)[0].shape[1]
    terms = list(plain)
    for value in values:
        for _ in range(3):
            term = value.astype(bf16)
            terms.append(term)
            value = value - term.astype(f32)
    out = jnp.dot(mask, jnp.concatenate(terms, axis=1), preferred_element_type=f32)
    parts = [out[:, k * width : (k + 1) * width] for k in range(len(terms))]
    results = parts[: len(plain)]
    for k in range(len(plain), len(parts), 3):
        results.append(parts[k] + (parts[k + 1] + parts[k + 2]))
    return results


def second_kernel(
    starts, sums, far_two, picked_two, rest_two, weight, keep, scales, *refs
):
    cotangents, (readout, grad, gain_grad, shift_grad) = refs[:-14], refs[-14:-10]
    middle, slope, lower, upper, joint, hold, wide, full, sems, joint_sems = refs[-10:]
    mel_count, total, width = middle.shape
    half = mel_count // 2
    place = lax.axis_index("tm")
    pooled_total = total // 2
    own = readout.shape[0]
    copies = []
    pieces = [(part, i) for part in cotangents for i in range(part.shape[0])]
    bits = gather_bits(len(pieces))
    for k, (part, i) in enumerate(pieces):
        source = place ^ sum(bit for j, bit in enumerate(bits) if k >> j & 1)
        copies.append(
            pltpu.make_async_copy(
                part.at[i],
                full.at[pl.ds(pl.multiple_of(source * own, own), own)],
                sems.at[k],
            )
        )
    for copy in copies:
        copy.start()

    halves = join_halves((picked_two, rest_two), joint, joint_sems)
    clear_edges(lower, upper, total)
    for copy in halves:
        copy.wait()
    fields = [[a.at[k] for a in (far_two, joint) for k in range(half)]]
    targets = ((lower, TILE), (middle, 0), (upper, TILE))
    group_sums(fields, weight, group_starts((3,), width), targets, sums)
    blank = jnp.zeros((TILE, width), f32)

    def combine(at, sums):
        before, after = same_clip(starts, at, (ROWS, width), total)
        mask = widen(keep[pl.ds(at, ROWS)], width)
        first, second, num = sums
        num = num + fold(mask)
        for m in range(mel_count):
            rows = joined(lower, middle, upper, m, at, before, after)
            middle[m, pl.ds(at, ROWS)] = rows
            kept = rows * mask
            first = first + fold(kept)
            second = second + fold(kept * rows)
        return first, second, num

    first, second, num = by_rows(total, combine, (blank, blank, blank))
    pixels = column_sum(num) * mel_count
    center, inverse = moments((first, second), keep, pixels)
    scale = scales[2:3] * inverse
    offset = scales[3:4] - center * scale

    def activate(at, carry):
        mask = widen(keep[pl.ds(at, ROWS)], width)
        pooled = jnp.zeros((ROWS, width), f32)
        for m in range(mel_count):
            value = middle[m, pl.ds(at, ROWS)] * scale + offset
            share = phi_parts(value)
            pooled = pooled + value * share
            slope[m, pl.ds(at, ROWS)] = mask * (share + value * bell(value))
        pooled = pooled * mask
        for c in range(width // LANES):
            hold[c, pl.ds(at, ROWS)] = pooled[:, c * LANES : (c + 1) * LANES]
        return carry

    by_rows(total, activate, 0)

    even = pl.ds(0, pooled_total, stride=2)
    odd = pl.ds(1, pooled_total, stride=2)
    pooled = jnp.concatenate(
        [hold[c, even] + hold[c, odd] for c in range(width // LANES)], axis=1
    ) * (0.5 / mel_count)
    present = widen(keep[even], width)
    square = (pooled_total, pooled_total)
    row = lax.broadcasted_iota(jnp.int32, square, 0)
    col = lax.broadcasted_iota(jnp.int32, square, 1)
    same = row >= col
    back = row <= col
    for k in range(1, starts.shape[0]):
        crossed = (2 * row < starts[k]) != (2 * col < starts[k])
        same = same & ~crossed
        back = back & ~crossed
    ahead, behind = same.astype(f32).astype(bf16), back.astype(f32).astype(bf16)
    exponent = jnp.exp(pooled)
    counts, totals, sums = run_sums(
        ahead, (present.astype(bf16),), (present * pooled, present * exponent)
    )
    wide[...] = totals / counts + jnp.log(sums)
    readout[...] = wide[pl.ds(pl.multiple_of(place * own, own), own)]
    for copy in copies:
        copy.wait()
    cotangent = full[...]
    by_count, by_sum = run_sums(behind, (), (cotangent / counts, cotangent / sums))
    down = present * (by_count + exponent * by_sum) * (0.5 / mel_count)
    for c in range(width // LANES):
        hold[c, even] = down[:, c * LANES : (c + 1) * LANES]
        hold[c, odd] = down[:, c * LANES : (c + 1) * LANES]

    def slopes(at, sums):
        down_rows = jnp.concatenate(
            [hold[c, pl.ds(at, ROWS)] for c in range(width // LANES)], axis=1
        )
        plain, along = sums
        for m in range(mel_count):
            step = down_rows * slope[m, pl.ds(at, ROWS)]
            slope[m, pl.ds(at, ROWS)] = step
            plain = plain + fold(step)
            along = along + fold(step * ((middle[m, pl.ds(at, ROWS)] - center) * inverse))
        return plain, along

    plain, along = by_rows(total, slopes, (blank, blank))
    plain, along = column_sum(plain), column_sum(along)
    shift_grad[...] = plain
    gain_grad[...] = along
    plain, along = plain / pixels, along / pixels

    def finish(at, carry):
        mask = widen(keep[pl.ds(at, ROWS)], width)
        for m in range(mel_count):
            normed = (middle[m, pl.ds(at, ROWS)] - center) * inverse
            rows = slope[m, pl.ds(at, ROWS)] - plain - normed * along
            grad[m, pl.ds(at, ROWS)] = (mask * (scale * rows)).astype(bf16)
        return carry

    by_rows(total, finish, 0)


def second_block(sums, arrays, weight, keep, scales, starts, cotangents, own):
    _, mel_count, total, width = sums.shape
    padded = (mel_count, total + 2 * TILE, width)
    full = (mel_count, total, width)
    return call(
        second_kernel,
        (starts, sums, *arrays, weight, keep, scales, *cotangents),
        [scalar_spec()] + [whole_spec()] * (len(arrays) + 4) + [place_spec()] * len(cotangents),
        [((own, width), f32), (full, bf16), ((1, width), f32), ((1, width), f32)],
        [whole_spec()] * 4,
        [
            pltpu.VMEM(full, f32),
            pltpu.VMEM(full, f32),
            pltpu.VMEM(padded, f32),
            pltpu.VMEM(padded, f32),
            pltpu.VMEM(arrays[0].shape, bf16),
            pltpu.VMEM((width // LANES, total, LANES), f32),
            pltpu.VMEM((total // 2, width), f32),
            pltpu.VMEM((total // 2, width), f32),
            pltpu.SemaphoreType.DMA((sum(part.shape[0] for part in cotangents),)),
            pltpu.SemaphoreType.DMA((2,)),
        ],
        0,
        20,
    )


def back_kernel(bit, mels, halved, starts, one, two, weight, weight_two, out, lower, middle, upper):
    mel_count, total, width = one.shape
    reach, rows_out = middle.shape[1], out.shape[1]
    side = lax.axis_index("tm") % 2 if halved else 0
    edge = reach - rows_out
    first = side * (total - reach)
    skip = side * edge
    if halved:
        first, skip = pl.multiple_of(first, 16), pl.multiple_of(skip, 16)
    (start,) = group_starts((bit,), width)
    for k in range(len(mels)):
        for ref in (lower, upper):
            ref[k, :TILE] = jnp.zeros((TILE, width), f32)
            ref[k, TILE + reach :] = jnp.zeros((TILE, width), f32)
    for k, n in enumerate(mels):
        for a in range(3):
            acc = None
            for field, matrix in ((one, weight), (two, weight_two)):
                for b in range(3):
                    if 0 <= n - b + 1 < mel_count:
                        part = lax.dot_general(
                            field[n - b + 1, pl.ds(first, reach)],
                            matrix[a, b, pl.ds(start, width)],
                            (((1,), (1,)), ((), ())),
                            preferred_element_type=f32,
                        )
                        acc = part if acc is None else acc + part
            if a == 2:
                lower[k, TILE : TILE + reach] = acc
            elif a == 1:
                middle[k] = acc
            else:
                upper[k, TILE : TILE + reach] = acc

    def combine(at, carry):
        near = pl.multiple_of(at + skip, TILE)
        before, after = same_clip(starts, first + near, (ROWS, width), total)
        for k in range(len(mels)):
            rows = joined(lower, middle, upper, k, near, before, after)
            out[k, pl.ds(at, ROWS)] = rows.astype(out.dtype)
        return carry

    by_rows(rows_out, combine, 0)


def hidden_back(bit, mels, halved, one, two, weight, weight_two, starts, kind):
    _, total, width = one.shape
    rows = total // 2 if halved else total
    reach = rows + 16 if halved else total
    count = len(mels)
    padded = (count, reach + 2 * TILE, width)
    return call(
        functools.partial(back_kernel, bit, mels, halved),
        (starts, one, two, weight, weight_two),
        [scalar_spec()] + [whole_spec()] * 4,
        [((count, rows, width), kind)],
        [whole_spec()],
        [
            pltpu.VMEM(padded, f32),
            pltpu.VMEM((count, reach, width), f32),
            pltpu.VMEM(padded, f32),
        ],
        0,
        14,
    )


def norm_kernel(mine, low, picked, rest, slope, pre, stats, scales, keep, *refs):
    grad, window, gain_grad, shift_grad, padded = refs
    mel_count, total, width = mine.shape
    center, inverse, pixels = stats[0:1], stats[1:2], stats[2:3]
    blank = jnp.zeros((TILE, width), f32)
    edge = (padded.shape[1] - total) // 2
    reach = window.shape[1]
    frames = reach - 2 * edge
    place = lax.axis_index("tm")

    half = mel_count // 2

    def add(field, base, mels):
        def slopes(at, sums):
            plain, along = sums
            place_rows = pl.ds(pl.multiple_of(base + at, ROWS), ROWS)
            for k, m in enumerate(mels):
                rows = mine[m, place_rows] + field[k, pl.ds(at, ROWS)].astype(f32)
                step = rows * slope[m, place_rows]
                mine[m, place_rows] = step
                plain = plain + fold(step)
                along = along + fold(step * ((pre[m, place_rows] - center) * inverse))
            return plain, along

        return slopes

    side = place % 2
    sums = by_rows(total, add(low, 0, range(half)), (blank, blank))
    upper = range(half, mel_count)
    parts = []
    for field, base in ((picked, side), (rest, 1 - side)):
        parts.append(by_rows(total // 2, add(field, base * (total // 2), upper), (blank, blank)))
    plain, along = [
        a + jnp.where(side == 0, b + c, c + b) for a, b, c in zip(sums, parts[0], parts[1])
    ]
    plain, along = column_sum(plain), column_sum(along)
    shift_grad[...] = plain
    gain_grad[...] = along
    plain, along = plain / pixels, along / pixels
    scale = scales[0:1] * inverse
    for m in range(mel_count):
        padded[m, :edge] = jnp.zeros((edge, width), bf16)
        padded[m, edge + total :] = jnp.zeros((edge, width), bf16)

    def finish(at, carry):
        mask = widen(keep[pl.ds(at, ROWS)], width)
        for m in range(mel_count):
            normed = (pre[m, pl.ds(at, ROWS)] - center) * inverse
            rows = mine[m, pl.ds(at, ROWS)] - plain - normed * along
            rows = (mask * (scale * rows)).astype(bf16)
            grad[m, pl.ds(at, ROWS)] = rows
            padded[m, pl.ds(pl.multiple_of(at + edge, 16), ROWS)] = rows
        return carry

    by_rows(total, finish, 0)
    for m in range(mel_count):
        window[m] = padded[m, pl.ds(pl.multiple_of(place * frames, frames), reach)]


def norm_back_first(mine, low, picked, rest, slope, pre, stats, scales, keep, frames):
    mel_count, total, width = mine.shape
    edge = 16
    return call(
        norm_kernel,
        (mine, low, picked, rest, slope, pre, stats, scales, keep),
        [whole_spec()] * 9,
        [
            ((mel_count, total, width), bf16),
            ((mel_count, frames + 2 * edge, width), bf16),
            ((1, width), f32),
            ((1, width), f32),
        ],
        [whole_spec()] * 4,
        [pltpu.VMEM((mel_count, total + 2 * edge, width), bf16)],
        2**28,
        12,
    )


def spread_kernel(starts, grad, steps, spaced):
    mel_count, total, width = grad.shape
    for m in range(mel_count):
        spaced[m, :TILE] = jnp.zeros((TILE, width), f32)
        spaced[m, TILE + total :] = jnp.zeros((TILE, width), f32)

    def expand(at, carry):
        for m in range(mel_count):
            rows = grad[m, pl.ds(at, ROWS)].astype(f32)
            spaced[m, pl.ds(pl.multiple_of(at + TILE, TILE), ROWS)] = rows
        return carry

    by_rows(total, expand, 0)

    def shift(at, carry):
        before, after = same_clip(starts, at, (ROWS, width), total)
        for m in range(mel_count):
            rows = spaced[m, pl.ds(at, ROWS + 2 * TILE)]
            ahead = jnp.where(after, rows[TILE + 1 : TILE + 1 + ROWS], 0.0)
            behind = jnp.where(before, rows[TILE - 1 : TILE - 1 + ROWS], 0.0)
            steps[0, m, pl.ds(at, ROWS)] = ahead.astype(bf16)
            steps[1, m, pl.ds(at, ROWS)] = behind.astype(bf16)
        return carry

    by_rows(total, shift, 0)


def spread(grad, starts):
    mel_count, total, width = grad.shape
    return call(
        spread_kernel,
        (starts, grad),
        [scalar_spec(), whole_spec()],
        [((2, mel_count, total, width), bf16)],
        [whole_spec()],
        [pltpu.VMEM((mel_count, total + 2 * TILE, width), f32)],
        0,
        6,
    )[0]


def weight_kernel(layout, halves, *refs):
    count = len(refs) - 7
    fields, grad, steps = list(refs[:count]), refs[count], refs[count + 1]
    out, results, joint, sems, move_sems = refs[count + 2 :]
    mel_count, total, out_width = grad.shape
    width = results.shape[2]
    side = lax.axis_index("tm") % 2
    column = lax.axis_index("chan")
    moves = []
    for i, pair in enumerate(halves):
        for index, begin in zip(pair, (side, 1 - side)):
            rows = pl.ds(pl.multiple_of(begin * (total // 2), total // 2), total // 2)
            moves.append(
                pltpu.make_async_copy(fields[index], joint.at[i, :, rows], move_sems.at[len(moves)])
            )
            moves[-1].start()
        fields.append(joint.at[i])
    copies = [[], []]
    for i, (places, pieces) in enumerate(layout):
        slot = i % 2
        for copy in copies[slot]:
            copy.wait()
        if any(piece[0] >= count for piece in pieces):
            while moves:
                moves.pop().wait()
        for a in range(3):
            for b in range(3):
                right = grad if a == 1 else steps.at[a // 2]
                acc = None
                for m in range(mel_count):
                    if 0 <= m + b - 1 < mel_count:
                        index, k, lane = pieces[m + b - 1]
                        part = lax.dot_general(
                            fields[index][k, :, lane : lane + width],
                            right[m],
                            (((0,), (0,)), ((), ())),
                            preferred_element_type=f32,
                        )
                        acc = part if acc is None else acc + part
                results[slot, 3 * a + b] = acc
        each = width // len(places)
        copies[slot] = []
        for j, bit in enumerate(places):
            start = pl.multiple_of((column ^ bit) * each, each)
            copies[slot].append(
                pltpu.make_async_copy(
                    results.at[slot, :, j * each : (j + 1) * each],
                    out.at[:, pl.ds(start, each)],
                    sems.at[slot, j],
                )
            )
            copies[slot][-1].start()
    for copy in copies[0] + copies[1]:
        copy.wait()


def weight_back(layout, halves, fields, grad, steps, in_width):
    mel_count, total, out_width = grad.shape
    width = in_width // len(layout)
    joint = (max(len(halves), 1), mel_count // 2, total, width)
    out = call(
        functools.partial(weight_kernel, layout, halves),
        (*fields, grad, steps),
        [whole_spec()] * (len(fields) + 2),
        [((9, in_width, out_width), f32)],
        [place_spec()],
        [
            pltpu.VMEM((2, 9, width, out_width), f32),
            pltpu.VMEM(joint, bf16),
            pltpu.SemaphoreType.DMA((2, 2)),
            pltpu.SemaphoreType.DMA((max(2 * len(halves), 1),)),
        ],
        0,
        12,
    )[0]
    return out.reshape(3, 3, in_width, out_width)


def input_kernel(starts, one, two, weight, weight_two, mine, other, lower, middle, upper):
    mel_count, reach, width = one.shape
    frames, lanes = mine.shape[1], mine.shape[2]
    edge = (reach - frames) // 2
    total = frames * lax.axis_size("tm")
    place = lax.axis_index("tm")
    groups = group_starts((2, 0), lanes)
    for a in range(3):
        target, shift = ((upper, TILE), (middle, 0), (lower, TILE))[a]
        for b in (1, 0, 2):
            low, count = ((1, mel_count - 1), (0, mel_count), (0, mel_count - 1))[b]
            acc = None
            for field, matrix in ((one, weight), (two, weight_two)):
                rows = field[low : low + count].reshape(count * reach, width)
                wing = jnp.concatenate([matrix[a, b, pl.ds(g, lanes)] for g in groups])
                part = lax.dot_general(
                    rows, wing, (((1,), (1,)), ((), ())), preferred_element_type=f32
                )
                acc = part if acc is None else acc + part
            acc = acc.reshape(count, reach, 2 * lanes)
            for k in range(count):
                n = low + k + b - 1
                if b == 1:
                    target[n, shift : shift + reach] = acc[k]
                else:
                    target[n, shift : shift + reach] += acc[k]
    before, after = same_clip(starts, place * frames, (frames, 2 * lanes), total)
    for m in range(mel_count):
        low = lower[m, TILE + edge - 1 : TILE + edge - 1 + frames]
        high = upper[m, TILE + edge + 1 : TILE + edge + 1 + frames]
        rows = (
            middle[m, edge : edge + frames]
            + jnp.where(before, low, 0.0)
            + jnp.where(after, high, 0.0)
        )
        other[m] = rows[:, :lanes]
        mine[m] = rows[:, lanes:]


def input_back(one, two, weight, weight_two, starts, frames, lanes):
    mel_count, reach, width = one.shape
    shape = (mel_count, frames, lanes)
    return call(
        input_kernel,
        (starts, one, two, weight, weight_two),
        [scalar_spec()] + [whole_spec()] * 4,
        [(shape, f32), (shape, f32)],
        [whole_spec()] * 2,
        [
            pltpu.VMEM((mel_count, reach + 2 * TILE, 2 * lanes), f32),
            pltpu.VMEM((mel_count, reach, 2 * lanes), f32),
            pltpu.VMEM((mel_count, reach + 2 * TILE, 2 * lanes), f32),
        ],
        0,
        10,
    )


def close_kernel(mine, other, keep, out):
    mel_count, frames, lanes = mine.shape
    begin = pl.multiple_of(lax.axis_index("tm") * frames, frames)
    mask = keep[pl.ds(begin, frames)]
    for m in range(mel_count):
        out[:, m, :] = (mine[m] + other[m]) * mask


def close(mine, other, keep):
    mel_count, frames, lanes = mine.shape
    return call(
        close_kernel,
        (mine, other, keep),
        [whole_spec()] * 3,
        [((frames, mel_count, lanes), f32)],
        [whole_spec()],
        [],
        0,
        4,
    )[0]


def whole_frames(
    features,
    conv1_weight,
    norm1_gain,
    norm1_bias,
    conv2_weight,
    norm2_gain,
    norm2_bias,
    clip_starts,
    valid,
    readout_grad,
):
    frames, mel_count, lanes = features.shape
    places = lax.axis_size("tm")
    total = frames * places
    clip_starts, conv1_weight = bring(clip_starts, conv1_weight)
    scales = jnp.stack([norm1_gain, norm1_bias, norm2_gain, norm2_bias])

    marked = jnp.where(valid[:, None, None] > 0, features, jnp.asarray(ABSENT, bf16))
    own = jnp.transpose(marked, (1, 0, 2))
    pieces = [swap(own, "tm", 2 * k) for k in range(1, places // 2)]
    along = jnp.stack([own] + pieces)
    near = [
        along,
        swap(along, "tm", 1),
        swap(along, "chan", 2),
        swap_both(along, "tm", 1, "chan", 2),
    ]
    readout_grad, _ = lax.optimization_barrier((readout_grad, pieces[0]))
    bits = gather_bits(places)
    cotangents = [readout_grad[None]]
    cotangents.append(swap(cotangents[0], "tm", bits[0]))
    near[3], clip_starts, conv1_weight, scales, cotangents = lax.optimization_barrier(
        (near[3], clip_starts, conv1_weight, scales, cotangents)
    )
    others = [swap(block, "chan", 1) for block in near]
    column, keep, *sources = column_part(near, conv1_weight, total)
    column, others = lax.optimization_barrier((column, others))
    other_conv2 = swap(conv2_weight, "chan", 1)
    others, other_conv2 = lax.optimization_barrier((others, other_conv2))

    low, high, picked, other_column, pre, stats = first_block(
        others, conv1_weight, scales, keep, sources, clip_starts, total
    )
    fields1 = (column, other_column)

    far_picked = swap(picked, "chan", 2)
    far = swap(low, "chan", 2)
    far_rest = swap(far_picked, "tm", 1)

    low_two, high_two = swap(low, "chan", 1), swap(high, "chan", 1)
    near = near_part(low, high, low_two, high_two, conv2_weight)
    far_picked, near, cotangents = lax.optimization_barrier((far_picked, near, cotangents))
    picked_two = swap(far_picked, "chan", 1)
    for bit in bits[1:-1]:
        cotangents.append(swap(jnp.concatenate(cotangents), "tm", bit))
    picked_two, pre, cotangents = lax.optimization_barrier((picked_two, pre, cotangents))
    cotangents.append(swap(jnp.concatenate(cotangents), "tm", bits[-1]))
    slope = first_slope(pre, stats, scales, keep)
    far, far_rest, slope, cotangents = lax.optimization_barrier((far, far_rest, slope, cotangents))
    far_two, rest_two = swap(far, "chan", 1), swap(far_rest, "chan", 1)
    sums = far_part(far, far_picked, far_rest, conv2_weight, near)
    far_two, rest_two, sums = lax.optimization_barrier((far_two, rest_two, sums))

    readout, grad2, gain2_grad, shift2_grad = second_block(
        sums,
        (far_two, picked_two, rest_two),
        conv2_weight,
        keep,
        scales,
        clip_starts,
        cotangents,
        readout_grad.shape[0],
    )
    grad2_near = swap(grad2, "chan", 1)
    steps2 = spread(grad2, clip_starts)
    grad2_near, steps2 = lax.optimization_barrier((grad2_near, steps2))
    back = functools.partial(
        hidden_back,
        one=grad2,
        two=grad2_near,
        weight=conv2_weight,
        weight_two=other_conv2,
        starts=clip_starts,
    )
    came_picked = swap(back(2, (2, 3), True, kind=bf16)[0], "chan", 2)
    (away_low,) = back(2, (0, 1), False, kind=bf16)
    came_low = swap(away_low, "chan", 2)

    away_low, other_conv2 = lax.optimization_barrier((away_low, other_conv2))
    (mine,) = back(0, (0, 1, 2, 3), False, weight_two=other_conv2, kind=f32)
    came_picked, mine, conv1_weight = lax.optimization_barrier((came_picked, mine, conv1_weight))
    came_rest = swap(came_picked, "tm", 1)
    other_conv1 = swap(conv1_weight, "chan", 1)
    fields = (low, high, low_two, high_two)
    fields += (far, far_picked, far_rest, far_two, picked_two, rest_two)
    layout = [
        ((0,), [(0, 0, 0), (0, 1, 0), (1, 0, 0), (1, 1, 0)]),
        ((1,), [(2, 0, 0), (2, 1, 0), (3, 0, 0), (3, 1, 0)]),
        ((2,), [(4, 0, 0), (4, 1, 0), (10, 0, 0), (10, 1, 0)]),
        ((3,), [(7, 0, 0), (7, 1, 0), (11, 0, 0), (11, 1, 0)]),
    ]
    weight2_grad = weight_back(
        layout, ((5, 6), (8, 9)), fields, grad2, steps2, conv2_weight.shape[2]
    )
    came_low, came_rest, mine, weight2_grad, other_conv1 = lax.optimization_barrier(
        (came_low, came_rest, mine, weight2_grad, other_conv1)
    )

    grad1, window, gain1_grad, shift1_grad = norm_back_first(
        mine, came_low, came_picked, came_rest, slope, pre, stats, scales, keep, frames
    )
    window_near = swap(window, "chan", 1)
    steps1 = spread(grad1, clip_starts)
    window_near, steps1 = lax.optimization_barrier((window_near, steps1))
    input_mine, input_away = input_back(
        window, window_near, conv1_weight, other_conv1, clip_starts, frames, lanes
    )
    input_came = swap(input_away, "chan", 2)
    layout = [(bits, [(i, m, 0) for m in range(mel_count)]) for i, bits in enumerate(((0, 2), (1, 3)))]
    weight1_grad = weight_back(layout, (), fields1, grad1, steps1, conv1_weight.shape[2])
    input_came, weight1_grad = lax.optimization_barrier((input_came, weight1_grad))
    return (
        readout,
        close(input_mine, input_came, keep),
        weight1_grad,
        gain1_grad[0],
        shift1_grad[0],
        weight2_grad,
        gain2_grad[0],
        shift2_grad[0],
    )


def fits_whole(frames, mels, places, columns, widths):
    return (
        places > 1
        and places & (places - 1) == 0
        and columns == 4
        and frames % ROWS == 0
        and frames * places <= 512
        and mels == 4
        and all(w % (columns * LANES) == 0 for w in widths)
        and widths[1] == columns * 256
    )


def shards(*arrays):
    features, conv1_weight, conv2_weight = arrays[0], arrays[1], arrays[4]
    if fits_whole(
        features.shape[0],
        features.shape[1],
        lax.axis_size("tm"),
        lax.axis_size("chan"),
        (conv1_weight.shape[2], conv2_weight.shape[2]),
    ):
        return whole_frames(*arrays)
    return split_frames(*arrays)


def solution(mesh):
    return jax.shard_map(
        shards,
        mesh=mesh,
        in_specs=(
            P("tm", None, "chan"),
            P(None, None, None, "chan"),
            P("chan"),
            P("chan"),
            P(None, None, None, "chan"),
            P("chan"),
            P("chan"),
            P(),
            P("tm"),
            P("tm", "chan"),
        ),
        out_specs=(
            P("tm", "chan"),
            P("tm", None, "chan"),
            P(None, None, None, "chan"),
            P("chan"),
            P("chan"),
            P(None, None, None, "chan"),
            P("chan"),
            P("chan"),
        ),
        check_vma=False,
    )
```

```python
import functools

import jax
import jax.numpy as jnp
from jax import lax
from jax.experimental import pallas as pl
from jax.experimental.pallas import tpu as pltpu
from jax.sharding import PartitionSpec as P

EPS = 1e-05
highest = lax.Precision.HIGHEST
f32 = jnp.float32
bf16 = jnp.bfloat16


def padded_2(shard, sides, width):
    for axis, dim in sides:
        count, length = (lax.axis_size(axis), shard.shape[dim])
        up = [(i, (i + 1) % count) for i in range(count - 1)]
        down = [(j, i) for i, j in up]
        last = lax.slice_in_dim(shard, length - width, length, axis=dim)
        leading = lax.slice_in_dim(shard, 0, width, axis=dim)
        before = lax.ppermute(last, axis, up)
        after = lax.ppermute(leading, axis, down)
        shard = jnp.concatenate([before, shard, after], axis=dim)
    return shard


def entering(part, axis, combine, identity, reverse):
    count = lax.axis_size(axis)
    place = lax.axis_index(axis)
    ahead = count - 1 - place if reverse else place
    gathered = jax.tree.map(lambda a: lax.all_gather(a, axis), part)
    state = jax.tree.map(lambda a, e: jnp.zeros_like(a) + jnp.asarray(e, a.dtype), part, identity)

    def one(step, state):
        source = count - 1 - step if reverse else step
        return combine(
            state, jax.tree.map(lambda a: lax.dynamic_index_in_dim(a, source, 0, False), gathered)
        )

    return lax.fori_loop(0, ahead, one, state)


def frame_flags(clip_starts, first_frame, frame_count, frame_total):
    position = first_frame - 2 + jnp.arange(frame_count + 4, dtype=jnp.int32)
    segment = jnp.sum((clip_starts[None, :] <= position[:, None]).astype(jnp.int32), axis=1) - 1
    inside = (position >= 0) & (position < frame_total)
    middle = segment[1:-1]
    before_same = inside[1:-1] & inside[:-2] & (middle == segment[:-2])
    after_same = inside[1:-1] & inside[2:] & (middle == segment[2:])
    return (segment[2:-2], before_same, after_same)


def conv_forward(padded, weight, factors):
    frame_count = padded.shape[0] - 2
    mel_count = padded.shape[1]
    wide_field = jnp.pad(padded, ((0, 0), (1, 1), (0, 0)))
    result = jnp.zeros((frame_count, mel_count, weight.shape[3]), jnp.float32)
    for tap_row in range(3):
        partial_value = jnp.zeros((frame_count * mel_count, weight.shape[3]), jnp.float32)
        for tap_col in range(3):
            window = wide_field[
                tap_row : tap_row + frame_count, tap_col : tap_col + mel_count, :
            ].reshape(frame_count * mel_count, -1)
            partial_value = partial_value + jnp.dot(
                window, weight[tap_row, tap_col], preferred_element_type=jnp.float32
            )
        result = (
            result
            + partial_value.reshape(frame_count, mel_count, -1) * factors[tap_row][:, None, None]
        )
    return result


def conv_weight_grad(padded, grad_out, factors):
    frame_count = grad_out.shape[0]
    mel_count = grad_out.shape[1]
    wide_field = jnp.pad(padded, ((0, 0), (1, 1), (0, 0)))
    rows_out = []
    for tap_row in range(3):
        scaled = (grad_out * factors[tap_row][:, None, None].astype(jnp.bfloat16)).reshape(
            frame_count * mel_count, -1
        )
        taps_out = []
        for tap_col in range(3):
            window = wide_field[
                tap_row : tap_row + frame_count, tap_col : tap_col + mel_count, :
            ].reshape(frame_count * mel_count, -1)
            taps_out.append(
                lax.dot_general(
                    window, scaled, (((0,), (0,)), ((), ())), preferred_element_type=jnp.float32
                )
            )
        rows_out.append(jnp.stack(taps_out))
    return jnp.stack(rows_out)


def conv_input_grad(grad_padded, weight, edge_factors):
    frame_count = grad_padded.shape[0] - 2
    mel_count = grad_padded.shape[1]
    wide_field = jnp.pad(grad_padded, ((0, 0), (1, 1), (0, 0)))
    result = jnp.zeros((frame_count * mel_count, weight.shape[2]), jnp.float32)
    for tap_row in range(3):
        scaled = wide_field * edge_factors[tap_row][:, None, None]
        for tap_col in range(3):
            window = scaled[
                2 - tap_row : 2 - tap_row + frame_count, 2 - tap_col : 2 - tap_col + mel_count, :
            ].reshape(frame_count * mel_count, -1)
            result = result + lax.dot_general(
                window,
                weight[tap_row, tap_col],
                (((1,), (1,)), ((), ())),
                preferred_element_type=jnp.float32,
            )
    return result.reshape(frame_count, mel_count, -1)


def join_keyed(earlier_item, later_item):
    keep_first = later_item[0] < 0.0
    same_key = later_item[0] == earlier_item[0]
    merged = [jnp.where(keep_first, earlier_item[0], later_item[0])]
    for first_part, second_part in zip(earlier_item[1:], later_item[1:]):
        extra = (1,) * (first_part.ndim - keep_first.ndim)
        keep_wide = jnp.reshape(keep_first, keep_first.shape + extra)
        same_wide = jnp.reshape(same_key, same_key.shape + extra)
        merged.append(
            jnp.where(
                keep_wide, first_part, jnp.where(same_wide, first_part + second_part, second_part)
            )
        )
    return tuple(merged)


def smooth(argument):
    return jax.nn.gelu(argument, approximate=False)


def split_frames(
    features,
    conv1_weight,
    norm1_gain,
    norm1_bias,
    conv2_weight,
    norm2_gain,
    norm2_bias,
    clip_starts,
    valid,
    readout_grad,
):
    frame_count = features.shape[0]
    mel_count = features.shape[1]
    cycle_size = lax.axis_size("tm")
    cycle_index = lax.axis_index("tm")
    segment, before_same, after_same = frame_flags(
        clip_starts, cycle_index * frame_count, frame_count, frame_count * cycle_size
    )
    keep_mask = valid.astype(jnp.float32)
    keep_cube = keep_mask[:, None, None]
    own_factors = (
        before_same[1:-1].astype(jnp.float32),
        jnp.ones((frame_count,), jnp.float32),
        after_same[1:-1].astype(jnp.float32),
    )
    edge_factors = (
        before_same.astype(jnp.bfloat16),
        jnp.ones((frame_count + 2,), jnp.bfloat16),
        after_same.astype(jnp.bfloat16),
    )
    local_count = jnp.sum(keep_mask) * mel_count

    def spread(shard):
        padded = padded_2(shard, (("tm", 0),), 1)
        return lax.all_gather(padded, "chan", axis=2, tiled=True)

    def normalize(field_in, gain_vec, shift_vec):
        value_sums, squares, pixel_count = lax.psum(
            (
                jnp.sum(field_in * keep_cube, axis=(0, 1)),
                jnp.sum(field_in * field_in * keep_cube, axis=(0, 1)),
                local_count,
            ),
            "tm",
        )
        center = value_sums / pixel_count
        variance = squares / pixel_count - center * center
        inverse_std = lax.rsqrt(variance + EPS)
        normed = (field_in - center) * inverse_std
        return (gain_vec * normed + shift_vec, normed, inverse_std, pixel_count)

    def norm_back(grad_norm, normed, inverse_std, gain_vec, pixel_count):
        bias_grad, gain_grad = lax.psum(
            (jnp.sum(grad_norm, axis=(0, 1)), jnp.sum(grad_norm * normed, axis=(0, 1))), "tm"
        )
        grad_pre = (
            keep_cube
            * (gain_vec * inverse_std)
            * (grad_norm - bias_grad / pixel_count - normed * (gain_grad / pixel_count))
        )
        return (grad_pre.astype(jnp.bfloat16), gain_grad, bias_grad)

    def send_back(grad_pre, weight):
        padded = padded_2(grad_pre, (("tm", 0),), 1)
        partial_sum = conv_input_grad(padded, weight, edge_factors)
        return lax.psum_scatter(partial_sum, "chan", scatter_dimension=2, tiled=True)

    wide_in = spread(features * keep_cube.astype(jnp.bfloat16))
    first_pre = conv_forward(wide_in, conv1_weight, own_factors)
    first_norm, first_hat, first_scale, pixel_count = normalize(first_pre, norm1_gain, norm1_bias)
    first_act, first_pull = jax.vjp(smooth, first_norm)
    hidden = (first_act * keep_cube).astype(jnp.bfloat16)
    wide_mid = spread(hidden)
    second_pre = conv_forward(wide_mid, conv2_weight, own_factors)
    second_norm, second_hat, second_scale, pixel_count = normalize(
        second_pre, norm2_gain, norm2_bias
    )
    second_act, second_pull = jax.vjp(smooth, second_norm)
    pooled = (second_act * keep_cube).reshape(frame_count // 2, 2, mel_count, -1).mean(axis=(1, 2))
    pooled_keep = keep_mask[0::2]
    pooled_segment = segment[0::2]
    segment_key = pooled_segment.astype(jnp.float32)
    row_order = jnp.arange(frame_count // 2)
    lower_runs = (
        (pooled_segment[:, None] == pooled_segment[None, :])
        & (row_order[:, None] >= row_order[None, :])
    ).astype(jnp.float32)
    exponent = jnp.exp(pooled)
    counts = jnp.dot(lower_runs, pooled_keep, precision=highest)
    totals = jnp.dot(lower_runs, pooled_keep[:, None] * pooled, precision=highest)
    expsums = jnp.dot(lower_runs, pooled_keep[:, None] * exponent, precision=highest)
    zero_row = jnp.zeros_like(totals[0])
    prior_runs = entering(
        (segment_key[-1], counts[-1], totals[-1], expsums[-1]),
        "tm",
        join_keyed,
        (jnp.float32(-1.0), jnp.float32(0.0), zero_row, zero_row),
        False,
    )
    joined = (segment_key == prior_runs[0]).astype(jnp.float32)
    counts = counts + joined * prior_runs[1]
    totals = totals + joined[:, None] * prior_runs[2]
    expsums = expsums + joined[:, None] * prior_runs[3]
    readout = totals / counts[:, None] + jnp.log(expsums)
    by_count = readout_grad / counts[:, None]
    by_expsum = readout_grad / expsums
    later_mean = lax.dot_general(lower_runs, by_count, (((0,), (0,)), ((), ())), precision=highest)
    later_soft = lax.dot_general(lower_runs, by_expsum, (((0,), (0,)), ((), ())), precision=highest)
    beyond = entering(
        (segment_key[0], later_mean[0], later_soft[0]),
        "tm",
        join_keyed,
        (jnp.float32(-1.0), zero_row, zero_row),
        True,
    )
    joined_back = (segment_key == beyond[0]).astype(jnp.float32)[:, None]
    later_mean = later_mean + joined_back * beyond[1]
    later_soft = later_soft + joined_back * beyond[2]
    pooled_grad = pooled_keep[:, None] * (later_mean + exponent * later_soft)
    spread_grad = jnp.broadcast_to(
        (pooled_grad / (2 * mel_count))[:, None, None, :],
        (frame_count // 2, 2, mel_count, pooled_grad.shape[1]),
    )
    act_grad = spread_grad.reshape(frame_count, mel_count, -1) * keep_cube
    second_grad_norm = second_pull(act_grad)[0]
    second_grad_pre, gain2_grad, bias2_grad = norm_back(
        second_grad_norm, second_hat, second_scale, norm2_gain, pixel_count
    )
    weight2_grad = conv_weight_grad(wide_mid, second_grad_pre, own_factors)
    weight2_grad = lax.psum(weight2_grad, "tm")
    hidden_grad = send_back(second_grad_pre, conv2_weight)
    first_grad_norm = first_pull(hidden_grad * keep_cube)[0]
    first_grad_pre, gain1_grad, bias1_grad = norm_back(
        first_grad_norm, first_hat, first_scale, norm1_gain, pixel_count
    )
    weight1_grad = conv_weight_grad(wide_in, first_grad_pre, own_factors)
    weight1_grad = lax.psum(weight1_grad, "tm")
    input_grad = send_back(first_grad_pre, conv1_weight) * keep_cube
    return (
        readout,
        input_grad,
        weight1_grad,
        gain1_grad,
        bias1_grad,
        weight2_grad,
        gain2_grad,
        bias2_grad,
    )


ABSENT = 1024.0
ROWS = 64
TILE = 8
NORMS = 4
LANES = 128


def whole_spec():
    return pl.BlockSpec(memory_space=pltpu.VMEM)


def place_spec():
    return pl.BlockSpec(memory_space=pl.ANY)


def far_spec():
    return pl.BlockSpec(memory_space=pltpu.HBM)


def call(body, operands, in_specs, outs, out_specs, scratch, flops, megabytes):
    return pl.pallas_call(
        body,
        out_shape=tuple(jax.ShapeDtypeStruct(s, d) for s, d in outs),
        in_specs=in_specs,
        out_specs=tuple(out_specs),
        scratch_shapes=scratch,
        compiler_params=pltpu.CompilerParams(vmem_limit_bytes=megabytes * 2**20),
        cost_estimate=pl.CostEstimate(flops=1000, bytes_accessed=1000, transcendentals=0),
    )(*operands)


def swap(shard, axis, bit):
    count = lax.axis_size(axis)
    return lax.ppermute(shard, axis, [(i, i ^ bit) for i in range(count)])


def gather_bits(places):
    bits = [1 << k for k in range(places.bit_length() - 1)]
    return bits[2:][::-1] + bits[:2] if len(bits) > 2 else bits


def swap_both(shard, first, first_bit, second, second_bit):
    rows, columns = lax.axis_size(first), lax.axis_size(second)
    pairs = [
        (i * columns + j, (i ^ first_bit) * columns + (j ^ second_bit))
        for i in range(rows)
        for j in range(columns)
    ]
    return lax.ppermute(shard, (first, second), pairs)


def same_clip(starts, at, shape, total):
    frame = lax.broadcasted_iota(jnp.int32, shape, 0) + at
    first, *others = clip_rows(starts)
    before = frame != first
    after = frame != total - 1
    for start in others:
        before = before & (frame != start)
        after = after & (frame != start - 1)
    return before, after


def clip_rows(table):
    return [table[k : k + 1].astype(jnp.int32) for k in range(NORMS, table.shape[0])]


def widen(mask, width):
    return jnp.concatenate([mask] * (width // mask.shape[1]), axis=1)


def fold(value):
    total = value[:TILE]
    for k in range(TILE, value.shape[0], TILE):
        total = total + value[k : k + TILE]
    return total


def column_sum(value):
    return jnp.sum(value, axis=0, keepdims=True)


def joined(lower, middle, upper, m, at, before, after):
    low = lower[m, pl.ds(at, ROWS + 2 * TILE)]
    high = upper[m, pl.ds(at, ROWS + 2 * TILE)]
    return (
        middle[m, pl.ds(at, ROWS)]
        + jnp.where(before, low[TILE - 1 : TILE - 1 + ROWS], 0.0)
        + jnp.where(after, high[TILE + 1 : TILE + 1 + ROWS], 0.0)
    )


def by_rows(total, body, init):
    return lax.fori_loop(
        0, total // ROWS, lambda i, c: body(pl.multiple_of(i * ROWS, ROWS), c), init
    )


def clear_edges(lower, upper, total):
    for m in range(lower.shape[0]):
        for ref in (lower, upper):
            ref[m, :TILE] = jnp.zeros((TILE, ref.shape[2]), f32)
            ref[m, TILE + total :] = jnp.zeros((TILE, ref.shape[2]), f32)


def moments(field, keep, count):
    first, second = column_sum(field[0]), column_sum(field[1])
    center = first / count
    return center, lax.rsqrt(second / count - center * center + EPS)


def phi_parts(value):
    return 0.5 * (1.0 + lax.erf(value * 0.7071067811865476))


def bell(value):
    return 0.3989422804014327 * jnp.exp(-0.5 * value * value)


def bring_kernel(weight_in, weight, sem):
    copy = pltpu.make_async_copy(weight_in, weight, sem)
    copy.start()
    copy.wait()


def bring(weight):
    return call(
        bring_kernel,
        (weight,),
        [place_spec()],
        [(weight.shape, bf16)],
        [whole_spec()],
        [pltpu.SemaphoreType.DMA],
        0,
        4,
    )[0]


def settle(blocks, field, keep):
    mel_count = field.shape[0]
    place = lax.axis_index("tm")
    frames, lanes = blocks[0].shape[2], blocks[0].shape[3]
    for i, block in enumerate(blocks):
        row, side = i // 2, i % 2
        to_columns = slice(row * lanes, (row + 1) * lanes)
        for k in range(block.shape[0]):
            to_rows = pl.ds(pl.multiple_of((place ^ (2 * k + side)) * frames, frames), frames)
            for m in range(mel_count):
                rows = block[k, m]
                if m == 0 and row == 0 and keep is not None:
                    keep[to_rows] = (rows.astype(f32) < ABSENT / 2).astype(f32)
                field[m, to_rows, to_columns] = jnp.where(
                    rows < ABSENT / 2, rows, jnp.zeros_like(rows)
                )


def products(field, weight, bits, targets, sources=None):
    mel_count, total, width = field.shape
    lanes = width // len(bits)
    groups = group_starts(bits, lanes)
    for m in range(mel_count):
        for a in range(3):
            target, at = targets[a]
            acc = None
            for b in range(3):
                if 0 <= m + b - 1 < mel_count:
                    wing = jnp.concatenate([weight[a, b, pl.ds(g, lanes)] for g in groups])
                    part = jnp.dot(field[m + b - 1], wing, preferred_element_type=f32)
                    acc = part if acc is None else acc + part
            if sources is not None:
                acc = acc + sources[a][m, at : at + total]
            target[m, at : at + total] = acc


def column_kernel(*refs):
    blocks, weight, (field, keep, lower, middle, upper) = refs[:4], refs[4], refs[5:]
    clear_edges(lower, upper, middle.shape[1])
    settle(blocks, field, keep)
    products(field, weight, (0, 2), ((lower, TILE), (middle, 0), (upper, TILE)))


def column_part(blocks, weight, total):
    _, mel_count, frames, lanes = blocks[0].shape
    out_width = weight.shape[3]
    padded = (mel_count, total + 2 * TILE, out_width)
    return call(
        column_kernel,
        (*blocks, weight),
        [whole_spec()] * 5,
        [
            ((mel_count, total, 2 * lanes), bf16),
            ((total, LANES), f32),
            (padded, f32),
            ((mel_count, total, out_width), f32),
            (padded, f32),
        ],
        [whole_spec()] * 5,
        [],
        0,
        8,
    )


def first_kernel(starts, *refs):
    blocks, (weight, scales, keep), sources = refs[:4], refs[4:7], refs[7:10]
    low, high, picked, field, middle, stats = refs[10:16]
    lower, upper = refs[16:]
    mel_count, total, _ = field.shape
    out_width = middle.shape[2]
    place = lax.axis_index("tm")
    clear_edges(lower, upper, total)
    settle(blocks, field, None)
    targets = ((lower, TILE), (middle, 0), (upper, TILE))
    products(field, weight, (1, 3), targets, sources)

    def combine(at, sums):
        before, after = same_clip(starts, at, (ROWS, out_width), total)
        mask = widen(keep[pl.ds(at, ROWS)], out_width)
        one, two, num = sums
        num = num + fold(mask)
        for m in range(mel_count):
            rows = joined(lower, middle, upper, m, at, before, after)
            middle[m, pl.ds(at, ROWS)] = rows
            kept = rows * mask
            one = one + fold(kept)
            two = two + fold(kept * rows)
        return one, two, num

    blank = jnp.zeros((TILE, out_width), f32)
    one, two, num = by_rows(total, combine, (blank, blank, blank))
    pixels = column_sum(num) * mel_count
    center, inverse = moments((one, two), keep, pixels)
    stats[0:1] = center
    stats[1:2] = inverse
    stats[2:3] = pixels
    scale = scales[0:1] * inverse
    offset = scales[1:2] - center * scale

    def activate(at, carry):
        mask = widen(keep[pl.ds(at, ROWS)], out_width)
        for m in range(mel_count):
            value = middle[m, pl.ds(at, ROWS)] * scale + offset
            rows = (value * phi_parts(value) * mask).astype(bf16)
            if m < mel_count // 2:
                low[m, pl.ds(at, ROWS)] = rows
            else:
                high[m - mel_count // 2, pl.ds(at, ROWS)] = rows
        return carry

    by_rows(total, activate, 0)
    reach = picked.shape[1]
    for m in range(picked.shape[0]):
        picked[m] = high[m, pl.ds(pl.multiple_of((place % 2) * reach, reach), reach)]


def first_block(blocks, weight, scales, keep, sources, starts, total):
    _, mel_count, frames, lanes = blocks[0].shape
    out_width = weight.shape[3]
    padded = (mel_count, total + 2 * TILE, out_width)
    half = (mel_count // 2, total, out_width)
    return call(
        first_kernel,
        (starts, *blocks, weight, scales, keep, *sources),
        [whole_spec()] + [whole_spec()] * 10,
        [
            (half, bf16),
            (half, bf16),
            ((mel_count // 2, total // 2, out_width), bf16),
            ((mel_count, total, 2 * lanes), bf16),
            ((mel_count, total, out_width), f32),
            ((TILE, out_width), f32),
        ],
        [whole_spec()] * 6,
        [pltpu.VMEM(padded, f32), pltpu.VMEM(padded, f32)],
        0,
        16,
    )


def slope_kernel(pre, stats, scales, keep, slope):
    mel_count, total, width = pre.shape
    center, inverse = stats[0:1], stats[1:2]
    scale = scales[0:1] * inverse
    offset = scales[1:2] - center * scale

    def rows(at, carry):
        mask = widen(keep[pl.ds(at, ROWS)], width)
        for m in range(mel_count):
            value = pre[m, pl.ds(at, ROWS)] * scale + offset
            slope[m, pl.ds(at, ROWS)] = mask * (phi_parts(value) + value * bell(value))
        return carry

    by_rows(total, rows, 0)


def first_slope(pre, stats, scales, keep):
    return call(
        slope_kernel,
        (pre, stats, scales, keep),
        [whole_spec()] * 4,
        [(pre.shape, f32)],
        [whole_spec()],
        [],
        2**28,
        6,
    )[0]


def group_sums(fields, weight, starts, targets, sources=None):
    mel_count, (_, total, width) = len(fields[0]), targets[1][0].shape
    for m in range(mel_count):
        for a in range(3):
            acc = None
            for mels, start in zip(fields, starts):
                for b in range(3):
                    if 0 <= m + b - 1 < mel_count:
                        part = jnp.dot(
                            mels[m + b - 1][...],
                            weight[a, b, pl.ds(start, width)],
                            preferred_element_type=f32,
                        )
                        acc = part if acc is None else acc + part
            if sources is not None:
                acc = acc + sources[a, m]
            target, at = targets[a]
            target[m, at : at + total] = acc


def join_halves(pair, joint, sems):
    side = lax.axis_index("tm") % 2
    half = pair[0].shape[1]
    copies = []
    for i, (part, begin) in enumerate(zip(pair, (side, 1 - side))):
        rows = pl.ds(pl.multiple_of(begin * half, half), half)
        copies.append(pltpu.make_async_copy(part, joint.at[:, rows], sems.at[i]))
        copies[-1].start()
    return copies


def group_starts(bits, width):
    column = lax.axis_index("chan")
    return [pl.multiple_of((column ^ bit) * width, width) for bit in bits]


def near_kernel(low, high, low_two, high_two, weight, sums):
    half, _, width = low.shape
    fields = [
        [a.at[k] for a in pair for k in range(half)] for pair in ((low, high), (low_two, high_two))
    ]
    targets = [(sums.at[a], 0) for a in range(3)]
    group_sums(fields, weight, group_starts((0, 1), width), targets)


def near_part(low, high, low_two, high_two, weight):
    half, total, width = low.shape
    return call(
        near_kernel,
        (low, high, low_two, high_two, weight),
        [whole_spec()] * 5,
        [((3, 2 * half, total, width), f32)],
        [whole_spec()],
        [],
        0,
        6,
    )[0]


def far_kernel(far, picked, rest, weight, near, sums, joint, sems):
    half, _, width = far.shape
    copies = join_halves((picked, rest), joint, sems)
    for copy in copies:
        copy.wait()
    fields = [[a.at[k] for a in (far, joint) for k in range(half)]]
    targets = [(sums.at[a], 0) for a in range(3)]
    group_sums(fields, weight, group_starts((2,), width), targets, near)


def far_part(far, picked, rest, weight, near):
    return call(
        far_kernel,
        (far, picked, rest, weight, near),
        [whole_spec()] * 5,
        [(near.shape, f32)],
        [whole_spec()],
        [pltpu.VMEM(far.shape, bf16), pltpu.SemaphoreType.DMA((2,))],
        0,
        8,
    )[0]


def run_sums(mask, plain, values):
    width = (plain + values)[0].shape[1]
    terms = list(plain)
    for value in values:
        for _ in range(3):
            term = value.astype(bf16)
            terms.append(term)
            value = value - term.astype(f32)
    out = jnp.dot(mask, jnp.concatenate(terms, axis=1), preferred_element_type=f32)
    parts = [out[:, k * width : (k + 1) * width] for k in range(len(terms))]
    results = parts[: len(plain)]
    for k in range(len(plain), len(parts), 3):
        results.append(parts[k] + (parts[k + 1] + parts[k + 2]))
    return results


def second_kernel(
    starts, sums, far_two, picked_two, rest_two, weight, keep, scales, *refs
):
    cotangents, (readout, grad, gain_grad, shift_grad) = refs[:-14], refs[-14:-10]
    middle, slope, lower, upper, joint, hold, wide, full, sems, joint_sems = refs[-10:]
    mel_count, total, width = middle.shape
    half = mel_count // 2
    place = lax.axis_index("tm")
    pooled_total = total // 2
    own = readout.shape[0]
    copies = []
    pieces = [(part, i) for part in cotangents for i in range(part.shape[0])]
    bits = gather_bits(len(pieces))
    for k, (part, i) in enumerate(pieces):
        source = place ^ sum(bit for j, bit in enumerate(bits) if k >> j & 1)
        copies.append(
            pltpu.make_async_copy(
                part.at[i],
                full.at[pl.ds(pl.multiple_of(source * own, own), own)],
                sems.at[k],
            )
        )
    for copy in copies:
        copy.start()

    halves = join_halves((picked_two, rest_two), joint, joint_sems)
    clear_edges(lower, upper, total)
    for copy in halves:
        copy.wait()
    fields = [[a.at[k] for a in (far_two, joint) for k in range(half)]]
    targets = ((lower, TILE), (middle, 0), (upper, TILE))
    group_sums(fields, weight, group_starts((3,), width), targets, sums)
    blank = jnp.zeros((TILE, width), f32)

    def combine(at, sums):
        before, after = same_clip(starts, at, (ROWS, width), total)
        mask = widen(keep[pl.ds(at, ROWS)], width)
        first, second, num = sums
        num = num + fold(mask)
        for m in range(mel_count):
            rows = joined(lower, middle, upper, m, at, before, after)
            middle[m, pl.ds(at, ROWS)] = rows
            kept = rows * mask
            first = first + fold(kept)
            second = second + fold(kept * rows)
        return first, second, num

    first, second, num = by_rows(total, combine, (blank, blank, blank))
    pixels = column_sum(num) * mel_count
    center, inverse = moments((first, second), keep, pixels)
    scale = scales[2:3] * inverse
    offset = scales[3:4] - center * scale

    def activate(at, carry):
        mask = widen(keep[pl.ds(at, ROWS)], width)
        pooled = jnp.zeros((ROWS, width), f32)
        for m in range(mel_count):
            value = middle[m, pl.ds(at, ROWS)] * scale + offset
            share = phi_parts(value)
            pooled = pooled + value * share
            slope[m, pl.ds(at, ROWS)] = mask * (share + value * bell(value))
        pooled = pooled * mask
        for c in range(width // LANES):
            hold[c, pl.ds(at, ROWS)] = pooled[:, c * LANES : (c + 1) * LANES]
        return carry

    by_rows(total, activate, 0)

    even = pl.ds(0, pooled_total, stride=2)
    odd = pl.ds(1, pooled_total, stride=2)
    pooled = jnp.concatenate(
        [hold[c, even] + hold[c, odd] for c in range(width // LANES)], axis=1
    ) * (0.5 / mel_count)
    present = widen(keep[even], width)
    square = (pooled_total, pooled_total)
    row = lax.broadcasted_iota(jnp.int32, square, 0)
    col = lax.broadcasted_iota(jnp.int32, square, 1)
    same = row >= col
    back = row <= col
    for start in clip_rows(starts)[1:]:
        start = start[:, :pooled_total]
        crossed = (2 * row < start) != (2 * col < start)
        same = same & ~crossed
        back = back & ~crossed
    ahead, behind = same.astype(f32).astype(bf16), back.astype(f32).astype(bf16)
    exponent = jnp.exp(pooled)
    counts, totals, sums = run_sums(
        ahead, (present.astype(bf16),), (present * pooled, present * exponent)
    )
    wide[...] = totals / counts + jnp.log(sums)
    readout[...] = wide[pl.ds(pl.multiple_of(place * own, own), own)]
    for copy in copies:
        copy.wait()
    cotangent = full[...]
    by_count, by_sum = run_sums(behind, (), (cotangent / counts, cotangent / sums))
    down = present * (by_count + exponent * by_sum) * (0.5 / mel_count)
    for c in range(width // LANES):
        hold[c, even] = down[:, c * LANES : (c + 1) * LANES]
        hold[c, odd] = down[:, c * LANES : (c + 1) * LANES]

    def slopes(at, sums):
        down_rows = jnp.concatenate(
            [hold[c, pl.ds(at, ROWS)] for c in range(width // LANES)], axis=1
        )
        plain, along = sums
        for m in range(mel_count):
            step = down_rows * slope[m, pl.ds(at, ROWS)]
            slope[m, pl.ds(at, ROWS)] = step
            plain = plain + fold(step)
            along = along + fold(step * ((middle[m, pl.ds(at, ROWS)] - center) * inverse))
        return plain, along

    plain, along = by_rows(total, slopes, (blank, blank))
    plain, along = column_sum(plain), column_sum(along)
    shift_grad[...] = plain
    gain_grad[...] = along
    plain, along = plain / pixels, along / pixels

    def finish(at, carry):
        mask = widen(keep[pl.ds(at, ROWS)], width)
        for m in range(mel_count):
            normed = (middle[m, pl.ds(at, ROWS)] - center) * inverse
            rows = slope[m, pl.ds(at, ROWS)] - plain - normed * along
            grad[m, pl.ds(at, ROWS)] = (mask * (scale * rows)).astype(bf16)
        return carry

    by_rows(total, finish, 0)


def second_block(sums, arrays, weight, keep, scales, starts, cotangents, own):
    _, mel_count, total, width = sums.shape
    padded = (mel_count, total + 2 * TILE, width)
    full = (mel_count, total, width)
    return call(
        second_kernel,
        (starts, sums, *arrays, weight, keep, scales, *cotangents),
        [whole_spec()] + [whole_spec()] * (len(arrays) + 4) + [place_spec()] * len(cotangents),
        [((own, width), f32), (full, bf16), ((1, width), f32), ((1, width), f32)],
        [whole_spec()] * 4,
        [
            pltpu.VMEM(full, f32),
            pltpu.VMEM(full, f32),
            pltpu.VMEM(padded, f32),
            pltpu.VMEM(padded, f32),
            pltpu.VMEM(arrays[0].shape, bf16),
            pltpu.VMEM((width // LANES, total, LANES), f32),
            pltpu.VMEM((total // 2, width), f32),
            pltpu.VMEM((total // 2, width), f32),
            pltpu.SemaphoreType.DMA((sum(part.shape[0] for part in cotangents),)),
            pltpu.SemaphoreType.DMA((2,)),
        ],
        0,
        20,
    )


def wings_kernel(weight, wings, sems):
    width = wings.shape[3]
    copies = []
    for i, start in enumerate(group_starts((2, 0), width)):
        for a in range(3):
            for b in range(3):
                copies.append(
                    pltpu.make_async_copy(
                        weight.at[a, b, pl.ds(start, width)], wings.at[i, 3 * a + b], sems.at[len(copies)]
                    )
                )
    for copy in copies:
        copy.start()
    for copy in copies:
        copy.wait()


def bring_wings(weight):
    width = weight.shape[3]
    return call(
        wings_kernel,
        (weight,),
        [place_spec()],
        [((2, 9, width, width), bf16)],
        [whole_spec()],
        [pltpu.SemaphoreType.DMA((18,))],
        0,
        4,
    )[0]


def back_sums(field, wing, mels, reach, first, targets, sources=None):
    mel_count = field.shape[0]
    for k, n in enumerate(mels):
        for a in range(3):
            acc = None
            for b in range(3):
                if 0 <= n - b + 1 < mel_count:
                    part = lax.dot_general(
                        field[n - b + 1, pl.ds(first, reach)],
                        wing(a, b),
                        (((1,), (1,)), ((), ())),
                        preferred_element_type=f32,
                    )
                    acc = part if acc is None else acc + part
            if sources is not None:
                acc = sources[a, k] + acc
            target, at = targets[a]
            target[k, at : at + reach] = acc


def half_rows(total, reach):
    side = lax.axis_index("tm") % 2
    return (
        pl.multiple_of(side * (total - reach), 16),
        pl.multiple_of(side * (reach - total // 2), 16),
    )


def ahead_kernel(bit, mels, one, weight, sums):
    _, total, width = one.shape
    reach = sums.shape[2]
    first, _ = half_rows(total, reach)
    (start,) = group_starts((bit,), width)
    targets = [(sums.at[a], 0) for a in range(3)]
    back_sums(one, lambda a, b: weight[a, b, pl.ds(start, width)], mels, reach, first, targets)


def hidden_ahead(bit, mels, one, weight):
    _, total, width = one.shape
    return call(
        functools.partial(ahead_kernel, bit, mels),
        (one, weight),
        [whole_spec()] * 2,
        [((3, len(mels), total // 2 + 16, width), f32)],
        [whole_spec()],
        [],
        0,
        4,
    )[0]


def half_kernel(bit, mels, starts, two, wings, sums, out, lower, middle, upper):
    _, total, width = two.shape
    reach = sums.shape[2]
    first, skip = half_rows(total, reach)
    for k in range(len(mels)):
        for ref in (lower, upper):
            ref[k, :TILE] = jnp.zeros((TILE, width), f32)
            ref[k, TILE + reach :] = jnp.zeros((TILE, width), f32)
    wing = wings.at[0 if bit else 1]
    targets = ((upper, TILE), (middle, 0), (lower, TILE))
    back_sums(two, lambda a, b: wing[3 * a + b], mels, reach, first, targets, sums)

    def combine(at, carry):
        near = pl.multiple_of(at + skip, TILE)
        before, after = same_clip(starts, first + near, (ROWS, width), total)
        for k in range(len(mels)):
            rows = joined(lower, middle, upper, k, near, before, after)
            out[k, pl.ds(at, ROWS)] = rows.astype(out.dtype)
        return carry

    by_rows(total // 2, combine, 0)


def hidden_half(bit, mels, two, wings, sums, starts, kind):
    _, total, width = two.shape
    reach, count = sums.shape[2], len(mels)
    padded = (count, reach + 2 * TILE, width)
    return call(
        functools.partial(half_kernel, bit, mels),
        (starts, two, wings, sums),
        [whole_spec()] * 4,
        [((count, total // 2, width), kind)],
        [whole_spec()],
        [
            pltpu.VMEM(padded, f32),
            pltpu.VMEM((count, reach, width), f32),
            pltpu.VMEM(padded, f32),
        ],
        0,
        8,
    )[0]


def back_kernel(bit, mels, starts, one, two, weight, wings, out, lower, middle, upper):
    mel_count, total, width = one.shape
    (start,) = group_starts((bit,), width)
    wing = wings.at[0 if bit else 1]
    clear_edges(lower, upper, total)
    for k, n in enumerate(mels):
        for a, (target, at) in enumerate(((upper, TILE), (middle, 0), (lower, TILE))):
            acc = None
            for field, matrix in (
                (one, lambda b, a=a: weight[a, b, pl.ds(start, width)]),
                (two, lambda b, a=a: wing[3 * a + b]),
            ):
                for b in range(3):
                    if 0 <= n - b + 1 < mel_count:
                        part = lax.dot_general(
                            field[n - b + 1],
                            matrix(b),
                            (((1,), (1,)), ((), ())),
                            preferred_element_type=f32,
                        )
                        acc = part if acc is None else acc + part
            target[k, at : at + total] = acc

    def combine(at, carry):
        before, after = same_clip(starts, at, (ROWS, width), total)
        for k in range(len(mels)):
            rows = joined(lower, middle, upper, k, at, before, after)
            out[k, pl.ds(at, ROWS)] = rows.astype(out.dtype)
        return carry

    by_rows(total, combine, 0)


def hidden_back(bit, mels, one, two, weight, wings, starts, kind):
    _, total, width = one.shape
    count = len(mels)
    padded = (count, total + 2 * TILE, width)
    return call(
        functools.partial(back_kernel, bit, mels),
        (starts, one, two, weight, wings),
        [whole_spec()] * 5,
        [((count, total, width), kind)],
        [whole_spec()],
        [
            pltpu.VMEM(padded, f32),
            pltpu.VMEM((count, total, width), f32),
            pltpu.VMEM(padded, f32),
        ],
        0,
        14,
    )[0]


def norm_kernel(mine, low, picked, rest, slope, pre, stats, scales, keep, *refs):
    grad, window, gain_grad, shift_grad, padded = refs
    mel_count, total, width = mine.shape
    center, inverse, pixels = stats[0:1], stats[1:2], stats[2:3]
    blank = jnp.zeros((TILE, width), f32)
    edge = (padded.shape[1] - total) // 2
    reach = window.shape[1]
    frames = reach - 2 * edge
    place = lax.axis_index("tm")

    half = mel_count // 2

    def add(field, base, mels):
        def slopes(at, sums):
            plain, along = sums
            place_rows = pl.ds(pl.multiple_of(base + at, ROWS), ROWS)
            for k, m in enumerate(mels):
                rows = mine[m, place_rows] + field[k, pl.ds(at, ROWS)].astype(f32)
                step = rows * slope[m, place_rows]
                mine[m, place_rows] = step
                plain = plain + fold(step)
                along = along + fold(step * ((pre[m, place_rows] - center) * inverse))
            return plain, along

        return slopes

    side = place % 2
    sums = by_rows(total, add(low, 0, range(half)), (blank, blank))
    upper = range(half, mel_count)
    parts = []
    for field, base in ((picked, side), (rest, 1 - side)):
        parts.append(by_rows(total // 2, add(field, base * (total // 2), upper), (blank, blank)))
    plain, along = [
        a + jnp.where(side == 0, b + c, c + b) for a, b, c in zip(sums, parts[0], parts[1])
    ]
    plain, along = column_sum(plain), column_sum(along)
    shift_grad[...] = plain
    gain_grad[...] = along
    plain, along = plain / pixels, along / pixels
    scale = scales[0:1] * inverse
    for m in range(mel_count):
        padded[m, :edge] = jnp.zeros((edge, width), bf16)
        padded[m, edge + total :] = jnp.zeros((edge, width), bf16)

    def finish(at, carry):
        mask = widen(keep[pl.ds(at, ROWS)], width)
        for m in range(mel_count):
            normed = (pre[m, pl.ds(at, ROWS)] - center) * inverse
            rows = mine[m, pl.ds(at, ROWS)] - plain - normed * along
            rows = (mask * (scale * rows)).astype(bf16)
            grad[m, pl.ds(at, ROWS)] = rows
            padded[m, pl.ds(pl.multiple_of(at + edge, 16), ROWS)] = rows
        return carry

    by_rows(total, finish, 0)
    for m in range(mel_count):
        window[m] = padded[m, pl.ds(pl.multiple_of(place * frames, frames), reach)]


def norm_back_first(mine, low, picked, rest, slope, pre, stats, scales, keep, frames):
    mel_count, total, width = mine.shape
    edge = 16
    return call(
        norm_kernel,
        (mine, low, picked, rest, slope, pre, stats, scales, keep),
        [whole_spec()] * 9,
        [
            ((mel_count, total, width), bf16),
            ((mel_count, frames + 2 * edge, width), bf16),
            ((1, width), f32),
            ((1, width), f32),
        ],
        [whole_spec()] * 4,
        [pltpu.VMEM((mel_count, total + 2 * edge, width), bf16)],
        2**28,
        12,
    )


def spread_kernel(starts, grad, steps, spaced):
    mel_count, total, width = grad.shape
    for m in range(mel_count):
        spaced[m, :TILE] = jnp.zeros((TILE, width), f32)
        spaced[m, TILE + total :] = jnp.zeros((TILE, width), f32)

    def expand(at, carry):
        for m in range(mel_count):
            rows = grad[m, pl.ds(at, ROWS)].astype(f32)
            spaced[m, pl.ds(pl.multiple_of(at + TILE, TILE), ROWS)] = rows
        return carry

    by_rows(total, expand, 0)

    def shift(at, carry):
        before, after = same_clip(starts, at, (ROWS, width), total)
        for m in range(mel_count):
            rows = spaced[m, pl.ds(at, ROWS + 2 * TILE)]
            ahead = jnp.where(after, rows[TILE + 1 : TILE + 1 + ROWS], 0.0)
            behind = jnp.where(before, rows[TILE - 1 : TILE - 1 + ROWS], 0.0)
            steps[0, m, pl.ds(at, ROWS)] = ahead.astype(bf16)
            steps[1, m, pl.ds(at, ROWS)] = behind.astype(bf16)
        return carry

    by_rows(total, shift, 0)


def spread(grad, starts):
    mel_count, total, width = grad.shape
    return call(
        spread_kernel,
        (starts, grad),
        [whole_spec()] * 2,
        [((2, mel_count, total, width), bf16)],
        [whole_spec()],
        [pltpu.VMEM((mel_count, total + 2 * TILE, width), f32)],
        0,
        6,
    )[0]


def weight_kernel(layout, halves, *refs):
    count = len(refs) - 7
    fields, grad, steps = list(refs[:count]), refs[count], refs[count + 1]
    out, results, joint, sems, move_sems = refs[count + 2 :]
    mel_count, total, out_width = grad.shape
    width = results.shape[2]
    side = lax.axis_index("tm") % 2
    column = lax.axis_index("chan")
    moves = []
    for i, pair in enumerate(halves):
        for index, begin in zip(pair, (side, 1 - side)):
            rows = pl.ds(pl.multiple_of(begin * (total // 2), total // 2), total // 2)
            moves.append(
                pltpu.make_async_copy(fields[index], joint.at[i, :, rows], move_sems.at[len(moves)])
            )
            moves[-1].start()
        fields.append(joint.at[i])
    copies = [[], []]
    for i, (places, pieces) in enumerate(layout):
        slot = i % 2
        for copy in copies[slot]:
            copy.wait()
        copies[slot] = []
        each = width // len(places)
        if any(piece[0] >= count for piece in pieces):
            while moves:
                moves.pop().wait()
        for a in range(3):
            for b in range(3):
                right = grad if a == 1 else steps.at[a // 2]
                acc = None
                for m in range(mel_count):
                    if 0 <= m + b - 1 < mel_count:
                        index, k, lane = pieces[m + b - 1]
                        part = lax.dot_general(
                            fields[index][k, :, lane : lane + width],
                            right[m],
                            (((0,), (0,)), ((), ())),
                            preferred_element_type=f32,
                        )
                        acc = part if acc is None else acc + part
                tap = 3 * a + b
                results[slot, tap] = acc
                for j, bit in enumerate(places):
                    start = pl.multiple_of((column ^ bit) * each, each)
                    copies[slot].append(
                        pltpu.make_async_copy(
                            results.at[slot, tap, j * each : (j + 1) * each],
                            out.at[tap, pl.ds(start, each)],
                            sems.at[slot, tap, j],
                        )
                    )
                    copies[slot][-1].start()
    for copy in copies[0] + copies[1]:
        copy.wait()


def weight_back(layout, halves, fields, grad, steps, in_width):
    mel_count, total, out_width = grad.shape
    width = in_width // len(layout)
    joint = (max(len(halves), 1), mel_count // 2, total, width)
    out = call(
        functools.partial(weight_kernel, layout, halves),
        (*fields, grad, steps),
        [whole_spec()] * (len(fields) + 2),
        [((9, in_width, out_width), f32)],
        [place_spec()],
        [
            pltpu.VMEM((2, 9, width, out_width), f32),
            pltpu.VMEM(joint, bf16),
            pltpu.SemaphoreType.DMA((2, 9, 2)),
            pltpu.SemaphoreType.DMA((max(2 * len(halves), 1),)),
        ],
        0,
        12,
    )[0]
    return out.reshape(3, 3, in_width, out_width)


def input_kernel(starts, one, two, weight, weight_two, mine, other, lower, middle, upper):
    mel_count, reach, width = one.shape
    frames, lanes = mine.shape[1], mine.shape[2]
    edge = (reach - frames) // 2
    total = frames * lax.axis_size("tm")
    place = lax.axis_index("tm")
    groups = group_starts((2, 0), lanes)
    for a in range(3):
        target, shift = ((upper, TILE), (middle, 0), (lower, TILE))[a]
        for b in (1, 0, 2):
            low, count = ((1, mel_count - 1), (0, mel_count), (0, mel_count - 1))[b]
            acc = None
            for field, matrix in ((one, weight), (two, weight_two)):
                rows = field[low : low + count].reshape(count * reach, width)
                wing = jnp.concatenate([matrix[a, b, pl.ds(g, lanes)] for g in groups])
                part = lax.dot_general(
                    rows, wing, (((1,), (1,)), ((), ())), preferred_element_type=f32
                )
                acc = part if acc is None else acc + part
            acc = acc.reshape(count, reach, 2 * lanes)
            for k in range(count):
                n = low + k + b - 1
                if b == 1:
                    target[n, shift : shift + reach] = acc[k]
                else:
                    target[n, shift : shift + reach] += acc[k]
    before, after = same_clip(starts, place * frames, (frames, 2 * lanes), total)
    for m in range(mel_count):
        low = lower[m, TILE + edge - 1 : TILE + edge - 1 + frames]
        high = upper[m, TILE + edge + 1 : TILE + edge + 1 + frames]
        rows = (
            middle[m, edge : edge + frames]
            + jnp.where(before, low, 0.0)
            + jnp.where(after, high, 0.0)
        )
        other[m] = rows[:, :lanes]
        mine[m] = rows[:, lanes:]


def input_back(one, two, weight, weight_two, starts, frames, lanes):
    mel_count, reach, width = one.shape
    shape = (mel_count, frames, lanes)
    return call(
        input_kernel,
        (starts, one, two, weight, weight_two),
        [whole_spec()] + [whole_spec()] * 4,
        [(shape, f32), (shape, f32)],
        [whole_spec()] * 2,
        [
            pltpu.VMEM((mel_count, reach + 2 * TILE, 2 * lanes), f32),
            pltpu.VMEM((mel_count, reach, 2 * lanes), f32),
            pltpu.VMEM((mel_count, reach + 2 * TILE, 2 * lanes), f32),
        ],
        0,
        10,
    )


def close_kernel(mine, other, keep, out):
    mel_count, frames, lanes = mine.shape
    begin = pl.multiple_of(lax.axis_index("tm") * frames, frames)
    mask = keep[pl.ds(begin, frames)]
    for m in range(mel_count):
        out[:, m, :] = (mine[m] + other[m]) * mask


def close(mine, other, keep):
    mel_count, frames, lanes = mine.shape
    return call(
        close_kernel,
        (mine, other, keep),
        [whole_spec()] * 3,
        [((frames, mel_count, lanes), f32)],
        [whole_spec()],
        [],
        0,
        4,
    )[0]


def whole_frames(
    features,
    conv1_weight,
    norm1_gain,
    norm1_bias,
    conv2_weight,
    norm2_gain,
    norm2_bias,
    clip_starts,
    valid,
    readout_grad,
):
    frames, mel_count, lanes = features.shape
    places = lax.axis_size("tm")
    total = frames * places
    conv1_weight = bring(conv1_weight)
    starts = jnp.broadcast_to(clip_starts.astype(f32)[:, None], clip_starts.shape + norm1_gain.shape)
    norms = jnp.stack([norm1_gain, norm1_bias, norm2_gain, norm2_bias])
    table = jnp.concatenate([norms, starts])

    marked = jnp.where(valid[:, None, None] > 0, features, jnp.asarray(ABSENT, bf16))
    own = jnp.transpose(marked, (1, 0, 2))
    pieces = [swap(own, "tm", 2 * k) for k in range(1, places // 2)]
    along = jnp.stack([own] + pieces)
    near = [
        along,
        swap(along, "tm", 1),
        swap(along, "chan", 2),
        swap_both(along, "tm", 1, "chan", 2),
    ]
    readout_grad, _ = lax.optimization_barrier((readout_grad, pieces[0]))
    bits = gather_bits(places)
    cotangents = [readout_grad[None]]
    cotangents.append(swap(cotangents[0], "tm", bits[0]))
    near[3], conv1_weight, table, cotangents = lax.optimization_barrier(
        (near[3], conv1_weight, table, cotangents)
    )
    others = [swap(block, "chan", 1) for block in near]
    column, keep, *sources = column_part(near, conv1_weight, total)
    column, others = lax.optimization_barrier((column, others))
    other_conv2 = swap(conv2_weight, "chan", 1)
    others, other_conv2 = lax.optimization_barrier((others, other_conv2))

    low, high, picked, other_column, pre, stats = first_block(
        others, conv1_weight, table, keep, sources, table, total
    )
    fields1 = (column, other_column)

    far_picked = swap(picked, "chan", 2)
    far = swap(low, "chan", 2)
    far_rest = swap(far_picked, "tm", 1)

    low_two, high_two = swap(low, "chan", 1), swap(high, "chan", 1)
    near = near_part(low, high, low_two, high_two, conv2_weight)
    far_picked, near, cotangents = lax.optimization_barrier((far_picked, near, cotangents))
    picked_two = swap(far_picked, "chan", 1)
    other_conv2, near = lax.optimization_barrier((other_conv2, near))
    wings = bring_wings(other_conv2)
    for bit in bits[1:-1]:
        cotangents.append(swap(jnp.concatenate(cotangents), "tm", bit))
    picked_two, pre, cotangents, wings = lax.optimization_barrier(
        (picked_two, pre, cotangents, wings)
    )
    cotangents.append(swap(jnp.concatenate(cotangents), "tm", bits[-1]))
    slope = first_slope(pre, stats, table, keep)
    far, far_rest, slope, cotangents = lax.optimization_barrier((far, far_rest, slope, cotangents))
    far_two, rest_two = swap(far, "chan", 1), swap(far_rest, "chan", 1)
    sums = far_part(far, far_picked, far_rest, conv2_weight, near)
    far_two, rest_two, sums = lax.optimization_barrier((far_two, rest_two, sums))

    readout, grad2, gain2_grad, shift2_grad = second_block(
        sums,
        (far_two, picked_two, rest_two),
        conv2_weight,
        keep,
        table,
        table,
        cotangents,
        readout_grad.shape[0],
    )
    grad2_near = swap(grad2, "chan", 1)
    steps2 = spread(grad2, table)
    ahead = hidden_ahead(2, (2, 3), grad2, conv2_weight)
    grad2_near, steps2, ahead = lax.optimization_barrier((grad2_near, steps2, ahead))
    away = hidden_half(2, (2, 3), grad2_near, wings, ahead, table, bf16)
    came_picked = swap(away, "chan", 2)
    back = functools.partial(
        hidden_back, one=grad2, two=grad2_near, weight=conv2_weight, starts=table
    )
    away_low = back(2, (0, 1), wings=wings, kind=bf16)
    came_low = swap(away_low, "chan", 2)

    away_low, wings = lax.optimization_barrier((away_low, wings))
    mine = back(0, (0, 1, 2, 3), wings=wings, kind=f32)
    came_picked, mine, conv1_weight = lax.optimization_barrier((came_picked, mine, conv1_weight))
    came_rest = swap(came_picked, "tm", 1)
    other_conv1 = swap(conv1_weight, "chan", 1)
    fields = (low, high, low_two, high_two)
    fields += (far, far_picked, far_rest, far_two, picked_two, rest_two)
    layout = [
        ((0,), [(0, 0, 0), (0, 1, 0), (1, 0, 0), (1, 1, 0)]),
        ((1,), [(2, 0, 0), (2, 1, 0), (3, 0, 0), (3, 1, 0)]),
        ((2,), [(4, 0, 0), (4, 1, 0), (10, 0, 0), (10, 1, 0)]),
        ((3,), [(7, 0, 0), (7, 1, 0), (11, 0, 0), (11, 1, 0)]),
    ]
    weight2_grad = weight_back(
        layout, ((5, 6), (8, 9)), fields, grad2, steps2, conv2_weight.shape[2]
    )
    came_low, came_rest, mine, weight2_grad, other_conv1 = lax.optimization_barrier(
        (came_low, came_rest, mine, weight2_grad, other_conv1)
    )

    grad1, window, gain1_grad, shift1_grad = norm_back_first(
        mine, came_low, came_picked, came_rest, slope, pre, stats, table, keep, frames
    )
    window_near = swap(window, "chan", 1)
    steps1 = spread(grad1, table)
    window_near, steps1 = lax.optimization_barrier((window_near, steps1))
    input_mine, input_away = input_back(
        window, window_near, conv1_weight, other_conv1, table, frames, lanes
    )
    input_came = swap(input_away, "chan", 2)
    layout = [(bits, [(i, m, 0) for m in range(mel_count)]) for i, bits in enumerate(((0, 2), (1, 3)))]
    weight1_grad = weight_back(layout, (), fields1, grad1, steps1, conv1_weight.shape[2])
    input_came, weight1_grad = lax.optimization_barrier((input_came, weight1_grad))
    return (
        readout,
        close(input_mine, input_came, keep),
        weight1_grad,
        gain1_grad[0],
        shift1_grad[0],
        weight2_grad,
        gain2_grad[0],
        shift2_grad[0],
    )


def fits_whole(frames, mels, places, columns, widths):
    return (
        places > 1
        and places & (places - 1) == 0
        and columns == 4
        and frames % ROWS == 0
        and frames * places <= 512
        and mels == 4
        and all(w % (columns * LANES) == 0 for w in widths)
        and widths[1] == columns * 256
    )


def shards(*arrays):
    features, conv1_weight, conv2_weight = arrays[0], arrays[1], arrays[4]
    if fits_whole(
        features.shape[0],
        features.shape[1],
        lax.axis_size("tm"),
        lax.axis_size("chan"),
        (conv1_weight.shape[2], conv2_weight.shape[2]),
    ):
        return whole_frames(*arrays)
    return split_frames(*arrays)


def solution(mesh):
    return jax.shard_map(
        shards,
        mesh=mesh,
        in_specs=(
            P("tm", None, "chan"),
            P(None, None, None, "chan"),
            P("chan"),
            P("chan"),
            P(None, None, None, "chan"),
            P("chan"),
            P("chan"),
            P(),
            P("tm"),
            P("tm", "chan"),
        ),
        out_specs=(
            P("tm", "chan"),
            P("tm", None, "chan"),
            P(None, None, None, "chan"),
            P("chan"),
            P("chan"),
            P(None, None, None, "chan"),
            P("chan"),
            P("chan"),
        ),
        check_vma=False,
    )
```

```python
import functools

import jax
import jax.numpy as jnp
from jax import lax
from jax.experimental import pallas as pl
from jax.experimental.pallas import tpu as pltpu
from jax.sharding import PartitionSpec as P

EPS = 1e-05
highest = lax.Precision.HIGHEST
f32 = jnp.float32
bf16 = jnp.bfloat16


def padded_2(shard, sides, width):
    for axis, dim in sides:
        count, length = (lax.axis_size(axis), shard.shape[dim])
        up = [(i, (i + 1) % count) for i in range(count - 1)]
        down = [(j, i) for i, j in up]
        last = lax.slice_in_dim(shard, length - width, length, axis=dim)
        leading = lax.slice_in_dim(shard, 0, width, axis=dim)
        before = lax.ppermute(last, axis, up)
        after = lax.ppermute(leading, axis, down)
        shard = jnp.concatenate([before, shard, after], axis=dim)
    return shard


def entering(part, axis, combine, identity, reverse):
    count = lax.axis_size(axis)
    place = lax.axis_index(axis)
    ahead = count - 1 - place if reverse else place
    gathered = jax.tree.map(lambda a: lax.all_gather(a, axis), part)
    state = jax.tree.map(lambda a, e: jnp.zeros_like(a) + jnp.asarray(e, a.dtype), part, identity)

    def one(step, state):
        source = count - 1 - step if reverse else step
        return combine(
            state, jax.tree.map(lambda a: lax.dynamic_index_in_dim(a, source, 0, False), gathered)
        )

    return lax.fori_loop(0, ahead, one, state)


def frame_flags(clip_starts, first_frame, frame_count, frame_total):
    position = first_frame - 2 + jnp.arange(frame_count + 4, dtype=jnp.int32)
    segment = jnp.sum((clip_starts[None, :] <= position[:, None]).astype(jnp.int32), axis=1) - 1
    inside = (position >= 0) & (position < frame_total)
    middle = segment[1:-1]
    before_same = inside[1:-1] & inside[:-2] & (middle == segment[:-2])
    after_same = inside[1:-1] & inside[2:] & (middle == segment[2:])
    return (segment[2:-2], before_same, after_same)


def conv_forward(padded, weight, factors):
    frame_count = padded.shape[0] - 2
    mel_count = padded.shape[1]
    wide_field = jnp.pad(padded, ((0, 0), (1, 1), (0, 0)))
    result = jnp.zeros((frame_count, mel_count, weight.shape[3]), jnp.float32)
    for tap_row in range(3):
        partial_value = jnp.zeros((frame_count * mel_count, weight.shape[3]), jnp.float32)
        for tap_col in range(3):
            window = wide_field[
                tap_row : tap_row + frame_count, tap_col : tap_col + mel_count, :
            ].reshape(frame_count * mel_count, -1)
            partial_value = partial_value + jnp.dot(
                window, weight[tap_row, tap_col], preferred_element_type=jnp.float32
            )
        result = (
            result
            + partial_value.reshape(frame_count, mel_count, -1) * factors[tap_row][:, None, None]
        )
    return result


def conv_weight_grad(padded, grad_out, factors):
    frame_count = grad_out.shape[0]
    mel_count = grad_out.shape[1]
    wide_field = jnp.pad(padded, ((0, 0), (1, 1), (0, 0)))
    rows_out = []
    for tap_row in range(3):
        scaled = (grad_out * factors[tap_row][:, None, None].astype(jnp.bfloat16)).reshape(
            frame_count * mel_count, -1
        )
        taps_out = []
        for tap_col in range(3):
            window = wide_field[
                tap_row : tap_row + frame_count, tap_col : tap_col + mel_count, :
            ].reshape(frame_count * mel_count, -1)
            taps_out.append(
                lax.dot_general(
                    window, scaled, (((0,), (0,)), ((), ())), preferred_element_type=jnp.float32
                )
            )
        rows_out.append(jnp.stack(taps_out))
    return jnp.stack(rows_out)


def conv_input_grad(grad_padded, weight, edge_factors):
    frame_count = grad_padded.shape[0] - 2
    mel_count = grad_padded.shape[1]
    wide_field = jnp.pad(grad_padded, ((0, 0), (1, 1), (0, 0)))
    result = jnp.zeros((frame_count * mel_count, weight.shape[2]), jnp.float32)
    for tap_row in range(3):
        scaled = wide_field * edge_factors[tap_row][:, None, None]
        for tap_col in range(3):
            window = scaled[
                2 - tap_row : 2 - tap_row + frame_count, 2 - tap_col : 2 - tap_col + mel_count, :
            ].reshape(frame_count * mel_count, -1)
            result = result + lax.dot_general(
                window,
                weight[tap_row, tap_col],
                (((1,), (1,)), ((), ())),
                preferred_element_type=jnp.float32,
            )
    return result.reshape(frame_count, mel_count, -1)


def join_keyed(earlier_item, later_item):
    keep_first = later_item[0] < 0.0
    same_key = later_item[0] == earlier_item[0]
    merged = [jnp.where(keep_first, earlier_item[0], later_item[0])]
    for first_part, second_part in zip(earlier_item[1:], later_item[1:]):
        extra = (1,) * (first_part.ndim - keep_first.ndim)
        keep_wide = jnp.reshape(keep_first, keep_first.shape + extra)
        same_wide = jnp.reshape(same_key, same_key.shape + extra)
        merged.append(
            jnp.where(
                keep_wide, first_part, jnp.where(same_wide, first_part + second_part, second_part)
            )
        )
    return tuple(merged)


def smooth(argument):
    return jax.nn.gelu(argument, approximate=False)


def split_frames(
    features,
    conv1_weight,
    norm1_gain,
    norm1_bias,
    conv2_weight,
    norm2_gain,
    norm2_bias,
    clip_starts,
    valid,
    readout_grad,
):
    frame_count = features.shape[0]
    mel_count = features.shape[1]
    cycle_size = lax.axis_size("tm")
    cycle_index = lax.axis_index("tm")
    segment, before_same, after_same = frame_flags(
        clip_starts, cycle_index * frame_count, frame_count, frame_count * cycle_size
    )
    keep_mask = valid.astype(jnp.float32)
    keep_cube = keep_mask[:, None, None]
    own_factors = (
        before_same[1:-1].astype(jnp.float32),
        jnp.ones((frame_count,), jnp.float32),
        after_same[1:-1].astype(jnp.float32),
    )
    edge_factors = (
        before_same.astype(jnp.bfloat16),
        jnp.ones((frame_count + 2,), jnp.bfloat16),
        after_same.astype(jnp.bfloat16),
    )
    local_count = jnp.sum(keep_mask) * mel_count

    def spread(shard):
        padded = padded_2(shard, (("tm", 0),), 1)
        return lax.all_gather(padded, "chan", axis=2, tiled=True)

    def normalize(field_in, gain_vec, shift_vec):
        value_sums, squares, pixel_count = lax.psum(
            (
                jnp.sum(field_in * keep_cube, axis=(0, 1)),
                jnp.sum(field_in * field_in * keep_cube, axis=(0, 1)),
                local_count,
            ),
            "tm",
        )
        center = value_sums / pixel_count
        variance = squares / pixel_count - center * center
        inverse_std = lax.rsqrt(variance + EPS)
        normed = (field_in - center) * inverse_std
        return (gain_vec * normed + shift_vec, normed, inverse_std, pixel_count)

    def norm_back(grad_norm, normed, inverse_std, gain_vec, pixel_count):
        bias_grad, gain_grad = lax.psum(
            (jnp.sum(grad_norm, axis=(0, 1)), jnp.sum(grad_norm * normed, axis=(0, 1))), "tm"
        )
        grad_pre = (
            keep_cube
            * (gain_vec * inverse_std)
            * (grad_norm - bias_grad / pixel_count - normed * (gain_grad / pixel_count))
        )
        return (grad_pre.astype(jnp.bfloat16), gain_grad, bias_grad)

    def send_back(grad_pre, weight):
        padded = padded_2(grad_pre, (("tm", 0),), 1)
        partial_sum = conv_input_grad(padded, weight, edge_factors)
        return lax.psum_scatter(partial_sum, "chan", scatter_dimension=2, tiled=True)

    wide_in = spread(features * keep_cube.astype(jnp.bfloat16))
    first_pre = conv_forward(wide_in, conv1_weight, own_factors)
    first_norm, first_hat, first_scale, pixel_count = normalize(first_pre, norm1_gain, norm1_bias)
    first_act, first_pull = jax.vjp(smooth, first_norm)
    hidden = (first_act * keep_cube).astype(jnp.bfloat16)
    wide_mid = spread(hidden)
    second_pre = conv_forward(wide_mid, conv2_weight, own_factors)
    second_norm, second_hat, second_scale, pixel_count = normalize(
        second_pre, norm2_gain, norm2_bias
    )
    second_act, second_pull = jax.vjp(smooth, second_norm)
    pooled = (second_act * keep_cube).reshape(frame_count // 2, 2, mel_count, -1).mean(axis=(1, 2))
    pooled_keep = keep_mask[0::2]
    pooled_segment = segment[0::2]
    segment_key = pooled_segment.astype(jnp.float32)
    row_order = jnp.arange(frame_count // 2)
    lower_runs = (
        (pooled_segment[:, None] == pooled_segment[None, :])
        & (row_order[:, None] >= row_order[None, :])
    ).astype(jnp.float32)
    exponent = jnp.exp(pooled)
    counts = jnp.dot(lower_runs, pooled_keep, precision=highest)
    totals = jnp.dot(lower_runs, pooled_keep[:, None] * pooled, precision=highest)
    expsums = jnp.dot(lower_runs, pooled_keep[:, None] * exponent, precision=highest)
    zero_row = jnp.zeros_like(totals[0])
    prior_runs = entering(
        (segment_key[-1], counts[-1], totals[-1], expsums[-1]),
        "tm",
        join_keyed,
        (jnp.float32(-1.0), jnp.float32(0.0), zero_row, zero_row),
        False,
    )
    joined = (segment_key == prior_runs[0]).astype(jnp.float32)
    counts = counts + joined * prior_runs[1]
    totals = totals + joined[:, None] * prior_runs[2]
    expsums = expsums + joined[:, None] * prior_runs[3]
    readout = totals / counts[:, None] + jnp.log(expsums)
    by_count = readout_grad / counts[:, None]
    by_expsum = readout_grad / expsums
    later_mean = lax.dot_general(lower_runs, by_count, (((0,), (0,)), ((), ())), precision=highest)
    later_soft = lax.dot_general(lower_runs, by_expsum, (((0,), (0,)), ((), ())), precision=highest)
    beyond = entering(
        (segment_key[0], later_mean[0], later_soft[0]),
        "tm",
        join_keyed,
        (jnp.float32(-1.0), zero_row, zero_row),
        True,
    )
    joined_back = (segment_key == beyond[0]).astype(jnp.float32)[:, None]
    later_mean = later_mean + joined_back * beyond[1]
    later_soft = later_soft + joined_back * beyond[2]
    pooled_grad = pooled_keep[:, None] * (later_mean + exponent * later_soft)
    spread_grad = jnp.broadcast_to(
        (pooled_grad / (2 * mel_count))[:, None, None, :],
        (frame_count // 2, 2, mel_count, pooled_grad.shape[1]),
    )
    act_grad = spread_grad.reshape(frame_count, mel_count, -1) * keep_cube
    second_grad_norm = second_pull(act_grad)[0]
    second_grad_pre, gain2_grad, bias2_grad = norm_back(
        second_grad_norm, second_hat, second_scale, norm2_gain, pixel_count
    )
    weight2_grad = conv_weight_grad(wide_mid, second_grad_pre, own_factors)
    weight2_grad = lax.psum(weight2_grad, "tm")
    hidden_grad = send_back(second_grad_pre, conv2_weight)
    first_grad_norm = first_pull(hidden_grad * keep_cube)[0]
    first_grad_pre, gain1_grad, bias1_grad = norm_back(
        first_grad_norm, first_hat, first_scale, norm1_gain, pixel_count
    )
    weight1_grad = conv_weight_grad(wide_in, first_grad_pre, own_factors)
    weight1_grad = lax.psum(weight1_grad, "tm")
    input_grad = send_back(first_grad_pre, conv1_weight) * keep_cube
    return (
        readout,
        input_grad,
        weight1_grad,
        gain1_grad,
        bias1_grad,
        weight2_grad,
        gain2_grad,
        bias2_grad,
    )


ABSENT = 1024.0
ROWS = 64
TILE = 8
NORMS = 4
LANES = 128


def whole_spec():
    return pl.BlockSpec(memory_space=pltpu.VMEM)


def place_spec():
    return pl.BlockSpec(memory_space=pl.ANY)


def far_spec():
    return pl.BlockSpec(memory_space=pltpu.HBM)


def call(body, operands, in_specs, outs, out_specs, scratch, flops, megabytes):
    return pl.pallas_call(
        body,
        out_shape=tuple(jax.ShapeDtypeStruct(s, d) for s, d in outs),
        in_specs=in_specs,
        out_specs=tuple(out_specs),
        scratch_shapes=scratch,
        compiler_params=pltpu.CompilerParams(vmem_limit_bytes=megabytes * 2**20),
        cost_estimate=pl.CostEstimate(flops=1000, bytes_accessed=1000, transcendentals=0),
    )(*operands)


def swap(shard, axis, bit):
    count = lax.axis_size(axis)
    return lax.ppermute(shard, axis, [(i, i ^ bit) for i in range(count)])


def gather_bits(places):
    bits = [1 << k for k in range(places.bit_length() - 1)]
    return bits[2:][::-1] + bits[:2] if len(bits) > 2 else bits


def swap_both(shard, first, first_bit, second, second_bit):
    rows, columns = lax.axis_size(first), lax.axis_size(second)
    pairs = [
        (i * columns + j, (i ^ first_bit) * columns + (j ^ second_bit))
        for i in range(rows)
        for j in range(columns)
    ]
    return lax.ppermute(shard, (first, second), pairs)


def same_clip(starts, at, shape, total):
    frame = lax.broadcasted_iota(jnp.int32, shape, 0) + at
    first, *others = clip_rows(starts)
    before = frame != first
    after = frame != total - 1
    for start in others:
        before = before & (frame != start)
        after = after & (frame != start - 1)
    return before, after


def clip_rows(table):
    return [table[k : k + 1].astype(jnp.int32) for k in range(NORMS, table.shape[0])]


def widen(mask, width):
    return jnp.concatenate([mask] * (width // mask.shape[1]), axis=1)


def fold(value):
    total = value[:TILE]
    for k in range(TILE, value.shape[0], TILE):
        total = total + value[k : k + TILE]
    return total


def column_sum(value):
    return jnp.sum(value, axis=0, keepdims=True)


def joined(lower, middle, upper, m, at, before, after):
    low = lower[m, pl.ds(at, ROWS + 2 * TILE)]
    high = upper[m, pl.ds(at, ROWS + 2 * TILE)]
    return (
        middle[m, pl.ds(at, ROWS)]
        + jnp.where(before, low[TILE - 1 : TILE - 1 + ROWS], 0.0)
        + jnp.where(after, high[TILE + 1 : TILE + 1 + ROWS], 0.0)
    )


def by_rows(total, body, init):
    return lax.fori_loop(
        0, total // ROWS, lambda i, c: body(pl.multiple_of(i * ROWS, ROWS), c), init
    )


def clear_edges(lower, upper, total):
    for m in range(lower.shape[0]):
        for ref in (lower, upper):
            ref[m, :TILE] = jnp.zeros((TILE, ref.shape[2]), f32)
            ref[m, TILE + total :] = jnp.zeros((TILE, ref.shape[2]), f32)


def moments(field, keep, count):
    first, second = column_sum(field[0]), column_sum(field[1])
    center = first / count
    return center, lax.rsqrt(second / count - center * center + EPS)


def phi_parts(value):
    return 0.5 * (1.0 + lax.erf(value * 0.7071067811865476))


def bell(value):
    return 0.3989422804014327 * jnp.exp(-0.5 * value * value)


def bring_kernel(weight_in, weight, sem):
    copy = pltpu.make_async_copy(weight_in, weight, sem)
    copy.start()
    copy.wait()


def bring(weight):
    return call(
        bring_kernel,
        (weight,),
        [place_spec()],
        [(weight.shape, bf16)],
        [whole_spec()],
        [pltpu.SemaphoreType.DMA],
        0,
        4,
    )[0]


def settle(blocks, field, keep):
    mel_count = field.shape[0]
    place = lax.axis_index("tm")
    frames, lanes = blocks[0].shape[2], blocks[0].shape[3]
    for i, block in enumerate(blocks):
        row, side = i // 2, i % 2
        to_columns = slice(row * lanes, (row + 1) * lanes)
        for k in range(block.shape[0]):
            to_rows = pl.ds(pl.multiple_of((place ^ (2 * k + side)) * frames, frames), frames)
            for m in range(mel_count):
                rows = block[k, m]
                if m == 0 and row == 0 and keep is not None:
                    keep[to_rows] = (rows.astype(f32) < ABSENT / 2).astype(f32)
                field[m, to_rows, to_columns] = jnp.where(
                    rows < ABSENT / 2, rows, jnp.zeros_like(rows)
                )


def products(field, weight, bits, targets, sources=None):
    mel_count, total, width = field.shape
    lanes = width // len(bits)
    groups = group_starts(bits, lanes)
    for m in range(mel_count):
        for a in range(3):
            target, at = targets[a]
            acc = None
            for b in range(3):
                if 0 <= m + b - 1 < mel_count:
                    wing = jnp.concatenate([weight[a, b, pl.ds(g, lanes)] for g in groups])
                    part = jnp.dot(field[m + b - 1], wing, preferred_element_type=f32)
                    acc = part if acc is None else acc + part
            if sources is not None:
                acc = acc + sources[a][m, at : at + total]
            target[m, at : at + total] = acc


def column_kernel(*refs):
    blocks, weight, (field, keep, lower, middle, upper) = refs[:4], refs[4], refs[5:]
    clear_edges(lower, upper, middle.shape[1])
    settle(blocks, field, keep)
    products(field, weight, (0, 2), ((lower, TILE), (middle, 0), (upper, TILE)))


def column_part(blocks, weight, total):
    _, mel_count, frames, lanes = blocks[0].shape
    out_width = weight.shape[3]
    padded = (mel_count, total + 2 * TILE, out_width)
    return call(
        column_kernel,
        (*blocks, weight),
        [whole_spec()] * 5,
        [
            ((mel_count, total, 2 * lanes), bf16),
            ((total, LANES), f32),
            (padded, f32),
            ((mel_count, total, out_width), f32),
            (padded, f32),
        ],
        [whole_spec()] * 5,
        [],
        0,
        8,
    )


def first_kernel(starts, *refs):
    blocks, (weight, scales, keep), sources = refs[:4], refs[4:7], refs[7:10]
    low, high, picked, field, middle, stats = refs[10:16]
    lower, upper = refs[16:]
    mel_count, total, _ = field.shape
    out_width = middle.shape[2]
    place = lax.axis_index("tm")
    clear_edges(lower, upper, total)
    settle(blocks, field, None)
    targets = ((lower, TILE), (middle, 0), (upper, TILE))
    products(field, weight, (1, 3), targets, sources)

    def combine(at, sums):
        before, after = same_clip(starts, at, (ROWS, out_width), total)
        mask = widen(keep[pl.ds(at, ROWS)], out_width)
        one, two, num = sums
        num = num + fold(mask)
        for m in range(mel_count):
            rows = joined(lower, middle, upper, m, at, before, after)
            middle[m, pl.ds(at, ROWS)] = rows
            kept = rows * mask
            one = one + fold(kept)
            two = two + fold(kept * rows)
        return one, two, num

    blank = jnp.zeros((TILE, out_width), f32)
    one, two, num = by_rows(total, combine, (blank, blank, blank))
    pixels = column_sum(num) * mel_count
    center, inverse = moments((one, two), keep, pixels)
    stats[0:1] = center
    stats[1:2] = inverse
    stats[2:3] = pixels
    scale = scales[0:1] * inverse
    offset = scales[1:2] - center * scale

    def activate(at, carry):
        mask = widen(keep[pl.ds(at, ROWS)], out_width)
        for m in range(mel_count):
            value = middle[m, pl.ds(at, ROWS)] * scale + offset
            rows = (value * phi_parts(value) * mask).astype(bf16)
            if m < mel_count // 2:
                low[m, pl.ds(at, ROWS)] = rows
            else:
                high[m - mel_count // 2, pl.ds(at, ROWS)] = rows
        return carry

    by_rows(total, activate, 0)
    reach = picked.shape[1]
    for m in range(picked.shape[0]):
        picked[m] = high[m, pl.ds(pl.multiple_of((place % 2) * reach, reach), reach)]


def first_block(blocks, weight, scales, keep, sources, starts, total):
    _, mel_count, frames, lanes = blocks[0].shape
    out_width = weight.shape[3]
    padded = (mel_count, total + 2 * TILE, out_width)
    half = (mel_count // 2, total, out_width)
    return call(
        first_kernel,
        (starts, *blocks, weight, scales, keep, *sources),
        [whole_spec()] + [whole_spec()] * 10,
        [
            (half, bf16),
            (half, bf16),
            ((mel_count // 2, total // 2, out_width), bf16),
            ((mel_count, total, 2 * lanes), bf16),
            ((mel_count, total, out_width), f32),
            ((TILE, out_width), f32),
        ],
        [whole_spec()] * 6,
        [pltpu.VMEM(padded, f32), pltpu.VMEM(padded, f32)],
        0,
        16,
    )


def slope_kernel(pre, stats, scales, keep, slope):
    mel_count, total, width = pre.shape
    center, inverse = stats[0:1], stats[1:2]
    scale = scales[0:1] * inverse
    offset = scales[1:2] - center * scale

    def rows(at, carry):
        mask = widen(keep[pl.ds(at, ROWS)], width)
        for m in range(mel_count):
            value = pre[m, pl.ds(at, ROWS)] * scale + offset
            slope[m, pl.ds(at, ROWS)] = mask * (phi_parts(value) + value * bell(value))
        return carry

    by_rows(total, rows, 0)


def first_slope(pre, stats, scales, keep):
    return call(
        slope_kernel,
        (pre, stats, scales, keep),
        [whole_spec()] * 4,
        [(pre.shape, f32)],
        [whole_spec()],
        [],
        2**28,
        6,
    )[0]


def group_sums(fields, weight, starts, targets, sources=None):
    mel_count, (_, total, width) = len(fields[0]), targets[1][0].shape
    for m in range(mel_count):
        for a in range(3):
            acc = None
            for mels, start in zip(fields, starts):
                for b in range(3):
                    if 0 <= m + b - 1 < mel_count:
                        part = jnp.dot(
                            mels[m + b - 1][...],
                            weight[a, b, pl.ds(start, width)],
                            preferred_element_type=f32,
                        )
                        acc = part if acc is None else acc + part
            if sources is not None:
                acc = acc + sources[a, m]
            target, at = targets[a]
            target[m, at : at + total] = acc


def join_halves(pair, joint):
    side = lax.axis_index("tm") % 2
    half = pair[0].shape[1]
    for part, begin in zip(pair, (side, 1 - side)):
        joint[:, pl.ds(pl.multiple_of(begin * half, half), half)] = part[...]


def group_starts(bits, width):
    column = lax.axis_index("chan")
    return [pl.multiple_of((column ^ bit) * width, width) for bit in bits]


def near_kernel(low, high, low_two, high_two, weight, sums):
    half, _, width = low.shape
    fields = [
        [a.at[k] for a in pair for k in range(half)] for pair in ((low, high), (low_two, high_two))
    ]
    targets = [(sums.at[a], 0) for a in range(3)]
    group_sums(fields, weight, group_starts((0, 1), width), targets)


def near_part(low, high, low_two, high_two, weight):
    half, total, width = low.shape
    return call(
        near_kernel,
        (low, high, low_two, high_two, weight),
        [whole_spec()] * 5,
        [((3, 2 * half, total, width), f32)],
        [whole_spec()],
        [],
        0,
        6,
    )[0]


def far_kernel(far, picked, rest, weight, near, sums, joint):
    half, _, width = far.shape
    join_halves((picked, rest), joint)
    fields = [[a.at[k] for a in (far, joint) for k in range(half)]]
    targets = [(sums.at[a], 0) for a in range(3)]
    group_sums(fields, weight, group_starts((2,), width), targets, near)


def far_part(far, picked, rest, weight, near):
    return call(
        far_kernel,
        (far, picked, rest, weight, near),
        [whole_spec()] * 5,
        [(near.shape, f32)],
        [whole_spec()],
        [pltpu.VMEM(far.shape, bf16)],
        0,
        8,
    )[0]


def run_sums(mask, plain, values):
    width = (plain + values)[0].shape[1]
    terms = list(plain)
    for value in values:
        for _ in range(3):
            term = value.astype(bf16)
            terms.append(term)
            value = value - term.astype(f32)
    out = jnp.dot(mask, jnp.concatenate(terms, axis=1), preferred_element_type=f32)
    parts = [out[:, k * width : (k + 1) * width] for k in range(len(terms))]
    results = parts[: len(plain)]
    for k in range(len(plain), len(parts), 3):
        results.append(parts[k] + (parts[k + 1] + parts[k + 2]))
    return results


def second_kernel(
    starts, sums, far_two, picked_two, rest_two, weight, keep, scales, *refs
):
    cotangents, (readout, grad, gain_grad, shift_grad) = refs[:-13], refs[-13:-9]
    middle, slope, lower, upper, joint, hold, wide, full, sems = refs[-9:]
    mel_count, total, width = middle.shape
    half = mel_count // 2
    place = lax.axis_index("tm")
    pooled_total = total // 2
    own = readout.shape[0]
    copies = []
    pieces = [(part, i) for part in cotangents for i in range(part.shape[0])]
    bits = gather_bits(len(pieces))
    for k, (part, i) in enumerate(pieces):
        source = place ^ sum(bit for j, bit in enumerate(bits) if k >> j & 1)
        copies.append(
            pltpu.make_async_copy(
                part.at[i],
                full.at[pl.ds(pl.multiple_of(source * own, own), own)],
                sems.at[k],
            )
        )
    for copy in copies:
        copy.start()

    join_halves((picked_two, rest_two), joint)
    clear_edges(lower, upper, total)
    fields = [[a.at[k] for a in (far_two, joint) for k in range(half)]]
    targets = ((lower, TILE), (middle, 0), (upper, TILE))
    group_sums(fields, weight, group_starts((3,), width), targets, sums)
    blank = jnp.zeros((TILE, width), f32)

    def combine(at, sums):
        before, after = same_clip(starts, at, (ROWS, width), total)
        mask = widen(keep[pl.ds(at, ROWS)], width)
        first, second, num = sums
        num = num + fold(mask)
        for m in range(mel_count):
            rows = joined(lower, middle, upper, m, at, before, after)
            middle[m, pl.ds(at, ROWS)] = rows
            kept = rows * mask
            first = first + fold(kept)
            second = second + fold(kept * rows)
        return first, second, num

    first, second, num = by_rows(total, combine, (blank, blank, blank))
    pixels = column_sum(num) * mel_count
    center, inverse = moments((first, second), keep, pixels)
    scale = scales[2:3] * inverse
    offset = scales[3:4] - center * scale

    def activate(at, carry):
        mask = widen(keep[pl.ds(at, ROWS)], width)
        pooled = jnp.zeros((ROWS, width), f32)
        for m in range(mel_count):
            value = middle[m, pl.ds(at, ROWS)] * scale + offset
            share = phi_parts(value)
            pooled = pooled + value * share
            slope[m, pl.ds(at, ROWS)] = mask * (share + value * bell(value))
        pooled = pooled * mask
        for c in range(width // LANES):
            hold[c, pl.ds(at, ROWS)] = pooled[:, c * LANES : (c + 1) * LANES]
        return carry

    by_rows(total, activate, 0)

    even = pl.ds(0, pooled_total, stride=2)
    odd = pl.ds(1, pooled_total, stride=2)
    pooled = jnp.concatenate(
        [hold[c, even] + hold[c, odd] for c in range(width // LANES)], axis=1
    ) * (0.5 / mel_count)
    present = widen(keep[even], width)
    square = (pooled_total, pooled_total)
    row = lax.broadcasted_iota(jnp.int32, square, 0)
    col = lax.broadcasted_iota(jnp.int32, square, 1)
    same = row >= col
    back = row <= col
    for start in clip_rows(starts)[1:]:
        start = start[:, :pooled_total]
        crossed = (2 * row < start) != (2 * col < start)
        same = same & ~crossed
        back = back & ~crossed
    ahead, behind = same.astype(f32).astype(bf16), back.astype(f32).astype(bf16)
    exponent = jnp.exp(pooled)
    counts, totals, sums = run_sums(
        ahead, (present.astype(bf16),), (present * pooled, present * exponent)
    )
    wide[...] = totals / counts + jnp.log(sums)
    readout[...] = wide[pl.ds(pl.multiple_of(place * own, own), own)]
    for copy in copies:
        copy.wait()
    cotangent = full[...]
    by_count, by_sum = run_sums(behind, (), (cotangent / counts, cotangent / sums))
    down = present * (by_count + exponent * by_sum) * (0.5 / mel_count)
    for c in range(width // LANES):
        hold[c, even] = down[:, c * LANES : (c + 1) * LANES]
        hold[c, odd] = down[:, c * LANES : (c + 1) * LANES]

    def slopes(at, sums):
        down_rows = jnp.concatenate(
            [hold[c, pl.ds(at, ROWS)] for c in range(width // LANES)], axis=1
        )
        plain, along = sums
        for m in range(mel_count):
            step = down_rows * slope[m, pl.ds(at, ROWS)]
            slope[m, pl.ds(at, ROWS)] = step
            plain = plain + fold(step)
            along = along + fold(step * ((middle[m, pl.ds(at, ROWS)] - center) * inverse))
        return plain, along

    plain, along = by_rows(total, slopes, (blank, blank))
    plain, along = column_sum(plain), column_sum(along)
    shift_grad[...] = plain
    gain_grad[...] = along
    plain, along = plain / pixels, along / pixels

    def finish(at, carry):
        mask = widen(keep[pl.ds(at, ROWS)], width)
        for m in range(mel_count):
            normed = (middle[m, pl.ds(at, ROWS)] - center) * inverse
            rows = slope[m, pl.ds(at, ROWS)] - plain - normed * along
            grad[m, pl.ds(at, ROWS)] = (mask * (scale * rows)).astype(bf16)
        return carry

    by_rows(total, finish, 0)


def second_block(sums, arrays, weight, keep, scales, starts, cotangents, own):
    _, mel_count, total, width = sums.shape
    padded = (mel_count, total + 2 * TILE, width)
    full = (mel_count, total, width)
    return call(
        second_kernel,
        (starts, sums, *arrays, weight, keep, scales, *cotangents),
        [whole_spec()] + [whole_spec()] * (len(arrays) + 4) + [place_spec()] * len(cotangents),
        [((own, width), f32), (full, bf16), ((1, width), f32), ((1, width), f32)],
        [whole_spec()] * 4,
        [
            pltpu.VMEM(full, f32),
            pltpu.VMEM(full, f32),
            pltpu.VMEM(padded, f32),
            pltpu.VMEM(padded, f32),
            pltpu.VMEM(arrays[0].shape, bf16),
            pltpu.VMEM((width // LANES, total, LANES), f32),
            pltpu.VMEM((total // 2, width), f32),
            pltpu.VMEM((total // 2, width), f32),
            pltpu.SemaphoreType.DMA((sum(part.shape[0] for part in cotangents),)),
        ],
        0,
        20,
    )


def wings_kernel(weight, wings, sems):
    width = wings.shape[3]
    copies = []
    for i, start in enumerate(group_starts((2, 0), width)):
        for a in range(3):
            for b in range(3):
                copies.append(
                    pltpu.make_async_copy(
                        weight.at[a, b, pl.ds(start, width)], wings.at[i, 3 * a + b], sems.at[len(copies)]
                    )
                )
    for copy in copies:
        copy.start()
    for copy in copies:
        copy.wait()


def bring_wings(weight):
    width = weight.shape[3]
    return call(
        wings_kernel,
        (weight,),
        [place_spec()],
        [((2, 9, width, width), bf16)],
        [whole_spec()],
        [pltpu.SemaphoreType.DMA((18,))],
        0,
        4,
    )[0]


def back_sums(field, wing, mels, reach, first, targets, sources=None):
    mel_count = field.shape[0]
    for k, n in enumerate(mels):
        for a in range(3):
            acc = None
            for b in range(3):
                if 0 <= n - b + 1 < mel_count:
                    part = lax.dot_general(
                        field[n - b + 1, pl.ds(first, reach)],
                        wing(a, b),
                        (((1,), (1,)), ((), ())),
                        preferred_element_type=f32,
                    )
                    acc = part if acc is None else acc + part
            if sources is not None:
                acc = sources[a, k] + acc
            target, at = targets[a]
            target[k, at : at + reach] = acc


def half_rows(total, reach):
    side = lax.axis_index("tm") % 2
    return (
        pl.multiple_of(side * (total - reach), 16),
        pl.multiple_of(side * (reach - total // 2), 16),
    )


def ahead_kernel(bit, mels, one, weight, sums):
    _, total, width = one.shape
    reach = sums.shape[2]
    first, _ = half_rows(total, reach)
    (start,) = group_starts((bit,), width)
    targets = [(sums.at[a], 0) for a in range(3)]
    back_sums(one, lambda a, b: weight[a, b, pl.ds(start, width)], mels, reach, first, targets)


def hidden_ahead(bit, mels, one, weight):
    _, total, width = one.shape
    return call(
        functools.partial(ahead_kernel, bit, mels),
        (one, weight),
        [whole_spec()] * 2,
        [((3, len(mels), total // 2 + 16, width), f32)],
        [whole_spec()],
        [],
        0,
        4,
    )[0]


def half_kernel(bit, mels, starts, two, wings, sums, out, lower, middle, upper):
    _, total, width = two.shape
    reach = sums.shape[2]
    first, skip = half_rows(total, reach)
    for k in range(len(mels)):
        for ref in (lower, upper):
            ref[k, :TILE] = jnp.zeros((TILE, width), f32)
            ref[k, TILE + reach :] = jnp.zeros((TILE, width), f32)
    wing = wings.at[0 if bit else 1]
    targets = ((upper, TILE), (middle, 0), (lower, TILE))
    back_sums(two, lambda a, b: wing[3 * a + b], mels, reach, first, targets, sums)

    def combine(at, carry):
        near = pl.multiple_of(at + skip, TILE)
        before, after = same_clip(starts, first + near, (ROWS, width), total)
        for k in range(len(mels)):
            rows = joined(lower, middle, upper, k, near, before, after)
            out[k, pl.ds(at, ROWS)] = rows.astype(out.dtype)
        return carry

    by_rows(total // 2, combine, 0)


def hidden_half(bit, mels, two, wings, sums, starts, kind):
    _, total, width = two.shape
    reach, count = sums.shape[2], len(mels)
    padded = (count, reach + 2 * TILE, width)
    return call(
        functools.partial(half_kernel, bit, mels),
        (starts, two, wings, sums),
        [whole_spec()] * 4,
        [((count, total // 2, width), kind)],
        [whole_spec()],
        [
            pltpu.VMEM(padded, f32),
            pltpu.VMEM((count, reach, width), f32),
            pltpu.VMEM(padded, f32),
        ],
        0,
        8,
    )[0]


def back_kernel(bit, mels, starts, one, two, weight, wings, out, lower, middle, upper):
    mel_count, total, width = one.shape
    (start,) = group_starts((bit,), width)
    wing = wings.at[0 if bit else 1]
    clear_edges(lower, upper, total)
    for k, n in enumerate(mels):
        for a, (target, at) in enumerate(((upper, TILE), (middle, 0), (lower, TILE))):
            acc = None
            for field, matrix in (
                (one, lambda b, a=a: weight[a, b, pl.ds(start, width)]),
                (two, lambda b, a=a: wing[3 * a + b]),
            ):
                for b in range(3):
                    if 0 <= n - b + 1 < mel_count:
                        part = lax.dot_general(
                            field[n - b + 1],
                            matrix(b),
                            (((1,), (1,)), ((), ())),
                            preferred_element_type=f32,
                        )
                        acc = part if acc is None else acc + part
            target[k, at : at + total] = acc

    def combine(at, carry):
        before, after = same_clip(starts, at, (ROWS, width), total)
        for k in range(len(mels)):
            rows = joined(lower, middle, upper, k, at, before, after)
            out[k, pl.ds(at, ROWS)] = rows.astype(out.dtype)
        return carry

    by_rows(total, combine, 0)


def hidden_back(bit, mels, one, two, weight, wings, starts, kind):
    _, total, width = one.shape
    count = len(mels)
    padded = (count, total + 2 * TILE, width)
    return call(
        functools.partial(back_kernel, bit, mels),
        (starts, one, two, weight, wings),
        [whole_spec()] * 5,
        [((count, total, width), kind)],
        [whole_spec()],
        [
            pltpu.VMEM(padded, f32),
            pltpu.VMEM((count, total, width), f32),
            pltpu.VMEM(padded, f32),
        ],
        0,
        14,
    )[0]


def norm_kernel(mine, low, picked, rest, slope, pre, stats, scales, keep, *refs):
    grad, window, gain_grad, shift_grad, padded, held = refs
    mel_count, total, width = mine.shape
    center, inverse, pixels = stats[0:1], stats[1:2], stats[2:3]
    blank = jnp.zeros((TILE, width), f32)
    edge = (padded.shape[1] - total) // 2
    reach = window.shape[1]
    frames = reach - 2 * edge
    place = lax.axis_index("tm")

    half = mel_count // 2

    def add(field, base, mels):
        def slopes(at, sums):
            plain, along = sums
            place_rows = pl.ds(pl.multiple_of(base + at, ROWS), ROWS)
            for k, m in enumerate(mels):
                rows = mine[m, place_rows] + field[k, pl.ds(at, ROWS)].astype(f32)
                step = rows * slope[m, place_rows]
                held[m, place_rows] = step
                plain = plain + fold(step)
                along = along + fold(step * ((pre[m, place_rows] - center) * inverse))
            return plain, along

        return slopes

    side = place % 2
    sums = by_rows(total, add(low, 0, range(half)), (blank, blank))
    upper = range(half, mel_count)
    parts = []
    for field, base in ((picked, side), (rest, 1 - side)):
        parts.append(by_rows(total // 2, add(field, base * (total // 2), upper), (blank, blank)))
    plain, along = [
        a + jnp.where(side == 0, b + c, c + b) for a, b, c in zip(sums, parts[0], parts[1])
    ]
    plain, along = column_sum(plain), column_sum(along)
    shift_grad[...] = plain
    gain_grad[...] = along
    plain, along = plain / pixels, along / pixels
    scale = scales[0:1] * inverse
    for m in range(mel_count):
        padded[m, :edge] = jnp.zeros((edge, width), bf16)
        padded[m, edge + total :] = jnp.zeros((edge, width), bf16)

    def finish(at, carry):
        mask = widen(keep[pl.ds(at, ROWS)], width)
        for m in range(mel_count):
            normed = (pre[m, pl.ds(at, ROWS)] - center) * inverse
            rows = held[m, pl.ds(at, ROWS)] - plain - normed * along
            rows = (mask * (scale * rows)).astype(bf16)
            grad[m, pl.ds(at, ROWS)] = rows
            padded[m, pl.ds(pl.multiple_of(at + edge, 16), ROWS)] = rows
        return carry

    by_rows(total, finish, 0)
    for m in range(mel_count):
        window[m] = padded[m, pl.ds(pl.multiple_of(place * frames, frames), reach)]


def norm_back_first(mine, low, picked, rest, slope, pre, stats, scales, keep, frames):
    mel_count, total, width = mine.shape
    edge = 16
    return call(
        norm_kernel,
        (mine, low, picked, rest, slope, pre, stats, scales, keep),
        [whole_spec()] * 9,
        [
            ((mel_count, total, width), bf16),
            ((mel_count, frames + 2 * edge, width), bf16),
            ((1, width), f32),
            ((1, width), f32),
        ],
        [whole_spec()] * 4,
        [pltpu.VMEM((mel_count, total + 2 * edge, width), bf16), pltpu.VMEM(mine.shape, f32)],
        2**28,
        12,
    )


def spread_kernel(starts, grad, steps, spaced):
    mel_count, total, width = grad.shape
    for m in range(mel_count):
        spaced[m, :TILE] = jnp.zeros((TILE, width), f32)
        spaced[m, TILE + total :] = jnp.zeros((TILE, width), f32)

    def expand(at, carry):
        for m in range(mel_count):
            rows = grad[m, pl.ds(at, ROWS)].astype(f32)
            spaced[m, pl.ds(pl.multiple_of(at + TILE, TILE), ROWS)] = rows
        return carry

    by_rows(total, expand, 0)

    def shift(at, carry):
        before, after = same_clip(starts, at, (ROWS, width), total)
        for m in range(mel_count):
            rows = spaced[m, pl.ds(at, ROWS + 2 * TILE)]
            ahead = jnp.where(after, rows[TILE + 1 : TILE + 1 + ROWS], 0.0)
            behind = jnp.where(before, rows[TILE - 1 : TILE - 1 + ROWS], 0.0)
            steps[0, m, pl.ds(at, ROWS)] = ahead.astype(bf16)
            steps[1, m, pl.ds(at, ROWS)] = behind.astype(bf16)
        return carry

    by_rows(total, shift, 0)


def spread(grad, starts):
    mel_count, total, width = grad.shape
    return call(
        spread_kernel,
        (starts, grad),
        [whole_spec()] * 2,
        [((2, mel_count, total, width), bf16)],
        [whole_spec()],
        [pltpu.VMEM((mel_count, total + 2 * TILE, width), f32)],
        0,
        6,
    )[0]


def weight_kernel(layout, halves, *refs):
    count = len(refs) - 7
    fields, grad, steps = list(refs[:count]), refs[count], refs[count + 1]
    out, results, joint, sems, move_sems = refs[count + 2 :]
    mel_count, total, out_width = grad.shape
    width = results.shape[2]
    side = lax.axis_index("tm") % 2
    column = lax.axis_index("chan")
    moves = []
    for i, pair in enumerate(halves):
        for index, begin in zip(pair, (side, 1 - side)):
            rows = pl.ds(pl.multiple_of(begin * (total // 2), total // 2), total // 2)
            moves.append(
                pltpu.make_async_copy(fields[index], joint.at[i, :, rows], move_sems.at[len(moves)])
            )
            moves[-1].start()
        fields.append(joint.at[i])
    copies = [[], []]
    for i, (places, pieces) in enumerate(layout):
        slot = i % 2
        for copy in copies[slot]:
            copy.wait()
        copies[slot] = []
        each = width // len(places)
        if any(piece[0] >= count for piece in pieces):
            while moves:
                moves.pop().wait()
        for a in range(3):
            for b in range(3):
                right = grad if a == 1 else steps.at[a // 2]
                acc = None
                for m in range(mel_count):
                    if 0 <= m + b - 1 < mel_count:
                        index, k, lane = pieces[m + b - 1]
                        part = lax.dot_general(
                            fields[index][k, :, lane : lane + width],
                            right[m],
                            (((0,), (0,)), ((), ())),
                            preferred_element_type=f32,
                        )
                        acc = part if acc is None else acc + part
                tap = 3 * a + b
                results[slot, tap] = acc
                for j, bit in enumerate(places):
                    start = pl.multiple_of((column ^ bit) * each, each)
                    copies[slot].append(
                        pltpu.make_async_copy(
                            results.at[slot, tap, j * each : (j + 1) * each],
                            out.at[tap, pl.ds(start, each)],
                            sems.at[slot, tap, j],
                        )
                    )
                    copies[slot][-1].start()
    for copy in copies[0] + copies[1]:
        copy.wait()


def weight_back(layout, halves, fields, grad, steps, in_width):
    mel_count, total, out_width = grad.shape
    width = in_width // len(layout)
    joint = (max(len(halves), 1), mel_count // 2, total, width)
    out = call(
        functools.partial(weight_kernel, layout, halves),
        (*fields, grad, steps),
        [whole_spec()] * (len(fields) + 2),
        [((9, in_width, out_width), f32)],
        [place_spec()],
        [
            pltpu.VMEM((2, 9, width, out_width), f32),
            pltpu.VMEM(joint, bf16),
            pltpu.SemaphoreType.DMA((2, 9, 2)),
            pltpu.SemaphoreType.DMA((max(2 * len(halves), 1),)),
        ],
        0,
        12,
    )[0]
    return out.reshape(3, 3, in_width, out_width)


def input_kernel(starts, one, two, weight, weight_two, mine, other, lower, middle, upper):
    mel_count, reach, width = one.shape
    frames, lanes = mine.shape[1], mine.shape[2]
    edge = (reach - frames) // 2
    total = frames * lax.axis_size("tm")
    place = lax.axis_index("tm")
    groups = group_starts((2, 0), lanes)
    for a in range(3):
        target, shift = ((upper, TILE), (middle, 0), (lower, TILE))[a]
        for b in (1, 0, 2):
            low, count = ((1, mel_count - 1), (0, mel_count), (0, mel_count - 1))[b]
            acc = None
            for field, matrix in ((one, weight), (two, weight_two)):
                rows = field[low : low + count].reshape(count * reach, width)
                wing = jnp.concatenate([matrix[a, b, pl.ds(g, lanes)] for g in groups])
                part = lax.dot_general(
                    rows, wing, (((1,), (1,)), ((), ())), preferred_element_type=f32
                )
                acc = part if acc is None else acc + part
            acc = acc.reshape(count, reach, 2 * lanes)
            for k in range(count):
                n = low + k + b - 1
                if b == 1:
                    target[n, shift : shift + reach] = acc[k]
                else:
                    target[n, shift : shift + reach] += acc[k]
    before, after = same_clip(starts, place * frames, (frames, 2 * lanes), total)
    for m in range(mel_count):
        low = lower[m, TILE + edge - 1 : TILE + edge - 1 + frames]
        high = upper[m, TILE + edge + 1 : TILE + edge + 1 + frames]
        rows = (
            middle[m, edge : edge + frames]
            + jnp.where(before, low, 0.0)
            + jnp.where(after, high, 0.0)
        )
        other[m] = rows[:, :lanes]
        mine[m] = rows[:, lanes:]


def input_back(one, two, weight, weight_two, starts, frames, lanes):
    mel_count, reach, width = one.shape
    shape = (mel_count, frames, lanes)
    return call(
        input_kernel,
        (starts, one, two, weight, weight_two),
        [whole_spec()] + [whole_spec()] * 4,
        [(shape, f32), (shape, f32)],
        [whole_spec()] * 2,
        [
            pltpu.VMEM((mel_count, reach + 2 * TILE, 2 * lanes), f32),
            pltpu.VMEM((mel_count, reach, 2 * lanes), f32),
            pltpu.VMEM((mel_count, reach + 2 * TILE, 2 * lanes), f32),
        ],
        0,
        10,
    )


def close_kernel(mine, other, keep, *refs):
    count = len(refs) // 2
    small, out, small_out = refs[:count], refs[count], refs[count + 1 :]
    mel_count, frames, lanes = mine.shape
    begin = pl.multiple_of(lax.axis_index("tm") * frames, frames)
    mask = keep[pl.ds(begin, frames)]
    for m in range(mel_count):
        out[:, m, :] = (mine[m] + other[m]) * mask
    for source, target in zip(small, small_out):
        target[...] = source[...]


def close(mine, other, keep, small):
    mel_count, frames, lanes = mine.shape
    return call(
        close_kernel,
        (mine, other, keep, *small),
        [whole_spec()] * (3 + len(small)),
        [((frames, mel_count, lanes), f32)] + [(a.shape, f32) for a in small],
        [whole_spec()] * (1 + len(small)),
        [],
        0,
        4,
    )


def whole_frames(
    features,
    conv1_weight,
    norm1_gain,
    norm1_bias,
    conv2_weight,
    norm2_gain,
    norm2_bias,
    clip_starts,
    valid,
    readout_grad,
):
    frames, mel_count, lanes = features.shape
    places = lax.axis_size("tm")
    total = frames * places
    conv1_weight = bring(conv1_weight)
    starts = jnp.broadcast_to(clip_starts.astype(f32)[:, None], clip_starts.shape + norm1_gain.shape)
    norms = jnp.stack([norm1_gain, norm1_bias, norm2_gain, norm2_bias])
    table = jnp.concatenate([norms, starts])

    marked = jnp.where(valid[:, None, None] > 0, features, jnp.asarray(ABSENT, bf16))
    own = jnp.transpose(marked, (1, 0, 2))
    pieces = [swap(own, "tm", 2 * k) for k in range(1, places // 2)]
    along = jnp.stack([own] + pieces)
    near = [
        along,
        swap(along, "tm", 1),
        swap(along, "chan", 2),
        swap_both(along, "tm", 1, "chan", 2),
    ]
    readout_grad, _ = lax.optimization_barrier((readout_grad, pieces[0]))
    bits = gather_bits(places)
    cotangents = [readout_grad[None]]
    cotangents.append(swap(cotangents[0], "tm", bits[0]))
    near[3], conv1_weight, table, cotangents = lax.optimization_barrier(
        (near[3], conv1_weight, table, cotangents)
    )
    others = [swap(block, "chan", 1) for block in near]
    column, keep, *sources = column_part(near, conv1_weight, total)
    column, others = lax.optimization_barrier((column, others))
    other_conv2 = swap(conv2_weight, "chan", 1)
    others, other_conv2 = lax.optimization_barrier((others, other_conv2))

    low, high, picked, other_column, pre, stats = first_block(
        others, conv1_weight, table, keep, sources, table, total
    )
    fields1 = (column, other_column)

    far_picked = swap(picked, "chan", 2)
    far = swap(low, "chan", 2)
    far_rest = swap(far_picked, "tm", 1)

    low_two, high_two = swap(low, "chan", 1), swap(high, "chan", 1)
    near = near_part(low, high, low_two, high_two, conv2_weight)
    far_picked, near, cotangents = lax.optimization_barrier((far_picked, near, cotangents))
    picked_two = swap(far_picked, "chan", 1)
    other_conv2, near = lax.optimization_barrier((other_conv2, near))
    wings = bring_wings(other_conv2)
    for bit in bits[1:-1]:
        cotangents.append(swap(jnp.concatenate(cotangents), "tm", bit))
    picked_two, pre, cotangents, wings = lax.optimization_barrier(
        (picked_two, pre, cotangents, wings)
    )
    cotangents.append(swap(jnp.concatenate(cotangents), "tm", bits[-1]))
    slope = first_slope(pre, stats, table, keep)
    far, far_rest, slope, cotangents = lax.optimization_barrier((far, far_rest, slope, cotangents))
    far_two, rest_two = swap(far, "chan", 1), swap(far_rest, "chan", 1)
    sums = far_part(far, far_picked, far_rest, conv2_weight, near)
    far_two, rest_two, sums = lax.optimization_barrier((far_two, rest_two, sums))

    readout, grad2, gain2_grad, shift2_grad = second_block(
        sums,
        (far_two, picked_two, rest_two),
        conv2_weight,
        keep,
        table,
        table,
        cotangents,
        readout_grad.shape[0],
    )
    grad2_near = swap(grad2, "chan", 1)
    steps2 = spread(grad2, table)
    ahead = hidden_ahead(2, (2, 3), grad2, conv2_weight)
    grad2_near, steps2, ahead = lax.optimization_barrier((grad2_near, steps2, ahead))
    away = hidden_half(2, (2, 3), grad2_near, wings, ahead, table, bf16)
    came_picked = swap(away, "chan", 2)
    back = functools.partial(
        hidden_back, one=grad2, two=grad2_near, weight=conv2_weight, starts=table
    )
    away_low = back(2, (0, 1), wings=wings, kind=bf16)
    came_low = swap(away_low, "chan", 2)

    away_low, wings = lax.optimization_barrier((away_low, wings))
    mine = back(0, (0, 1, 2, 3), wings=wings, kind=f32)
    came_picked, mine, conv1_weight = lax.optimization_barrier((came_picked, mine, conv1_weight))
    came_rest = swap(came_picked, "tm", 1)
    other_conv1 = swap(conv1_weight, "chan", 1)
    fields = (low, high, low_two, high_two)
    fields += (far, far_picked, far_rest, far_two, picked_two, rest_two)
    layout = [
        ((0,), [(0, 0, 0), (0, 1, 0), (1, 0, 0), (1, 1, 0)]),
        ((1,), [(2, 0, 0), (2, 1, 0), (3, 0, 0), (3, 1, 0)]),
        ((2,), [(4, 0, 0), (4, 1, 0), (10, 0, 0), (10, 1, 0)]),
        ((3,), [(7, 0, 0), (7, 1, 0), (11, 0, 0), (11, 1, 0)]),
    ]
    weight2_grad = weight_back(
        layout, ((5, 6), (8, 9)), fields, grad2, steps2, conv2_weight.shape[2]
    )
    came_low, came_rest, mine, weight2_grad, other_conv1 = lax.optimization_barrier(
        (came_low, came_rest, mine, weight2_grad, other_conv1)
    )

    grad1, window, gain1_grad, shift1_grad = norm_back_first(
        mine, came_low, came_picked, came_rest, slope, pre, stats, table, keep, frames
    )
    window_near = swap(window, "chan", 1)
    steps1 = spread(grad1, table)
    window_near, steps1 = lax.optimization_barrier((window_near, steps1))
    input_mine, input_away = input_back(
        window, window_near, conv1_weight, other_conv1, table, frames, lanes
    )
    input_came = swap(input_away, "chan", 2)
    layout = [(bits, [(i, m, 0) for m in range(mel_count)]) for i, bits in enumerate(((0, 2), (1, 3)))]
    weight1_grad = weight_back(layout, (), fields1, grad1, steps1, conv1_weight.shape[2])
    input_came, weight1_grad = lax.optimization_barrier((input_came, weight1_grad))
    input_grad, readout, gain1_grad, shift1_grad, gain2_grad, shift2_grad = close(
        input_mine,
        input_came,
        keep,
        (readout, gain1_grad, shift1_grad, gain2_grad, shift2_grad),
    )
    return (
        readout,
        input_grad,
        weight1_grad,
        gain1_grad[0],
        shift1_grad[0],
        weight2_grad,
        gain2_grad[0],
        shift2_grad[0],
    )


def fits_whole(frames, mels, places, columns, widths):
    return (
        places > 1
        and places & (places - 1) == 0
        and columns == 4
        and frames % ROWS == 0
        and frames * places <= 512
        and mels == 4
        and all(w % (columns * LANES) == 0 for w in widths)
        and widths[1] == columns * 256
    )


def shards(*arrays):
    features, conv1_weight, conv2_weight = arrays[0], arrays[1], arrays[4]
    if fits_whole(
        features.shape[0],
        features.shape[1],
        lax.axis_size("tm"),
        lax.axis_size("chan"),
        (conv1_weight.shape[2], conv2_weight.shape[2]),
    ):
        return whole_frames(*arrays)
    return split_frames(*arrays)


def solution(mesh):
    return jax.shard_map(
        shards,
        mesh=mesh,
        in_specs=(
            P("tm", None, "chan"),
            P(None, None, None, "chan"),
            P("chan"),
            P("chan"),
            P(None, None, None, "chan"),
            P("chan"),
            P("chan"),
            P(),
            P("tm"),
            P("tm", "chan"),
        ),
        out_specs=(
            P("tm", "chan"),
            P("tm", None, "chan"),
            P(None, None, None, "chan"),
            P("chan"),
            P("chan"),
            P(None, None, None, "chan"),
            P("chan"),
            P("chan"),
        ),
        check_vma=False,
    )
```

```python
import functools

import jax
import jax.numpy as jnp
from jax import lax
from jax.experimental import pallas as pl
from jax.experimental.pallas import tpu as pltpu
from jax.sharding import PartitionSpec as P

EPS = 1e-05
highest = lax.Precision.HIGHEST
f32 = jnp.float32
bf16 = jnp.bfloat16


def padded_2(shard, sides, width):
    for axis, dim in sides:
        count, length = (lax.axis_size(axis), shard.shape[dim])
        up = [(i, (i + 1) % count) for i in range(count - 1)]
        down = [(j, i) for i, j in up]
        last = lax.slice_in_dim(shard, length - width, length, axis=dim)
        leading = lax.slice_in_dim(shard, 0, width, axis=dim)
        before = lax.ppermute(last, axis, up)
        after = lax.ppermute(leading, axis, down)
        shard = jnp.concatenate([before, shard, after], axis=dim)
    return shard


def entering(part, axis, combine, identity, reverse):
    count = lax.axis_size(axis)
    place = lax.axis_index(axis)
    ahead = count - 1 - place if reverse else place
    gathered = jax.tree.map(lambda a: lax.all_gather(a, axis), part)
    state = jax.tree.map(lambda a, e: jnp.zeros_like(a) + jnp.asarray(e, a.dtype), part, identity)

    def one(step, state):
        source = count - 1 - step if reverse else step
        return combine(
            state, jax.tree.map(lambda a: lax.dynamic_index_in_dim(a, source, 0, False), gathered)
        )

    return lax.fori_loop(0, ahead, one, state)


def frame_flags(clip_starts, first_frame, frame_count, frame_total):
    position = first_frame - 2 + jnp.arange(frame_count + 4, dtype=jnp.int32)
    segment = jnp.sum((clip_starts[None, :] <= position[:, None]).astype(jnp.int32), axis=1) - 1
    inside = (position >= 0) & (position < frame_total)
    middle = segment[1:-1]
    before_same = inside[1:-1] & inside[:-2] & (middle == segment[:-2])
    after_same = inside[1:-1] & inside[2:] & (middle == segment[2:])
    return (segment[2:-2], before_same, after_same)


def conv_forward(padded, weight, factors):
    frame_count = padded.shape[0] - 2
    mel_count = padded.shape[1]
    wide_field = jnp.pad(padded, ((0, 0), (1, 1), (0, 0)))
    result = jnp.zeros((frame_count, mel_count, weight.shape[3]), jnp.float32)
    for tap_row in range(3):
        partial_value = jnp.zeros((frame_count * mel_count, weight.shape[3]), jnp.float32)
        for tap_col in range(3):
            window = wide_field[
                tap_row : tap_row + frame_count, tap_col : tap_col + mel_count, :
            ].reshape(frame_count * mel_count, -1)
            partial_value = partial_value + jnp.dot(
                window, weight[tap_row, tap_col], preferred_element_type=jnp.float32
            )
        result = (
            result
            + partial_value.reshape(frame_count, mel_count, -1) * factors[tap_row][:, None, None]
        )
    return result


def conv_weight_grad(padded, grad_out, factors):
    frame_count = grad_out.shape[0]
    mel_count = grad_out.shape[1]
    wide_field = jnp.pad(padded, ((0, 0), (1, 1), (0, 0)))
    rows_out = []
    for tap_row in range(3):
        scaled = (grad_out * factors[tap_row][:, None, None].astype(jnp.bfloat16)).reshape(
            frame_count * mel_count, -1
        )
        taps_out = []
        for tap_col in range(3):
            window = wide_field[
                tap_row : tap_row + frame_count, tap_col : tap_col + mel_count, :
            ].reshape(frame_count * mel_count, -1)
            taps_out.append(
                lax.dot_general(
                    window, scaled, (((0,), (0,)), ((), ())), preferred_element_type=jnp.float32
                )
            )
        rows_out.append(jnp.stack(taps_out))
    return jnp.stack(rows_out)


def conv_input_grad(grad_padded, weight, edge_factors):
    frame_count = grad_padded.shape[0] - 2
    mel_count = grad_padded.shape[1]
    wide_field = jnp.pad(grad_padded, ((0, 0), (1, 1), (0, 0)))
    result = jnp.zeros((frame_count * mel_count, weight.shape[2]), jnp.float32)
    for tap_row in range(3):
        scaled = wide_field * edge_factors[tap_row][:, None, None]
        for tap_col in range(3):
            window = scaled[
                2 - tap_row : 2 - tap_row + frame_count, 2 - tap_col : 2 - tap_col + mel_count, :
            ].reshape(frame_count * mel_count, -1)
            result = result + lax.dot_general(
                window,
                weight[tap_row, tap_col],
                (((1,), (1,)), ((), ())),
                preferred_element_type=jnp.float32,
            )
    return result.reshape(frame_count, mel_count, -1)


def join_keyed(earlier_item, later_item):
    keep_first = later_item[0] < 0.0
    same_key = later_item[0] == earlier_item[0]
    merged = [jnp.where(keep_first, earlier_item[0], later_item[0])]
    for first_part, second_part in zip(earlier_item[1:], later_item[1:]):
        extra = (1,) * (first_part.ndim - keep_first.ndim)
        keep_wide = jnp.reshape(keep_first, keep_first.shape + extra)
        same_wide = jnp.reshape(same_key, same_key.shape + extra)
        merged.append(
            jnp.where(
                keep_wide, first_part, jnp.where(same_wide, first_part + second_part, second_part)
            )
        )
    return tuple(merged)


def smooth(argument):
    return jax.nn.gelu(argument, approximate=False)


def split_frames(
    features,
    conv1_weight,
    norm1_gain,
    norm1_bias,
    conv2_weight,
    norm2_gain,
    norm2_bias,
    clip_starts,
    valid,
    readout_grad,
):
    frame_count = features.shape[0]
    mel_count = features.shape[1]
    cycle_size = lax.axis_size("tm")
    cycle_index = lax.axis_index("tm")
    segment, before_same, after_same = frame_flags(
        clip_starts, cycle_index * frame_count, frame_count, frame_count * cycle_size
    )
    keep_mask = valid.astype(jnp.float32)
    keep_cube = keep_mask[:, None, None]
    own_factors = (
        before_same[1:-1].astype(jnp.float32),
        jnp.ones((frame_count,), jnp.float32),
        after_same[1:-1].astype(jnp.float32),
    )
    edge_factors = (
        before_same.astype(jnp.bfloat16),
        jnp.ones((frame_count + 2,), jnp.bfloat16),
        after_same.astype(jnp.bfloat16),
    )
    local_count = jnp.sum(keep_mask) * mel_count

    def spread(shard):
        padded = padded_2(shard, (("tm", 0),), 1)
        return lax.all_gather(padded, "chan", axis=2, tiled=True)

    def normalize(field_in, gain_vec, shift_vec):
        value_sums, squares, pixel_count = lax.psum(
            (
                jnp.sum(field_in * keep_cube, axis=(0, 1)),
                jnp.sum(field_in * field_in * keep_cube, axis=(0, 1)),
                local_count,
            ),
            "tm",
        )
        center = value_sums / pixel_count
        variance = squares / pixel_count - center * center
        inverse_std = lax.rsqrt(variance + EPS)
        normed = (field_in - center) * inverse_std
        return (gain_vec * normed + shift_vec, normed, inverse_std, pixel_count)

    def norm_back(grad_norm, normed, inverse_std, gain_vec, pixel_count):
        bias_grad, gain_grad = lax.psum(
            (jnp.sum(grad_norm, axis=(0, 1)), jnp.sum(grad_norm * normed, axis=(0, 1))), "tm"
        )
        grad_pre = (
            keep_cube
            * (gain_vec * inverse_std)
            * (grad_norm - bias_grad / pixel_count - normed * (gain_grad / pixel_count))
        )
        return (grad_pre.astype(jnp.bfloat16), gain_grad, bias_grad)

    def send_back(grad_pre, weight):
        padded = padded_2(grad_pre, (("tm", 0),), 1)
        partial_sum = conv_input_grad(padded, weight, edge_factors)
        return lax.psum_scatter(partial_sum, "chan", scatter_dimension=2, tiled=True)

    wide_in = spread(features * keep_cube.astype(jnp.bfloat16))
    first_pre = conv_forward(wide_in, conv1_weight, own_factors)
    first_norm, first_hat, first_scale, pixel_count = normalize(first_pre, norm1_gain, norm1_bias)
    first_act, first_pull = jax.vjp(smooth, first_norm)
    hidden = (first_act * keep_cube).astype(jnp.bfloat16)
    wide_mid = spread(hidden)
    second_pre = conv_forward(wide_mid, conv2_weight, own_factors)
    second_norm, second_hat, second_scale, pixel_count = normalize(
        second_pre, norm2_gain, norm2_bias
    )
    second_act, second_pull = jax.vjp(smooth, second_norm)
    pooled = (second_act * keep_cube).reshape(frame_count // 2, 2, mel_count, -1).mean(axis=(1, 2))
    pooled_keep = keep_mask[0::2]
    pooled_segment = segment[0::2]
    segment_key = pooled_segment.astype(jnp.float32)
    row_order = jnp.arange(frame_count // 2)
    lower_runs = (
        (pooled_segment[:, None] == pooled_segment[None, :])
        & (row_order[:, None] >= row_order[None, :])
    ).astype(jnp.float32)
    exponent = jnp.exp(pooled)
    counts = jnp.dot(lower_runs, pooled_keep, precision=highest)
    totals = jnp.dot(lower_runs, pooled_keep[:, None] * pooled, precision=highest)
    expsums = jnp.dot(lower_runs, pooled_keep[:, None] * exponent, precision=highest)
    zero_row = jnp.zeros_like(totals[0])
    prior_runs = entering(
        (segment_key[-1], counts[-1], totals[-1], expsums[-1]),
        "tm",
        join_keyed,
        (jnp.float32(-1.0), jnp.float32(0.0), zero_row, zero_row),
        False,
    )
    joined = (segment_key == prior_runs[0]).astype(jnp.float32)
    counts = counts + joined * prior_runs[1]
    totals = totals + joined[:, None] * prior_runs[2]
    expsums = expsums + joined[:, None] * prior_runs[3]
    readout = totals / counts[:, None] + jnp.log(expsums)
    by_count = readout_grad / counts[:, None]
    by_expsum = readout_grad / expsums
    later_mean = lax.dot_general(lower_runs, by_count, (((0,), (0,)), ((), ())), precision=highest)
    later_soft = lax.dot_general(lower_runs, by_expsum, (((0,), (0,)), ((), ())), precision=highest)
    beyond = entering(
        (segment_key[0], later_mean[0], later_soft[0]),
        "tm",
        join_keyed,
        (jnp.float32(-1.0), zero_row, zero_row),
        True,
    )
    joined_back = (segment_key == beyond[0]).astype(jnp.float32)[:, None]
    later_mean = later_mean + joined_back * beyond[1]
    later_soft = later_soft + joined_back * beyond[2]
    pooled_grad = pooled_keep[:, None] * (later_mean + exponent * later_soft)
    spread_grad = jnp.broadcast_to(
        (pooled_grad / (2 * mel_count))[:, None, None, :],
        (frame_count // 2, 2, mel_count, pooled_grad.shape[1]),
    )
    act_grad = spread_grad.reshape(frame_count, mel_count, -1) * keep_cube
    second_grad_norm = second_pull(act_grad)[0]
    second_grad_pre, gain2_grad, bias2_grad = norm_back(
        second_grad_norm, second_hat, second_scale, norm2_gain, pixel_count
    )
    weight2_grad = conv_weight_grad(wide_mid, second_grad_pre, own_factors)
    weight2_grad = lax.psum(weight2_grad, "tm")
    hidden_grad = send_back(second_grad_pre, conv2_weight)
    first_grad_norm = first_pull(hidden_grad * keep_cube)[0]
    first_grad_pre, gain1_grad, bias1_grad = norm_back(
        first_grad_norm, first_hat, first_scale, norm1_gain, pixel_count
    )
    weight1_grad = conv_weight_grad(wide_in, first_grad_pre, own_factors)
    weight1_grad = lax.psum(weight1_grad, "tm")
    input_grad = send_back(first_grad_pre, conv1_weight) * keep_cube
    return (
        readout,
        input_grad,
        weight1_grad,
        gain1_grad,
        bias1_grad,
        weight2_grad,
        gain2_grad,
        bias2_grad,
    )


ABSENT = 1024.0
ROWS = 64
TILE = 8
NORMS = 4
LANES = 128


def whole_spec():
    return pl.BlockSpec(memory_space=pltpu.VMEM)


def place_spec():
    return pl.BlockSpec(memory_space=pl.ANY)


def far_spec():
    return pl.BlockSpec(memory_space=pltpu.HBM)


def call(body, operands, in_specs, outs, out_specs, scratch, flops, megabytes):
    return pl.pallas_call(
        body,
        out_shape=tuple(jax.ShapeDtypeStruct(s, d) for s, d in outs),
        in_specs=in_specs,
        out_specs=tuple(out_specs),
        scratch_shapes=scratch,
        compiler_params=pltpu.CompilerParams(vmem_limit_bytes=megabytes * 2**20),
        cost_estimate=pl.CostEstimate(flops=1000, bytes_accessed=1000, transcendentals=0),
    )(*operands)


def swap(shard, axis, bit):
    count = lax.axis_size(axis)
    return lax.ppermute(shard, axis, [(i, i ^ bit) for i in range(count)])


def gather_bits(places):
    bits = [1 << k for k in range(places.bit_length() - 1)]
    return bits[2:][::-1] + bits[:2] if len(bits) > 2 else bits


def swap_both(shard, first, first_bit, second, second_bit):
    rows, columns = lax.axis_size(first), lax.axis_size(second)
    pairs = [
        (i * columns + j, (i ^ first_bit) * columns + (j ^ second_bit))
        for i in range(rows)
        for j in range(columns)
    ]
    return lax.ppermute(shard, (first, second), pairs)


def same_clip(starts, at, shape, total):
    frame = lax.broadcasted_iota(jnp.int32, shape, 0) + at
    first, *others = clip_rows(starts)
    before = frame != first
    after = frame != total - 1
    for start in others:
        before = before & (frame != start)
        after = after & (frame != start - 1)
    return before, after


def clip_rows(table):
    return [table[k : k + 1].astype(jnp.int32) for k in range(NORMS, table.shape[0])]


def widen(mask, width):
    return jnp.concatenate([mask] * (width // mask.shape[1]), axis=1)


def fold(value):
    total = value[:TILE]
    for k in range(TILE, value.shape[0], TILE):
        total = total + value[k : k + TILE]
    return total


def column_sum(value):
    return jnp.sum(value, axis=0, keepdims=True)


def joined(lower, middle, upper, m, at, before, after):
    low = lower[m, pl.ds(at, ROWS + 2 * TILE)]
    high = upper[m, pl.ds(at, ROWS + 2 * TILE)]
    return (
        middle[m, pl.ds(at, ROWS)]
        + jnp.where(before, low[TILE - 1 : TILE - 1 + ROWS], 0.0)
        + jnp.where(after, high[TILE + 1 : TILE + 1 + ROWS], 0.0)
    )


def by_rows(total, body, init):
    return lax.fori_loop(
        0, total // ROWS, lambda i, c: body(pl.multiple_of(i * ROWS, ROWS), c), init
    )


def clear_edges(lower, upper, total):
    for m in range(lower.shape[0]):
        for ref in (lower, upper):
            ref[m, :TILE] = jnp.zeros((TILE, ref.shape[2]), f32)
            ref[m, TILE + total :] = jnp.zeros((TILE, ref.shape[2]), f32)


def moments(field, keep, count):
    first, second = column_sum(field[0]), column_sum(field[1])
    center = first / count
    return center, lax.rsqrt(second / count - center * center + EPS)


def phi_parts(value):
    return 0.5 * (1.0 + lax.erf(value * 0.7071067811865476))


def bell(value):
    return 0.3989422804014327 * jnp.exp(-0.5 * value * value)


def bring_kernel(weight_in, weight, sem):
    copy = pltpu.make_async_copy(weight_in, weight, sem)
    copy.start()
    copy.wait()


def bring(weight):
    return call(
        bring_kernel,
        (weight,),
        [place_spec()],
        [(weight.shape, bf16)],
        [whole_spec()],
        [pltpu.SemaphoreType.DMA],
        0,
        4,
    )[0]


def settle(blocks, field, keep):
    mel_count = field.shape[0]
    place = lax.axis_index("tm")
    frames, lanes = blocks[0].shape[2], blocks[0].shape[3]
    for i, block in enumerate(blocks):
        row, side = i // 2, i % 2
        to_columns = slice(row * lanes, (row + 1) * lanes)
        for k in range(block.shape[0]):
            to_rows = pl.ds(pl.multiple_of((place ^ (2 * k + side)) * frames, frames), frames)
            for m in range(mel_count):
                rows = block[k, m]
                if m == 0 and row == 0 and keep is not None:
                    keep[to_rows] = (rows.astype(f32) < ABSENT / 2).astype(f32)
                field[m, to_rows, to_columns] = jnp.where(
                    rows < ABSENT / 2, rows, jnp.zeros_like(rows)
                )


def products(field, weight, bits, targets, sources=None):
    mel_count, total, width = field.shape
    lanes = width // len(bits)
    groups = group_starts(bits, lanes)
    for m in range(mel_count):
        for a in range(3):
            target, at = targets[a]
            acc = None
            for b in range(3):
                if 0 <= m + b - 1 < mel_count:
                    wing = jnp.concatenate([weight[a, b, pl.ds(g, lanes)] for g in groups])
                    part = jnp.dot(field[m + b - 1], wing, preferred_element_type=f32)
                    acc = part if acc is None else acc + part
            if sources is not None:
                acc = acc + sources[a][m, at : at + total]
            target[m, at : at + total] = acc


def column_kernel(*refs):
    blocks, weight, (field, keep, lower, middle, upper) = refs[:4], refs[4], refs[5:]
    clear_edges(lower, upper, middle.shape[1])
    settle(blocks, field, keep)
    products(field, weight, (0, 2), ((lower, TILE), (middle, 0), (upper, TILE)))


def column_part(blocks, weight, total):
    _, mel_count, frames, lanes = blocks[0].shape
    out_width = weight.shape[3]
    padded = (mel_count, total + 2 * TILE, out_width)
    return call(
        column_kernel,
        (*blocks, weight),
        [whole_spec()] * 5,
        [
            ((mel_count, total, 2 * lanes), bf16),
            ((total, LANES), f32),
            (padded, f32),
            ((mel_count, total, out_width), f32),
            (padded, f32),
        ],
        [whole_spec()] * 5,
        [],
        0,
        8,
    )


def first_kernel(starts, *refs):
    blocks, (weight, scales, keep), sources = refs[:4], refs[4:7], refs[7:10]
    low, high, picked, field, middle, stats = refs[10:16]
    lower, upper = refs[16:]
    mel_count, total, _ = field.shape
    out_width = middle.shape[2]
    place = lax.axis_index("tm")
    clear_edges(lower, upper, total)
    settle(blocks, field, None)
    targets = ((lower, TILE), (middle, 0), (upper, TILE))
    products(field, weight, (1, 3), targets, sources)

    def combine(at, sums):
        before, after = same_clip(starts, at, (ROWS, out_width), total)
        mask = widen(keep[pl.ds(at, ROWS)], out_width)
        one, two, num = sums
        num = num + fold(mask)
        for m in range(mel_count):
            rows = joined(lower, middle, upper, m, at, before, after)
            middle[m, pl.ds(at, ROWS)] = rows
            kept = rows * mask
            one = one + fold(kept)
            two = two + fold(kept * rows)
        return one, two, num

    blank = jnp.zeros((TILE, out_width), f32)
    one, two, num = by_rows(total, combine, (blank, blank, blank))
    pixels = column_sum(num) * mel_count
    center, inverse = moments((one, two), keep, pixels)
    stats[0:1] = center
    stats[1:2] = inverse
    stats[2:3] = pixels
    scale = scales[0:1] * inverse
    offset = scales[1:2] - center * scale

    def activate(at, carry):
        mask = widen(keep[pl.ds(at, ROWS)], out_width)
        for m in range(mel_count):
            value = middle[m, pl.ds(at, ROWS)] * scale + offset
            rows = (value * phi_parts(value) * mask).astype(bf16)
            if m < mel_count // 2:
                low[m, pl.ds(at, ROWS)] = rows
            else:
                high[m - mel_count // 2, pl.ds(at, ROWS)] = rows
        return carry

    by_rows(total, activate, 0)
    reach = picked.shape[1]
    for m in range(picked.shape[0]):
        picked[m] = high[m, pl.ds(pl.multiple_of((place % 2) * reach, reach), reach)]


def first_block(blocks, weight, scales, keep, sources, starts, total):
    _, mel_count, frames, lanes = blocks[0].shape
    out_width = weight.shape[3]
    padded = (mel_count, total + 2 * TILE, out_width)
    half = (mel_count // 2, total, out_width)
    return call(
        first_kernel,
        (starts, *blocks, weight, scales, keep, *sources),
        [whole_spec()] + [whole_spec()] * 10,
        [
            (half, bf16),
            (half, bf16),
            ((mel_count // 2, total // 2, out_width), bf16),
            ((mel_count, total, 2 * lanes), bf16),
            ((mel_count, total, out_width), f32),
            ((TILE, out_width), f32),
        ],
        [whole_spec()] * 6,
        [pltpu.VMEM(padded, f32), pltpu.VMEM(padded, f32)],
        0,
        16,
    )


def slope_kernel(pre, stats, scales, keep, slope, hats):
    mel_count, total, width = pre.shape
    center, inverse = stats[0:1], stats[1:2]

    def rows(at, carry):
        mask = widen(keep[pl.ds(at, ROWS)], width)
        for m in range(mel_count):
            normed = (pre[m, pl.ds(at, ROWS)] - center) * inverse
            hats[m, pl.ds(at, ROWS)] = normed
            value = normed * scales[0:1] + scales[1:2]
            slope[m, pl.ds(at, ROWS)] = mask * (phi_parts(value) + value * bell(value))
        return carry

    by_rows(total, rows, 0)


def first_slope(pre, stats, scales, keep):
    return call(
        slope_kernel,
        (pre, stats, scales, keep),
        [whole_spec()] * 4,
        [(pre.shape, f32)] * 2,
        [whole_spec()] * 2,
        [],
        2**28,
        6,
    )


def group_sums(fields, weight, starts, targets, sources=None):
    mel_count, (_, total, width) = len(fields[0]), targets[1][0].shape
    for m in range(mel_count):
        for a in range(3):
            acc = None
            for mels, start in zip(fields, starts):
                for b in range(3):
                    if 0 <= m + b - 1 < mel_count:
                        part = jnp.dot(
                            mels[m + b - 1][...],
                            weight[a, b, pl.ds(start, width)],
                            preferred_element_type=f32,
                        )
                        acc = part if acc is None else acc + part
            if sources is not None:
                acc = acc + sources[a, m]
            target, at = targets[a]
            target[m, at : at + total] = acc


def join_halves(pair, joint):
    side = lax.axis_index("tm") % 2
    half = pair[0].shape[1]
    for part, begin in zip(pair, (side, 1 - side)):
        joint[:, pl.ds(pl.multiple_of(begin * half, half), half)] = part[...]


def group_starts(bits, width):
    column = lax.axis_index("chan")
    return [pl.multiple_of((column ^ bit) * width, width) for bit in bits]


def near_kernel(low, high, low_two, high_two, weight, sums):
    half, _, width = low.shape
    fields = [
        [a.at[k] for a in pair for k in range(half)] for pair in ((low, high), (low_two, high_two))
    ]
    targets = [(sums.at[a], 0) for a in range(3)]
    group_sums(fields, weight, group_starts((0, 1), width), targets)


def near_part(low, high, low_two, high_two, weight):
    half, total, width = low.shape
    return call(
        near_kernel,
        (low, high, low_two, high_two, weight),
        [whole_spec()] * 5,
        [((3, 2 * half, total, width), f32)],
        [whole_spec()],
        [],
        0,
        6,
    )[0]


def far_kernel(far, picked, rest, weight, near, sums, joint):
    half, _, width = far.shape
    join_halves((picked, rest), joint)
    fields = [[a.at[k] for a in (far, joint) for k in range(half)]]
    targets = [(sums.at[a], 0) for a in range(3)]
    group_sums(fields, weight, group_starts((2,), width), targets, near)


def far_part(far, picked, rest, weight, near):
    return call(
        far_kernel,
        (far, picked, rest, weight, near),
        [whole_spec()] * 5,
        [(near.shape, f32)],
        [whole_spec()],
        [pltpu.VMEM(far.shape, bf16)],
        0,
        8,
    )[0]


def run_sums(mask, plain, values):
    width = (plain + values)[0].shape[1]
    terms = list(plain)
    for value in values:
        for _ in range(2):
            term = value.astype(bf16)
            terms.append(term)
            value = value - term.astype(f32)
    out = jnp.dot(mask, jnp.concatenate(terms, axis=1), preferred_element_type=f32)
    parts = [out[:, k * width : (k + 1) * width] for k in range(len(terms))]
    results = parts[: len(plain)]
    for k in range(len(plain), len(parts), 2):
        results.append(parts[k] + parts[k + 1])
    return results


def second_kernel(
    starts, sums, far_two, picked_two, rest_two, weight, keep, scales, *refs
):
    cotangents, (readout, grad, gain_grad, shift_grad) = refs[:-13], refs[-13:-9]
    middle, slope, lower, upper, joint, hold, wide, full, sems = refs[-9:]
    mel_count, total, width = middle.shape
    half = mel_count // 2
    place = lax.axis_index("tm")
    pooled_total = total // 2
    own = readout.shape[0]
    copies = []
    pieces = [(part, i) for part in cotangents for i in range(part.shape[0])]
    bits = gather_bits(len(pieces))
    for k, (part, i) in enumerate(pieces):
        source = place ^ sum(bit for j, bit in enumerate(bits) if k >> j & 1)
        copies.append(
            pltpu.make_async_copy(
                part.at[i],
                full.at[pl.ds(pl.multiple_of(source * own, own), own)],
                sems.at[k],
            )
        )
    for copy in copies:
        copy.start()

    join_halves((picked_two, rest_two), joint)
    clear_edges(lower, upper, total)
    fields = [[a.at[k] for a in (far_two, joint) for k in range(half)]]
    targets = ((lower, TILE), (middle, 0), (upper, TILE))
    group_sums(fields, weight, group_starts((3,), width), targets, sums)
    blank = jnp.zeros((TILE, width), f32)

    def combine(at, sums):
        before, after = same_clip(starts, at, (ROWS, width), total)
        mask = widen(keep[pl.ds(at, ROWS)], width)
        first, second, num = sums
        num = num + fold(mask)
        for m in range(mel_count):
            rows = joined(lower, middle, upper, m, at, before, after)
            middle[m, pl.ds(at, ROWS)] = rows
            kept = rows * mask
            first = first + fold(kept)
            second = second + fold(kept * rows)
        return first, second, num

    first, second, num = by_rows(total, combine, (blank, blank, blank))
    pixels = column_sum(num) * mel_count
    center, inverse = moments((first, second), keep, pixels)
    scale = scales[2:3] * inverse

    def activate(at, carry):
        mask = widen(keep[pl.ds(at, ROWS)], width)
        pooled = jnp.zeros((ROWS, width), f32)
        for m in range(mel_count):
            normed = (middle[m, pl.ds(at, ROWS)] - center) * inverse
            middle[m, pl.ds(at, ROWS)] = normed
            value = normed * scales[2:3] + scales[3:4]
            share = phi_parts(value)
            pooled = pooled + value * share
            slope[m, pl.ds(at, ROWS)] = mask * (share + value * bell(value))
        pooled = pooled * mask
        for c in range(width // LANES):
            hold[c, pl.ds(at, ROWS)] = pooled[:, c * LANES : (c + 1) * LANES]
        return carry

    by_rows(total, activate, 0)

    even = pl.ds(0, pooled_total, stride=2)
    odd = pl.ds(1, pooled_total, stride=2)
    pooled = jnp.concatenate(
        [hold[c, even] + hold[c, odd] for c in range(width // LANES)], axis=1
    ) * (0.5 / mel_count)
    present = widen(keep[even], width)
    square = (pooled_total, pooled_total)
    row = lax.broadcasted_iota(jnp.int32, square, 0)
    col = lax.broadcasted_iota(jnp.int32, square, 1)
    same = row >= col
    back = row <= col
    for start in clip_rows(starts)[1:]:
        start = start[:, :pooled_total]
        crossed = (2 * row < start) != (2 * col < start)
        same = same & ~crossed
        back = back & ~crossed
    ahead, behind = same.astype(f32).astype(bf16), back.astype(f32).astype(bf16)
    exponent = jnp.exp(pooled)
    counts, totals, sums = run_sums(
        ahead, (present.astype(bf16),), (present * pooled, present * exponent)
    )
    mine = pl.ds(pl.multiple_of(place * own, own), own)
    for i, value in enumerate((totals, counts, sums)):
        wide[i] = value
    readout[...] = wide[0, mine] / wide[1, mine] + jnp.log(wide[2, mine])
    for copy in copies:
        copy.wait()
    cotangent = full[...]
    by_count, by_sum = run_sums(behind, (), (cotangent / counts, cotangent / sums))
    down = present * (by_count + exponent * by_sum) * (0.5 / mel_count)
    for c in range(width // LANES):
        hold[c, even] = down[:, c * LANES : (c + 1) * LANES]
        hold[c, odd] = down[:, c * LANES : (c + 1) * LANES]

    def slopes(at, sums):
        down_rows = jnp.concatenate(
            [hold[c, pl.ds(at, ROWS)] for c in range(width // LANES)], axis=1
        )
        plain, along = sums
        for m in range(mel_count):
            step = down_rows * slope[m, pl.ds(at, ROWS)]
            slope[m, pl.ds(at, ROWS)] = step
            plain = plain + fold(step)
            along = along + fold(step * middle[m, pl.ds(at, ROWS)])
        return plain, along

    plain, along = by_rows(total, slopes, (blank, blank))
    plain, along = column_sum(plain), column_sum(along)
    shift_grad[...] = plain
    gain_grad[...] = along
    plain, along = plain / pixels, along / pixels

    def finish(at, carry):
        mask = widen(keep[pl.ds(at, ROWS)], width)
        for m in range(mel_count):
            rows = slope[m, pl.ds(at, ROWS)] - plain - middle[m, pl.ds(at, ROWS)] * along
            grad[m, pl.ds(at, ROWS)] = (mask * (scale * rows)).astype(bf16)
        return carry

    by_rows(total, finish, 0)


def second_block(sums, arrays, weight, keep, scales, starts, cotangents, own):
    _, mel_count, total, width = sums.shape
    padded = (mel_count, total + 2 * TILE, width)
    full = (mel_count, total, width)
    return call(
        second_kernel,
        (starts, sums, *arrays, weight, keep, scales, *cotangents),
        [whole_spec()] + [whole_spec()] * (len(arrays) + 4) + [place_spec()] * len(cotangents),
        [((own, width), f32), (full, bf16), ((1, width), f32), ((1, width), f32)],
        [whole_spec()] * 4,
        [
            pltpu.VMEM(full, f32),
            pltpu.VMEM(full, f32),
            pltpu.VMEM(padded, f32),
            pltpu.VMEM(padded, f32),
            pltpu.VMEM(arrays[0].shape, bf16),
            pltpu.VMEM((width // LANES, total, LANES), f32),
            pltpu.VMEM((3, total // 2, width), f32),
            pltpu.VMEM((total // 2, width), f32),
            pltpu.SemaphoreType.DMA((sum(part.shape[0] for part in cotangents),)),
        ],
        0,
        20,
    )


def wings_kernel(weight, wings, sems):
    width = wings.shape[3]
    copies = []
    for i, start in enumerate(group_starts((2, 0), width)):
        for a in range(3):
            for b in range(3):
                copies.append(
                    pltpu.make_async_copy(
                        weight.at[a, b, pl.ds(start, width)], wings.at[i, 3 * a + b], sems.at[len(copies)]
                    )
                )
    for copy in copies:
        copy.start()
    for copy in copies:
        copy.wait()


def bring_wings(weight):
    width = weight.shape[3]
    return call(
        wings_kernel,
        (weight,),
        [place_spec()],
        [((2, 9, width, width), bf16)],
        [whole_spec()],
        [pltpu.SemaphoreType.DMA((18,))],
        0,
        4,
    )[0]


def back_sums(field, wing, mels, reach, first, targets, sources=None):
    mel_count = field.shape[0]
    for k, n in enumerate(mels):
        for a in range(3):
            acc = None
            for b in range(3):
                if 0 <= n - b + 1 < mel_count:
                    part = lax.dot_general(
                        field[n - b + 1, pl.ds(first, reach)],
                        wing(a, b),
                        (((1,), (1,)), ((), ())),
                        preferred_element_type=f32,
                    )
                    acc = part if acc is None else acc + part
            if sources is not None:
                acc = sources[a, k] + acc
            target, at = targets[a]
            target[k, at : at + reach] = acc


def half_rows(total, reach):
    side = lax.axis_index("tm") % 2
    return (
        pl.multiple_of(side * (total - reach), 16),
        pl.multiple_of(side * (reach - total // 2), 16),
    )


def ahead_kernel(bit, mels, one, weight, sums):
    _, total, width = one.shape
    reach = sums.shape[2]
    first, _ = half_rows(total, reach)
    (start,) = group_starts((bit,), width)
    targets = [(sums.at[a], 0) for a in range(3)]
    back_sums(one, lambda a, b: weight[a, b, pl.ds(start, width)], mels, reach, first, targets)


def hidden_ahead(bit, mels, one, weight):
    _, total, width = one.shape
    return call(
        functools.partial(ahead_kernel, bit, mels),
        (one, weight),
        [whole_spec()] * 2,
        [((3, len(mels), total // 2 + 16, width), f32)],
        [whole_spec()],
        [],
        0,
        4,
    )[0]


def half_kernel(bit, mels, starts, two, wings, sums, out, lower, middle, upper):
    _, total, width = two.shape
    reach = sums.shape[2]
    first, skip = half_rows(total, reach)
    for k in range(len(mels)):
        for ref in (lower, upper):
            ref[k, :TILE] = jnp.zeros((TILE, width), f32)
            ref[k, TILE + reach :] = jnp.zeros((TILE, width), f32)
    wing = wings.at[0 if bit else 1]
    targets = ((upper, TILE), (middle, 0), (lower, TILE))
    back_sums(two, lambda a, b: wing[3 * a + b], mels, reach, first, targets, sums)

    def combine(at, carry):
        near = pl.multiple_of(at + skip, TILE)
        before, after = same_clip(starts, first + near, (ROWS, width), total)
        for k in range(len(mels)):
            rows = joined(lower, middle, upper, k, near, before, after)
            out[k, pl.ds(at, ROWS)] = rows.astype(out.dtype)
        return carry

    by_rows(total // 2, combine, 0)


def hidden_half(bit, mels, two, wings, sums, starts, kind):
    _, total, width = two.shape
    reach, count = sums.shape[2], len(mels)
    padded = (count, reach + 2 * TILE, width)
    return call(
        functools.partial(half_kernel, bit, mels),
        (starts, two, wings, sums),
        [whole_spec()] * 4,
        [((count, total // 2, width), kind)],
        [whole_spec()],
        [
            pltpu.VMEM(padded, f32),
            pltpu.VMEM((count, reach, width), f32),
            pltpu.VMEM(padded, f32),
        ],
        0,
        8,
    )[0]


def back_kernel(bit, mels, starts, one, two, weight, wings, out, lower, middle, upper):
    mel_count, total, width = one.shape
    (start,) = group_starts((bit,), width)
    wing = wings.at[0 if bit else 1]
    clear_edges(lower, upper, total)
    for k, n in enumerate(mels):
        for a, (target, at) in enumerate(((upper, TILE), (middle, 0), (lower, TILE))):
            acc = None
            for field, matrix in (
                (one, lambda b, a=a: weight[a, b, pl.ds(start, width)]),
                (two, lambda b, a=a: wing[3 * a + b]),
            ):
                for b in range(3):
                    if 0 <= n - b + 1 < mel_count:
                        part = lax.dot_general(
                            field[n - b + 1],
                            matrix(b),
                            (((1,), (1,)), ((), ())),
                            preferred_element_type=f32,
                        )
                        acc = part if acc is None else acc + part
            target[k, at : at + total] = acc

    def combine(at, carry):
        before, after = same_clip(starts, at, (ROWS, width), total)
        for k in range(len(mels)):
            rows = joined(lower, middle, upper, k, at, before, after)
            out[k, pl.ds(at, ROWS)] = rows.astype(out.dtype)
        return carry

    by_rows(total, combine, 0)


def hidden_back(bit, mels, one, two, weight, wings, starts, kind):
    _, total, width = one.shape
    count = len(mels)
    padded = (count, total + 2 * TILE, width)
    return call(
        functools.partial(back_kernel, bit, mels),
        (starts, one, two, weight, wings),
        [whole_spec()] * 5,
        [((count, total, width), kind)],
        [whole_spec()],
        [
            pltpu.VMEM(padded, f32),
            pltpu.VMEM((count, total, width), f32),
            pltpu.VMEM(padded, f32),
        ],
        0,
        14,
    )[0]


def norm_kernel(mine, low, picked, rest, slope, hats, stats, scales, keep, *refs):
    grad, window, gain_grad, shift_grad, padded, held = refs
    mel_count, total, width = mine.shape
    inverse, pixels = stats[1:2], stats[2:3]
    blank = jnp.zeros((TILE, width), f32)
    edge = (padded.shape[1] - total) // 2
    reach = window.shape[1]
    frames = reach - 2 * edge
    place = lax.axis_index("tm")

    half = mel_count // 2

    def add(field, base, mels):
        def slopes(at, sums):
            plain, along = sums
            place_rows = pl.ds(pl.multiple_of(base + at, ROWS), ROWS)
            for k, m in enumerate(mels):
                rows = mine[m, place_rows] + field[k, pl.ds(at, ROWS)].astype(f32)
                step = rows * slope[m, place_rows]
                held[m, place_rows] = step
                plain = plain + fold(step)
                along = along + fold(step * hats[m, place_rows])
            return plain, along

        return slopes

    side = place % 2
    sums = by_rows(total, add(low, 0, range(half)), (blank, blank))
    upper = range(half, mel_count)
    parts = []
    for field, base in ((picked, side), (rest, 1 - side)):
        parts.append(by_rows(total // 2, add(field, base * (total // 2), upper), (blank, blank)))
    plain, along = [
        a + jnp.where(side == 0, b + c, c + b) for a, b, c in zip(sums, parts[0], parts[1])
    ]
    plain, along = column_sum(plain), column_sum(along)
    shift_grad[...] = plain
    gain_grad[...] = along
    plain, along = plain / pixels, along / pixels
    scale = scales[0:1] * inverse
    for m in range(mel_count):
        padded[m, :edge] = jnp.zeros((edge, width), bf16)
        padded[m, edge + total :] = jnp.zeros((edge, width), bf16)

    def finish(at, carry):
        mask = widen(keep[pl.ds(at, ROWS)], width)
        for m in range(mel_count):
            rows = held[m, pl.ds(at, ROWS)] - plain - hats[m, pl.ds(at, ROWS)] * along
            rows = (mask * (scale * rows)).astype(bf16)
            grad[m, pl.ds(at, ROWS)] = rows
            padded[m, pl.ds(pl.multiple_of(at + edge, 16), ROWS)] = rows
        return carry

    by_rows(total, finish, 0)
    for m in range(mel_count):
        window[m] = padded[m, pl.ds(pl.multiple_of(place * frames, frames), reach)]


def norm_back_first(mine, low, picked, rest, slope, pre, stats, scales, keep, frames):
    mel_count, total, width = mine.shape
    edge = 16
    return call(
        norm_kernel,
        (mine, low, picked, rest, slope, pre, stats, scales, keep),
        [whole_spec()] * 9,
        [
            ((mel_count, total, width), bf16),
            ((mel_count, frames + 2 * edge, width), bf16),
            ((1, width), f32),
            ((1, width), f32),
        ],
        [whole_spec()] * 4,
        [pltpu.VMEM((mel_count, total + 2 * edge, width), bf16), pltpu.VMEM(mine.shape, f32)],
        2**28,
        12,
    )


def spread_kernel(starts, grad, steps, spaced):
    mel_count, total, width = grad.shape
    for m in range(mel_count):
        spaced[m, :TILE] = jnp.zeros((TILE, width), f32)
        spaced[m, TILE + total :] = jnp.zeros((TILE, width), f32)

    def expand(at, carry):
        for m in range(mel_count):
            rows = grad[m, pl.ds(at, ROWS)].astype(f32)
            spaced[m, pl.ds(pl.multiple_of(at + TILE, TILE), ROWS)] = rows
        return carry

    by_rows(total, expand, 0)

    def shift(at, carry):
        before, after = same_clip(starts, at, (ROWS, width), total)
        for m in range(mel_count):
            rows = spaced[m, pl.ds(at, ROWS + 2 * TILE)]
            ahead = jnp.where(after, rows[TILE + 1 : TILE + 1 + ROWS], 0.0)
            behind = jnp.where(before, rows[TILE - 1 : TILE - 1 + ROWS], 0.0)
            steps[0, m, pl.ds(at, ROWS)] = ahead.astype(bf16)
            steps[1, m, pl.ds(at, ROWS)] = behind.astype(bf16)
        return carry

    by_rows(total, shift, 0)


def spread(grad, starts):
    mel_count, total, width = grad.shape
    return call(
        spread_kernel,
        (starts, grad),
        [whole_spec()] * 2,
        [((2, mel_count, total, width), bf16)],
        [whole_spec()],
        [pltpu.VMEM((mel_count, total + 2 * TILE, width), f32)],
        0,
        6,
    )[0]


def weight_kernel(layout, halves, *refs):
    count = len(refs) - 7
    fields, grad, steps = list(refs[:count]), refs[count], refs[count + 1]
    out, results, joint, sems, move_sems = refs[count + 2 :]
    mel_count, total, out_width = grad.shape
    width = results.shape[2]
    side = lax.axis_index("tm") % 2
    column = lax.axis_index("chan")
    moves = []
    for i, pair in enumerate(halves):
        for index, begin in zip(pair, (side, 1 - side)):
            rows = pl.ds(pl.multiple_of(begin * (total // 2), total // 2), total // 2)
            moves.append(
                pltpu.make_async_copy(fields[index], joint.at[i, :, rows], move_sems.at[len(moves)])
            )
            moves[-1].start()
        fields.append(joint.at[i])
    copies = [[], []]
    for i, (places, pieces) in enumerate(layout):
        slot = i % 2
        for copy in copies[slot]:
            copy.wait()
        copies[slot] = []
        each = width // len(places)
        if any(piece[0] >= count for piece in pieces):
            while moves:
                moves.pop().wait()
        for a in range(3):
            for b in range(3):
                right = grad if a == 1 else steps.at[a // 2]
                acc = None
                for m in range(mel_count):
                    if 0 <= m + b - 1 < mel_count:
                        index, k, lane = pieces[m + b - 1]
                        part = lax.dot_general(
                            fields[index][k, :, lane : lane + width],
                            right[m],
                            (((0,), (0,)), ((), ())),
                            preferred_element_type=f32,
                        )
                        acc = part if acc is None else acc + part
                tap = 3 * a + b
                results[slot, tap] = acc
                for j, bit in enumerate(places):
                    start = pl.multiple_of((column ^ bit) * each, each)
                    copies[slot].append(
                        pltpu.make_async_copy(
                            results.at[slot, tap, j * each : (j + 1) * each],
                            out.at[tap, pl.ds(start, each)],
                            sems.at[slot, tap, j],
                        )
                    )
                    copies[slot][-1].start()
    for copy in copies[0] + copies[1]:
        copy.wait()


def weight_back(layout, halves, fields, grad, steps, in_width):
    mel_count, total, out_width = grad.shape
    width = in_width // len(layout)
    joint = (max(len(halves), 1), mel_count // 2, total, width)
    out = call(
        functools.partial(weight_kernel, layout, halves),
        (*fields, grad, steps),
        [whole_spec()] * (len(fields) + 2),
        [((9, in_width, out_width), f32)],
        [place_spec()],
        [
            pltpu.VMEM((2, 9, width, out_width), f32),
            pltpu.VMEM(joint, bf16),
            pltpu.SemaphoreType.DMA((2, 9, 2)),
            pltpu.SemaphoreType.DMA((max(2 * len(halves), 1),)),
        ],
        0,
        12,
    )[0]
    return out.reshape(3, 3, in_width, out_width)


def input_kernel(starts, one, two, weight, weight_two, mine, other, lower, middle, upper):
    mel_count, reach, width = one.shape
    frames, lanes = mine.shape[1], mine.shape[2]
    edge = (reach - frames) // 2
    total = frames * lax.axis_size("tm")
    place = lax.axis_index("tm")
    groups = group_starts((2, 0), lanes)
    for a in range(3):
        target, shift = ((upper, TILE), (middle, 0), (lower, TILE))[a]
        for b in (1, 0, 2):
            low, count = ((1, mel_count - 1), (0, mel_count), (0, mel_count - 1))[b]
            acc = None
            for field, matrix in ((one, weight), (two, weight_two)):
                rows = field[low : low + count].reshape(count * reach, width)
                wing = jnp.concatenate([matrix[a, b, pl.ds(g, lanes)] for g in groups])
                part = lax.dot_general(
                    rows, wing, (((1,), (1,)), ((), ())), preferred_element_type=f32
                )
                acc = part if acc is None else acc + part
            acc = acc.reshape(count, reach, 2 * lanes)
            for k in range(count):
                n = low + k + b - 1
                if b == 1:
                    target[n, shift : shift + reach] = acc[k]
                else:
                    target[n, shift : shift + reach] += acc[k]
    before, after = same_clip(starts, place * frames, (frames, 2 * lanes), total)
    for m in range(mel_count):
        low = lower[m, TILE + edge - 1 : TILE + edge - 1 + frames]
        high = upper[m, TILE + edge + 1 : TILE + edge + 1 + frames]
        rows = (
            middle[m, edge : edge + frames]
            + jnp.where(before, low, 0.0)
            + jnp.where(after, high, 0.0)
        )
        other[m] = rows[:, :lanes]
        mine[m] = rows[:, lanes:]


def input_back(one, two, weight, weight_two, starts, frames, lanes):
    mel_count, reach, width = one.shape
    shape = (mel_count, frames, lanes)
    return call(
        input_kernel,
        (starts, one, two, weight, weight_two),
        [whole_spec()] + [whole_spec()] * 4,
        [(shape, f32), (shape, f32)],
        [whole_spec()] * 2,
        [
            pltpu.VMEM((mel_count, reach + 2 * TILE, 2 * lanes), f32),
            pltpu.VMEM((mel_count, reach, 2 * lanes), f32),
            pltpu.VMEM((mel_count, reach + 2 * TILE, 2 * lanes), f32),
        ],
        0,
        10,
    )


def close_kernel(mine, other, keep, *refs):
    count = len(refs) // 2
    small, out, small_out = refs[:count], refs[count], refs[count + 1 :]
    mel_count, frames, lanes = mine.shape
    begin = pl.multiple_of(lax.axis_index("tm") * frames, frames)
    mask = keep[pl.ds(begin, frames)]
    for m in range(mel_count):
        out[:, m, :] = (mine[m] + other[m]) * mask
    for source, target in zip(small, small_out):
        target[...] = source[...]


def close(mine, other, keep, small):
    mel_count, frames, lanes = mine.shape
    return call(
        close_kernel,
        (mine, other, keep, *small),
        [whole_spec()] * (3 + len(small)),
        [((frames, mel_count, lanes), f32)] + [(a.shape, f32) for a in small],
        [whole_spec()] * (1 + len(small)),
        [],
        0,
        4,
    )


def whole_frames(
    features,
    conv1_weight,
    norm1_gain,
    norm1_bias,
    conv2_weight,
    norm2_gain,
    norm2_bias,
    clip_starts,
    valid,
    readout_grad,
):
    frames, mel_count, lanes = features.shape
    places = lax.axis_size("tm")
    total = frames * places
    conv1_weight = bring(conv1_weight)
    starts = jnp.broadcast_to(clip_starts.astype(f32)[:, None], clip_starts.shape + norm1_gain.shape)
    norms = jnp.stack([norm1_gain, norm1_bias, norm2_gain, norm2_bias])
    table = jnp.concatenate([norms, starts])

    marked = jnp.where(valid[:, None, None] > 0, features, jnp.asarray(ABSENT, bf16))
    own = jnp.transpose(marked, (1, 0, 2))
    pieces = [swap(own, "tm", 2 * k) for k in range(1, places // 2)]
    along = jnp.stack([own] + pieces)
    near = [
        along,
        swap(along, "tm", 1),
        swap(along, "chan", 2),
        swap_both(along, "tm", 1, "chan", 2),
    ]
    readout_grad, _ = lax.optimization_barrier((readout_grad, pieces[0]))
    bits = gather_bits(places)
    cotangents = [readout_grad[None]]
    cotangents.append(swap(cotangents[0], "tm", bits[0]))
    near[3], conv1_weight, table, cotangents = lax.optimization_barrier(
        (near[3], conv1_weight, table, cotangents)
    )
    others = [swap(block, "chan", 1) for block in near]
    column, keep, *sources = column_part(near, conv1_weight, total)
    column, others = lax.optimization_barrier((column, others))
    other_conv2 = swap(conv2_weight, "chan", 1)
    others, other_conv2 = lax.optimization_barrier((others, other_conv2))

    low, high, picked, other_column, pre, stats = first_block(
        others, conv1_weight, table, keep, sources, table, total
    )
    fields1 = (column, other_column)

    far_picked = swap(picked, "chan", 2)
    far = swap(low, "chan", 2)
    far_rest = swap(far_picked, "tm", 1)

    low_two, high_two = swap(low, "chan", 1), swap(high, "chan", 1)
    near = near_part(low, high, low_two, high_two, conv2_weight)
    far_picked, near, cotangents = lax.optimization_barrier((far_picked, near, cotangents))
    picked_two = swap(far_picked, "chan", 1)
    other_conv2, near = lax.optimization_barrier((other_conv2, near))
    wings = bring_wings(other_conv2)
    for bit in bits[1:-1]:
        cotangents.append(swap(jnp.concatenate(cotangents), "tm", bit))
    picked_two, pre, cotangents, wings = lax.optimization_barrier(
        (picked_two, pre, cotangents, wings)
    )
    cotangents.append(swap(jnp.concatenate(cotangents), "tm", bits[-1]))
    slope, pre = first_slope(pre, stats, table, keep)
    far, far_rest, slope, pre, cotangents = lax.optimization_barrier(
        (far, far_rest, slope, pre, cotangents)
    )
    far_two, rest_two = swap(far, "chan", 1), swap(far_rest, "chan", 1)
    sums = far_part(far, far_picked, far_rest, conv2_weight, near)
    far_two, rest_two, sums = lax.optimization_barrier((far_two, rest_two, sums))

    readout, grad2, gain2_grad, shift2_grad = second_block(
        sums,
        (far_two, picked_two, rest_two),
        conv2_weight,
        keep,
        table,
        table,
        cotangents,
        readout_grad.shape[0],
    )
    grad2_near = swap(grad2, "chan", 1)
    steps2 = spread(grad2, table)
    ahead = hidden_ahead(2, (2, 3), grad2, conv2_weight)
    grad2_near, steps2, ahead = lax.optimization_barrier((grad2_near, steps2, ahead))
    away = hidden_half(2, (2, 3), grad2_near, wings, ahead, table, bf16)
    came_picked = swap(away, "chan", 2)
    back = functools.partial(
        hidden_back, one=grad2, two=grad2_near, weight=conv2_weight, starts=table
    )
    away_low = back(2, (0, 1), wings=wings, kind=bf16)
    came_low = swap(away_low, "chan", 2)

    away_low, wings = lax.optimization_barrier((away_low, wings))
    mine = back(0, (0, 1, 2, 3), wings=wings, kind=f32)
    came_picked, mine, conv1_weight = lax.optimization_barrier((came_picked, mine, conv1_weight))
    came_rest = swap(came_picked, "tm", 1)
    other_conv1 = swap(conv1_weight, "chan", 1)
    fields = (low, high, low_two, high_two)
    fields += (far, far_picked, far_rest, far_two, picked_two, rest_two)
    layout = [
        ((0,), [(0, 0, 0), (0, 1, 0), (1, 0, 0), (1, 1, 0)]),
        ((1,), [(2, 0, 0), (2, 1, 0), (3, 0, 0), (3, 1, 0)]),
        ((2,), [(4, 0, 0), (4, 1, 0), (10, 0, 0), (10, 1, 0)]),
        ((3,), [(7, 0, 0), (7, 1, 0), (11, 0, 0), (11, 1, 0)]),
    ]
    weight2_grad = weight_back(
        layout, ((5, 6), (8, 9)), fields, grad2, steps2, conv2_weight.shape[2]
    )
    came_low, came_rest, mine, weight2_grad, other_conv1 = lax.optimization_barrier(
        (came_low, came_rest, mine, weight2_grad, other_conv1)
    )

    grad1, window, gain1_grad, shift1_grad = norm_back_first(
        mine, came_low, came_picked, came_rest, slope, pre, stats, table, keep, frames
    )
    window_near = swap(window, "chan", 1)
    steps1 = spread(grad1, table)
    window_near, steps1 = lax.optimization_barrier((window_near, steps1))
    input_mine, input_away = input_back(
        window, window_near, conv1_weight, other_conv1, table, frames, lanes
    )
    input_came = swap(input_away, "chan", 2)
    layout = [(bits, [(i, m, 0) for m in range(mel_count)]) for i, bits in enumerate(((0, 2), (1, 3)))]
    weight1_grad = weight_back(layout, (), fields1, grad1, steps1, conv1_weight.shape[2])
    input_came, weight1_grad = lax.optimization_barrier((input_came, weight1_grad))
    input_grad, readout, gain1_grad, shift1_grad, gain2_grad, shift2_grad = close(
        input_mine,
        input_came,
        keep,
        (readout, gain1_grad, shift1_grad, gain2_grad, shift2_grad),
    )
    return (
        readout,
        input_grad,
        weight1_grad,
        gain1_grad[0],
        shift1_grad[0],
        weight2_grad,
        gain2_grad[0],
        shift2_grad[0],
    )


def fits_whole(frames, mels, places, columns, widths):
    return (
        places > 1
        and places & (places - 1) == 0
        and columns == 4
        and frames % ROWS == 0
        and frames * places <= 512
        and mels == 4
        and all(w % (columns * LANES) == 0 for w in widths)
        and widths[1] == columns * 256
    )


def shards(*arrays):
    features, conv1_weight, conv2_weight = arrays[0], arrays[1], arrays[4]
    if fits_whole(
        features.shape[0],
        features.shape[1],
        lax.axis_size("tm"),
        lax.axis_size("chan"),
        (conv1_weight.shape[2], conv2_weight.shape[2]),
    ):
        return whole_frames(*arrays)
    return split_frames(*arrays)


def solution(mesh):
    return jax.shard_map(
        shards,
        mesh=mesh,
        in_specs=(
            P("tm", None, "chan"),
            P(None, None, None, "chan"),
            P("chan"),
            P("chan"),
            P(None, None, None, "chan"),
            P("chan"),
            P("chan"),
            P(),
            P("tm"),
            P("tm", "chan"),
        ),
        out_specs=(
            P("tm", "chan"),
            P("tm", None, "chan"),
            P(None, None, None, "chan"),
            P("chan"),
            P("chan"),
            P(None, None, None, "chan"),
            P("chan"),
            P("chan"),
        ),
        check_vma=False,
    )
```

```python
import functools

import jax
import jax.numpy as jnp
from jax import lax
from jax.experimental import pallas as pl
from jax.experimental.pallas import tpu as pltpu
from jax.sharding import PartitionSpec as P

EPS = 1e-05
highest = lax.Precision.HIGHEST
f32 = jnp.float32
bf16 = jnp.bfloat16


def padded_2(shard, sides, width):
    for axis, dim in sides:
        count, length = (lax.axis_size(axis), shard.shape[dim])
        up = [(i, (i + 1) % count) for i in range(count - 1)]
        down = [(j, i) for i, j in up]
        last = lax.slice_in_dim(shard, length - width, length, axis=dim)
        leading = lax.slice_in_dim(shard, 0, width, axis=dim)
        before = lax.ppermute(last, axis, up)
        after = lax.ppermute(leading, axis, down)
        shard = jnp.concatenate([before, shard, after], axis=dim)
    return shard


def entering(part, axis, combine, identity, reverse):
    count = lax.axis_size(axis)
    place = lax.axis_index(axis)
    ahead = count - 1 - place if reverse else place
    gathered = jax.tree.map(lambda a: lax.all_gather(a, axis), part)
    state = jax.tree.map(lambda a, e: jnp.zeros_like(a) + jnp.asarray(e, a.dtype), part, identity)

    def one(step, state):
        source = count - 1 - step if reverse else step
        return combine(
            state, jax.tree.map(lambda a: lax.dynamic_index_in_dim(a, source, 0, False), gathered)
        )

    return lax.fori_loop(0, ahead, one, state)


def frame_flags(clip_starts, first_frame, frame_count, frame_total):
    position = first_frame - 2 + jnp.arange(frame_count + 4, dtype=jnp.int32)
    segment = jnp.sum((clip_starts[None, :] <= position[:, None]).astype(jnp.int32), axis=1) - 1
    inside = (position >= 0) & (position < frame_total)
    middle = segment[1:-1]
    before_same = inside[1:-1] & inside[:-2] & (middle == segment[:-2])
    after_same = inside[1:-1] & inside[2:] & (middle == segment[2:])
    return (segment[2:-2], before_same, after_same)


def conv_forward(padded, weight, factors):
    frame_count = padded.shape[0] - 2
    mel_count = padded.shape[1]
    wide_field = jnp.pad(padded, ((0, 0), (1, 1), (0, 0)))
    result = jnp.zeros((frame_count, mel_count, weight.shape[3]), jnp.float32)
    for tap_row in range(3):
        partial_value = jnp.zeros((frame_count * mel_count, weight.shape[3]), jnp.float32)
        for tap_col in range(3):
            window = wide_field[
                tap_row : tap_row + frame_count, tap_col : tap_col + mel_count, :
            ].reshape(frame_count * mel_count, -1)
            partial_value = partial_value + jnp.dot(
                window, weight[tap_row, tap_col], preferred_element_type=jnp.float32
            )
        result = (
            result
            + partial_value.reshape(frame_count, mel_count, -1) * factors[tap_row][:, None, None]
        )
    return result


def conv_weight_grad(padded, grad_out, factors):
    frame_count = grad_out.shape[0]
    mel_count = grad_out.shape[1]
    wide_field = jnp.pad(padded, ((0, 0), (1, 1), (0, 0)))
    rows_out = []
    for tap_row in range(3):
        scaled = (grad_out * factors[tap_row][:, None, None].astype(jnp.bfloat16)).reshape(
            frame_count * mel_count, -1
        )
        taps_out = []
        for tap_col in range(3):
            window = wide_field[
                tap_row : tap_row + frame_count, tap_col : tap_col + mel_count, :
            ].reshape(frame_count * mel_count, -1)
            taps_out.append(
                lax.dot_general(
                    window, scaled, (((0,), (0,)), ((), ())), preferred_element_type=jnp.float32
                )
            )
        rows_out.append(jnp.stack(taps_out))
    return jnp.stack(rows_out)


def conv_input_grad(grad_padded, weight, edge_factors):
    frame_count = grad_padded.shape[0] - 2
    mel_count = grad_padded.shape[1]
    wide_field = jnp.pad(grad_padded, ((0, 0), (1, 1), (0, 0)))
    result = jnp.zeros((frame_count * mel_count, weight.shape[2]), jnp.float32)
    for tap_row in range(3):
        scaled = wide_field * edge_factors[tap_row][:, None, None]
        for tap_col in range(3):
            window = scaled[
                2 - tap_row : 2 - tap_row + frame_count, 2 - tap_col : 2 - tap_col + mel_count, :
            ].reshape(frame_count * mel_count, -1)
            result = result + lax.dot_general(
                window,
                weight[tap_row, tap_col],
                (((1,), (1,)), ((), ())),
                preferred_element_type=jnp.float32,
            )
    return result.reshape(frame_count, mel_count, -1)


def join_keyed(earlier_item, later_item):
    keep_first = later_item[0] < 0.0
    same_key = later_item[0] == earlier_item[0]
    merged = [jnp.where(keep_first, earlier_item[0], later_item[0])]
    for first_part, second_part in zip(earlier_item[1:], later_item[1:]):
        extra = (1,) * (first_part.ndim - keep_first.ndim)
        keep_wide = jnp.reshape(keep_first, keep_first.shape + extra)
        same_wide = jnp.reshape(same_key, same_key.shape + extra)
        merged.append(
            jnp.where(
                keep_wide, first_part, jnp.where(same_wide, first_part + second_part, second_part)
            )
        )
    return tuple(merged)


def smooth(argument):
    return jax.nn.gelu(argument, approximate=False)


def split_frames(
    features,
    conv1_weight,
    norm1_gain,
    norm1_bias,
    conv2_weight,
    norm2_gain,
    norm2_bias,
    clip_starts,
    valid,
    readout_grad,
):
    frame_count = features.shape[0]
    mel_count = features.shape[1]
    cycle_size = lax.axis_size("tm")
    cycle_index = lax.axis_index("tm")
    segment, before_same, after_same = frame_flags(
        clip_starts, cycle_index * frame_count, frame_count, frame_count * cycle_size
    )
    keep_mask = valid.astype(jnp.float32)
    keep_cube = keep_mask[:, None, None]
    own_factors = (
        before_same[1:-1].astype(jnp.float32),
        jnp.ones((frame_count,), jnp.float32),
        after_same[1:-1].astype(jnp.float32),
    )
    edge_factors = (
        before_same.astype(jnp.bfloat16),
        jnp.ones((frame_count + 2,), jnp.bfloat16),
        after_same.astype(jnp.bfloat16),
    )
    local_count = jnp.sum(keep_mask) * mel_count

    def spread(shard):
        padded = padded_2(shard, (("tm", 0),), 1)
        return lax.all_gather(padded, "chan", axis=2, tiled=True)

    def normalize(field_in, gain_vec, shift_vec):
        value_sums, squares, pixel_count = lax.psum(
            (
                jnp.sum(field_in * keep_cube, axis=(0, 1)),
                jnp.sum(field_in * field_in * keep_cube, axis=(0, 1)),
                local_count,
            ),
            "tm",
        )
        center = value_sums / pixel_count
        variance = squares / pixel_count - center * center
        inverse_std = lax.rsqrt(variance + EPS)
        normed = (field_in - center) * inverse_std
        return (gain_vec * normed + shift_vec, normed, inverse_std, pixel_count)

    def norm_back(grad_norm, normed, inverse_std, gain_vec, pixel_count):
        bias_grad, gain_grad = lax.psum(
            (jnp.sum(grad_norm, axis=(0, 1)), jnp.sum(grad_norm * normed, axis=(0, 1))), "tm"
        )
        grad_pre = (
            keep_cube
            * (gain_vec * inverse_std)
            * (grad_norm - bias_grad / pixel_count - normed * (gain_grad / pixel_count))
        )
        return (grad_pre.astype(jnp.bfloat16), gain_grad, bias_grad)

    def send_back(grad_pre, weight):
        padded = padded_2(grad_pre, (("tm", 0),), 1)
        partial_sum = conv_input_grad(padded, weight, edge_factors)
        return lax.psum_scatter(partial_sum, "chan", scatter_dimension=2, tiled=True)

    wide_in = spread(features * keep_cube.astype(jnp.bfloat16))
    first_pre = conv_forward(wide_in, conv1_weight, own_factors)
    first_norm, first_hat, first_scale, pixel_count = normalize(first_pre, norm1_gain, norm1_bias)
    first_act, first_pull = jax.vjp(smooth, first_norm)
    hidden = (first_act * keep_cube).astype(jnp.bfloat16)
    wide_mid = spread(hidden)
    second_pre = conv_forward(wide_mid, conv2_weight, own_factors)
    second_norm, second_hat, second_scale, pixel_count = normalize(
        second_pre, norm2_gain, norm2_bias
    )
    second_act, second_pull = jax.vjp(smooth, second_norm)
    pooled = (second_act * keep_cube).reshape(frame_count // 2, 2, mel_count, -1).mean(axis=(1, 2))
    pooled_keep = keep_mask[0::2]
    pooled_segment = segment[0::2]
    segment_key = pooled_segment.astype(jnp.float32)
    row_order = jnp.arange(frame_count // 2)
    lower_runs = (
        (pooled_segment[:, None] == pooled_segment[None, :])
        & (row_order[:, None] >= row_order[None, :])
    ).astype(jnp.float32)
    exponent = jnp.exp(pooled)
    counts = jnp.dot(lower_runs, pooled_keep, precision=highest)
    totals = jnp.dot(lower_runs, pooled_keep[:, None] * pooled, precision=highest)
    expsums = jnp.dot(lower_runs, pooled_keep[:, None] * exponent, precision=highest)
    zero_row = jnp.zeros_like(totals[0])
    prior_runs = entering(
        (segment_key[-1], counts[-1], totals[-1], expsums[-1]),
        "tm",
        join_keyed,
        (jnp.float32(-1.0), jnp.float32(0.0), zero_row, zero_row),
        False,
    )
    joined = (segment_key == prior_runs[0]).astype(jnp.float32)
    counts = counts + joined * prior_runs[1]
    totals = totals + joined[:, None] * prior_runs[2]
    expsums = expsums + joined[:, None] * prior_runs[3]
    readout = totals / counts[:, None] + jnp.log(expsums)
    by_count = readout_grad / counts[:, None]
    by_expsum = readout_grad / expsums
    later_mean = lax.dot_general(lower_runs, by_count, (((0,), (0,)), ((), ())), precision=highest)
    later_soft = lax.dot_general(lower_runs, by_expsum, (((0,), (0,)), ((), ())), precision=highest)
    beyond = entering(
        (segment_key[0], later_mean[0], later_soft[0]),
        "tm",
        join_keyed,
        (jnp.float32(-1.0), zero_row, zero_row),
        True,
    )
    joined_back = (segment_key == beyond[0]).astype(jnp.float32)[:, None]
    later_mean = later_mean + joined_back * beyond[1]
    later_soft = later_soft + joined_back * beyond[2]
    pooled_grad = pooled_keep[:, None] * (later_mean + exponent * later_soft)
    spread_grad = jnp.broadcast_to(
        (pooled_grad / (2 * mel_count))[:, None, None, :],
        (frame_count // 2, 2, mel_count, pooled_grad.shape[1]),
    )
    act_grad = spread_grad.reshape(frame_count, mel_count, -1) * keep_cube
    second_grad_norm = second_pull(act_grad)[0]
    second_grad_pre, gain2_grad, bias2_grad = norm_back(
        second_grad_norm, second_hat, second_scale, norm2_gain, pixel_count
    )
    weight2_grad = conv_weight_grad(wide_mid, second_grad_pre, own_factors)
    weight2_grad = lax.psum(weight2_grad, "tm")
    hidden_grad = send_back(second_grad_pre, conv2_weight)
    first_grad_norm = first_pull(hidden_grad * keep_cube)[0]
    first_grad_pre, gain1_grad, bias1_grad = norm_back(
        first_grad_norm, first_hat, first_scale, norm1_gain, pixel_count
    )
    weight1_grad = conv_weight_grad(wide_in, first_grad_pre, own_factors)
    weight1_grad = lax.psum(weight1_grad, "tm")
    input_grad = send_back(first_grad_pre, conv1_weight) * keep_cube
    return (
        readout,
        input_grad,
        weight1_grad,
        gain1_grad,
        bias1_grad,
        weight2_grad,
        gain2_grad,
        bias2_grad,
    )


ABSENT = 1024.0
ROWS = 64
TILE = 8
NORMS = 4
LANES = 128


def whole_spec():
    return pl.BlockSpec(memory_space=pltpu.VMEM)


def place_spec():
    return pl.BlockSpec(memory_space=pl.ANY)


def far_spec():
    return pl.BlockSpec(memory_space=pltpu.HBM)


def call(body, operands, in_specs, outs, out_specs, scratch, flops, megabytes):
    return pl.pallas_call(
        body,
        out_shape=tuple(jax.ShapeDtypeStruct(s, d) for s, d in outs),
        in_specs=in_specs,
        out_specs=tuple(out_specs),
        scratch_shapes=scratch,
        compiler_params=pltpu.CompilerParams(vmem_limit_bytes=megabytes * 2**20),
        cost_estimate=pl.CostEstimate(flops=1000, bytes_accessed=1000, transcendentals=0),
    )(*operands)


def swap(shard, axis, bit):
    count = lax.axis_size(axis)
    return lax.ppermute(shard, axis, [(i, i ^ bit) for i in range(count)])


def gather_bits(places):
    bits = [1 << k for k in range(places.bit_length() - 1)]
    return bits[2:][::-1] + bits[:2] if len(bits) > 2 else bits


def swap_both(shard, first, first_bit, second, second_bit):
    rows, columns = lax.axis_size(first), lax.axis_size(second)
    pairs = [
        (i * columns + j, (i ^ first_bit) * columns + (j ^ second_bit))
        for i in range(rows)
        for j in range(columns)
    ]
    return lax.ppermute(shard, (first, second), pairs)


def same_clip(starts, at, shape, total):
    frame = lax.broadcasted_iota(jnp.int32, shape, 0) + at
    first, *others = clip_rows(starts)
    before = frame != first
    after = frame != total - 1
    for start in others:
        before = before & (frame != start)
        after = after & (frame != start - 1)
    return before, after


def clip_rows(table):
    return [table[k : k + 1].astype(jnp.int32) for k in range(NORMS, table.shape[0])]


def widen(mask, width):
    return jnp.concatenate([mask] * (width // mask.shape[1]), axis=1)


def fold(value):
    total = value[:TILE]
    for k in range(TILE, value.shape[0], TILE):
        total = total + value[k : k + TILE]
    return total


def column_sum(value):
    return jnp.sum(value, axis=0, keepdims=True)


def joined(lower, middle, upper, m, at, before, after):
    low = lower[m, pl.ds(at, ROWS + 2 * TILE)]
    high = upper[m, pl.ds(at, ROWS + 2 * TILE)]
    return (
        middle[m, pl.ds(at, ROWS)]
        + jnp.where(before, low[TILE - 1 : TILE - 1 + ROWS], 0.0)
        + jnp.where(after, high[TILE + 1 : TILE + 1 + ROWS], 0.0)
    )


def by_rows(total, body, init):
    return lax.fori_loop(
        0, total // ROWS, lambda i, c: body(pl.multiple_of(i * ROWS, ROWS), c), init
    )


def clear_edges(lower, upper, total):
    for m in range(lower.shape[0]):
        for ref in (lower, upper):
            ref[m, :TILE] = jnp.zeros((TILE, ref.shape[2]), f32)
            ref[m, TILE + total :] = jnp.zeros((TILE, ref.shape[2]), f32)


def moments(field, keep, count):
    first, second = column_sum(field[0]), column_sum(field[1])
    center = first / count
    return center, lax.rsqrt(second / count - center * center + EPS)


def phi_parts(value):
    return 0.5 * (1.0 + lax.erf(value * 0.7071067811865476))


def bell(value):
    return 0.3989422804014327 * jnp.exp(-0.5 * value * value)


def bring_kernel(weight_in, weight, sem):
    copy = pltpu.make_async_copy(weight_in, weight, sem)
    copy.start()
    copy.wait()


def bring(weight):
    return call(
        bring_kernel,
        (weight,),
        [place_spec()],
        [(weight.shape, bf16)],
        [whole_spec()],
        [pltpu.SemaphoreType.DMA],
        0,
        4,
    )[0]


def settle(blocks, field, keep):
    mel_count = field.shape[0]
    place = lax.axis_index("tm")
    frames, lanes = blocks[0].shape[2], blocks[0].shape[3]
    for i, block in enumerate(blocks):
        row, side = i // 2, i % 2
        to_columns = slice(row * lanes, (row + 1) * lanes)
        for k in range(block.shape[0]):
            to_rows = pl.ds(pl.multiple_of((place ^ (2 * k + side)) * frames, frames), frames)
            for m in range(mel_count):
                rows = block[k, m]
                if m == 0 and row == 0 and keep is not None:
                    keep[to_rows] = (rows.astype(f32) < ABSENT / 2).astype(f32)
                field[m, to_rows, to_columns] = jnp.where(
                    rows < ABSENT / 2, rows, jnp.zeros_like(rows)
                )


def products(field, weight, bits, targets, sources=None):
    mel_count, total, width = field.shape
    lanes = width // len(bits)
    groups = group_starts(bits, lanes)
    for m in range(mel_count):
        for a in range(3):
            target, at = targets[a]
            acc = None
            for b in range(3):
                if 0 <= m + b - 1 < mel_count:
                    wing = jnp.concatenate([weight[a, b, pl.ds(g, lanes)] for g in groups])
                    part = jnp.dot(field[m + b - 1], wing, preferred_element_type=f32)
                    acc = part if acc is None else acc + part
            if sources is not None:
                acc = acc + sources[a][m, at : at + total]
            target[m, at : at + total] = acc


def column_kernel(*refs):
    blocks, weight, (field, keep, lower, middle, upper) = refs[:4], refs[4], refs[5:]
    clear_edges(lower, upper, middle.shape[1])
    settle(blocks, field, keep)
    products(field, weight, (0, 2), ((lower, TILE), (middle, 0), (upper, TILE)))


def column_part(blocks, weight, total):
    _, mel_count, frames, lanes = blocks[0].shape
    out_width = weight.shape[3]
    padded = (mel_count, total + 2 * TILE, out_width)
    return call(
        column_kernel,
        (*blocks, weight),
        [whole_spec()] * 5,
        [
            ((mel_count, total, 2 * lanes), bf16),
            ((total, LANES), f32),
            (padded, f32),
            ((mel_count, total, out_width), f32),
            (padded, f32),
        ],
        [whole_spec()] * 5,
        [],
        0,
        8,
    )


def first_kernel(starts, *refs):
    blocks, (weight, scales, keep), sources = refs[:4], refs[4:7], refs[7:10]
    field, middle, stats = refs[10:13]
    lower, upper = refs[13:]
    mel_count, total, _ = field.shape
    out_width = middle.shape[2]
    place = lax.axis_index("tm")
    clear_edges(lower, upper, total)
    settle(blocks, field, None)
    targets = ((lower, TILE), (middle, 0), (upper, TILE))
    products(field, weight, (1, 3), targets, sources)

    def combine(at, sums):
        before, after = same_clip(starts, at, (ROWS, out_width), total)
        mask = widen(keep[pl.ds(at, ROWS)], out_width)
        one, two, num = sums
        num = num + fold(mask)
        for m in range(mel_count):
            rows = joined(lower, middle, upper, m, at, before, after)
            middle[m, pl.ds(at, ROWS)] = rows
            kept = rows * mask
            one = one + fold(kept)
            two = two + fold(kept * rows)
        return one, two, num

    blank = jnp.zeros((TILE, out_width), f32)
    one, two, num = by_rows(total, combine, (blank, blank, blank))
    pixels = column_sum(num) * mel_count
    center, inverse = moments((one, two), keep, pixels)
    stats[0:1] = center
    stats[1:2] = inverse
    stats[2:3] = pixels

def active_kernel(first, pre, stats, scales, keep, out, *picked):
    mel_count, total, width = out.shape
    scale = scales[0:1] * stats[1:2]
    offset = scales[1:2] - stats[0:1] * scale

    def activate(at, carry):
        mask = widen(keep[pl.ds(at, ROWS)], width)
        for m in range(mel_count):
            value = pre[first + m, pl.ds(at, ROWS)] * scale + offset
            out[m, pl.ds(at, ROWS)] = (value * phi_parts(value) * mask).astype(bf16)
        return carry

    by_rows(total, activate, 0)
    for part in picked:
        reach = part.shape[1]
        side = lax.axis_index("tm") % 2
        part[...] = out[:, pl.ds(pl.multiple_of(side * reach, reach), reach)]


def active(first, count, pick, pre, stats, scales, keep):
    _, total, width = pre.shape
    shapes = [(count, total, width)] + [(count, total // 2, width)] * pick
    return call(
        functools.partial(active_kernel, first),
        (pre, stats, scales, keep),
        [whole_spec()] * 4,
        [(shape, bf16) for shape in shapes],
        [whole_spec()] * len(shapes),
        [],
        0,
        4,
    )


def first_block(blocks, weight, scales, keep, sources, starts, total):
    _, mel_count, frames, lanes = blocks[0].shape
    out_width = weight.shape[3]
    padded = (mel_count, total + 2 * TILE, out_width)
    return call(
        first_kernel,
        (starts, *blocks, weight, scales, keep, *sources),
        [whole_spec()] + [whole_spec()] * 10,
        [
            ((mel_count, total, 2 * lanes), bf16),
            ((mel_count, total, out_width), f32),
            ((TILE, out_width), f32),
        ],
        [whole_spec()] * 3,
        [pltpu.VMEM(padded, f32), pltpu.VMEM(padded, f32)],
        0,
        16,
    )


def slope_kernel(pre, stats, scales, keep, slope, hats):
    mel_count, total, width = pre.shape
    center, inverse = stats[0:1], stats[1:2]

    def rows(at, carry):
        mask = widen(keep[pl.ds(at, ROWS)], width)
        for m in range(mel_count):
            normed = (pre[m, pl.ds(at, ROWS)] - center) * inverse
            hats[m, pl.ds(at, ROWS)] = normed
            value = normed * scales[0:1] + scales[1:2]
            slope[m, pl.ds(at, ROWS)] = mask * (phi_parts(value) + value * bell(value))
        return carry

    by_rows(total, rows, 0)


def first_slope(pre, stats, scales, keep):
    return call(
        slope_kernel,
        (pre, stats, scales, keep),
        [whole_spec()] * 4,
        [(pre.shape, f32)] * 2,
        [whole_spec()] * 2,
        [],
        2**28,
        6,
    )


def group_sums(fields, weight, starts, targets, sources=None):
    mel_count, (_, total, width) = len(fields[0]), targets[1][0].shape
    for m in range(mel_count):
        for a in range(3):
            acc = None
            for mels, start in zip(fields, starts):
                for b in range(3):
                    if 0 <= m + b - 1 < mel_count:
                        part = jnp.dot(
                            mels[m + b - 1][...],
                            weight[a, b, pl.ds(start, width)],
                            preferred_element_type=f32,
                        )
                        acc = part if acc is None else acc + part
            if sources is not None:
                acc = acc + sources[a, m]
            target, at = targets[a]
            target[m, at : at + total] = acc


def join_halves(pair, joint):
    side = lax.axis_index("tm") % 2
    half = pair[0].shape[1]
    for part, begin in zip(pair, (side, 1 - side)):
        joint[:, pl.ds(pl.multiple_of(begin * half, half), half)] = part[...]


def group_starts(bits, width):
    column = lax.axis_index("chan")
    return [pl.multiple_of((column ^ bit) * width, width) for bit in bits]


def near_kernel(low, high, low_two, high_two, weight, sums):
    half, _, width = low.shape
    fields = [
        [a.at[k] for a in pair for k in range(half)] for pair in ((low, high), (low_two, high_two))
    ]
    targets = [(sums.at[a], 0) for a in range(3)]
    group_sums(fields, weight, group_starts((0, 1), width), targets)


def near_part(low, high, low_two, high_two, weight):
    half, total, width = low.shape
    return call(
        near_kernel,
        (low, high, low_two, high_two, weight),
        [whole_spec()] * 5,
        [((3, 2 * half, total, width), f32)],
        [whole_spec()],
        [],
        0,
        6,
    )[0]


def far_kernel(far, picked, rest, weight, near, sums, joint):
    half, _, width = far.shape
    join_halves((picked, rest), joint)
    fields = [[a.at[k] for a in (far, joint) for k in range(half)]]
    targets = [(sums.at[a], 0) for a in range(3)]
    group_sums(fields, weight, group_starts((2,), width), targets, near)


def far_part(far, picked, rest, weight, near):
    return call(
        far_kernel,
        (far, picked, rest, weight, near),
        [whole_spec()] * 5,
        [(near.shape, f32)],
        [whole_spec()],
        [pltpu.VMEM(far.shape, bf16)],
        0,
        8,
    )[0]


def run_sums(mask, plain, values):
    width = (plain + values)[0].shape[1]
    terms = list(plain)
    for value in values:
        for _ in range(2):
            term = value.astype(bf16)
            terms.append(term)
            value = value - term.astype(f32)
    out = jnp.dot(mask, jnp.concatenate(terms, axis=1), preferred_element_type=f32)
    parts = [out[:, k * width : (k + 1) * width] for k in range(len(terms))]
    results = parts[: len(plain)]
    for k in range(len(plain), len(parts), 2):
        results.append(parts[k] + parts[k + 1])
    return results


def second_kernel(
    starts, sums, far_two, picked_two, rest_two, weight, keep, scales, *refs
):
    cotangents, (readout, grad, gain_grad, shift_grad) = refs[:-13], refs[-13:-9]
    middle, slope, lower, upper, joint, hold, wide, full, sems = refs[-9:]
    mel_count, total, width = middle.shape
    half = mel_count // 2
    place = lax.axis_index("tm")
    pooled_total = total // 2
    own = readout.shape[0]
    copies = []
    pieces = [(part, i) for part in cotangents for i in range(part.shape[0])]
    bits = gather_bits(len(pieces))
    for k, (part, i) in enumerate(pieces):
        source = place ^ sum(bit for j, bit in enumerate(bits) if k >> j & 1)
        copies.append(
            pltpu.make_async_copy(
                part.at[i],
                full.at[pl.ds(pl.multiple_of(source * own, own), own)],
                sems.at[k],
            )
        )
    for copy in copies:
        copy.start()

    join_halves((picked_two, rest_two), joint)
    clear_edges(lower, upper, total)
    fields = [[a.at[k] for a in (far_two, joint) for k in range(half)]]
    targets = ((lower, TILE), (middle, 0), (upper, TILE))
    group_sums(fields, weight, group_starts((3,), width), targets, sums)
    blank = jnp.zeros((TILE, width), f32)

    def combine(at, sums):
        before, after = same_clip(starts, at, (ROWS, width), total)
        mask = widen(keep[pl.ds(at, ROWS)], width)
        first, second, num = sums
        num = num + fold(mask)
        for m in range(mel_count):
            rows = joined(lower, middle, upper, m, at, before, after)
            middle[m, pl.ds(at, ROWS)] = rows
            kept = rows * mask
            first = first + fold(kept)
            second = second + fold(kept * rows)
        return first, second, num

    first, second, num = by_rows(total, combine, (blank, blank, blank))
    pixels = column_sum(num) * mel_count
    center, inverse = moments((first, second), keep, pixels)
    scale = scales[2:3] * inverse

    def activate(at, carry):
        mask = widen(keep[pl.ds(at, ROWS)], width)
        pooled = jnp.zeros((ROWS, width), f32)
        for m in range(mel_count):
            normed = (middle[m, pl.ds(at, ROWS)] - center) * inverse
            middle[m, pl.ds(at, ROWS)] = normed
            value = normed * scales[2:3] + scales[3:4]
            share = phi_parts(value)
            pooled = pooled + value * share
            slope[m, pl.ds(at, ROWS)] = mask * (share + value * bell(value))
        pooled = pooled * mask
        for c in range(width // LANES):
            hold[c, pl.ds(at, ROWS)] = pooled[:, c * LANES : (c + 1) * LANES]
        return carry

    by_rows(total, activate, 0)

    even = pl.ds(0, pooled_total, stride=2)
    odd = pl.ds(1, pooled_total, stride=2)
    pooled = jnp.concatenate(
        [hold[c, even] + hold[c, odd] for c in range(width // LANES)], axis=1
    ) * (0.5 / mel_count)
    present = widen(keep[even], width)
    square = (pooled_total, pooled_total)
    row = lax.broadcasted_iota(jnp.int32, square, 0)
    col = lax.broadcasted_iota(jnp.int32, square, 1)
    same = row >= col
    back = row <= col
    for start in clip_rows(starts)[1:]:
        start = start[:, :pooled_total]
        crossed = (2 * row < start) != (2 * col < start)
        same = same & ~crossed
        back = back & ~crossed
    ahead, behind = same.astype(f32).astype(bf16), back.astype(f32).astype(bf16)
    exponent = jnp.exp(pooled)
    counts, totals, sums = run_sums(
        ahead, (present.astype(bf16),), (present * pooled, present * exponent)
    )
    mine = pl.ds(pl.multiple_of(place * own, own), own)
    for i, value in enumerate((totals, counts, sums)):
        wide[i] = value
    readout[...] = wide[0, mine] / wide[1, mine] + jnp.log(wide[2, mine])
    for copy in copies:
        copy.wait()
    cotangent = full[...]
    by_count, by_sum = run_sums(behind, (), (cotangent / counts, cotangent / sums))
    down = present * (by_count + exponent * by_sum) * (0.5 / mel_count)
    for c in range(width // LANES):
        hold[c, even] = down[:, c * LANES : (c + 1) * LANES]
        hold[c, odd] = down[:, c * LANES : (c + 1) * LANES]

    def slopes(at, sums):
        down_rows = jnp.concatenate(
            [hold[c, pl.ds(at, ROWS)] for c in range(width // LANES)], axis=1
        )
        plain, along = sums
        for m in range(mel_count):
            step = down_rows * slope[m, pl.ds(at, ROWS)]
            slope[m, pl.ds(at, ROWS)] = step
            plain = plain + fold(step)
            along = along + fold(step * middle[m, pl.ds(at, ROWS)])
        return plain, along

    plain, along = by_rows(total, slopes, (blank, blank))
    plain, along = column_sum(plain), column_sum(along)
    shift_grad[...] = plain
    gain_grad[...] = along
    plain, along = plain / pixels, along / pixels

    def finish(at, carry):
        mask = widen(keep[pl.ds(at, ROWS)], width)
        for m in range(mel_count):
            rows = slope[m, pl.ds(at, ROWS)] - plain - middle[m, pl.ds(at, ROWS)] * along
            grad[m, pl.ds(at, ROWS)] = (mask * (scale * rows)).astype(bf16)
        return carry

    by_rows(total, finish, 0)


def second_block(sums, arrays, weight, keep, scales, starts, cotangents, own):
    _, mel_count, total, width = sums.shape
    padded = (mel_count, total + 2 * TILE, width)
    full = (mel_count, total, width)
    return call(
        second_kernel,
        (starts, sums, *arrays, weight, keep, scales, *cotangents),
        [whole_spec()] + [whole_spec()] * (len(arrays) + 4) + [place_spec()] * len(cotangents),
        [((own, width), f32), (full, bf16), ((1, width), f32), ((1, width), f32)],
        [whole_spec()] * 4,
        [
            pltpu.VMEM(full, f32),
            pltpu.VMEM(full, f32),
            pltpu.VMEM(padded, f32),
            pltpu.VMEM(padded, f32),
            pltpu.VMEM(arrays[0].shape, bf16),
            pltpu.VMEM((width // LANES, total, LANES), f32),
            pltpu.VMEM((3, total // 2, width), f32),
            pltpu.VMEM((total // 2, width), f32),
            pltpu.SemaphoreType.DMA((sum(part.shape[0] for part in cotangents),)),
        ],
        0,
        20,
    )


def wings_kernel(weight, wings, sems):
    width = wings.shape[3]
    copies = []
    for i, start in enumerate(group_starts((2, 0), width)):
        for a in range(3):
            for b in range(3):
                copies.append(
                    pltpu.make_async_copy(
                        weight.at[a, b, pl.ds(start, width)], wings.at[i, 3 * a + b], sems.at[len(copies)]
                    )
                )
    for copy in copies:
        copy.start()
    for copy in copies:
        copy.wait()


def bring_wings(weight):
    width = weight.shape[3]
    return call(
        wings_kernel,
        (weight,),
        [place_spec()],
        [((2, 9, width, width), bf16)],
        [whole_spec()],
        [pltpu.SemaphoreType.DMA((18,))],
        0,
        4,
    )[0]


def back_sums(field, wing, mels, reach, first, targets, sources=None):
    mel_count = field.shape[0]
    for k, n in enumerate(mels):
        for a in range(3):
            acc = None
            for b in range(3):
                if 0 <= n - b + 1 < mel_count:
                    part = lax.dot_general(
                        field[n - b + 1, pl.ds(first, reach)],
                        wing(a, b),
                        (((1,), (1,)), ((), ())),
                        preferred_element_type=f32,
                    )
                    acc = part if acc is None else acc + part
            if sources is not None:
                acc = sources[a, k] + acc
            target, at = targets[a]
            target[k, at : at + reach] = acc


def half_rows(total, reach):
    side = lax.axis_index("tm") % 2
    return (
        pl.multiple_of(side * (total - reach), 16),
        pl.multiple_of(side * (reach - total // 2), 16),
    )


def ahead_kernel(bit, mels, one, weight, sums):
    _, total, width = one.shape
    reach = sums.shape[2]
    first, _ = half_rows(total, reach)
    (start,) = group_starts((bit,), width)
    targets = [(sums.at[a], 0) for a in range(3)]
    back_sums(one, lambda a, b: weight[a, b, pl.ds(start, width)], mels, reach, first, targets)


def hidden_ahead(bit, mels, one, weight):
    _, total, width = one.shape
    return call(
        functools.partial(ahead_kernel, bit, mels),
        (one, weight),
        [whole_spec()] * 2,
        [((3, len(mels), total // 2 + 16, width), f32)],
        [whole_spec()],
        [],
        0,
        4,
    )[0]


def half_kernel(bit, mels, starts, two, wings, sums, out, lower, middle, upper):
    _, total, width = two.shape
    reach = sums.shape[2]
    first, skip = half_rows(total, reach)
    for k in range(len(mels)):
        for ref in (lower, upper):
            ref[k, :TILE] = jnp.zeros((TILE, width), f32)
            ref[k, TILE + reach :] = jnp.zeros((TILE, width), f32)
    wing = wings.at[0 if bit else 1]
    targets = ((upper, TILE), (middle, 0), (lower, TILE))
    back_sums(two, lambda a, b: wing[3 * a + b], mels, reach, first, targets, sums)

    def combine(at, carry):
        near = pl.multiple_of(at + skip, TILE)
        before, after = same_clip(starts, first + near, (ROWS, width), total)
        for k in range(len(mels)):
            rows = joined(lower, middle, upper, k, near, before, after)
            out[k, pl.ds(at, ROWS)] = rows.astype(out.dtype)
        return carry

    by_rows(total // 2, combine, 0)


def hidden_half(bit, mels, two, wings, sums, starts, kind):
    _, total, width = two.shape
    reach, count = sums.shape[2], len(mels)
    padded = (count, reach + 2 * TILE, width)
    return call(
        functools.partial(half_kernel, bit, mels),
        (starts, two, wings, sums),
        [whole_spec()] * 4,
        [((count, total // 2, width), kind)],
        [whole_spec()],
        [
            pltpu.VMEM(padded, f32),
            pltpu.VMEM((count, reach, width), f32),
            pltpu.VMEM(padded, f32),
        ],
        0,
        8,
    )[0]


def back_kernel(bit, mels, starts, one, two, weight, wings, out, lower, middle, upper):
    mel_count, total, width = one.shape
    (start,) = group_starts((bit,), width)
    wing = wings.at[0 if bit else 1]
    clear_edges(lower, upper, total)
    for k, n in enumerate(mels):
        for a, (target, at) in enumerate(((upper, TILE), (middle, 0), (lower, TILE))):
            acc = None
            for field, matrix in (
                (one, lambda b, a=a: weight[a, b, pl.ds(start, width)]),
                (two, lambda b, a=a: wing[3 * a + b]),
            ):
                for b in range(3):
                    if 0 <= n - b + 1 < mel_count:
                        part = lax.dot_general(
                            field[n - b + 1],
                            matrix(b),
                            (((1,), (1,)), ((), ())),
                            preferred_element_type=f32,
                        )
                        acc = part if acc is None else acc + part
            target[k, at : at + total] = acc

    def combine(at, carry):
        before, after = same_clip(starts, at, (ROWS, width), total)
        for k in range(len(mels)):
            rows = joined(lower, middle, upper, k, at, before, after)
            out[k, pl.ds(at, ROWS)] = rows.astype(out.dtype)
        return carry

    by_rows(total, combine, 0)


def hidden_back(bit, mels, one, two, weight, wings, starts, kind):
    _, total, width = one.shape
    count = len(mels)
    padded = (count, total + 2 * TILE, width)
    return call(
        functools.partial(back_kernel, bit, mels),
        (starts, one, two, weight, wings),
        [whole_spec()] * 5,
        [((count, total, width), kind)],
        [whole_spec()],
        [
            pltpu.VMEM(padded, f32),
            pltpu.VMEM((count, total, width), f32),
            pltpu.VMEM(padded, f32),
        ],
        0,
        14,
    )[0]


def norm_kernel(mine, low, picked, rest, slope, hats, stats, scales, keep, *refs):
    grad, window, gain_grad, shift_grad, padded, held = refs
    mel_count, total, width = mine.shape
    inverse, pixels = stats[1:2], stats[2:3]
    blank = jnp.zeros((TILE, width), f32)
    edge = (padded.shape[1] - total) // 2
    reach = window.shape[1]
    frames = reach - 2 * edge
    place = lax.axis_index("tm")

    half = mel_count // 2

    def add(field, base, mels):
        def slopes(at, sums):
            plain, along = sums
            place_rows = pl.ds(pl.multiple_of(base + at, ROWS), ROWS)
            for k, m in enumerate(mels):
                rows = mine[m, place_rows] + field[k, pl.ds(at, ROWS)].astype(f32)
                step = rows * slope[m, place_rows]
                held[m, place_rows] = step
                plain = plain + fold(step)
                along = along + fold(step * hats[m, place_rows])
            return plain, along

        return slopes

    side = place % 2
    sums = by_rows(total, add(low, 0, range(half)), (blank, blank))
    upper = range(half, mel_count)
    parts = []
    for field, base in ((picked, side), (rest, 1 - side)):
        parts.append(by_rows(total // 2, add(field, base * (total // 2), upper), (blank, blank)))
    plain, along = [
        a + jnp.where(side == 0, b + c, c + b) for a, b, c in zip(sums, parts[0], parts[1])
    ]
    plain, along = column_sum(plain), column_sum(along)
    shift_grad[...] = plain
    gain_grad[...] = along
    plain, along = plain / pixels, along / pixels
    scale = scales[0:1] * inverse
    for m in range(mel_count):
        padded[m, :edge] = jnp.zeros((edge, width), bf16)
        padded[m, edge + total :] = jnp.zeros((edge, width), bf16)

    def finish(at, carry):
        mask = widen(keep[pl.ds(at, ROWS)], width)
        for m in range(mel_count):
            rows = held[m, pl.ds(at, ROWS)] - plain - hats[m, pl.ds(at, ROWS)] * along
            rows = (mask * (scale * rows)).astype(bf16)
            grad[m, pl.ds(at, ROWS)] = rows
            padded[m, pl.ds(pl.multiple_of(at + edge, 16), ROWS)] = rows
        return carry

    by_rows(total, finish, 0)
    for m in range(mel_count):
        window[m] = padded[m, pl.ds(pl.multiple_of(place * frames, frames), reach)]


def norm_back_first(mine, low, picked, rest, slope, pre, stats, scales, keep, frames):
    mel_count, total, width = mine.shape
    edge = 16
    return call(
        norm_kernel,
        (mine, low, picked, rest, slope, pre, stats, scales, keep),
        [whole_spec()] * 9,
        [
            ((mel_count, total, width), bf16),
            ((mel_count, frames + 2 * edge, width), bf16),
            ((1, width), f32),
            ((1, width), f32),
        ],
        [whole_spec()] * 4,
        [pltpu.VMEM((mel_count, total + 2 * edge, width), bf16), pltpu.VMEM(mine.shape, f32)],
        2**28,
        12,
    )


def spread_kernel(starts, grad, steps, spaced):
    mel_count, total, width = grad.shape
    for m in range(mel_count):
        spaced[m, :TILE] = jnp.zeros((TILE, width), f32)
        spaced[m, TILE + total :] = jnp.zeros((TILE, width), f32)

    def expand(at, carry):
        for m in range(mel_count):
            rows = grad[m, pl.ds(at, ROWS)].astype(f32)
            spaced[m, pl.ds(pl.multiple_of(at + TILE, TILE), ROWS)] = rows
        return carry

    by_rows(total, expand, 0)

    def shift(at, carry):
        before, after = same_clip(starts, at, (ROWS, width), total)
        for m in range(mel_count):
            rows = spaced[m, pl.ds(at, ROWS + 2 * TILE)]
            ahead = jnp.where(after, rows[TILE + 1 : TILE + 1 + ROWS], 0.0)
            behind = jnp.where(before, rows[TILE - 1 : TILE - 1 + ROWS], 0.0)
            steps[0, m, pl.ds(at, ROWS)] = ahead.astype(bf16)
            steps[1, m, pl.ds(at, ROWS)] = behind.astype(bf16)
        return carry

    by_rows(total, shift, 0)


def spread(grad, starts):
    mel_count, total, width = grad.shape
    return call(
        spread_kernel,
        (starts, grad),
        [whole_spec()] * 2,
        [((2, mel_count, total, width), bf16)],
        [whole_spec()],
        [pltpu.VMEM((mel_count, total + 2 * TILE, width), f32)],
        0,
        6,
    )[0]


def weight_kernel(layout, halves, *refs):
    count = len(refs) - 7
    fields, grad, steps = list(refs[:count]), refs[count], refs[count + 1]
    out, results, joint, sems, move_sems = refs[count + 2 :]
    mel_count, total, out_width = grad.shape
    width = results.shape[2]
    side = lax.axis_index("tm") % 2
    column = lax.axis_index("chan")
    moves = []
    for i, pair in enumerate(halves):
        for index, begin in zip(pair, (side, 1 - side)):
            rows = pl.ds(pl.multiple_of(begin * (total // 2), total // 2), total // 2)
            moves.append(
                pltpu.make_async_copy(fields[index], joint.at[i, :, rows], move_sems.at[len(moves)])
            )
            moves[-1].start()
        fields.append(joint.at[i])
    copies = [[], []]
    for i, (places, pieces) in enumerate(layout):
        slot = i % 2
        for copy in copies[slot]:
            copy.wait()
        copies[slot] = []
        each = width // len(places)
        if any(piece[0] >= count for piece in pieces):
            while moves:
                moves.pop().wait()
        for a in range(3):
            for b in range(3):
                right = grad if a == 1 else steps.at[a // 2]
                acc = None
                for m in range(mel_count):
                    if 0 <= m + b - 1 < mel_count:
                        index, k, lane = pieces[m + b - 1]
                        part = lax.dot_general(
                            fields[index][k, :, lane : lane + width],
                            right[m],
                            (((0,), (0,)), ((), ())),
                            preferred_element_type=f32,
                        )
                        acc = part if acc is None else acc + part
                tap = 3 * a + b
                results[slot, tap] = acc
                for j, bit in enumerate(places):
                    start = pl.multiple_of((column ^ bit) * each, each)
                    copies[slot].append(
                        pltpu.make_async_copy(
                            results.at[slot, tap, j * each : (j + 1) * each],
                            out.at[tap, pl.ds(start, each)],
                            sems.at[slot, tap, j],
                        )
                    )
                    copies[slot][-1].start()
    for copy in copies[0] + copies[1]:
        copy.wait()


def weight_back(layout, halves, fields, grad, steps, in_width):
    mel_count, total, out_width = grad.shape
    width = in_width // len(layout)
    joint = (max(len(halves), 1), mel_count // 2, total, width)
    out = call(
        functools.partial(weight_kernel, layout, halves),
        (*fields, grad, steps),
        [whole_spec()] * (len(fields) + 2),
        [((9, in_width, out_width), f32)],
        [place_spec()],
        [
            pltpu.VMEM((2, 9, width, out_width), f32),
            pltpu.VMEM(joint, bf16),
            pltpu.SemaphoreType.DMA((2, 9, 2)),
            pltpu.SemaphoreType.DMA((max(2 * len(halves), 1),)),
        ],
        0,
        12,
    )[0]
    return out.reshape(3, 3, in_width, out_width)


def input_kernel(starts, one, two, weight, weight_two, mine, other, lower, middle, upper):
    mel_count, reach, width = one.shape
    frames, lanes = mine.shape[1], mine.shape[2]
    edge = (reach - frames) // 2
    total = frames * lax.axis_size("tm")
    place = lax.axis_index("tm")
    groups = group_starts((2, 0), lanes)
    for a in range(3):
        target, shift = ((upper, TILE), (middle, 0), (lower, TILE))[a]
        for b in (1, 0, 2):
            low, count = ((1, mel_count - 1), (0, mel_count), (0, mel_count - 1))[b]
            acc = None
            for field, matrix in ((one, weight), (two, weight_two)):
                rows = field[low : low + count].reshape(count * reach, width)
                wing = jnp.concatenate([matrix[a, b, pl.ds(g, lanes)] for g in groups])
                part = lax.dot_general(
                    rows, wing, (((1,), (1,)), ((), ())), preferred_element_type=f32
                )
                acc = part if acc is None else acc + part
            acc = acc.reshape(count, reach, 2 * lanes)
            for k in range(count):
                n = low + k + b - 1
                if b == 1:
                    target[n, shift : shift + reach] = acc[k]
                else:
                    target[n, shift : shift + reach] += acc[k]
    before, after = same_clip(starts, place * frames, (frames, 2 * lanes), total)
    for m in range(mel_count):
        low = lower[m, TILE + edge - 1 : TILE + edge - 1 + frames]
        high = upper[m, TILE + edge + 1 : TILE + edge + 1 + frames]
        rows = (
            middle[m, edge : edge + frames]
            + jnp.where(before, low, 0.0)
            + jnp.where(after, high, 0.0)
        )
        other[m] = rows[:, :lanes]
        mine[m] = rows[:, lanes:]


def input_back(one, two, weight, weight_two, starts, frames, lanes):
    mel_count, reach, width = one.shape
    shape = (mel_count, frames, lanes)
    return call(
        input_kernel,
        (starts, one, two, weight, weight_two),
        [whole_spec()] + [whole_spec()] * 4,
        [(shape, f32), (shape, f32)],
        [whole_spec()] * 2,
        [
            pltpu.VMEM((mel_count, reach + 2 * TILE, 2 * lanes), f32),
            pltpu.VMEM((mel_count, reach, 2 * lanes), f32),
            pltpu.VMEM((mel_count, reach + 2 * TILE, 2 * lanes), f32),
        ],
        0,
        10,
    )


def close_kernel(mine, other, keep, *refs):
    count = len(refs) // 2
    small, out, small_out = refs[:count], refs[count], refs[count + 1 :]
    mel_count, frames, lanes = mine.shape
    begin = pl.multiple_of(lax.axis_index("tm") * frames, frames)
    mask = keep[pl.ds(begin, frames)]
    for m in range(mel_count):
        out[:, m, :] = (mine[m] + other[m]) * mask
    for source, target in zip(small, small_out):
        target[...] = source[...]


def close(mine, other, keep, small):
    mel_count, frames, lanes = mine.shape
    return call(
        close_kernel,
        (mine, other, keep, *small),
        [whole_spec()] * (3 + len(small)),
        [((frames, mel_count, lanes), f32)] + [(a.shape, f32) for a in small],
        [whole_spec()] * (1 + len(small)),
        [],
        0,
        4,
    )


def whole_frames(
    features,
    conv1_weight,
    norm1_gain,
    norm1_bias,
    conv2_weight,
    norm2_gain,
    norm2_bias,
    clip_starts,
    valid,
    readout_grad,
):
    frames, mel_count, lanes = features.shape
    places = lax.axis_size("tm")
    total = frames * places
    conv1_weight = bring(conv1_weight)
    starts = jnp.broadcast_to(clip_starts.astype(f32)[:, None], clip_starts.shape + norm1_gain.shape)
    norms = jnp.stack([norm1_gain, norm1_bias, norm2_gain, norm2_bias])
    table = jnp.concatenate([norms, starts])

    marked = jnp.where(valid[:, None, None] > 0, features, jnp.asarray(ABSENT, bf16))
    own = jnp.transpose(marked, (1, 0, 2))
    pieces = [swap(own, "tm", 2 * k) for k in range(1, places // 2)]
    along = jnp.stack([own] + pieces)
    near = [
        along,
        swap(along, "tm", 1),
        swap(along, "chan", 2),
        swap_both(along, "tm", 1, "chan", 2),
    ]
    readout_grad, _ = lax.optimization_barrier((readout_grad, pieces[0]))
    bits = gather_bits(places)
    cotangents = [readout_grad[None]]
    cotangents.append(swap(cotangents[0], "tm", bits[0]))
    near[3], conv1_weight, table, cotangents = lax.optimization_barrier(
        (near[3], conv1_weight, table, cotangents)
    )
    others = [swap(block, "chan", 1) for block in near]
    column, keep, *sources = column_part(near, conv1_weight, total)
    column, others = lax.optimization_barrier((column, others))
    other_conv2 = swap(conv2_weight, "chan", 1)
    others, other_conv2 = lax.optimization_barrier((others, other_conv2))

    other_column, pre, stats = first_block(
        others, conv1_weight, table, keep, sources, table, total
    )
    half = mel_count // 2
    high, picked = active(half, half, 1, pre, stats, table, keep)
    picked, low_pre = lax.optimization_barrier((picked, pre))
    (low,) = active(0, half, 0, low_pre, stats, table, keep)
    fields1 = (column, other_column)

    far_picked = swap(picked, "chan", 2)
    far = swap(low, "chan", 2)
    far_rest = swap(far_picked, "tm", 1)

    low_two, high_two = swap(low, "chan", 1), swap(high, "chan", 1)
    near = near_part(low, high, low_two, high_two, conv2_weight)
    far_picked, near, cotangents = lax.optimization_barrier((far_picked, near, cotangents))
    picked_two = swap(far_picked, "chan", 1)
    other_conv2, near = lax.optimization_barrier((other_conv2, near))
    wings = bring_wings(other_conv2)
    for bit in bits[1:-1]:
        cotangents.append(swap(jnp.concatenate(cotangents), "tm", bit))
    picked_two, pre, cotangents, wings = lax.optimization_barrier(
        (picked_two, pre, cotangents, wings)
    )
    cotangents.append(swap(jnp.concatenate(cotangents), "tm", bits[-1]))
    slope, pre = first_slope(pre, stats, table, keep)
    far, far_rest, slope, pre, cotangents = lax.optimization_barrier(
        (far, far_rest, slope, pre, cotangents)
    )
    far_two, rest_two = swap(far, "chan", 1), swap(far_rest, "chan", 1)
    sums = far_part(far, far_picked, far_rest, conv2_weight, near)
    far_two, rest_two, sums = lax.optimization_barrier((far_two, rest_two, sums))

    readout, grad2, gain2_grad, shift2_grad = second_block(
        sums,
        (far_two, picked_two, rest_two),
        conv2_weight,
        keep,
        table,
        table,
        cotangents,
        readout_grad.shape[0],
    )
    grad2_near = swap(grad2, "chan", 1)
    steps2 = spread(grad2, table)
    ahead = hidden_ahead(2, (2, 3), grad2, conv2_weight)
    grad2_near, steps2, ahead = lax.optimization_barrier((grad2_near, steps2, ahead))
    away = hidden_half(2, (2, 3), grad2_near, wings, ahead, table, bf16)
    came_picked = swap(away, "chan", 2)
    back = functools.partial(
        hidden_back, one=grad2, two=grad2_near, weight=conv2_weight, starts=table
    )
    away_low = back(2, (0, 1), wings=wings, kind=bf16)
    came_low = swap(away_low, "chan", 2)

    away_low, wings = lax.optimization_barrier((away_low, wings))
    mine = back(0, (0, 1, 2, 3), wings=wings, kind=f32)
    came_picked, mine, conv1_weight = lax.optimization_barrier((came_picked, mine, conv1_weight))
    came_rest = swap(came_picked, "tm", 1)
    other_conv1 = swap(conv1_weight, "chan", 1)
    fields = (low, high, low_two, high_two)
    fields += (far, far_picked, far_rest, far_two, picked_two, rest_two)
    layout = [
        ((0,), [(0, 0, 0), (0, 1, 0), (1, 0, 0), (1, 1, 0)]),
        ((1,), [(2, 0, 0), (2, 1, 0), (3, 0, 0), (3, 1, 0)]),
        ((2,), [(4, 0, 0), (4, 1, 0), (10, 0, 0), (10, 1, 0)]),
        ((3,), [(7, 0, 0), (7, 1, 0), (11, 0, 0), (11, 1, 0)]),
    ]
    weight2_grad = weight_back(
        layout, ((5, 6), (8, 9)), fields, grad2, steps2, conv2_weight.shape[2]
    )
    came_low, came_rest, mine, weight2_grad, other_conv1 = lax.optimization_barrier(
        (came_low, came_rest, mine, weight2_grad, other_conv1)
    )

    grad1, window, gain1_grad, shift1_grad = norm_back_first(
        mine, came_low, came_picked, came_rest, slope, pre, stats, table, keep, frames
    )
    window_near = swap(window, "chan", 1)
    steps1 = spread(grad1, table)
    window_near, steps1 = lax.optimization_barrier((window_near, steps1))
    input_mine, input_away = input_back(
        window, window_near, conv1_weight, other_conv1, table, frames, lanes
    )
    input_came = swap(input_away, "chan", 2)
    layout = [(bits, [(i, m, 0) for m in range(mel_count)]) for i, bits in enumerate(((0, 2), (1, 3)))]
    weight1_grad = weight_back(layout, (), fields1, grad1, steps1, conv1_weight.shape[2])
    input_came, weight1_grad = lax.optimization_barrier((input_came, weight1_grad))
    input_grad, readout, gain1_grad, shift1_grad, gain2_grad, shift2_grad = close(
        input_mine,
        input_came,
        keep,
        (readout, gain1_grad, shift1_grad, gain2_grad, shift2_grad),
    )
    return (
        readout,
        input_grad,
        weight1_grad,
        gain1_grad[0],
        shift1_grad[0],
        weight2_grad,
        gain2_grad[0],
        shift2_grad[0],
    )


def fits_whole(frames, mels, places, columns, widths):
    return (
        places > 1
        and places & (places - 1) == 0
        and columns == 4
        and frames % ROWS == 0
        and frames * places <= 512
        and mels == 4
        and all(w % (columns * LANES) == 0 for w in widths)
        and widths[1] == columns * 256
    )


def shards(*arrays):
    features, conv1_weight, conv2_weight = arrays[0], arrays[1], arrays[4]
    if fits_whole(
        features.shape[0],
        features.shape[1],
        lax.axis_size("tm"),
        lax.axis_size("chan"),
        (conv1_weight.shape[2], conv2_weight.shape[2]),
    ):
        return whole_frames(*arrays)
    return split_frames(*arrays)


def solution(mesh):
    return jax.shard_map(
        shards,
        mesh=mesh,
        in_specs=(
            P("tm", None, "chan"),
            P(None, None, None, "chan"),
            P("chan"),
            P("chan"),
            P(None, None, None, "chan"),
            P("chan"),
            P("chan"),
            P(),
            P("tm"),
            P("tm", "chan"),
        ),
        out_specs=(
            P("tm", "chan"),
            P("tm", None, "chan"),
            P(None, None, None, "chan"),
            P("chan"),
            P("chan"),
            P(None, None, None, "chan"),
            P("chan"),
            P("chan"),
        ),
        check_vma=False,
    )
```
